32 devices in a mesh: dp: 8 (over z, x), tensor: 4 (over y, core).
Axes of the slice: x: 2, y: 2, z: 4, core: 2. Of those that a mesh axis runs over, the one named last changes fastest.
Arguments:
- latent: bfloat16 [8192, 1408], P(('dp', 'tensor')), may hold values from -6 to 6
- skip_states: bfloat16 [8192, 1408], P(('dp', 'tensor')), may hold values from -6 to 6
- text_states: bfloat16 [8, 333, 1024], P('dp'), may hold values from -6 to 6
- condition: bfloat16 [8, 1408], P('dp'), may hold values from -3 to 3
- teacher: bfloat16 [8192, 1408], P(('dp', 'tensor')), may hold values from -9 to 9
- loss_mask: int32 [8192], P(('dp', 'tensor')), may hold values 0 or 1
- true_counts: int32 [8], P('dp'), may hold values from 341 to 1024, as said below
- positions: int32 [2, 8192], P(None, 'dp'), may hold values from 0 to 63, as said below
- skip_proj: bfloat16 [2816, 1408], P('dp', 'tensor'), may hold values from -0.109375 to 0.109375
- shift_proj: bfloat16 [1408, 1408], P('dp'), may hold values from -0.15625 to 0.15625
- self_project: bfloat16 [1408, 3, 1408], P('dp', None, 'tensor'), may hold values from -0.15625 to 0.15625
- self_output: bfloat16 [1408, 1408], P('tensor', 'dp'), may hold values from -0.21875 to 0.21875
- cross_query: bfloat16 [1408, 1408], P('dp', 'tensor'), may hold values from -0.15625 to 0.15625
- cross_keyval: bfloat16 [1024, 2, 1408], P('dp', None, 'tensor'), may hold values from -0.1875 to 0.1875
- cross_output: bfloat16 [1408, 1408], P('tensor', 'dp'), may hold values from -0.21875 to 0.21875
- hidden_up: bfloat16 [1408, 6144], P('dp', 'tensor'), may hold values from -0.15625 to 0.15625
- hidden_down: bfloat16 [6144, 1408], P('tensor', 'dp'), may hold values from -0.078125 to 0.078125
- norm_gain: float32 [4, 1408], replicated, may hold values from 0.5 to 1.5
- norm_bias: float32 [4, 1408], replicated, may hold values from -1.8 to 1.8
- head_gain: float32 [4, 88], replicated, may hold values from 1 to 2
- head_bias: float32 [4, 88], replicated, may hold values from -1.8 to 1.8
- column_bias: float32 [5, 1408], replicated, may hold values from -0.9 to 0.9
- hidden_bias: float32 [6144], replicated, may hold values from -1.8 to 1.8
- row_bias: float32 [4, 1408], replicated, may hold values from -0.9 to 0.9
Outputs:
- block_out: bfloat16 [8192, 1408], P(('dp', 'tensor'))
- grad_latent: float32 [8192, 1408], P(('dp', 'tensor'))
- grad_skip: float32 [8192, 1408], P(('dp', 'tensor'))
- grad_text: float32 [8, 333, 1024], P('dp')
- grad_skip_proj: float32 [2816, 1408], P('dp', 'tensor')
- grad_shift_proj: float32 [1408, 1408], P('dp')
- grad_self_project: float32 [1408, 3, 1408], P('dp', None, 'tensor')
- grad_self_output: float32 [1408, 1408], P('tensor', 'dp')
- grad_cross_query: float32 [1408, 1408], P('dp', 'tensor')
- grad_cross_keyval: float32 [1024, 2, 1408], P('dp', None, 'tensor')
- grad_cross_output: float32 [1408, 1408], P('tensor', 'dp')
- grad_hidden_up: float32 [1408, 6144], P('dp', 'tensor')
- grad_hidden_down: float32 [6144, 1408], P('tensor', 'dp')
- grad_norm_gain: float32 [4, 1408], replicated
- grad_norm_bias: float32 [4, 1408], replicated
- grad_head_gain: float32 [4, 88], replicated
- grad_head_bias: float32 [4, 88], replicated
- grad_column_bias: float32 [5, 1408], replicated
- grad_hidden_bias: float32 [6144], replicated
- grad_row_bias: float32 [4, 1408], replicated
The draws below stay inside these ranges and needn't reach their ends.
Inputs may be any that keep to these rules, and one draw needn't show every extreme that they name: The loss counts the first true_counts tokens of each latent; the first latent counts 1024 // 3 of them and the last all 1024. positions[0] is a token's grid row and positions[1] its grid column, the grid of each latent being filled row by row; its width may differ between latents.
All inputs are finite; a program needn't handle non-finite values. No bound on the sum of `loss_mask` on one device may be relied on, other than what follows from the above.
Results may differ from the reference program's by a relative error of at most 0.024.
Values may be sent and summed in bfloat16 or wider, within the bound.
A program may use at most 256 MiB of HBM per device.

```python
import math
import jax
import jax.numpy as jnp
from jax import lax

D = 1408
HEADS = 16
HD = 88
FF = 6144
DT = 1024
TEXT = 333
SEQ = 1024
LATENTS = 8
TOKENS = 8192


def draw_true_counts(key, part):
    key = jax.random.fold_in(key, 11)
    lowest = SEQ // 3
    number = jnp.arange(LATENTS)
    base_count = lowest + (SEQ - lowest) * number // max(LATENTS - 1, 1)
    jitter = jax.random.randint(key, (LATENTS,), 0, SEQ // 8 + 1)
    at_edges = (number == 0) | (number == LATENTS - 1)
    return jnp.where(at_edges, base_count, jnp.maximum(base_count - jitter, lowest)).astype(jnp.int32)


def draw_positions(key, part):
    key = jax.random.fold_in(key, 23)
    number = jnp.arange(LATENTS)
    picked = jax.random.randint(key, (LATENTS,), 0, 3)
    picked = jnp.where(number == 0, 0, picked)
    columns_per = SEQ // 64 * jnp.where(picked == 0, 1, jnp.where(picked == 1, 2, 4))
    token_place = jnp.arange(SEQ)
    row_index = token_place[None, :] // columns_per[:, None]
    column_index = token_place[None, :] % columns_per[:, None]
    return jnp.stack([row_index, column_index]).reshape(2, TOKENS).astype(jnp.int32)


def place_ends(drawn, rng, least, high):
    longest = drawn.shape.index(max(drawn.shape))
    spots = []
    for shift in (0, 1):
        where = [jax.random.randint(jax.random.fold_in(rng, axis), (), 0, length) for axis, length in enumerate(drawn.shape)]
        where[longest] = (where[longest] + shift) % drawn.shape[longest]
        spots.append(tuple(where))
    return drawn.at[spots[0]].set(least).at[spots[1]].set(high)


def shard_levels(key, extent, pieces, least, largest):
    def one(axis_at, parts):
        draws = jax.random.uniform(jax.random.fold_in(jax.random.fold_in(key, 6), axis_at), (parts,), jnp.float32, least / len(pieces), largest / len(pieces))
        return jnp.repeat(jnp.exp(draws), extent[axis_at] // parts).reshape((-1,) + (1,) * (len(extent) - axis_at - 1))

    loudness = one(*pieces[0])
    for cut in pieces[1:]:
        loudness = loudness * one(*cut)
    return loudness


def gaussian(own_key, extent, scale, limit, shards=(), kind=jnp.bfloat16):
    factor_of = shard_levels(own_key, extent, shards, -0.22, 0.18) if shards else 1.0
    drawn = jax.random.normal(own_key, extent, jnp.float32) * scale * factor_of
    return jnp.minimum(jnp.maximum(drawn, -limit), limit).astype(kind)


def setup_inputs(seed: int = 0) -> dict:
    keys = jax.random.split(jax.random.key(seed), 25)
    return {
        "latent": gaussian(keys[0], (TOKENS, D), 1.0, 6.0, ((0, 32),)),
        "skip_states": gaussian(keys[1], (TOKENS, D), 1.0, 6.0, ((0, 32),)),
        "text_states": gaussian(keys[2], (LATENTS, TEXT, DT), 1.0, 6.0, ((0, 8),)),
        "condition": gaussian(keys[3], (LATENTS, D), 0.5, 3.0, ((0, 8),)),
        "teacher": gaussian(keys[4], (TOKENS, D), 1.5, 9.0, ((0, 32),)),
        "loss_mask": place_ends((jax.random.randint(keys[5], (TOKENS,), 0, 8) < 7).astype(jnp.int32), jax.random.fold_in(keys[5], 1), 0, 1),
        "true_counts": draw_true_counts(jax.random.fold_in(keys[24], 71), 0),
        "positions": draw_positions(jax.random.fold_in(keys[24], 71), 0),
        "skip_proj": gaussian(keys[8], (2 * D, D), (2 * D) ** -0.5, 0.109375, ((0, 8), (1, 4))),
        "shift_proj": gaussian(keys[9], (D, D), D ** -0.5, 0.15625, ((0, 8),)),
        "self_project": gaussian(keys[10], (D, 3, D), D ** -0.5, 0.15625, ((0, 8), (2, 4))),
        "self_output": gaussian(keys[11], (D, D), (D // 2) ** -0.5, 0.21875, ((0, 4), (1, 8))),
        "cross_query": gaussian(keys[12], (D, D), D ** -0.5, 0.15625, ((0, 8), (1, 4))),
        "cross_keyval": gaussian(keys[13], (DT, 2, D), DT ** -0.5, 0.1875, ((0, 8), (2, 4))),
        "cross_output": gaussian(keys[14], (D, D), (D // 2) ** -0.5, 0.21875, ((0, 4), (1, 8))),
        "hidden_up": gaussian(keys[15], (D, FF), D ** -0.5, 0.15625, ((0, 8), (1, 4))),
        "hidden_down": gaussian(keys[16], (FF, D), FF ** -0.5, 0.078125, ((0, 4), (1, 8))),
        "norm_gain": jnp.clip(1.0 + 0.1 * jax.random.normal(keys[17], (4, D), jnp.float32), 0.5, 1.5),
        "norm_bias": gaussian(keys[18], (4, D), 0.3, 1.8, (), jnp.float32),
        "head_gain": jnp.clip(jax.random.uniform(keys[19], (4, HD), jnp.float32, 1.0, 2.0), 1.0, 2.0),
        "head_bias": gaussian(keys[20], (4, HD), 0.3, 1.8, (), jnp.float32),
        "column_bias": gaussian(keys[21], (5, D), 0.15, 0.9, (), jnp.float32),
        "hidden_bias": gaussian(keys[22], (FF,), 0.3, 1.8, (), jnp.float32),
        "row_bias": gaussian(keys[23], (4, D), 0.15, 0.9, (), jnp.float32),
    }


EPSILON = 1e-06
HIGH = lax.Precision.HIGHEST

@jax.custom_vjp
def low(v):
    return lax.optimization_barrier(v.astype(jnp.bfloat16)).astype(jnp.float32)

@jax.custom_vjp
def low_back(v):
    return v

def low_keep(v):
    return (low(v), None)

def low_pass(kept, grad):
    return (grad,)

def back_keep(v):
    return (v, None)

def back_low(kept, grad):
    return (low(grad),)
low.defvjp(low_keep, low_pass)
low_back.defvjp(back_keep, back_low)

def layer_norm(values, gain_vector, offset):
    centred = values - lax.optimization_barrier(jnp.mean(values, axis=-1, keepdims=True))
    spread = lax.optimization_barrier(jnp.mean(centred * centred, axis=-1, keepdims=True))
    return centred * lax.rsqrt(spread + EPSILON) * gain_vector + offset

def rotary_tables(positions, head_size):
    quarter = head_size // 4
    frequency = 10000.0 ** (-jnp.arange(quarter, dtype=jnp.float32) / quarter)
    angles = positions.astype(jnp.float32)[:, :, None] * frequency[None, None, :]
    angles = jnp.repeat(angles, 2, axis=2)
    angles = jnp.concatenate([angles[0], angles[1]], axis=1)
    return (jnp.cos(angles), jnp.sin(angles))

def rotate(values, cosine_table, sine_table):
    value_pairs = values.reshape(values.shape[:-1] + (values.shape[-1] // 2, 2))
    turned = jnp.stack([-value_pairs[..., 1], value_pairs[..., 0]], axis=-1).reshape(values.shape)
    return values * cosine_table[:, None, :] + turned * sine_table[:, None, :]

def product(left_side, right_side):
    return jnp.dot(left_side, right_side, precision=HIGH, preferred_element_type=jnp.float32)

def attend(operands):
    query_rows, key_rows, value_rows = operands
    score_scale = HD ** (-0.5)
    scores = low_back(jnp.einsum('qhd,khd->hqk', query_rows, key_rows, precision=HIGH) * score_scale)
    prob_low = low(jax.nn.softmax(scores, axis=-1))
    return low(low_back(jnp.einsum('hqk,khd->qhd', prob_low, value_rows, precision=HIGH)))

def block_forward(latent, skip_states, text_states, params, condition, teacher, loss_weight, cosine_table, sine_table, factor):
    skip_proj, shift_proj, self_project, self_output, cross_query, cross_keyval, cross_output, hidden_up, hidden_down, norm_gain, norm_bias, head_gain, head_bias, column_bias, hidden_bias, row_bias = params
    group_size = condition.shape[0]
    row_count = latent.shape[0]
    sequence_len = row_count // group_size
    by_row = (row_count, HEADS, HD)
    by_latent = (group_size, sequence_len, HEADS, HD)
    zero_row = jnp.zeros_like(column_bias[0])
    joined = jnp.concatenate([latent, skip_states], axis=1)
    skipped = low(low_back(product(joined, skip_proj) + column_bias[4]))
    residual = layer_norm(skipped, norm_gain[0], norm_bias[0])
    shift_term = low_back(product(low(jax.nn.silu(condition)), shift_proj) + row_bias[3])
    first_input = low(layer_norm(residual, norm_gain[1], norm_bias[1]) + jnp.repeat(shift_term, sequence_len, axis=0))
    self_bias = jnp.stack([column_bias[0], zero_row, column_bias[1]])
    projected = low_back(jnp.einsum('nd,dce->nce', first_input, self_project, precision=HIGH) + self_bias)
    query_rows = low(rotate(layer_norm(projected[:, 0].reshape(by_row), head_gain[0], head_bias[0]), cosine_table, sine_table))
    key_rows = low(rotate(layer_norm(projected[:, 1].reshape(by_row), head_gain[1], head_bias[1]), cosine_table, sine_table))
    value_rows = low(projected[:, 2].reshape(by_row))
    mixed_heads = lax.map(jax.checkpoint(attend), (query_rows.reshape(by_latent), key_rows.reshape(by_latent), value_rows.reshape(by_latent)))
    attn_out = low_back(product(mixed_heads.reshape(row_count, HEADS * HD), self_output) + row_bias[0])
    second = residual + attn_out
    third_input = low(layer_norm(second, norm_gain[2], norm_bias[2]))
    cross_pre = low_back(product(third_input, cross_query) + column_bias[2])
    cross_rows = low(rotate(layer_norm(cross_pre.reshape(by_row), head_gain[2], head_bias[2]), cosine_table, sine_table))
    text_bias = jnp.stack([zero_row, column_bias[3]])
    text_proj = low_back(jnp.einsum('ltd,dce->ltce', text_states, cross_keyval, precision=HIGH) + text_bias)
    text_shape = (group_size, text_states.shape[1], HEADS, HD)
    text_keys = low(layer_norm(text_proj[:, :, 0].reshape(text_shape), head_gain[3], head_bias[3]))
    text_values = low(text_proj[:, :, 1].reshape(text_shape))
    cross_mixed = lax.map(jax.checkpoint(attend), (cross_rows.reshape(by_latent), text_keys, text_values))
    cross_out = low_back(product(cross_mixed.reshape(row_count, HEADS * HD), cross_output) + row_bias[1])
    third_sum = second + cross_out
    fourth_input = low(layer_norm(third_sum, norm_gain[3], norm_bias[3]))
    upper_pre = low_back(product(fourth_input, hidden_up) + hidden_bias)
    active = low(jax.nn.gelu(upper_pre, approximate=True))
    final_rows = third_sum + low_back(product(active, hidden_down) + row_bias[2])
    error_rows = final_rows - teacher
    loss_value = 0.5 * factor * jnp.sum(loss_weight[:, None] * error_rows * error_rows)
    return (loss_value, final_rows)

def reference(latent, skip_states, text_states, condition, teacher, loss_mask, true_counts, positions, skip_proj, shift_proj, self_project, self_output, cross_query, cross_keyval, cross_output, hidden_up, hidden_down, norm_gain, norm_bias, head_gain, head_bias, column_bias, hidden_bias, row_bias):
    params = tuple((member.astype(jnp.float32) for member in (skip_proj, shift_proj, self_project, self_output, cross_query, cross_keyval, cross_output, hidden_up, hidden_down, norm_gain, norm_bias, head_gain, head_bias, column_bias, hidden_bias, row_bias)))
    group_size = math.gcd(LATENTS, max(1, 4096 // SEQ))
    group_count = LATENTS // group_size
    rows_per = group_size * SEQ
    total_count = jnp.sum(true_counts).astype(jnp.float32)
    factor = LATENTS * SEQ / total_count
    keep_rows = (jnp.arange(SEQ)[None, :] < true_counts[:, None]).astype(jnp.float32)
    loss_weight = (loss_mask.reshape(LATENTS, SEQ).astype(jnp.float32) * keep_rows).reshape(group_count, rows_per)
    cosine_table, sine_table = rotary_tables(positions, HD)
    inputs = (latent.astype(jnp.float32).reshape(group_count, rows_per, D), skip_states.astype(jnp.float32).reshape(group_count, rows_per, D), text_states.astype(jnp.float32).reshape(group_count, group_size, TEXT, DT), condition.astype(jnp.float32).reshape(group_count, group_size, D), teacher.astype(jnp.float32).reshape(group_count, rows_per, D), loss_weight, cosine_table.reshape(group_count, rows_per, HD), sine_table.reshape(group_count, rows_per, HD))

    def one_group(totals, operands):
        group_latent, group_skip, group_text, group_cond, group_teacher, group_weight, group_cosine, group_sine = operands

        def closure(latent_in, skip_in, text_in, param_in):
            return block_forward(latent_in, skip_in, text_in, param_in, group_cond, group_teacher, group_weight, group_cosine, group_sine, factor)
        loss_value, pullback, final_rows = jax.vjp(closure, group_latent, group_skip, group_text, params, has_aux=True)
        grad_latent, grad_skip, grad_text, grad_params = pullback(jnp.ones_like(loss_value))
        totals = jax.tree.map(jnp.add, totals, grad_params)
        return (totals, (final_rows, grad_latent, grad_skip, grad_text))
    zero_totals = jax.tree.map(jnp.zeros_like, params)
    totals, stacked = lax.scan(one_group, zero_totals, inputs)
    final_rows, grad_latent, grad_skip, grad_text = stacked
    return (final_rows.reshape(TOKENS, D).astype(jnp.bfloat16), grad_latent.reshape(TOKENS, D), grad_skip.reshape(TOKENS, D), grad_text.reshape(LATENTS, TEXT, DT), totals[0], totals[1], totals[2], totals[3], totals[4], totals[5], totals[6], totals[7], totals[8], totals[9], totals[10], totals[11], totals[12], totals[13], totals[14], totals[15])
```

```python
import functools

import jax
import jax.numpy as jnp
import numpy as np
from jax import lax
from jax.experimental import pallas as pl
from jax.experimental.pallas import tpu as pltpu
from jax.sharding import PartitionSpec as P

EPSILON = 1e-06
MESH = pl.DeviceIdType.MESH
BF16, F32 = jnp.bfloat16, jnp.float32
LANES = 128
CHUNKS = 2
VMEM_BYTES = 56 * 2**20
NEGATIVE = -1e30


def dot_nn(left, right):
    return jnp.dot(left, right, preferred_element_type=F32)


def dot_nt(left, right):
    return lax.dot_general(left, right, (((1,), (1,)), ((), ())), preferred_element_type=F32)


def dot_tn(left, right):
    return lax.dot_general(left, right, (((0,), (0,)), ((), ())), preferred_element_type=F32)


def centre(x):
    cen = x - jnp.mean(x, axis=-1, keepdims=True)
    spread = jnp.mean(cen * cen, axis=-1, keepdims=True)
    return cen, lax.rsqrt(spread + EPSILON)


def norm_back(total, x, gain):
    cen, rstd = centre(x)
    xhat = cen * rstd
    dg = total * gain
    back = rstd * (
        dg - jnp.mean(dg, axis=-1, keepdims=True) - xhat * jnp.mean(dg * xhat, axis=-1, keepdims=True)
    )
    return back, xhat


def remote(src, dst, send_sem, recv_sem, device):
    return pltpu.make_async_remote_copy(
        src_ref=src, dst_ref=dst, send_sem=send_sem, recv_sem=recv_sem, device_id=device, device_id_type=MESH
    )


def tensor_place():
    d, t = lax.axis_index("dp"), lax.axis_index("tensor")
    y, c = t // 2, t % 2
    return d, t, y, c, (d, 2 * y + 1 - c), (d, 2 * (1 - y) + c)


def greet(peers):
    bar = pltpu.get_barrier_semaphore()
    for peer in peers:
        pl.semaphore_signal(bar, inc=1, device_id=peer, device_id_type=MESH)
    return bar


def gather_body(n_rows, n_weights, dp, *refs):
    n = n_rows + n_weights
    ins, outs = refs[:n], refs[n : 2 * n]
    own_sem, core_s, core_r, y_s, y_r, fw_s, fw_r, z_s, z_r, x_s, x_r = refs[2 * n :]
    d, t, y, c, sib, yp = tensor_place()
    line = dp // 2
    zi, par = d // 2, d % 2
    xp = (2 * zi + 1 - par, t)
    zps = [(2 * ((zi + j) % line) + par, t) for j in range(1, line)]
    peers = ([sib, yp] if n_rows else []) + ([xp] + zps if n_weights else [])
    bar = greet(peers)
    locals_ = []
    for i in range(n):
        me = t if i < n_rows else d
        cp = pltpu.make_async_copy(ins[i], outs[i].at[me], own_sem.at[i])
        cp.start()
        locals_.append(cp)
    pl.semaphore_wait(bar, len(peers))
    row_cps = []
    z_cps = [[] for _ in range(n_weights)]
    x_cps = []

    def start_z(w):
        src, dst = ins[n_rows + w], outs[n_rows + w]
        for j in range(1, line):
            cp = remote(src, dst.at[d], z_s.at[w, j], z_r.at[w, j], zps[j - 1])
            cp.start()
            z_cps[w].append(cp)
        cp = remote(src, dst.at[d], x_s.at[w, 0], x_r.at[w, 0], xp)
        cp.start()
        x_cps.append(cp)

    def forward_z(w):
        dst = outs[n_rows + w]
        for j in range(1, line):
            z_cps[w][j - 1].wait_recv()
            source = 2 * ((zi + line - j) % line) + par
            cp = remote(dst.at[source], dst.at[source], x_s.at[w, j], x_r.at[w, j], xp)
            cp.start()
            x_cps.append(cp)

    if n_weights:
        start_z(0)
    for i in range(n_rows):
        a = remote(ins[i], outs[i].at[t], y_s.at[i], y_r.at[i], yp)
        b = remote(ins[i], outs[i].at[t], core_s.at[i], core_r.at[i], sib)
        a.start()
        b.start()
        row_cps.append((a, b))
    for w in range(n_weights):
        forward_z(w)
        if w + 1 < n_weights:
            start_z(w + 1)
    fws = []
    yt = 2 * (1 - y) + c
    for i in range(n_rows):
        row_cps[i][0].wait_recv()
        cp = remote(outs[i].at[yt], outs[i].at[yt], fw_s.at[i], fw_r.at[i], sib)
        cp.start()
        fws.append(cp)
    for cp in locals_:
        cp.wait()
    for i in range(n_rows):
        a, b = row_cps[i]
        b.wait_recv()
        fws[i].wait_recv()
        a.wait_send()
        b.wait_send()
        fws[i].wait_send()
    for cps in z_cps:
        for cp in cps:
            cp.wait_send()
    for cp in x_cps:
        cp.wait_recv()
        cp.wait_send()


def gather_kernel(name, collective_id, dp, rows, weights=()):
    n_rows, n_weights = len(rows), len(weights)
    n = n_rows + n_weights
    dma = pltpu.SemaphoreType.DMA
    r, w, k = max(n_rows, 1), max(n_weights, 1), max(dp // 2, 1)
    outs = [jax.ShapeDtypeStruct((4,) + v.shape, v.dtype) for v in rows]
    outs += [jax.ShapeDtypeStruct((dp,) + v.shape, v.dtype) for v in weights]
    anywhere = pl.BlockSpec(memory_space=pl.ANY)
    return pl.pallas_call(
        functools.partial(gather_body, n_rows, n_weights, dp),
        out_shape=outs,
        in_specs=[anywhere] * n,
        out_specs=[anywhere] * n,
        scratch_shapes=[dma((n,))] + [dma((r,))] * 6 + [dma((w, k))] * 4,
        compiler_params=pltpu.CompilerParams(collective_id=collective_id, has_side_effects=True),
        name=name,
    )(*rows, *weights)


def row_body(mode, rows, n_in, n_out, *refs):
    ins, outs, scr = refs[:n_in], refs[n_in : n_in + n_out], refs[n_in + n_out :]
    lhs, w = ins[0], ins[1]
    far, near, csend, crecv, ysend, yrecv, cs, cr, ys, yr, gcs, gcr, gys, gyr, fs, fr = scr
    d, t, y, c, sib, yp = tensor_place()
    bar = greet((sib, yp))
    ch = rows // CHUNKS

    def partial_rows(base, acc):
        for r in range(2):
            here = pl.ds(pl.multiple_of(base + r * rows, rows), rows)
            acc[pl.ds(r * rows, rows), :] = dot_nt(lhs[here, :], w[...])

    def chunk_of(acc, k):
        return acc[pl.ds(pl.multiple_of(c * rows + k * ch, ch), ch), :]

    other = pl.ds(pl.multiple_of((1 - c) * rows, rows), rows)
    partial_rows((1 - y) * 2 * rows, far)
    csend[0] = far[other, :].astype(BF16)
    pl.semaphore_wait(bar, 2)
    c0 = remote(csend.at[0], crecv.at[0], cs.at[0], cr.at[0], sib)
    c0.start()
    c0.wait_recv()
    ycs = []
    for k in range(CHUNKS):
        sl = pl.ds(k * ch, ch)
        ysend[sl, :] = (chunk_of(far, k) + crecv[0, sl, :].astype(F32)).astype(BF16)
        cp = remote(ysend.at[sl], yrecv.at[sl], ys.at[k], yr.at[k], yp)
        cp.start()
        ycs.append(cp)
    partial_rows(y * 2 * rows, near)
    csend[1] = near[other, :].astype(BF16)
    c1 = remote(csend.at[1], crecv.at[1], cs.at[1], cr.at[1], sib)
    c1.start()
    c1.wait_recv()
    gathers = mode in ("fwd", "final", "bwd")
    sums = None
    ags = []
    for k in range(CHUNKS):
        sl = pl.ds(k * ch, ch)
        ycs[k].wait_recv()
        total = chunk_of(near, k) + crecv[1, sl, :].astype(F32) + yrecv[sl, :].astype(F32)
        parts = []
        if mode == "fwd":
            resid, bias, gain, offset = ins[2:]
            second = resid[sl, :] + (total + bias[...])
            outs[1][sl, :] = second
            cen, rstd = centre(second)
            low = (cen * rstd * gain[...] + offset[...]).astype(BF16)
        elif mode == "final":
            third, bias, teacher, weight = ins[2:]
            final = third[sl, :] + (total + bias[...])
            outs[1][sl, :] = final.astype(BF16)
            grad = weight[sl, :] * (final - teacher[sl, :].astype(F32))
            outs[2][sl, :] = grad
            low = grad.astype(BF16)
            parts = [low.astype(F32)]
        elif mode == "bwd":
            x, gain, before = ins[2:]
            back, xhat = norm_back(total, x[sl, :], gain[...])
            grad = before[sl, :] + back
            outs[1][sl, :] = grad
            low = grad.astype(BF16)
            parts = [low.astype(F32), total * xhat, total]
        elif mode == "first":
            x, gain, before, skipped, gain0 = ins[2:]
            back, xhat = norm_back(total, x[sl, :], gain[...])
            grad = before[sl, :] + back
            back0, xhat0 = norm_back(grad, skipped[sl, :].astype(F32), gain0[...])
            low = back0.astype(BF16)
            outs[0][sl, :] = low
            parts = [low.astype(F32), total * xhat, total, grad * xhat0, grad]
        else:
            outs[0][sl, :] = total
        parts = [jnp.sum(p, axis=0, keepdims=True) for p in parts]
        sums = parts if sums is None else [a + b for a, b in zip(sums, parts)]
        if gathers:
            here = pl.ds(pl.multiple_of(t * rows + k * ch, ch), ch)
            spread = outs[0]
            spread[here, :] = low
            a = remote(spread.at[here], spread.at[here], gys.at[k], gyr.at[k], yp)
            b = remote(spread.at[here], spread.at[here], gcs.at[k], gcr.at[k], sib)
            a.start()
            b.start()
            ags.append((a, b))
    for i, s in enumerate(sums):
        outs[n_out - len(sums) + i][...] = s
    if gathers:
        fws = []
        for k in range(CHUNKS):
            ags[k][0].wait_recv()
            there = pl.ds(pl.multiple_of((2 * (1 - y) + c) * rows + k * ch, ch), ch)
            cp = remote(spread.at[there], spread.at[there], fs.at[k], fr.at[k], sib)
            cp.start()
            fws.append(cp)
        for k in range(CHUNKS):
            a, b = ags[k]
            b.wait_recv()
            fws[k].wait_recv()
            a.wait_send()
            b.wait_send()
            fws[k].wait_send()
    c0.wait_send()
    c1.wait_send()
    for cp in ycs:
        cp.wait_send()


def row_kernel(mode, name, collective_id, lhs, w, *extra):
    rows = lhs.shape[0] // 4
    width = w.shape[0]
    full = jax.ShapeDtypeStruct((4 * rows, width), BF16)
    mine = jax.ShapeDtypeStruct((rows, width), F32)
    mine_low = jax.ShapeDtypeStruct((rows, width), BF16)
    line = jax.ShapeDtypeStruct((1, width), F32)
    outs = {
        "fwd": [full, mine],
        "final": [full, mine_low, mine, line],
        "bwd": [full, mine, line, line, line],
        "first": [mine_low] + [line] * 5,
        "plain": [mine],
    }[mode]
    ins = [lhs, w, *extra]
    vm = pl.BlockSpec(memory_space=pltpu.VMEM)
    dma = pltpu.SemaphoreType.DMA
    return pl.pallas_call(
        functools.partial(row_body, mode, rows, len(ins), len(outs)),
        out_shape=outs,
        in_specs=[vm] * len(ins),
        out_specs=[vm] * len(outs),
        scratch_shapes=[
            pltpu.VMEM((2 * rows, width), F32),
            pltpu.VMEM((2 * rows, width), F32),
            pltpu.VMEM((2, rows, width), BF16),
            pltpu.VMEM((2, rows, width), BF16),
            pltpu.VMEM((rows, width), BF16),
            pltpu.VMEM((rows, width), BF16),
            dma((2,)),
            dma((2,)),
        ]
        + [dma((CHUNKS,))] * 8,
        compiler_params=pltpu.CompilerParams(
            collective_id=collective_id, has_side_effects=True, vmem_limit_bytes=VMEM_BYTES
        ),
        name=name,
    )(*ins)


def head_stats(u, mask, size):
    mean = jnp.sum(u, axis=-1, keepdims=True) * (1.0 / size)
    cen = (u - mean) * mask
    spread = jnp.sum(cen * cen, axis=-1, keepdims=True) * (1.0 / size)
    return cen, lax.rsqrt(spread + EPSILON)


def head_norm(u, mask, gain, offset, size):
    cen, rstd = head_stats(u, mask, size)
    return cen * rstd * gain + offset


def turn(u, cosine, sine):
    return u * cosine + pltpu.roll(u, LANES // 2, 1) * sine


def turn_back(u, cosine, sine):
    return u * cosine - pltpu.roll(u, LANES // 2, 1) * sine


def head_back(grad, u, mask, gain, size):
    cen, rstd = head_stats(u, mask, size)
    xhat = cen * rstd
    dg = grad * gain
    mean = jnp.sum(dg, axis=-1, keepdims=True) * (1.0 / size)
    inner = jnp.sum(dg * xhat, axis=-1, keepdims=True) * (1.0 / size)
    back = rstd * ((dg - mean) * mask - xhat * inner)
    return back, jnp.sum(grad * xhat, axis=0, keepdims=True), jnp.sum(grad, axis=0, keepdims=True)


def head_at(h):
    return pl.ds(h * LANES, LANES)


def attend(q_ref, k_ref, v_ref, out_ref, lse_ref, heads, scale, block, real_keys):
    queries, keys = q_ref.shape[0], k_ref.shape[0]

    def step(i, _):
        here = pl.ds(pl.multiple_of(i * block, block), block)
        for h in range(heads):
            hs = head_at(h)
            scores = dot_nt(k_ref[:, hs], q_ref[here, hs]) * scale
            if real_keys < keys:
                place = lax.broadcasted_iota(jnp.int32, scores.shape, 0)
                scores = jnp.where(place < real_keys, scores, NEGATIVE)
            highest = jnp.max(scores, axis=0, keepdims=True)
            exponent = jnp.exp(scores - highest)
            denominator = jnp.sum(exponent, axis=0, keepdims=True)
            probs = (exponent * (1.0 / denominator)).astype(BF16)
            mixed = dot_tn(v_ref[:, hs], probs)
            out_ref[here, hs] = mixed.T.astype(BF16)
            lse_ref[i, pl.ds(h, 1), :] = highest + jnp.log(denominator)
        return 0

    lax.fori_loop(0, queries // block, step, 0)


def attend_back(q_ref, k_ref, v_ref, do_ref, lse_ref, dq_ref, dk_ref, dv_ref, heads, scale, block, real_keys):
    queries, keys = q_ref.shape[0], k_ref.shape[0]
    dk_ref[...] = jnp.zeros(dk_ref.shape, F32)
    dv_ref[...] = jnp.zeros(dv_ref.shape, F32)

    def step(i, _):
        here = pl.ds(pl.multiple_of(i * block, block), block)
        for h in range(heads):
            hs = head_at(h)
            q, k, v, do = q_ref[here, hs], k_ref[:, hs], v_ref[:, hs], do_ref[here, hs]
            scores = dot_nt(k, q) * scale
            if real_keys < keys:
                place = lax.broadcasted_iota(jnp.int32, scores.shape, 0)
                scores = jnp.where(place < real_keys, scores, NEGATIVE)
            probs = jnp.exp(scores - lse_ref[i, pl.ds(h, 1), :])
            grad_probs = dot_nt(v, do)
            inner = jnp.sum(probs * grad_probs, axis=0, keepdims=True)
            grad_scores = (probs * (grad_probs - inner)).astype(BF16)
            dv_ref[:, hs] += dot_nn(probs.astype(BF16), do)
            dk_ref[:, hs] += dot_nn(grad_scores, q) * scale
            dq_ref[here, hs] = dot_tn(k, grad_scores).T * scale
        return 0

    lax.fori_loop(0, queries // block, step, 0)


def self_fwd_body(size, scale, heads, block, x, w, bias, cosine, sine, gain, offset, mask, fold, pre, low, mixed, lse, padded):
    rows = x.shape[0]
    span = heads * LANES

    def project(i, _):
        here = pl.ds(pl.multiple_of(i * block, block), block)
        for part in range(3):
            cols = pl.ds(part * span, span)
            out = dot_nn(x[here, :], w[part]) + bias[part]
            if part < 2:
                pre[here, cols] = out
                for h in range(heads):
                    u = out[:, h * LANES : (h + 1) * LANES]
                    val = head_norm(u, mask[...], gain[pl.ds(part, 1), :], offset[pl.ds(part, 1), :], size)
                    val = turn(val, cosine[here, :], sine[here, :])
                    low[here, pl.ds(part * span + h * LANES, LANES)] = val.astype(BF16)
            else:
                low[here, cols] = out.astype(BF16)
        return 0

    lax.fori_loop(0, rows // block, project, 0)
    attend(
        low.at[:, pl.ds(0, span)], low.at[:, pl.ds(span, span)], low.at[:, pl.ds(2 * span, span)],
        padded, lse, heads, scale, block, rows,
    )
    mixed[...] = dot_nt(padded[...], fold[...]).astype(BF16)


def self_bwd_body(
    size, scale, heads, block, c_all, w_out, pre, low, lse, cosine, sine, gain, mask, fold,
    p, p_low, gains, offsets, sums, do, dq, dk, dv,
):
    rows = c_all.shape[0]
    span = heads * LANES

    def spread(i, _):
        here = pl.ds(pl.multiple_of(i * block, block), block)
        narrow = dot_nn(c_all[here, :], w_out[...]).astype(BF16)
        do[here, :] = dot_nn(narrow, fold[...]).astype(BF16)
        return 0

    lax.fori_loop(0, rows // block, spread, 0)
    attend_back(
        low.at[:, pl.ds(0, span)], low.at[:, pl.ds(span, span)], low.at[:, pl.ds(2 * span, span)],
        do, lse, dq, dk, dv, heads, scale, block, rows,
    )
    gains[...] = jnp.zeros(gains.shape, F32)
    offsets[...] = jnp.zeros(offsets.shape, F32)
    sums[...] = jnp.zeros(sums.shape, F32)

    def finish(i, _):
        here = pl.ds(pl.multiple_of(i * block, block), block)
        for part, grad_ref in enumerate((dq, dk, dv)):
            for h in range(heads):
                hs = head_at(h)
                wide = pl.ds(part * span + h * LANES, LANES)
                grad = grad_ref[here, hs]
                if part < 2:
                    grad = turn_back(grad, cosine[here, :], sine[here, :])
                    grad, g, o = head_back(grad, pre[here, wide], mask[...], gain[pl.ds(part, 1), :], size)
                    gains[pl.ds(part, 1), :] += g
                    offsets[pl.ds(part, 1), :] += o
                grad_low = grad.astype(BF16)
                p[here, wide] = grad_low
                if part != 1:
                    sums[:, wide] += jnp.sum(grad_low.astype(F32), axis=0, keepdims=True)
            p_low[part, here, :] = dot_nt(p[here, pl.ds(part * span, span)], fold[...]).astype(BF16)
        return 0

    lax.fori_loop(0, rows // block, finish, 0)


def text_body(size, heads, real, x, w, bias, gain, offset, mask, pre, low):
    span = heads * LANES
    for part in range(2):
        out = dot_nn(x[...], w[part]) + bias[part]
        if part == 0:
            pre[...] = out
            for h in range(heads):
                hs = head_at(h)
                val = head_norm(out[:, h * LANES : (h + 1) * LANES], mask[...], gain[...], offset[...], size)
                low[:, hs] = val.astype(BF16)
        else:
            low[:, pl.ds(span, span)] = out.astype(BF16)


def cross_fwd_body(
    size, scale, heads, block, real, x, w, bias, text_low, cosine, sine, gain, offset, mask, fold,
    pre, low, mixed, lse, padded,
):
    rows = x.shape[0]
    span = heads * LANES

    def project(i, _):
        here = pl.ds(pl.multiple_of(i * block, block), block)
        out = dot_nn(x[here, :], w[...]) + bias[...]
        pre[here, :] = out
        for h in range(heads):
            val = head_norm(out[:, h * LANES : (h + 1) * LANES], mask[...], gain[...], offset[...], size)
            low[here, head_at(h)] = turn(val, cosine[here, :], sine[here, :]).astype(BF16)
        return 0

    lax.fori_loop(0, rows // block, project, 0)
    attend(low, text_low.at[:, pl.ds(0, span)], text_low.at[:, pl.ds(span, span)], padded, lse, heads, scale, block, real)
    mixed[...] = dot_nt(padded[...], fold[...]).astype(BF16)


def cross_bwd_body(
    size, scale, heads, block, real, c_all, w_out, pre, low, text_pre, text_low, lse, cosine, sine, gain, text_gain, mask, fold,
    p, p_low, text_p, text_p_low, gains, offsets, sums, text_sums, do, dq, dk, dv,
):
    rows = c_all.shape[0]
    span = heads * LANES

    def spread(i, _):
        here = pl.ds(pl.multiple_of(i * block, block), block)
        narrow = dot_nn(c_all[here, :], w_out[...]).astype(BF16)
        do[here, :] = dot_nn(narrow, fold[...]).astype(BF16)
        return 0

    lax.fori_loop(0, rows // block, spread, 0)
    attend_back(
        low, text_low.at[:, pl.ds(0, span)], text_low.at[:, pl.ds(span, span)],
        do, lse, dq, dk, dv, heads, scale, block, real,
    )
    gains[...] = jnp.zeros(gains.shape, F32)
    offsets[...] = jnp.zeros(offsets.shape, F32)
    sums[...] = jnp.zeros(sums.shape, F32)

    def finish(i, _):
        here = pl.ds(pl.multiple_of(i * block, block), block)
        for h in range(heads):
            hs = head_at(h)
            grad = turn_back(dq[here, hs], cosine[here, :], sine[here, :])
            grad, g, o = head_back(grad, pre[here, hs], mask[...], gain[...], size)
            gains[pl.ds(0, 1), :] += g
            offsets[pl.ds(0, 1), :] += o
            grad_low = grad.astype(BF16)
            p[here, hs] = grad_low
            sums[:, hs] += jnp.sum(grad_low.astype(F32), axis=0, keepdims=True)
        p_low[here, :] = dot_nt(p[here, :], fold[...]).astype(BF16)
        return 0

    lax.fori_loop(0, rows // block, finish, 0)
    for h in range(heads):
        hs = head_at(h)
        grad, g, o = head_back(dk[:, hs], text_pre[:, hs], mask[...], text_gain[...], size)
        gains[pl.ds(1, 1), :] += g
        offsets[pl.ds(1, 1), :] += o
        text_p[:, hs] = grad.astype(BF16)
        low_v = dv[:, hs].astype(BF16)
        text_p[:, pl.ds(span + h * LANES, LANES)] = low_v
        text_sums[:, hs] = jnp.sum(low_v.astype(F32), axis=0, keepdims=True)
    for part in range(2):
        text_p_low[part] = dot_nt(text_p[:, pl.ds(part * span, span)], fold[...]).astype(BF16)


def local_kernel(name, body, ins, outs, scratch=()):
    vm = pl.BlockSpec(memory_space=pltpu.VMEM)
    return pl.pallas_call(
        body,
        out_shape=outs,
        in_specs=[vm] * len(ins),
        out_specs=[vm] * len(outs),
        scratch_shapes=list(scratch),
        compiler_params=pltpu.CompilerParams(vmem_limit_bytes=VMEM_BYTES),
        name=name,
    )(*ins)


def shaped(shape, dtype):
    return jax.ShapeDtypeStruct(shape, dtype)


def fold_matrix(heads, size):
    out = np.zeros((heads * size, heads * LANES), np.float32)
    for h in range(heads):
        for e in range(size):
            out[h * size + e, h * LANES + (e % 2) * (LANES // 2) + e // 2] = 1.0
    return out


def body(
    latent, skip_states, text_states, condition, teacher, loss_mask, true_counts, positions,
    skip_proj, shift_proj, self_project, self_output, cross_query, cross_keyval, cross_output, hidden_up, hidden_down,
    norm_gain, norm_bias, head_gain, head_bias, column_bias, hidden_bias, row_bias,
):
    d, t = lax.axis_index("dp"), lax.axis_index("tensor")
    dp, tensor = lax.axis_size("dp"), lax.axis_size("tensor")
    rows, width = latent.shape
    group = rows * tensor
    size = head_gain.shape[1]
    cols = self_project.shape[2]
    heads = cols // size
    span = heads * LANES
    hidden = hidden_up.shape[1]
    text_len = text_states.shape[1]
    text_pad = -(-text_len // 16) * 16
    scale = size ** (-0.5)
    block = min(256, group)
    fold_np = fold_matrix(heads, size)
    fold = jnp.asarray(fold_np, BF16)
    one_np = fold_np[:size, :LANES]
    mask = jnp.asarray(one_np.sum(0, keepdims=True), F32)

    def widen_head(v):
        return jnp.dot(v, jnp.asarray(one_np), precision=lax.Precision.HIGHEST)

    def widen_cols(v):
        return jnp.dot(v, jnp.asarray(fold_np), precision=lax.Precision.HIGHEST)

    def narrow_head(v):
        return jnp.dot(v, jnp.asarray(one_np.T), precision=lax.Precision.HIGHEST)

    def narrow_cols(v):
        return jnp.dot(v, jnp.asarray(fold_np.T), precision=lax.Precision.HIGHEST)

    small = jnp.concatenate([condition.astype(F32), true_counts.astype(F32)[:, None]], axis=1)
    small_all = lax.all_gather(small, "dp", axis=0, tiled=True)
    counted = jnp.sum(small_all[:, width])
    silu_all = jax.nn.silu(small_all[:, :width]).astype(BF16)
    silu_mine = lax.dynamic_slice_in_dim(silu_all, d * shift_proj.shape[0], shift_proj.shape[0], 1)
    shift_term = lax.psum_scatter(dot_nn(silu_mine, shift_proj), "dp", scatter_dimension=0, tiled=True) + row_bias[3:4]

    project_in = jnp.transpose(self_project, (1, 0, 2))
    joined0, joined1, skip_g, project_g = gather_kernel(
        "gather_joined", 0, dp, (latent, skip_states), (skip_proj, project_in)
    )
    out_t = lax.all_gather(self_output.T, "dp", axis=0, tiled=True)
    query_full = lax.all_gather(cross_query, "dp", axis=0, tiled=True)
    keyval_in = jnp.transpose(cross_keyval, (1, 0, 2))
    keyval_g = lax.all_gather(keyval_in, "dp", axis=0, tiled=False)
    cross_out_t = lax.all_gather(cross_output.T, "dp", axis=0, tiled=True)
    up_full = lax.all_gather(hidden_up, "dp", axis=0, tiled=True)
    down_t = lax.all_gather(hidden_down.T, "dp", axis=0, tiled=True)

    skip_full = skip_g.reshape(2 * width, cols)
    project_full = jnp.transpose(project_g, (1, 0, 2, 3)).reshape(3, width, cols)
    project_wide = jnp.einsum("cdk,kl->cdl", project_full, fold, preferred_element_type=F32).astype(BF16)
    query_wide = dot_nn(query_full, fold).astype(BF16)
    keyval_full = jnp.transpose(keyval_g, (1, 0, 2, 3)).reshape(2, text_states.shape[2], cols)
    keyval_wide = jnp.einsum("cdk,kl->cdl", keyval_full, fold, preferred_element_type=F32).astype(BF16)

    bias_cols = lax.dynamic_slice_in_dim(column_bias, t * cols, cols, 1)
    bias_wide = widen_cols(bias_cols)
    zero_wide = jnp.zeros((1, span), F32)
    self_bias = jnp.stack([bias_wide[0:1], zero_wide, bias_wide[1:2]])
    text_bias = jnp.stack([zero_wide, bias_wide[3:4]])
    hidden_cols_bias = lax.dynamic_slice_in_dim(hidden_bias, t * hidden, hidden, 0)
    gain_wide, offset_wide = widen_head(head_gain), widen_head(head_bias)

    quarter = size // 4
    lane_np = np.zeros((2, LANES), np.float32)
    sign_np = np.zeros((1, LANES), np.float32)
    for i in range(size // 2):
        f = np.float32(10000.0 ** (-(i % quarter) / quarter))
        for half in range(2):
            lane_np[i // quarter, half * (LANES // 2) + i] = f
            sign_np[0, half * (LANES // 2) + i] = 2 * half - 1
    place = positions.astype(F32)
    angles = place[0][:, None] * lane_np[0] + place[1][:, None] * lane_np[1]
    cosine = jnp.cos(angles) * mask
    sine = jnp.sin(angles) * sign_np

    joined0 = joined0.reshape(group, width)
    joined1 = joined1.reshape(group, width)
    skip_pre = dot_nn(joined0, skip_full[:width]) + dot_nn(joined1, skip_full[width:]) + bias_cols[4]
    skipped = lax.all_to_all(skip_pre.astype(BF16), "tensor", split_axis=0, concat_axis=1, tiled=True)
    cen, rstd = centre(skipped.astype(F32))
    residual = cen * rstd * norm_gain[0] + norm_bias[0]
    cen, rstd = centre(residual)
    first_input = (cen * rstd * norm_gain[1] + norm_bias[1] + shift_term).astype(BF16)
    (first_all,) = gather_kernel("gather_first", 1, dp, (first_input,))
    first_all = first_all.reshape(group, width)

    lse_shape = (group // block, heads, block)
    pre, low, mixed, lse = local_kernel(
        "self_fwd",
        functools.partial(self_fwd_body, size, scale, heads, block),
        [first_all, project_wide, self_bias, cosine, sine, gain_wide[0:2], offset_wide[0:2], mask, fold],
        [shaped((group, 2 * span), F32), shaped((group, 3 * span), BF16), shaped((group, cols), BF16), shaped(lse_shape, F32)],
        [pltpu.VMEM((group, span), BF16)],
    )
    third_all, second = row_kernel(
        "fwd", "rows_self", 2, mixed, out_t, residual, row_bias[0:1], norm_gain[2:3], norm_bias[2:3]
    )

    text_rows = jnp.pad(text_states[0], ((0, text_pad - text_len), (0, 0)))
    text_pre, text_low = local_kernel(
        "text_fwd",
        functools.partial(text_body, size, heads, text_len),
        [text_rows, keyval_wide, text_bias, gain_wide[3:4], offset_wide[3:4], mask],
        [shaped((text_pad, span), F32), shaped((text_pad, 2 * span), BF16)],
    )
    cross_pre, cross_low, cross_mixed, cross_lse = local_kernel(
        "cross_fwd",
        functools.partial(cross_fwd_body, size, scale, heads, block, text_len),
        [third_all, query_wide, bias_wide[2:3], text_low, cosine, sine, gain_wide[2:3], offset_wide[2:3], mask, fold],
        [shaped((group, span), F32), shaped((group, span), BF16), shaped((group, cols), BF16), shaped(lse_shape, F32)],
        [pltpu.VMEM((group, span), BF16)],
    )
    fourth_all, third_sum = row_kernel(
        "fwd", "rows_cross", 3, cross_mixed, cross_out_t, second, row_bias[1:2], norm_gain[3:4], norm_bias[3:4]
    )

    upper_pre = dot_nn(fourth_all, up_full) + hidden_cols_bias
    active, pull_gelu = jax.vjp(lambda v: jax.nn.gelu(v, approximate=True), upper_pre)
    active_low = active.astype(BF16)
    row_ids = t * rows + jnp.arange(rows)
    weight = loss_mask.astype(F32) * (row_ids < true_counts[0]).astype(F32)
    loss_scale = dp * group / counted
    grad_all, block_out, grad_final, bias_mlp = row_kernel(
        "final", "rows_mlp", 4, active_low, down_t, third_sum, row_bias[2:3], teacher, (loss_scale * weight)[:, None]
    )

    grad_active = dot_nn(grad_all, down_t)
    (grad_upper,) = pull_gelu(grad_active)
    grad_upper_low = grad_upper.astype(BF16)
    bias_hidden = jnp.sum(grad_upper_low.astype(F32), axis=0)
    grad_down_t = dot_tn(grad_all, active_low).astype(BF16)
    grad_up = dot_tn(fourth_all, grad_upper_low).astype(BF16)
    down_mine = lax.psum_scatter(grad_down_t, "dp", scatter_dimension=0, tiled=True)
    up_mine = lax.psum_scatter(grad_up, "dp", scatter_dimension=0, tiled=True)
    c_all, grad_third, bias_cross_out, gain_fourth, offset_fourth = row_kernel(
        "bwd", "rows_up", 5, grad_upper_low, up_full, third_sum, norm_gain[3:4], grad_final
    )

    qp, qp_low, text_p, text_p_low, cross_gains, cross_offsets, cross_sums, text_sums = local_kernel(
        "cross_bwd",
        functools.partial(cross_bwd_body, size, scale, heads, block, text_len),
        [c_all, cross_out_t, cross_pre, cross_low, text_pre, text_low, cross_lse, cosine, sine,
         gain_wide[2:3], gain_wide[3:4], mask, fold],
        [shaped((group, span), BF16), shaped((group, cols), BF16), shaped((text_pad, 2 * span), BF16),
         shaped((2, text_pad, cols), BF16), shaped((2, LANES), F32), shaped((2, LANES), F32), shaped((1, span), F32), shaped((1, span), F32)],
        [pltpu.VMEM((group, span), BF16), pltpu.VMEM((group, span), F32), pltpu.VMEM((text_pad, span), F32), pltpu.VMEM((text_pad, span), F32)],
    )
    s_all, grad_second, bias_attn, gain_third, offset_third = row_kernel(
        "bwd", "rows_query", 6, qp, query_wide, second, norm_gain[2:3], grad_third
    )
    grad_cross_out_t = dot_tn(c_all, cross_mixed).astype(BF16)
    grad_query = dot_tn(third_all, qp_low).astype(BF16)
    grad_keyval = jnp.stack([dot_tn(text_rows, text_p_low[i]).astype(BF16) for i in range(2)])
    grad_keyval = grad_keyval.reshape(2, dp, -1, cols).transpose(1, 0, 2, 3).reshape(-1, cols)
    text_part = dot_nt(text_p[:, :span], keyval_wide[0]) + dot_nt(text_p[:, span:], keyval_wide[1])
    grad_text = lax.psum(text_part[:text_len].astype(BF16), "tensor").astype(F32)[None]
    cross_out_mine = lax.psum_scatter(grad_cross_out_t, "dp", scatter_dimension=0, tiled=True)
    query_mine = lax.psum_scatter(grad_query, "dp", scatter_dimension=0, tiled=True)
    keyval_mine = lax.psum_scatter(grad_keyval, "dp", scatter_dimension=0, tiled=True)

    p, p_low, self_gains, self_offsets, self_sums = local_kernel(
        "self_bwd",
        functools.partial(self_bwd_body, size, scale, heads, block),
        [s_all, out_t, pre, low, lse, cosine, sine, gain_wide[0:2], mask, fold],
        [shaped((group, 3 * span), BF16), shaped((3, group, cols), BF16), shaped((2, LANES), F32), shaped((2, LANES), F32),
         shaped((1, 3 * span), F32)],
        [pltpu.VMEM((group, span), BF16)] + [pltpu.VMEM((group, span), F32)] * 3,
    )
    project_rows = jnp.transpose(project_wide, (1, 0, 2)).reshape(width, 3 * span)
    k_low, bias_skip, gain_first, offset_first, gain_skip, offset_skip = row_kernel(
        "first", "rows_project", 7, p, project_rows, residual, norm_gain[1:2], grad_second, skipped, norm_gain[0:1]
    )
    grad_out_t = dot_tn(s_all, mixed).astype(BF16)
    grad_project = jnp.stack([dot_tn(first_all, p_low[i]).astype(BF16) for i in range(3)])
    grad_project = grad_project.reshape(3, dp, -1, cols).transpose(1, 0, 2, 3).reshape(-1, cols)
    out_mine = lax.psum_scatter(grad_out_t, "dp", scatter_dimension=0, tiled=True)
    project_mine = lax.psum_scatter(grad_project, "dp", scatter_dimension=0, tiled=True)

    k_cols = lax.all_to_all(k_low, "tensor", split_axis=1, concat_axis=0, tiled=True)
    (grad_latent,) = row_kernel("plain", "rows_latent", 8, k_cols, skip_full[:width])
    (grad_skip,) = row_kernel("plain", "rows_skip", 9, k_cols, skip_full[width:])
    grad_skip_proj = jnp.concatenate([dot_tn(joined0, k_cols).astype(BF16), dot_tn(joined1, k_cols).astype(BF16)])
    skip_mine = lax.psum_scatter(grad_skip_proj, "dp", scatter_dimension=0, tiled=True)

    shift_parts = lax.all_gather(offset_first, ("dp", "tensor"), axis=0, tiled=True)
    shift_low = jnp.sum(shift_parts.reshape(dp, tensor, width), axis=1).astype(BF16)
    grad_shift_proj = dot_tn(silu_mine, shift_low)
    bias_shift = jnp.sum(shift_low.astype(F32), axis=0)

    head_gain_part = narrow_head(jnp.concatenate([self_gains, cross_gains], axis=0))
    head_bias_part = narrow_head(jnp.concatenate([self_offsets, cross_offsets], axis=0))
    column_rows = narrow_cols(
        jnp.concatenate([self_sums[:, :span], self_sums[:, 2 * span :], cross_sums, text_sums], axis=0)
    )
    column_part = lax.dynamic_update_slice_in_dim(jnp.zeros((4, width), F32), column_rows, t * cols, 1)
    hidden_part = lax.dynamic_update_slice_in_dim(jnp.zeros(hidden_bias.shape, F32), bias_hidden, t * hidden, 0)
    sums = lax.psum(
        (
            jnp.concatenate([gain_skip, gain_first, gain_third, gain_fourth]),
            jnp.concatenate([offset_skip, offset_first, offset_third, offset_fourth]),
            head_gain_part,
            head_bias_part,
            jnp.concatenate([column_part, bias_skip]),
            hidden_part,
            jnp.concatenate([bias_attn, bias_cross_out, bias_mlp]),
        ),
        ("dp", "tensor"),
    )
    return (
        block_out,
        grad_latent,
        grad_skip,
        grad_text,
        skip_mine.astype(F32),
        grad_shift_proj,
        jnp.transpose(project_mine.reshape(3, -1, cols), (1, 0, 2)).astype(F32),
        out_mine.T.astype(F32),
        query_mine.astype(F32),
        jnp.transpose(keyval_mine.reshape(2, -1, cols), (1, 0, 2)).astype(F32),
        cross_out_mine.T.astype(F32),
        up_mine.astype(F32),
        down_mine.T.astype(F32),
        sums[0],
        sums[1],
        sums[2],
        sums[3],
        sums[4],
        sums[5],
        jnp.concatenate([sums[6], bias_shift[None]]),
    )


def solution(mesh):
    both = ("dp", "tensor")
    rows2, split2, cross2 = P(both, None), P("dp", "tensor"), P("tensor", "dp")
    middle = P("dp", None, "tensor")
    return jax.shard_map(
        body,
        mesh=mesh,
        in_specs=(
            rows2, rows2, P("dp", None, None), P("dp", None), rows2, P(both), P("dp"), P(None, "dp"),
            split2, P("dp", None), middle, cross2, split2, middle, cross2, split2, cross2,
            P(), P(), P(), P(), P(), P(), P(),
        ),
        out_specs=(
            rows2, rows2, rows2, P("dp", None, None),
            split2, P("dp", None), middle, cross2, split2, middle, cross2, split2, cross2,
            P(), P(), P(), P(), P(), P(), P(),
        ),
        check_vma=False,
    )
```

```python
import functools

import jax
import jax.numpy as jnp
import numpy as np
from jax import lax
from jax.experimental import pallas as pl
from jax.experimental.pallas import tpu as pltpu
from jax.sharding import PartitionSpec as P

EPSILON = 1e-06
MESH = pl.DeviceIdType.MESH
BF16, F32 = jnp.bfloat16, jnp.float32
LANES = 128
CHUNKS = 2
VMEM_BYTES = 56 * 2**20
NEGATIVE = -1e30


def dot_nn(left, right):
    return jnp.dot(left, right, preferred_element_type=F32)


def dot_nt(left, right):
    return lax.dot_general(left, right, (((1,), (1,)), ((), ())), preferred_element_type=F32)


def dot_tn(left, right):
    return lax.dot_general(left, right, (((0,), (0,)), ((), ())), preferred_element_type=F32)


def centre(x):
    cen = x - jnp.mean(x, axis=-1, keepdims=True)
    spread = jnp.mean(cen * cen, axis=-1, keepdims=True)
    return cen, lax.rsqrt(spread + EPSILON)


def norm_back(total, x, gain):
    cen, rstd = centre(x)
    xhat = cen * rstd
    dg = total * gain
    back = rstd * (
        dg - jnp.mean(dg, axis=-1, keepdims=True) - xhat * jnp.mean(dg * xhat, axis=-1, keepdims=True)
    )
    return back, xhat


def remote(src, dst, send_sem, recv_sem, device):
    return pltpu.make_async_remote_copy(
        src_ref=src, dst_ref=dst, send_sem=send_sem, recv_sem=recv_sem, device_id=device, device_id_type=MESH
    )


def tensor_place():
    d, t = lax.axis_index("dp"), lax.axis_index("tensor")
    y, c = t // 2, t % 2
    return d, t, y, c, (d, 2 * y + 1 - c), (d, 2 * (1 - y) + c)


def greet(peers):
    bar = pltpu.get_barrier_semaphore()
    for peer in peers:
        pl.semaphore_signal(bar, inc=1, device_id=peer, device_id_type=MESH)
    return bar


class DpPlace:
    def __init__(self, dp):
        self.d, self.t = lax.axis_index("dp"), lax.axis_index("tensor")
        self.dp, self.line = dp, dp // 2
        self.zi, self.par = self.d // 2, self.d % 2
        self.pair = (2 * self.zi + 1 - self.par, self.t)

    def ahead(self, j):
        return 2 * ((self.zi + j) % self.line) + self.par

    def behind(self, j):
        return 2 * ((self.zi + self.line - j) % self.line) + self.par

    def others(self):
        return [((self.d + j) % self.dp, self.t) for j in range(1, self.dp)]


class ToAll:
    def __init__(self, place, source, land, send_sem, recv_sem):
        self.copies = []
        for j in range(1, place.dp):
            q = (place.d + j) % place.dp
            cp = remote(source(q), land.at[place.d], send_sem.at[j], recv_sem.at[j], (q, place.t))
            cp.start()
            self.copies.append(cp)

    def arrived(self):
        for cp in self.copies:
            cp.wait_recv()

    def sent(self):
        for cp in self.copies:
            cp.wait_send()


class WeightGather:
    def __init__(self, place, shard, land, z_s, z_r, x_s, x_r):
        self.place, self.land, self.x_s, self.x_r = place, land, x_s, x_r
        self.z = []
        for j in range(1, place.line):
            cp = remote(shard, land.at[place.d], z_s.at[j], z_r.at[j], (place.ahead(j), place.t))
            cp.start()
            self.z.append(cp)
        cp = remote(shard, land.at[place.d], x_s.at[0], x_r.at[0], place.pair)
        cp.start()
        self.x = [cp]

    def forward(self):
        for j in range(1, self.place.line):
            self.z[j - 1].wait_recv()
            source = self.place.behind(j)
            cp = remote(self.land.at[source], self.land.at[source], self.x_s.at[j], self.x_r.at[j], self.place.pair)
            cp.start()
            self.x.append(cp)

    def arrived(self):
        for cp in self.x:
            cp.wait_recv()

    def sent(self):
        for cp in self.z + self.x:
            cp.wait_send()


class GradScatter:
    def __init__(self, place, source, own, xland, zland, own_sem, z_s, z_r, x_s, x_r):
        self.place, self.own, self.xland, self.zland, self.z_s, self.z_r = place, own, xland, zland, z_s, z_r
        self.x, self.local, self.z = [], [], []
        for i in range(1, place.line + 1):
            j = (place.zi + i) % place.line
            cp = remote(source.at[2 * j + 1 - place.par], xland.at[j], x_s.at[i - 1], x_r.at[i - 1], place.pair)
            cp.start()
            self.x.append(cp)
            cp = pltpu.make_async_copy(source.at[2 * j + place.par], own.at[j], own_sem.at[i - 1])
            cp.start()
            self.local.append(cp)

    def pass_on(self):
        for i in range(1, self.place.line):
            j = (self.place.zi + i) % self.place.line
            self.local[i - 1].wait()
            self.x[i - 1].wait_recv()
            self.own[j] = (self.own[j].astype(F32) + self.xland[j].astype(F32)).astype(BF16)
            cp = remote(
                self.own.at[j], self.zland.at[i - 1], self.z_s.at[i], self.z_r.at[i], (self.place.ahead(i), self.place.t)
            )
            cp.start()
            self.z.append(cp)

    def result(self):
        last = self.place.line - 1
        self.local[last].wait()
        self.x[last].wait_recv()
        total = self.own[self.place.zi].astype(F32) + self.xland[self.place.zi].astype(F32)
        for i, cp in enumerate(self.z):
            cp.wait_recv()
            total = total + self.zland[i].astype(F32)
        return total

    def sent(self):
        for cp in self.x + self.z:
            cp.wait_send()


class TensorSum:
    def __init__(self, near, far, csend, crecv, ysend, yrecv, cs, cr, ys, yr):
        self.near, self.far, self.csend, self.crecv, self.ysend, self.yrecv = near, far, csend, crecv, ysend, yrecv
        self.cs, self.cr, self.ys, self.yr = cs, cr, ys, yr
        _, self.t, self.y, self.c, self.sib, self.yp = tensor_place()

    def core(self, i, value):
        self.csend[i] = value.astype(BF16)
        cp = remote(self.csend.at[i], self.crecv.at[i], self.cs.at[i], self.cr.at[i], self.sib)
        cp.start()
        return cp

    def start(self, product, ready=None):
        there, here = 2 * (1 - self.y), 2 * self.y
        first = product(there + 1 - self.c)
        if ready is not None:
            ready()
        self.c0 = self.core(0, first)
        self.far[...] = product(there + self.c)
        self.c1 = self.core(1, product(here + 1 - self.c))
        self.c0.wait_recv()
        self.ycs = []
        ch = self.far.shape[0] // CHUNKS
        for k in range(CHUNKS):
            sl = pl.ds(k * ch, ch)
            self.ysend[sl, :] = (self.far[sl, :] + self.crecv[0, sl, :].astype(F32)).astype(BF16)
            cp = remote(self.ysend.at[sl], self.yrecv.at[sl], self.ys.at[k], self.yr.at[k], self.yp)
            cp.start()
            self.ycs.append(cp)
        self.near[...] = product(here + self.c)
        self.c1.wait_recv()

    def chunk(self, k):
        ch = self.far.shape[0] // CHUNKS
        sl = pl.ds(k * ch, ch)
        self.ycs[k].wait_recv()
        return sl, self.near[sl, :] + self.crecv[1, sl, :].astype(F32) + self.yrecv[sl, :].astype(F32)

    def sent(self):
        for cp in [self.c0, self.c1] + self.ycs:
            cp.wait_send()

    @staticmethod
    def scratch(rows, width):
        dma = pltpu.SemaphoreType.DMA
        vm = pltpu.VMEM
        return [
            vm((rows, width), F32), vm((rows, width), F32), vm((2, rows, width), BF16), vm((2, rows, width), BF16),
            vm((rows, width), BF16), vm((rows, width), BF16), dma((2,)), dma((2,)), dma((CHUNKS,)), dma((CHUNKS,)),
        ]


class RowSpread:
    def __init__(self, spread, rows, ys, yr, cs, cr, fs, fr):
        self.spread, self.rows = spread, rows
        self.sems = (ys, yr, cs, cr, fs, fr)
        _, self.t, self.y, self.c, self.sib, self.yp = tensor_place()
        self.parts, self.passed = [], []

    def at(self, owner, start, count):
        return self.spread.at[pl.ds(pl.multiple_of(owner * self.rows + start, 16), count)]

    def send(self, start, count):
        ys, yr, cs, cr, _, _ = self.sems
        k = len(self.parts)
        here = self.at(self.t, start, count)
        a = remote(here, here, ys.at[k], yr.at[k], self.yp)
        b = remote(here, here, cs.at[k], cr.at[k], self.sib)
        a.start()
        b.start()
        self.parts.append((a, b, start, count))

    def forward(self):
        fs, fr = self.sems[4:]
        for k, (a, _, start, count) in enumerate(self.parts):
            a.wait_recv()
            there = self.at(2 * (1 - self.y) + self.c, start, count)
            cp = remote(there, there, fs.at[k], fr.at[k], self.sib)
            cp.start()
            self.passed.append(cp)

    def finish(self):
        for (a, b, _, _), cp in zip(self.parts, self.passed):
            b.wait_recv()
            cp.wait_recv()
            a.wait_send()
            b.wait_send()
            cp.wait_send()

    @staticmethod
    def scratch(parts=CHUNKS):
        return [pltpu.SemaphoreType.DMA((parts,))] * 6


def row_body(mode, rows, n_in, n_out, *refs):
    ins, outs, scr = refs[:n_in], refs[n_in : n_in + n_out], refs[n_in + n_out :]
    lhs, w = ins[0], ins[1]
    _, t, _, _, sib, yp = tensor_place()
    bar = greet((sib, yp))
    reduce = TensorSum(*scr[:10])
    spread = RowSpread(outs[0], rows, *scr[10:])

    def product(b):
        return dot_nt(lhs[pl.ds(pl.multiple_of(b * rows, rows), rows), :], w[...])

    reduce.start(product, lambda: pl.semaphore_wait(bar, 2))
    sums = None
    for k in range(CHUNKS):
        sl, total = reduce.chunk(k)
        parts = []
        if mode == "fwd":
            resid, bias, gain, offset = ins[2:]
            second = resid[sl, :] + (total + bias[...])
            outs[1][sl, :] = second
            cen, rstd = centre(second)
            low = (cen * rstd * gain[...] + offset[...]).astype(BF16)
        elif mode == "final":
            third, bias, teacher, weight = ins[2:]
            final = third[sl, :] + (total + bias[...])
            outs[1][sl, :] = final.astype(BF16)
            grad = weight[sl, :] * (final - teacher[sl, :].astype(F32))
            outs[2][sl, :] = grad
            low = grad.astype(BF16)
            parts = [low.astype(F32)]
        else:
            x, gain, before = ins[2:]
            back, xhat = norm_back(total, x[sl, :], gain[...])
            grad = before[sl, :] + back
            outs[1][sl, :] = grad
            low = grad.astype(BF16)
            parts = [low.astype(F32), total * xhat, total]
        ch = rows // CHUNKS
        outs[0][pl.ds(pl.multiple_of(t * rows + k * ch, ch), ch), :] = low
        spread.send(k * ch, ch)
        parts = [jnp.sum(p, axis=0, keepdims=True) for p in parts]
        sums = parts if sums is None else [a + b for a, b in zip(sums, parts)]
    for i, s in enumerate(sums):
        outs[n_out - len(sums) + i][...] = s
    spread.forward()
    spread.finish()
    reduce.sent()


def row_kernel(mode, name, collective_id, lhs, w, *extra):
    rows = lhs.shape[0] // 4
    width = w.shape[0]
    full = shaped((4 * rows, width), BF16)
    mine = shaped((rows, width), F32)
    line = shaped((1, width), F32)
    outs = {
        "fwd": [full, mine],
        "final": [full, shaped((rows, width), BF16), mine, line],
        "bwd": [full, mine, line, line, line],
    }[mode]
    ins = [lhs, w, *extra]
    return talking_kernel(
        name,
        collective_id,
        functools.partial(row_body, mode, rows, len(ins), len(outs)),
        ins,
        outs,
        TensorSum.scratch(rows, width) + RowSpread.scratch(),
    )


def talking_kernel(name, collective_id, body, ins, outs, scratch, in_hbm=(), out_hbm=()):
    vm, anywhere = pl.BlockSpec(memory_space=pltpu.VMEM), pl.BlockSpec(memory_space=pl.ANY)
    return pl.pallas_call(
        body,
        out_shape=outs,
        in_specs=[anywhere if i in in_hbm else vm for i in range(len(ins))],
        out_specs=[anywhere if i in out_hbm else vm for i in range(len(outs))],
        scratch_shapes=scratch,
        compiler_params=pltpu.CompilerParams(
            collective_id=collective_id, has_side_effects=True, vmem_limit_bytes=VMEM_BYTES
        ),
        name=name,
    )(*ins)


def shaped(shape, dtype):
    return jax.ShapeDtypeStruct(shape, dtype)


def head_body(dp, gather, *refs):
    (latent, skip_states, skip_in, project_in, small, shift_w, bias, norm_gain, norm_bias, row_bias,
     j0, j1, skip_full, project_g, skipped, residual, first_all, silu, counted,
     acc, psend, precv, small_land, part_out, part_land,
     own_sem, a_s, a_r, b_s, b_r, p_s, p_r, *sems) = refs
    w_sems, g_sems = sems[:16], sems[16:]
    _, t, y, c, sib, yp = tensor_place()
    d = lax.axis_index("dp")
    rows, cols = latent.shape[0], acc.shape[1]
    others = [(d, (t + o) % 4) for o in range(1, 4)]
    place = DpPlace(dp) if gather else None
    peers = others + (place.others() if gather else [])
    bar = greet(peers)
    own = [pltpu.make_async_copy(latent, j0.at[pl.ds(pl.multiple_of(t * rows, rows), rows)], own_sem.at[0]),
           pltpu.make_async_copy(skip_states, j1.at[pl.ds(pl.multiple_of(t * rows, rows), rows)], own_sem.at[1])]
    for cp in own:
        cp.start()
    if gather:
        skip_rows = skip_in.shape[0]
        skip_land = skip_full
        kept = [pltpu.make_async_copy(skip_in, skip_land.at[d], own_sem.at[2]),
                pltpu.make_async_copy(project_in, project_g.at[d], own_sem.at[3])]
        for cp in kept:
            cp.start()
    pl.semaphore_wait(bar, len(peers))
    if gather:
        small_land[d] = small[d]
        smalls = ToAll(place, lambda q: small.at[q], small_land, a_s, a_r)
        skip_g = WeightGather(place, skip_in, skip_land, *w_sems[0:4])
    for cp in own:
        cp.wait()
    spread0 = RowSpread(j0, rows, *g_sems[0:6])
    spread1 = RowSpread(j1, rows, *g_sems[6:12])
    spread0.send(0, rows)
    spread1.send(0, rows)
    if gather:
        smalls.arrived()
        given = small_land[0]
        for i in range(1, dp):
            given = given + small_land[i]
        r = shift_w.shape[0]
        silu[...] = jax.nn.silu(given[:, :r]).astype(BF16)
        counted[...] = jnp.sum(given[:, given.shape[1] - LANES :], axis=0, keepdims=True)
        part_out[...] = dot_nn(silu[...], shift_w[...])
        part_land[d] = part_out[...]
        shifts = ToAll(place, lambda q: part_out, part_land, b_s, b_r)
        skip_g.forward()
        project_gs = [
            WeightGather(place, project_in.at[i], project_g.at[:, i], *w_sems[4 * (i + 1) : 4 * (i + 2)]) for i in range(3)
        ]
    spread0.forward()
    if gather:
        skip_g.arrived()
        kept[0].wait()
        half = dp // 2
        w0 = lambda: skip_full[pl.ds(0, half)].reshape(half * skip_rows, cols)
        w1 = lambda: skip_full[pl.ds(half, half)].reshape(half * skip_rows, cols)
    else:
        half = skip_in.shape[0] // 2
        w0 = lambda: skip_in[pl.ds(0, half), :]
        w1 = lambda: skip_in[pl.ds(half, half), :]
    spread0.finish()
    for b in range(4):
        acc[pl.ds(b * rows, rows), :] = dot_nn(j0[pl.ds(b * rows, rows), :], w0())
    if gather:
        project_gs[0].forward()
    spread1.forward()
    spread1.finish()
    copies = []
    for o in (2, 3, 1, 0):
        b = (t + o) % 4
        here = pl.ds(pl.multiple_of(b * rows, rows), rows)
        value = (acc[here, :] + dot_nn(j1[here, :], w1()) + bias[...]).astype(BF16)
        if o:
            psend[o] = value
            cp = remote(psend.at[o], precv.at[t], p_s.at[o], p_r.at[o], (d, b))
            cp.start()
            copies.append(cp)
        else:
            precv[t] = value
    if gather:
        project_gs[1].forward()
        project_gs[2].forward()
        shifts.arrived()
        shift_all = part_land[0]
        for i in range(1, dp):
            shift_all = shift_all + part_land[i]
        place_row = lax.broadcasted_iota(jnp.int32, shift_all.shape, 0)
        shift = jnp.sum(jnp.where(place_row == d, shift_all, 0.0), axis=0, keepdims=True) + row_bias[pl.ds(3, 1), :]
    else:
        shift = shift_w[...]
    for cp in copies:
        cp.wait_recv()
    for s in range(4):
        skipped[:, s * cols : (s + 1) * cols] = precv[s]
    spread = RowSpread(first_all, rows, *g_sems[12:18])
    ch = rows // CHUNKS
    for k in range(CHUNKS):
        sl = pl.ds(k * ch, ch)
        cen, rstd = centre(skipped[sl, :].astype(F32))
        resid = cen * rstd * norm_gain[pl.ds(0, 1), :] + norm_bias[pl.ds(0, 1), :]
        residual[sl, :] = resid
        cen, rstd = centre(resid)
        first = cen * rstd * norm_gain[pl.ds(1, 1), :] + norm_bias[pl.ds(1, 1), :] + shift
        first_all[pl.ds(pl.multiple_of(t * rows + k * ch, ch), ch), :] = first.astype(BF16)
        spread.send(k * ch, ch)
    spread.forward()
    spread.finish()
    for cp in copies:
        cp.wait_send()
    if gather:
        for g in project_gs:
            g.arrived()
        kept[1].wait()
        for g in project_gs + [skip_g, smalls, shifts]:
            g.sent()


def head_kernel(collective_id, dp, gather, latent, skip_states, skip_in, project_in, small, shift_w, bias, norm_gain, norm_bias, row_bias):
    rows, width = latent.shape
    cols = bias.shape[1]
    line = max(dp // 2, 1)
    dma, vm = pltpu.SemaphoreType.DMA, pltpu.VMEM
    full = shaped((4 * rows, width), BF16)
    seats = small.shape[1]
    outs = [
        full, full,
        shaped((dp,) + skip_in.shape if gather else (16, LANES), BF16),
        shaped((dp,) + project_in.shape if gather else (16, LANES), BF16),
        shaped((rows, width), BF16), shaped((rows, width), F32), full,
        shaped((seats, shift_w.shape[0]) if gather else (16, LANES), BF16),
        shaped((1, LANES), F32),
    ]
    scratch = [
        vm((4 * rows, cols), F32), vm((4, rows, cols), BF16), vm((4, rows, cols), BF16),
        vm(small.shape, F32), vm((seats, width), F32), vm((dp, seats, width) if gather else (1, seats, width), F32),
        dma((4,)), dma((dp,)), dma((dp,)), dma((dp,)), dma((dp,)), dma((4,)), dma((4,)),
    ] + [dma((line,))] * 16 + RowSpread.scratch(1) * 2 + RowSpread.scratch()
    ins = [latent, skip_states, skip_in, project_in, small, shift_w, bias, norm_gain, norm_bias, row_bias]
    return talking_kernel(
        "head", collective_id, functools.partial(head_body, dp, gather), ins, outs, scratch,
        in_hbm=(0, 1, 2, 3) if gather else (0, 1), out_hbm=(3,),
    )


def tail_body(dp, scatter, *refs):
    (p, project_rows, residual, grad_second, skipped, norm_gain, skip_w, j0, j1, silu, pack_in, grad_out, grad_project,
     grad_latent, grad_skip, out_mine, project_mine, skip_mine, shift_grad, shift_bias, pack_sum, pack_cols,
     klow, ksend, krecv, gskip, tile, tile_land, low_out, low_land, pack, pack_x, pack_z, pack_t,
     o_own, o_x, o_z, q_own, q_x, q_z, s_own, s_x, s_z,
     k_s, k_r, t_s, t_r, l_s, l_r, px_s, px_r, pz_s, pz_r, pt_s, pt_r,
     *rest) = refs
    sum_refs, half_refs, rs = rest[:10], rest[10:20], rest[20:]
    _, t, y, c, sib, yp = tensor_place()
    d = lax.axis_index("dp")
    rows, cols = residual.shape[0], krecv.shape[2]
    width = residual.shape[1]
    others = [(d, (t + o) % 4) for o in range(1, 4)]
    place = DpPlace(dp) if scatter else None
    peers = others + (place.others() if scatter else [])
    bar = greet(peers)
    if not scatter:
        place = None
    reduce = TensorSum(*sum_refs)

    def product(b):
        return dot_nt(p[pl.ds(pl.multiple_of(b * rows, rows), rows), :], project_rows[...])

    scatters = []

    def ready():
        pl.semaphore_wait(bar, len(peers))
        if scatter:
            scatters.append(GradScatter(place, grad_out, o_own, o_x, o_z, *rs[0:5]))
            scatters.append(GradScatter(place, grad_project, q_own, q_x, q_z, *rs[5:10]))

    reduce.start(product, ready)
    sums = None
    for k in range(CHUNKS):
        sl, total = reduce.chunk(k)
        back, xhat = norm_back(total, residual[sl, :], norm_gain[pl.ds(1, 1), :])
        grad = grad_second[sl, :] + back
        back0, xhat0 = norm_back(grad, skipped[sl, :].astype(F32), norm_gain[pl.ds(0, 1), :])
        klow[sl, :] = back0.astype(BF16)
        parts = [back0.astype(BF16).astype(F32), total * xhat, total, grad * xhat0, grad]
        parts = [jnp.sum(v, axis=0, keepdims=True) for v in parts]
        sums = parts if sums is None else [a + b for a, b in zip(sums, parts)]
    for s in range(4):
        ksend[s] = klow[:, s * cols : (s + 1) * cols]
    copies = []
    for o in (2, 3, 1):
        b = (t + o) % 4
        cp = remote(ksend.at[b], krecv.at[t], k_s.at[o], k_r.at[o], (d, b))
        cp.start()
        copies.append(cp)
    krecv[t] = ksend[t]
    bias_skip, gain_first, offset_first, gain_skip, offset_skip = sums
    tile[...] = jnp.broadcast_to(offset_first, tile.shape)
    tile_land[t] = tile[...]
    tiles = []
    for o in (1, 2, 3):
        cp = remote(tile, tile_land.at[t], t_s.at[o], t_r.at[o], (d, (t + o) % 4))
        cp.start()
        tiles.append(cp)
    pack[...] = pack_in[...]
    for i, v in enumerate((gain_skip, gain_first, offset_skip, offset_first, bias_skip)):
        pack[pl.ds(i, 1), :] = v
    if scatter:
        pack_cp = remote(pack, pack_x, px_s.at[0], px_r.at[0], place.pair)
        pack_cp.start()
    for cp in copies:
        cp.wait_recv()
    reduce.sent()
    halves = [TensorSum(*sum_refs), TensorSum(*half_refs)]
    for h, half in enumerate(halves):
        half.start(lambda b, h=h: dot_nt(krecv[b], skip_w[pl.ds(h * width, width), :]))
    for cp in tiles:
        cp.wait_recv()
    shift_low = tile_land[0] + tile_land[1] + tile_land[2] + tile_land[3]
    low_out[...] = shift_low.astype(BF16).astype(F32)
    if scatter:
        low_land[d] = low_out[...]
        lows = ToAll(place, lambda q: low_out, low_land, l_s, l_r)
        pack_cp.wait_recv()
        pack_cp.wait_send()
        pack[...] = pack[...] + pack_x[...]
        pack_z[place.zi] = pack[...]
        packs = []
        for j in range(1, place.line):
            cp = remote(pack, pack_z.at[place.zi], pz_s.at[j], pz_r.at[j], (place.ahead(j), place.t))
            cp.start()
            packs.append(cp)
        scatters[0].pass_on()
        scatters[1].pass_on()
    k_all = krecv[...].reshape(4 * rows, cols)
    n = gskip.shape[0] // 2
    for h, joined in enumerate((j0, j1)):
        gskip[pl.ds(h * n, n)] = dot_tn(joined[...], k_all).astype(BF16).reshape((n,) + gskip.shape[1:])
    if scatter:
        scatters.append(GradScatter(place, gskip, s_own, s_x, s_z, *rs[10:15]))
        lows.arrived()
        seat = lax.broadcasted_iota(jnp.int32, low_out.shape, 0)
        low_all = jnp.zeros(low_out.shape, F32)
        for i in range(dp):
            low_all = low_all + jnp.where(seat == i, low_land[i], 0.0)
        shift_grad[...] = dot_tn(silu[...], low_all.astype(BF16))
        shift_bias[...] = jnp.sum(low_all, axis=0, keepdims=True)
        for cp in packs:
            cp.wait_recv()
            cp.wait_send()
        total = pack_z[0]
        for i in range(1, place.line):
            total = total + pack_z[i]
        pack[...] = total
    else:
        shift_grad[...] = low_out[...]
        shift_bias[...] = shift_grad[pl.ds(0, 1), :]
    pack_t[t] = pack[...]
    ends = []
    for o in (1, 2, 3):
        cp = remote(pack, pack_t.at[t], pt_s.at[o], pt_r.at[o], (d, (t + o) % 4))
        cp.start()
        ends.append(cp)
    for half, out in zip(halves, (grad_latent, grad_skip)):
        for k in range(CHUNKS):
            sl, total = half.chunk(k)
            out[sl, :] = total
        half.sent()
    if scatter:
        scatters[2].pass_on()
    for cp in ends:
        cp.wait_recv()
        cp.wait_send()
    pack_sum[...] = pack_t[0] + pack_t[1] + pack_t[2] + pack_t[3]
    for s in range(4):
        pack_cols[s] = pack_t[s, pl.ds(PACK_SUMS, PACK_ROWS - PACK_SUMS), :]
    if scatter:
        out_mine[...] = scatters[0].result()
        project_mine[...] = scatters[1].result()
        skip_mine[...] = scatters[2].result()
        for s in scatters:
            s.sent()
        lows.sent()
    else:
        out_mine[...] = jnp.zeros(out_mine.shape, F32)
        project_mine[...] = jnp.zeros(project_mine.shape, F32)
        skip_mine[...] = gskip[...]
    for cp in copies + tiles:
        cp.wait_send()


PACK_ROWS, PACK_SUMS = 24, 16


def tail_kernel(collective_id, dp, scatter, p, project_rows, residual, grad_second, skipped, norm_gain, skip_w, j0, j1, silu, pack_in, grad_out, grad_project):
    rows, width = residual.shape
    cols = skip_w.shape[1]
    line = max(dp // 2, 1)
    dma, vm = pltpu.SemaphoreType.DMA, pltpu.VMEM
    seats = max(8, -(-dp // 8) * 8) if scatter else 8
    skip_rows = skip_w.shape[0] // dp if scatter else skip_w.shape[0] // 2
    out_shape = grad_out.shape[1:] if scatter else (8, LANES)
    project_shape = grad_project.shape[1:] if scatter else (8, LANES)
    gskip = (dp if scatter else 2, skip_rows, cols)
    skip_shape = gskip[1:]
    outs = [
        shaped((rows, width), F32), shaped((rows, width), F32),
        shaped(out_shape, F32), shaped(project_shape, F32),
        shaped(skip_shape, F32) if scatter else shaped(gskip, BF16),
        shaped((silu.shape[1], width) if scatter else (seats, width), F32), shaped((1, width), F32),
        shaped((PACK_ROWS, width), F32), shaped((4, PACK_ROWS - PACK_SUMS, width), F32),
    ]

    def bufs(shape):
        n = line if scatter else 1
        s = shape if scatter else (16, LANES)
        return [vm((n,) + s, BF16), vm((n,) + s, BF16), vm((max(n - 1, 1),) + s, BF16)]

    scratch = [
        vm((rows, width), BF16), vm((4, rows, cols), BF16), vm((4, rows, cols), BF16), vm(gskip, BF16),
        vm((seats, width), F32), vm((4, seats, width), F32), vm((seats, width), F32), vm((dp if scatter else 1, seats, width), F32),
        vm((PACK_ROWS, width), F32), vm((PACK_ROWS, width), F32), vm((line if scatter else 1, PACK_ROWS, width), F32), vm((4, PACK_ROWS, width), F32),
        *bufs(out_shape), *bufs(project_shape), *bufs(skip_shape),
        dma((4,)), dma((4,)), dma((4,)), dma((4,)), dma((dp,)), dma((dp,)), dma((1,)), dma((1,)), dma((line,)), dma((line,)), dma((4,)), dma((4,)),
    ] + TensorSum.scratch(rows, width) * 2 + [dma((line,))] * 15
    ins = [p, project_rows, residual, grad_second, skipped, norm_gain, skip_w, j0, j1, silu, pack_in, grad_out, grad_project]
    return talking_kernel("tail", collective_id, functools.partial(tail_body, dp, scatter), ins, outs, scratch, in_hbm=(11, 12))


def head_stats(u, mask, size):
    mean = jnp.sum(u, axis=-1, keepdims=True) * (1.0 / size)
    cen = (u - mean) * mask
    spread = jnp.sum(cen * cen, axis=-1, keepdims=True) * (1.0 / size)
    return cen, lax.rsqrt(spread + EPSILON)


def head_norm(u, mask, gain, offset, size):
    cen, rstd = head_stats(u, mask, size)
    return cen * rstd * gain + offset


def turn(u, cosine, sine):
    return u * cosine + pltpu.roll(u, LANES // 2, 1) * sine


def turn_back(u, cosine, sine):
    return u * cosine - pltpu.roll(u, LANES // 2, 1) * sine


def head_back(grad, u, mask, gain, size):
    cen, rstd = head_stats(u, mask, size)
    xhat = cen * rstd
    dg = grad * gain
    mean = jnp.sum(dg, axis=-1, keepdims=True) * (1.0 / size)
    inner = jnp.sum(dg * xhat, axis=-1, keepdims=True) * (1.0 / size)
    back = rstd * ((dg - mean) * mask - xhat * inner)
    return back, jnp.sum(grad * xhat, axis=0, keepdims=True), jnp.sum(grad, axis=0, keepdims=True)


def head_at(h):
    return pl.ds(h * LANES, LANES)


def attend(q_ref, k_ref, v_ref, out_ref, lse_ref, heads, scale, block, real_keys):
    queries, keys = q_ref.shape[0], k_ref.shape[0]

    def step(i, _):
        here = pl.ds(pl.multiple_of(i * block, block), block)
        for h in range(heads):
            hs = head_at(h)
            scores = dot_nt(k_ref[:, hs], q_ref[here, hs]) * scale
            if real_keys < keys:
                place = lax.broadcasted_iota(jnp.int32, scores.shape, 0)
                scores = jnp.where(place < real_keys, scores, NEGATIVE)
            highest = jnp.max(scores, axis=0, keepdims=True)
            exponent = jnp.exp(scores - highest)
            denominator = jnp.sum(exponent, axis=0, keepdims=True)
            probs = (exponent * (1.0 / denominator)).astype(BF16)
            mixed = dot_tn(v_ref[:, hs], probs)
            out_ref[here, hs] = mixed.T.astype(BF16)
            lse_ref[i, pl.ds(h, 1), :] = highest + jnp.log(denominator)
        return 0

    lax.fori_loop(0, queries // block, step, 0)


def attend_back(q_ref, k_ref, v_ref, do_ref, lse_ref, dq_ref, dk_ref, dv_ref, heads, scale, block, real_keys):
    queries, keys = q_ref.shape[0], k_ref.shape[0]
    dk_ref[...] = jnp.zeros(dk_ref.shape, F32)
    dv_ref[...] = jnp.zeros(dv_ref.shape, F32)

    def step(i, _):
        here = pl.ds(pl.multiple_of(i * block, block), block)
        for h in range(heads):
            hs = head_at(h)
            q, k, v, do = q_ref[here, hs], k_ref[:, hs], v_ref[:, hs], do_ref[here, hs]
            scores = dot_nt(k, q) * scale
            if real_keys < keys:
                place = lax.broadcasted_iota(jnp.int32, scores.shape, 0)
                scores = jnp.where(place < real_keys, scores, NEGATIVE)
            probs = jnp.exp(scores - lse_ref[i, pl.ds(h, 1), :])
            grad_probs = dot_nt(v, do)
            inner = jnp.sum(probs * grad_probs, axis=0, keepdims=True)
            grad_scores = (probs * (grad_probs - inner)).astype(BF16)
            dv_ref[:, hs] += dot_nn(probs.astype(BF16), do)
            dk_ref[:, hs] += dot_nn(grad_scores, q) * scale
            dq_ref[here, hs] = dot_tn(k, grad_scores).T * scale
        return 0

    lax.fori_loop(0, queries // block, step, 0)


def self_fwd_body(size, scale, heads, block, x, w, bias, cosine, sine, gain, offset, mask, fold, pre, low, mixed, lse, padded):
    rows = x.shape[0]
    span = heads * LANES

    def project(i, _):
        here = pl.ds(pl.multiple_of(i * block, block), block)
        for part in range(3):
            cols = pl.ds(part * span, span)
            out = dot_nn(x[here, :], w[part]) + bias[part]
            if part < 2:
                pre[here, cols] = out
                for h in range(heads):
                    u = out[:, h * LANES : (h + 1) * LANES]
                    val = head_norm(u, mask[...], gain[pl.ds(part, 1), :], offset[pl.ds(part, 1), :], size)
                    val = turn(val, cosine[here, :], sine[here, :])
                    low[here, pl.ds(part * span + h * LANES, LANES)] = val.astype(BF16)
            else:
                low[here, cols] = out.astype(BF16)
        return 0

    lax.fori_loop(0, rows // block, project, 0)
    attend(
        low.at[:, pl.ds(0, span)], low.at[:, pl.ds(span, span)], low.at[:, pl.ds(2 * span, span)],
        padded, lse, heads, scale, block, rows,
    )
    mixed[...] = dot_nt(padded[...], fold[...]).astype(BF16)


def self_bwd_body(
    size, scale, heads, block, c_all, w_out, pre, low, lse, cosine, sine, gain, mask, fold, mixed, x,
    p, grad_out, grad_project, gains, offsets, sums, do, dq, dk, dv, p_low,
):
    rows = c_all.shape[0]
    span = heads * LANES

    def spread(i, _):
        here = pl.ds(pl.multiple_of(i * block, block), block)
        narrow = dot_nn(c_all[here, :], w_out[...]).astype(BF16)
        do[here, :] = dot_nn(narrow, fold[...]).astype(BF16)
        return 0

    lax.fori_loop(0, rows // block, spread, 0)
    attend_back(
        low.at[:, pl.ds(0, span)], low.at[:, pl.ds(span, span)], low.at[:, pl.ds(2 * span, span)],
        do, lse, dq, dk, dv, heads, scale, block, rows,
    )
    gains[...] = jnp.zeros(gains.shape, F32)
    offsets[...] = jnp.zeros(offsets.shape, F32)
    sums[...] = jnp.zeros(sums.shape, F32)

    def finish(i, _):
        here = pl.ds(pl.multiple_of(i * block, block), block)
        for part, grad_ref in enumerate((dq, dk, dv)):
            for h in range(heads):
                hs = head_at(h)
                wide = pl.ds(part * span + h * LANES, LANES)
                grad = grad_ref[here, hs]
                if part < 2:
                    grad = turn_back(grad, cosine[here, :], sine[here, :])
                    grad, g, o = head_back(grad, pre[here, wide], mask[...], gain[pl.ds(part, 1), :], size)
                    gains[pl.ds(part, 1), :] += g
                    offsets[pl.ds(part, 1), :] += o
                grad_low = grad.astype(BF16)
                p[here, wide] = grad_low
                if part != 1:
                    sums[:, wide] += jnp.sum(grad_low.astype(F32), axis=0, keepdims=True)
            p_low[part, here, :] = dot_nt(p[here, pl.ds(part * span, span)], fold[...]).astype(BF16)
        return 0

    lax.fori_loop(0, rows // block, finish, 0)
    by_place = lambda v: v.astype(BF16).reshape(grad_out.shape)
    grad_out[...] = by_place(dot_tn(c_all[...], mixed[...]))
    for part in range(3):
        grad_project[:, part] = by_place(dot_tn(x[...], p_low[part]))


def text_body(size, heads, real, x, w, bias, gain, offset, mask, pre, low):
    span = heads * LANES
    for part in range(2):
        out = dot_nn(x[...], w[part]) + bias[part]
        if part == 0:
            pre[...] = out
            for h in range(heads):
                hs = head_at(h)
                val = head_norm(out[:, h * LANES : (h + 1) * LANES], mask[...], gain[...], offset[...], size)
                low[:, hs] = val.astype(BF16)
        else:
            low[:, pl.ds(span, span)] = out.astype(BF16)


def cross_fwd_body(
    size, scale, heads, block, real, x, w, bias, text_low, cosine, sine, gain, offset, mask, fold,
    pre, low, mixed, lse, padded,
):
    rows = x.shape[0]
    span = heads * LANES

    def project(i, _):
        here = pl.ds(pl.multiple_of(i * block, block), block)
        out = dot_nn(x[here, :], w[...]) + bias[...]
        pre[here, :] = out
        for h in range(heads):
            val = head_norm(out[:, h * LANES : (h + 1) * LANES], mask[...], gain[...], offset[...], size)
            low[here, head_at(h)] = turn(val, cosine[here, :], sine[here, :]).astype(BF16)
        return 0

    lax.fori_loop(0, rows // block, project, 0)
    attend(low, text_low.at[:, pl.ds(0, span)], text_low.at[:, pl.ds(span, span)], padded, lse, heads, scale, block, real)
    mixed[...] = dot_nt(padded[...], fold[...]).astype(BF16)


def cross_bwd_body(
    size, scale, heads, block, real, c_all, w_out, pre, low, text_pre, text_low, lse, cosine, sine, gain, text_gain, mask, fold,
    mixed, x, text, text_w,
    p, grads, grad_text, gains, offsets, sums, text_sums, do, dq, dk, dv, p_low, text_p, text_p_low,
):
    rows = c_all.shape[0]
    span = heads * LANES

    def spread(i, _):
        here = pl.ds(pl.multiple_of(i * block, block), block)
        narrow = dot_nn(c_all[here, :], w_out[...]).astype(BF16)
        do[here, :] = dot_nn(narrow, fold[...]).astype(BF16)
        return 0

    lax.fori_loop(0, rows // block, spread, 0)
    attend_back(
        low, text_low.at[:, pl.ds(0, span)], text_low.at[:, pl.ds(span, span)],
        do, lse, dq, dk, dv, heads, scale, block, real,
    )
    gains[...] = jnp.zeros(gains.shape, F32)
    offsets[...] = jnp.zeros(offsets.shape, F32)
    sums[...] = jnp.zeros(sums.shape, F32)

    def finish(i, _):
        here = pl.ds(pl.multiple_of(i * block, block), block)
        for h in range(heads):
            hs = head_at(h)
            grad = turn_back(dq[here, hs], cosine[here, :], sine[here, :])
            grad, g, o = head_back(grad, pre[here, hs], mask[...], gain[...], size)
            gains[pl.ds(0, 1), :] += g
            offsets[pl.ds(0, 1), :] += o
            grad_low = grad.astype(BF16)
            p[here, hs] = grad_low
            sums[:, hs] += jnp.sum(grad_low.astype(F32), axis=0, keepdims=True)
        p_low[here, :] = dot_nt(p[here, :], fold[...]).astype(BF16)
        return 0

    lax.fori_loop(0, rows // block, finish, 0)
    for h in range(heads):
        hs = head_at(h)
        grad, g, o = head_back(dk[:, hs], text_pre[:, hs], mask[...], text_gain[...], size)
        gains[pl.ds(1, 1), :] += g
        offsets[pl.ds(1, 1), :] += o
        text_p[:, hs] = grad.astype(BF16)
        low_v = dv[:, hs].astype(BF16)
        text_p[:, pl.ds(span + h * LANES, LANES)] = low_v
        text_sums[:, hs] = jnp.sum(low_v.astype(F32), axis=0, keepdims=True)
    for part in range(2):
        text_p_low[part] = dot_nt(text_p[:, pl.ds(part * span, span)], fold[...]).astype(BF16)
    parts = grads.shape[0]

    def put(start, value):
        count = value.shape[0] // parts
        grads[:, pl.ds(start, count)] = value.astype(BF16).reshape(parts, count, value.shape[1])
        return start + count

    at = put(0, dot_tn(c_all[...], mixed[...]))
    at = put(at, dot_tn(x[...], p_low[...]))
    for part in range(2):
        at = put(at, dot_tn(text[...], text_p_low[part]))
    grad_text[...] = (
        dot_nt(text_p[:, pl.ds(0, span)], text_w[0]) + dot_nt(text_p[:, pl.ds(span, span)], text_w[1])
    ).astype(BF16)


def local_kernel(name, body, ins, outs, scratch=()):
    vm = pl.BlockSpec(memory_space=pltpu.VMEM)
    return pl.pallas_call(
        body,
        out_shape=outs,
        in_specs=[vm] * len(ins),
        out_specs=[vm] * len(outs),
        scratch_shapes=list(scratch),
        compiler_params=pltpu.CompilerParams(vmem_limit_bytes=VMEM_BYTES),
        name=name,
    )(*ins)


def fold_matrix(heads, size):
    out = np.zeros((heads * size, heads * LANES), np.float32)
    for h in range(heads):
        for e in range(size):
            out[h * size + e, h * LANES + (e % 2) * (LANES // 2) + e // 2] = 1.0
    return out


def body(
    latent, skip_states, text_states, condition, teacher, loss_mask, true_counts, positions,
    skip_proj, shift_proj, self_project, self_output, cross_query, cross_keyval, cross_output, hidden_up, hidden_down,
    norm_gain, norm_bias, head_gain, head_bias, column_bias, hidden_bias, row_bias,
):
    d, t = lax.axis_index("dp"), lax.axis_index("tensor")
    dp, tensor = lax.axis_size("dp"), lax.axis_size("tensor")
    rows, width = latent.shape
    group = rows * tensor
    size = head_gain.shape[1]
    cols = self_project.shape[2]
    heads = cols // size
    span = heads * LANES
    hidden = hidden_up.shape[1]
    text_len = text_states.shape[1]
    text_pad = -(-text_len // 16) * 16
    scale = size ** (-0.5)
    block = min(256, group)
    fold_np = fold_matrix(heads, size)
    fold = jnp.asarray(fold_np, BF16)
    one_np = fold_np[:size, :LANES]
    mask = jnp.asarray(one_np.sum(0, keepdims=True), F32)

    def widen_head(v):
        return jnp.dot(v, jnp.asarray(one_np), precision=lax.Precision.HIGHEST)

    def widen_cols(v):
        return jnp.dot(v, jnp.asarray(fold_np), precision=lax.Precision.HIGHEST)

    def narrow_head(v):
        return jnp.dot(v, jnp.asarray(one_np.T), precision=lax.Precision.HIGHEST)

    def narrow_cols(v):
        return jnp.dot(v, jnp.asarray(fold_np.T), precision=lax.Precision.HIGHEST)

    own = shift_proj.shape[0] % 16 == 0 and self_output.shape[1] % 16 == 0 and dp % 2 == 0
    parts = dp if own else 1
    text_rows = jnp.pad(text_states[0], ((0, text_pad - text_len), (0, 0)))
    share, text_share = self_output.shape[1], cross_keyval.shape[0]
    few = jnp.concatenate(
        [self_output.T, cross_query, cross_output.T, cross_keyval[:, 0], cross_keyval[:, 1]], axis=0
    )
    few_all = lax.all_gather(few, "dp", axis=0, tiled=False)
    out_t = few_all[:, :share].reshape(width, cols)
    query_full = few_all[:, share : 2 * share].reshape(width, cols)
    cross_out_t = few_all[:, 2 * share : 3 * share].reshape(width, cols)
    keyval_full = [
        few_all[:, 3 * share + i * text_share : 3 * share + (i + 1) * text_share].reshape(-1, cols) for i in range(2)
    ]
    query_wide = dot_nn(query_full, fold).astype(BF16)
    keyval_wide = jnp.stack([dot_nn(v, fold).astype(BF16) for v in keyval_full])

    bias_cols = lax.dynamic_slice_in_dim(column_bias, t * cols, cols, 1)
    bias_wide = widen_cols(bias_cols)
    zero_wide = jnp.zeros((1, span), F32)
    self_bias = jnp.stack([bias_wide[0:1], zero_wide, bias_wide[1:2]])
    text_bias = jnp.stack([zero_wide, bias_wide[3:4]])
    hidden_cols_bias = lax.dynamic_slice_in_dim(hidden_bias, t * hidden, hidden, 0)
    gain_wide, offset_wide = widen_head(head_gain), widen_head(head_bias)

    quarter = size // 4
    lane_np = np.zeros((2, LANES), np.float32)
    sign_np = np.zeros((1, LANES), np.float32)
    for i in range(size // 2):
        f = np.float32(10000.0 ** (-(i % quarter) / quarter))
        for half in range(2):
            lane_np[i // quarter, half * (LANES // 2) + i] = f
            sign_np[0, half * (LANES // 2) + i] = 2 * half - 1
    place = positions.astype(F32)
    angles = place[0][:, None] * lane_np[0] + place[1][:, None] * lane_np[1]
    cosine = jnp.cos(angles) * mask
    sine = jnp.sin(angles) * sign_np

    project_in = jnp.transpose(self_project, (1, 0, 2))
    r = shift_proj.shape[0]
    if own:
        seats = max(8, -(-dp // 8) * 8)
        lanes = -(-r // LANES) * LANES
        slices = jnp.pad(condition.astype(F32).reshape(dp, r), ((0, 0), (0, lanes - r)))
        slices = jnp.concatenate([slices, jnp.broadcast_to(true_counts.astype(F32)[:, None], (dp, LANES))], axis=1)
        seat = (jnp.arange(seats) == d).astype(F32)
        small = slices[:, None, :] * seat[None, :, None]
        skip_in, shift_in = skip_proj, shift_proj
    else:
        small_all = lax.all_gather(
            jnp.concatenate([condition.astype(F32), true_counts.astype(F32)[:, None]], axis=1), "dp", axis=0, tiled=True
        )
        silu_all = jax.nn.silu(small_all[:, :width]).astype(BF16)
        silu = lax.dynamic_slice_in_dim(silu_all, d * r, r, 1)
        shift_in = lax.psum_scatter(dot_nn(silu, shift_proj), "dp", scatter_dimension=0, tiled=True) + row_bias[3:4]
        small = jnp.zeros((1, 8, LANES), F32)
        skip_in = lax.all_gather(skip_proj, "dp", axis=0, tiled=True)
        project_in = lax.all_gather(project_in, "dp", axis=0, tiled=False)
    joined0, joined1, skip_g, project_g, skipped, residual, first_all, silu_k, counted = head_kernel(
        0, dp, own, latent, skip_states, skip_in, project_in, small, shift_in, bias_cols[4:5], norm_gain, norm_bias, row_bias
    )
    if own:
        silu, counted = silu_k, counted[0, 0]
        skip_full = skip_g.reshape(2 * width, cols)
    else:
        counted, project_g, skip_full = jnp.sum(small_all[:, width]), project_in, skip_in
    hold, first_hold = lax.optimization_barrier(((hidden_up, hidden_down.T), first_all))
    up_full = lax.all_gather(hold[0], "dp", axis=0, tiled=True)
    down_t = lax.all_gather(hold[1], "dp", axis=0, tiled=True)
    project_full = jnp.transpose(project_g, (1, 0, 2, 3)).reshape(3, width, cols)
    project_wide = jnp.einsum("cdk,kl->cdl", project_full, fold, preferred_element_type=F32).astype(BF16)

    lse_shape = (group // block, heads, block)
    pre, low, mixed, lse = local_kernel(
        "self_fwd",
        functools.partial(self_fwd_body, size, scale, heads, block),
        [first_all, project_wide, self_bias, cosine, sine, gain_wide[0:2], offset_wide[0:2], mask, fold],
        [shaped((group, 2 * span), F32), shaped((group, 3 * span), BF16), shaped((group, cols), BF16), shaped(lse_shape, F32)],
        [pltpu.VMEM((group, span), BF16)],
    )
    third_all, second = row_kernel(
        "fwd", "rows_self", 2, mixed, out_t, residual, row_bias[0:1], norm_gain[2:3], norm_bias[2:3]
    )

    text_pre, text_low = local_kernel(
        "text_fwd",
        functools.partial(text_body, size, heads, text_len),
        [text_rows, keyval_wide, text_bias, gain_wide[3:4], offset_wide[3:4], mask],
        [shaped((text_pad, span), F32), shaped((text_pad, 2 * span), BF16)],
    )
    cross_pre, cross_low, cross_mixed, cross_lse = local_kernel(
        "cross_fwd",
        functools.partial(cross_fwd_body, size, scale, heads, block, text_len),
        [third_all, query_wide, bias_wide[2:3], text_low, cosine, sine, gain_wide[2:3], offset_wide[2:3], mask, fold],
        [shaped((group, span), F32), shaped((group, span), BF16), shaped((group, cols), BF16), shaped(lse_shape, F32)],
        [pltpu.VMEM((group, span), BF16)],
    )
    fourth_all, third_sum = row_kernel(
        "fwd", "rows_cross", 3, cross_mixed, cross_out_t, second, row_bias[1:2], norm_gain[3:4], norm_bias[3:4]
    )

    upper_pre = dot_nn(fourth_all, up_full) + hidden_cols_bias
    active, pull_gelu = jax.vjp(lambda v: jax.nn.gelu(v, approximate=True), upper_pre)
    active_low = active.astype(BF16)
    row_ids = t * rows + jnp.arange(rows)
    weight = loss_mask.astype(F32) * (row_ids < true_counts[0]).astype(F32)
    loss_scale = dp * group / counted
    grad_all, block_out, grad_final, bias_mlp = row_kernel(
        "final", "rows_mlp", 4, active_low, down_t, third_sum, row_bias[2:3], teacher, (loss_scale * weight)[:, None]
    )

    grad_active = dot_nn(grad_all, down_t)
    (grad_upper,) = pull_gelu(grad_active)
    grad_upper_low = grad_upper.astype(BF16)
    bias_hidden = jnp.sum(grad_upper_low.astype(F32), axis=0)
    grad_down_t = dot_tn(grad_all, active_low).astype(BF16)
    grad_up = dot_tn(fourth_all, grad_upper_low).astype(BF16)
    down_mine = lax.psum_scatter(grad_down_t, "dp", scatter_dimension=0, tiled=True)
    up_mine = lax.psum_scatter(grad_up, "dp", scatter_dimension=0, tiled=True)
    c_all, grad_third, bias_cross_out, gain_fourth, offset_fourth = row_kernel(
        "bwd", "rows_up", 5, grad_upper_low, up_full, third_sum, norm_gain[3:4], grad_final
    )

    few_rows = 2 * share + 2 * text_share if own else 2 * width + 2 * text_states.shape[2]
    qp, few_grads, text_part, cross_gains, cross_offsets, cross_sums, text_sums = local_kernel(
        "cross_bwd",
        functools.partial(cross_bwd_body, size, scale, heads, block, text_len),
        [c_all, cross_out_t, cross_pre, cross_low, text_pre, text_low, cross_lse, cosine, sine,
         gain_wide[2:3], gain_wide[3:4], mask, fold, cross_mixed, third_all, text_rows, keyval_wide],
        [shaped((group, span), BF16), shaped((parts, few_rows, cols), BF16), shaped((text_pad, text_states.shape[2]), BF16),
         shaped((2, LANES), F32), shaped((2, LANES), F32), shaped((1, span), F32), shaped((1, span), F32)],
        [pltpu.VMEM((group, span), BF16), pltpu.VMEM((group, span), F32), pltpu.VMEM((text_pad, span), F32),
         pltpu.VMEM((text_pad, span), F32), pltpu.VMEM((group, cols), BF16), pltpu.VMEM((text_pad, 2 * span), BF16),
         pltpu.VMEM((2, text_pad, cols), BF16)],
    )
    s_all, grad_second, bias_attn, gain_third, offset_third = row_kernel(
        "bwd", "rows_query", 6, qp, query_wide, second, norm_gain[2:3], grad_third
    )
    if not own:
        cuts = np.cumsum([0, width, width, text_states.shape[2], text_states.shape[2]])
        few_grads = jnp.concatenate(
            [few_grads[0, a:b].reshape(dp, -1, cols) for a, b in zip(cuts[:-1], cuts[1:])], axis=1
        )
    grad_text = lax.psum(text_part[:text_len], "tensor").astype(F32)[None]
    few_mine = lax.psum_scatter(few_grads.reshape(-1, cols), "dp", scatter_dimension=0, tiled=True).astype(F32)

    p, grad_out, grad_project, self_gains, self_offsets, self_sums = local_kernel(
        "self_bwd",
        functools.partial(self_bwd_body, size, scale, heads, block),
        [s_all, out_t, pre, low, lse, cosine, sine, gain_wide[0:2], mask, fold, mixed, first_all],
        [shaped((group, 3 * span), BF16), shaped((parts, width // parts, cols), BF16), shaped((parts, 3, width // parts, cols), BF16),
         shaped((2, LANES), F32), shaped((2, LANES), F32), shaped((1, 3 * span), F32)],
        [pltpu.VMEM((group, span), BF16)] + [pltpu.VMEM((group, span), F32)] * 3 + [pltpu.VMEM((3, group, cols), BF16)],
    )

    head_part = jnp.concatenate([self_gains, cross_gains, self_offsets, cross_offsets], axis=0).reshape(1, -1)
    column_rows = narrow_cols(
        jnp.concatenate([self_sums[:, :span], self_sums[:, 2 * span :], cross_sums, text_sums], axis=0)
    )
    own_cols = jnp.concatenate([column_rows.reshape(-1), bias_hidden])
    sums_in = jnp.concatenate(
        [jnp.zeros((5, width), F32), gain_third, gain_fourth, offset_third, offset_fourth, bias_attn, bias_cross_out, bias_mlp,
         jnp.pad(head_part, ((0, 0), (0, width - head_part.shape[1]))), jnp.zeros((PACK_SUMS - 13, width), F32),
         jnp.pad(own_cols, (0, (PACK_ROWS - PACK_SUMS) * width - own_cols.shape[0])).reshape(-1, width)], axis=0
    )
    project_rows = jnp.transpose(project_wide, (1, 0, 2)).reshape(width, 3 * span)
    grad_latent, grad_skip, out_mine, project_mine, skip_mine, shift_grad, shift_bias, pack_sum, pack_cols = tail_kernel(
        7, dp, own, p, project_rows, residual, grad_second, skipped, norm_gain, skip_full, joined0, joined1,
        silu if own else jnp.zeros((8, LANES), BF16), sums_in, grad_out, grad_project,
    )
    if not own:
        shift_all = lax.all_gather(shift_grad[:1], "dp", axis=0, tiled=True)
        shift_bias = jnp.sum(shift_all, axis=0, keepdims=True)
        shift_grad = dot_tn(silu, shift_all.astype(BF16))
        pack_sum, pack_cols = lax.psum((pack_sum, pack_cols), "dp")
        out_mine = lax.psum_scatter(grad_out[0], "dp", scatter_dimension=0, tiled=True)
        project_mine = lax.psum_scatter(grad_project[0], "dp", scatter_dimension=1, tiled=True)
        skip_mine = lax.psum_scatter(skip_mine.reshape(-1, cols), "dp", scatter_dimension=0, tiled=True)
    cols_all = pack_cols.reshape(tensor, -1)
    column_sums = jnp.transpose(cols_all[:, : 4 * cols].reshape(tensor, 4, cols), (1, 0, 2)).reshape(4, width)
    hidden_sums = cols_all[:, 4 * cols : 4 * cols + hidden].reshape(-1)
    head_sums = narrow_head(pack_sum[12, : 8 * LANES].reshape(8, LANES))
    return (
        block_out,
        grad_latent,
        grad_skip,
        grad_text,
        skip_mine.astype(F32),
        shift_grad,
        jnp.transpose(project_mine, (1, 0, 2)).astype(F32),
        out_mine.T.astype(F32),
        few_mine[share : 2 * share],
        jnp.transpose(few_mine[2 * share :].reshape(2, text_share, cols), (1, 0, 2)),
        few_mine[:share].T,
        up_mine.astype(F32),
        down_mine.T.astype(F32),
        jnp.concatenate([pack_sum[0:2], pack_sum[5:7]]),
        jnp.concatenate([pack_sum[2:4], pack_sum[7:9]]),
        head_sums[:4],
        head_sums[4:],
        jnp.concatenate([column_sums, pack_sum[4:5]]),
        hidden_sums,
        jnp.concatenate([pack_sum[9:12], shift_bias]),
    )


def solution(mesh):
    both = ("dp", "tensor")
    rows2, split2, cross2 = P(both, None), P("dp", "tensor"), P("tensor", "dp")
    middle = P("dp", None, "tensor")
    return jax.shard_map(
        body,
        mesh=mesh,
        in_specs=(
            rows2, rows2, P("dp", None, None), P("dp", None), rows2, P(both), P("dp"), P(None, "dp"),
            split2, P("dp", None), middle, cross2, split2, middle, cross2, split2, cross2,
            P(), P(), P(), P(), P(), P(), P(),
        ),
        out_specs=(
            rows2, rows2, rows2, P("dp", None, None),
            split2, P("dp", None), middle, cross2, split2, middle, cross2, split2, cross2,
            P(), P(), P(), P(), P(), P(), P(),
        ),
        check_vma=False,
    )
```

```python
import functools
from types import SimpleNamespace

import jax
import jax.numpy as jnp
import numpy as np
from jax import lax
from jax.experimental import pallas as pl
from jax.experimental.pallas import tpu as pltpu
from jax.sharding import PartitionSpec as P

EPSILON = 1e-06
MESH = pl.DeviceIdType.MESH
BF16, F32 = jnp.bfloat16, jnp.float32
LANES = 128
CHUNKS = 2
VMEM_BYTES = 60 * 2**20
NEGATIVE = -1e30


def dot_nn(left, right):
    return jnp.dot(left, right, preferred_element_type=F32)


def dot_nt(left, right):
    return lax.dot_general(left, right, (((1,), (1,)), ((), ())), preferred_element_type=F32)


def dot_tn(left, right):
    return lax.dot_general(left, right, (((0,), (0,)), ((), ())), preferred_element_type=F32)


def centre(x):
    cen = x - jnp.mean(x, axis=-1, keepdims=True)
    spread = jnp.mean(cen * cen, axis=-1, keepdims=True)
    return cen, lax.rsqrt(spread + EPSILON)


def norm_back(total, x, gain):
    cen, rstd = centre(x)
    xhat = cen * rstd
    dg = total * gain
    back = rstd * (
        dg - jnp.mean(dg, axis=-1, keepdims=True) - xhat * jnp.mean(dg * xhat, axis=-1, keepdims=True)
    )
    return back, xhat


def remote(src, dst, send_sem, recv_sem, device):
    return pltpu.make_async_remote_copy(
        src_ref=src, dst_ref=dst, send_sem=send_sem, recv_sem=recv_sem, device_id=device, device_id_type=MESH
    )


def tensor_place():
    d, t = lax.axis_index("dp"), lax.axis_index("tensor")
    y, c = t // 2, t % 2
    return d, t, y, c, (d, 2 * y + 1 - c), (d, 2 * (1 - y) + c)


def greet(peers):
    bar = pltpu.get_barrier_semaphore()
    for peer in peers:
        pl.semaphore_signal(bar, inc=1, device_id=peer, device_id_type=MESH)
    return bar


class DpPlace:
    def __init__(self, dp):
        self.d, self.t = lax.axis_index("dp"), lax.axis_index("tensor")
        self.dp, self.line = dp, dp // 2
        self.zi, self.par = self.d // 2, self.d % 2
        self.pair = (2 * self.zi + 1 - self.par, self.t)
        self.e0, self.e3 = (3 - self.zi) // 3, self.zi // 3
        self.end = self.e0 + self.e3

    def at(self, zi):
        return 2 * zi + self.par

    def ahead(self, j):
        return 2 * ((self.zi + j) % self.line) + self.par

    def behind(self, j):
        return 2 * ((self.zi + self.line - j) % self.line) + self.par

    def near(self):
        return [self.pair] + [(self.ahead(j), self.t) for j in range(1, self.line)]

    def others(self):
        return [((self.d + j) % self.dp, self.t) for j in range(1, self.dp)]


class ToAll:
    def __init__(self, place, source, land, send_sem, recv_sem):
        self.copies = []
        for j in range(1, place.dp):
            q = (place.d + j) % place.dp
            cp = remote(source(q), land.at[place.d], send_sem.at[j], recv_sem.at[j], (q, place.t))
            cp.start()
            self.copies.append(cp)

    def arrived(self):
        for cp in self.copies:
            cp.wait_recv()

    def sent(self):
        for cp in self.copies:
            cp.wait_send()


class WeightGather:
    def __init__(self, place, shard, land, z_s, z_r, x_s, x_r):
        self.place, self.land, self.z_s, self.z_r, self.x_s, self.x_r = place, land, z_s, z_r, x_s, x_r
        self.z = {}
        for j in (2, 1, 3):
            self.z[j] = remote(shard, land.at[place.d], z_s.at[j], z_r.at[j], (place.ahead(j), place.t))
            self.sends(j, self.z[j].start)
        cp = remote(shard, land.at[place.d], x_s.at[0], x_r.at[0], place.pair)
        cp.start()
        self.x = [cp]
        source = place.behind(2)
        self.inner = remote(
            land.at[source], land.at[source], z_s.at[0], z_r.at[1 + 2 * (place.zi // 2)], (place.at(3 * (place.zi // 2)), place.t)
        )

    def sends(self, j, act):
        if j == 2:
            act()
        else:
            pl.when(self.place.zi != (0 if j == 3 else 3))(act)

    def forward(self):
        e0 = self.place.e0
        for j in (2, 1 + 2 * e0, 3 - 2 * e0):
            source = self.place.behind(j)
            here = self.land.at[source]
            remote(here, here, self.z_s.at[j], self.z_r.at[j], self.place.pair).wait_recv()
            if isinstance(j, int):
                pl.when(self.place.end == 0)(self.inner.start)
            cp = remote(here, here, self.x_s.at[j], self.x_r.at[j], self.place.pair)
            cp.start()
            self.x.append(cp)

    def arrived(self):
        for cp in self.x:
            cp.wait_recv()

    def sent(self):
        for j in (1, 2, 3):
            self.sends(j, self.z[j].wait_send)
        pl.when(self.place.end == 0)(self.inner.wait_send)
        for cp in self.x:
            cp.wait_send()


class Gathers:
    def __init__(self, place, z_s, z_r, x_s, x_r):
        self.place, self.sems, self.all, self.passed = place, (z_s, z_r, x_s, x_r), [], 0

    def add(self, shard, land, pieces=1):
        start = 0
        for i in range(pieces):
            count = piece_rows(shard.shape[0], pieces, i) if pieces > 1 else None
            src = shard if count is None else shard.at[pl.ds(start, count)]
            dst = land if count is None else land.at[:, pl.ds(start, count)]
            start += count or 0
            self.all.append(WeightGather(self.place, src, dst, *[v.at[len(self.all)] for v in self.sems]))

    def forward(self, count=1):
        for _ in range(count):
            self.all[self.passed].forward()
            self.passed += 1

    def arrived(self, first, last):
        for g in self.all[first:last]:
            g.arrived()

    def sent(self):
        for g in self.all:
            g.sent()

    @staticmethod
    def scratch(count, line):
        return [pltpu.SemaphoreType.DMA((count, line))] * 4


def piece_rows(rows, pieces, i):
    tiles = rows // 16
    return 16 * (tiles * (i + 1) // pieces - tiles * i // pieces)


class GradScatter:
    def __init__(self, place, source, own, xland, zland, own_sem, x_s, x_r, z_s, z_r):
        self.place, self.own, self.xland, self.zland, self.z_s, self.z_r = place, own, xland, zland, z_s, z_r
        self.at, self.x, self.local, self.z = 0, [], [], []
        zi, e0, e3, end = place.zi, place.e0, place.e3, place.end
        self.order = [1 + 2 * e0, 3 - end, 2 - e0 + e3, 0]
        self.owners = [(zi + i) % 4 for i in self.order]
        self.routes = [
            (zi + 1 - 2 * e3, 3 * end, 1 - end),
            (self.owners[1], self.order[1] - 1, self.order[1]),
            (self.owners[2], self.order[2] - 1, self.order[2]),
        ]
        for k, j in enumerate(self.owners):
            cp = remote(source.at[2 * j + 1 - place.par], xland.at[j], x_s.at[k], x_r.at[k], place.pair)
            cp.start()
            self.x.append(cp)
            cp = pltpu.make_async_copy(source.at[2 * j + place.par], own.at[j], own_sem.at[k])
            cp.start()
            self.local.append(cp)

    def arrival(self, slot, sem):
        return remote(self.own.at[0], self.zland.at[slot], self.z_s.at[0], self.z_r.at[sem], self.place.pair)

    def step(self):
        k = self.at
        self.at += 1
        j = self.owners[k]
        self.local[k].wait()
        self.x[k].wait_recv()
        self.own[j] = (self.own[j].astype(F32) + self.xland[j].astype(F32)).astype(BF16)
        if k == 2:

            @pl.when(self.place.end == 0)
            def _():
                self.arrival(3, 0).wait_recv()
                self.own[j] = (self.own[j].astype(F32) + self.zland[3].astype(F32)).astype(BF16)

        to, slot, sem = self.routes[k]
        cp = remote(self.own.at[j], self.zland.at[slot], self.z_s.at[k], self.z_r.at[sem], (self.place.at(to), self.place.t))
        cp.start()
        self.z.append(cp)

    def steps(self, count=3):
        while self.at < min(3, count):
            self.step()

    def result(self):
        zi = self.place.zi
        self.local[3].wait()
        self.x[3].wait_recv()
        for slot in range(3):
            if slot == 1:
                self.arrival(1, 2).wait_recv()
            else:
                absent = 0 if slot == 0 else 3

                @pl.when(zi == absent)
                def _(slot=slot):
                    self.zland[slot] = jnp.zeros(self.zland.shape[1:], BF16)

                pl.when(zi != absent)(self.arrival(slot, slot + 1).wait_recv)
        total = self.own[zi].astype(F32) + self.xland[zi].astype(F32)
        for slot in range(3):
            total = total + self.zland[slot].astype(F32)
        return total

    def sent(self):
        for cp in self.x + self.z:
            cp.wait_send()

    @staticmethod
    def buffers(shape):
        return [pltpu.VMEM((4,) + shape, BF16)] * 3

    @staticmethod
    def scratch():
        return [pltpu.SemaphoreType.DMA((4,))] * 5


class TensorSum:
    def __init__(self, near, far, csend, crecv, ysend, yrecv, cs, cr, ys, yr):
        self.near, self.far, self.csend, self.crecv, self.ysend, self.yrecv = near, far, csend, crecv, ysend, yrecv
        self.cs, self.cr, self.ys, self.yr = cs, cr, ys, yr
        _, self.t, self.y, self.c, self.sib, self.yp = tensor_place()

    def core(self, i, value):
        self.csend[i] = value.astype(BF16)
        cp = remote(self.csend.at[i], self.crecv.at[i], self.cs.at[i], self.cr.at[i], self.sib)
        cp.start()
        return cp

    def start(self, product, ready=None):
        there, here = 2 * (1 - self.y), 2 * self.y
        first = product(there + 1 - self.c)
        if ready is not None:
            ready()
        self.c0 = self.core(0, first)
        self.far[...] = product(there + self.c)
        self.c1 = self.core(1, product(here + 1 - self.c))
        self.c0.wait_recv()
        self.ycs = []
        ch = self.far.shape[0] // CHUNKS
        for k in range(CHUNKS):
            sl = pl.ds(k * ch, ch)
            self.ysend[sl, :] = (self.far[sl, :] + self.crecv[0, sl, :].astype(F32)).astype(BF16)
            cp = remote(self.ysend.at[sl], self.yrecv.at[sl], self.ys.at[k], self.yr.at[k], self.yp)
            cp.start()
            self.ycs.append(cp)
        self.near[...] = product(here + self.c)
        self.c1.wait_recv()

    def chunk(self, k):
        ch = self.far.shape[0] // CHUNKS
        sl = pl.ds(k * ch, ch)
        self.ycs[k].wait_recv()
        return sl, self.near[sl, :] + self.crecv[1, sl, :].astype(F32) + self.yrecv[sl, :].astype(F32)

    def sent(self):
        for cp in [self.c0, self.c1] + self.ycs:
            cp.wait_send()

    @staticmethod
    def scratch(rows, width):
        dma = pltpu.SemaphoreType.DMA
        vm = pltpu.VMEM
        return [
            vm((rows, width), F32), vm((rows, width), F32), vm((2, rows, width), BF16), vm((2, rows, width), BF16),
            vm((rows, width), BF16), vm((rows, width), BF16), dma((2,)), dma((2,)), dma((CHUNKS,)), dma((CHUNKS,)),
        ]


class RowSpread:
    def __init__(self, spread, rows, ys, yr, cs, cr, fs, fr):
        self.spread, self.rows = spread, rows
        self.sems = (ys, yr, cs, cr, fs, fr)
        _, self.t, self.y, self.c, self.sib, self.yp = tensor_place()
        self.parts, self.passed = [], []

    def at(self, owner, start, count):
        return self.spread.at[pl.ds(pl.multiple_of(owner * self.rows + start, 16), count)]

    def send(self, start, count):
        ys, yr, cs, cr, _, _ = self.sems
        k = len(self.parts)
        here = self.at(self.t, start, count)
        a = remote(here, here, ys.at[k], yr.at[k], self.yp)
        b = remote(here, here, cs.at[k], cr.at[k], self.sib)
        a.start()
        b.start()
        self.parts.append((a, b, start, count))

    def forward(self):
        fs, fr = self.sems[4:]
        for k, (a, _, start, count) in enumerate(self.parts):
            a.wait_recv()
            there = self.at(2 * (1 - self.y) + self.c, start, count)
            cp = remote(there, there, fs.at[k], fr.at[k], self.sib)
            cp.start()
            self.passed.append(cp)

    def finish(self):
        for (a, b, _, _), cp in zip(self.parts, self.passed):
            b.wait_recv()
            cp.wait_recv()
            a.wait_send()
            b.wait_send()
            cp.wait_send()

    @staticmethod
    def scratch(parts=CHUNKS):
        return [pltpu.SemaphoreType.DMA((parts,))] * 6


def shaped(shape, dtype):
    return jax.ShapeDtypeStruct(shape, dtype)


def named_kernel(name, collective_id, body, ins, outs, scratch, hbm=()):
    vm, anywhere = pl.BlockSpec(memory_space=pltpu.VMEM), pl.BlockSpec(memory_space=pl.ANY)
    flat = []
    for v in scratch.values():
        flat.extend(v if isinstance(v, list) else [v])

    def kernel(*refs):
        left = list(refs)
        n = SimpleNamespace()
        for k in [*ins, *outs]:
            setattr(n, k, left.pop(0))
        for k, v in scratch.items():
            if isinstance(v, list):
                setattr(n, k, [left.pop(0) for _ in v])
            else:
                setattr(n, k, left.pop(0))
        body(n)

    talks = {} if collective_id is None else {"collective_id": collective_id, "has_side_effects": True}
    got = pl.pallas_call(
        kernel,
        out_shape=list(outs.values()),
        in_specs=[anywhere if k in hbm else vm for k in ins],
        out_specs=[anywhere if k in hbm else vm for k in outs],
        scratch_shapes=flat,
        compiler_params=pltpu.CompilerParams(vmem_limit_bytes=VMEM_BYTES, **talks),
        name=name,
    )(*ins.values())
    return SimpleNamespace(**dict(zip(outs, got)))


def block_rows(b, rows):
    return pl.ds(pl.multiple_of(b * rows, rows), rows)


def add_sums(sums, parts):
    parts = [jnp.sum(v, axis=0, keepdims=True) for v in parts]
    return parts if sums is None else [a + b for a, b in zip(sums, parts)]


def forward_rows(reduce, spread, spread_ref, resid, bias, gain, offset, out, rows):
    ch = rows // CHUNKS
    for k in range(CHUNKS):
        sl, total = reduce.chunk(k)
        value = resid[sl, :] + (total + bias[...])
        out[sl, :] = value
        cen, rstd = centre(value)
        low = (cen * rstd * gain[...] + offset[...]).astype(BF16)
        spread_ref[pl.ds(pl.multiple_of(reduce.t * rows + k * ch, ch), ch), :] = low
        spread.send(k * ch, ch)


def backward_rows(reduce, spread, spread_ref, x, gain, before, out, sum_refs, rows):
    ch = rows // CHUNKS
    sums = None
    for k in range(CHUNKS):
        sl, total = reduce.chunk(k)
        back, xhat = norm_back(total, x[sl, :], gain[...])
        grad = before[sl, :] + back
        out[sl, :] = grad
        low = grad.astype(BF16)
        spread_ref[pl.ds(pl.multiple_of(reduce.t * rows + k * ch, ch), ch), :] = low
        spread.send(k * ch, ch)
        sums = add_sums(sums, [low.astype(F32), total * xhat, total])
    for ref, v in zip(sum_refs, sums):
        ref[...] = v


def head_stats(u, mask, size):
    mean = jnp.sum(u, axis=-1, keepdims=True) * (1.0 / size)
    cen = (u - mean) * mask
    spread = jnp.sum(cen * cen, axis=-1, keepdims=True) * (1.0 / size)
    return cen, lax.rsqrt(spread + EPSILON)


def head_norm(u, mask, gain, offset, size):
    cen, rstd = head_stats(u, mask, size)
    return cen * rstd * gain + offset


def turn(u, cosine, sine):
    return u * cosine + pltpu.roll(u, LANES // 2, 1) * sine


def turn_back(u, cosine, sine):
    return u * cosine - pltpu.roll(u, LANES // 2, 1) * sine


def head_back(grad, u, mask, gain, size):
    cen, rstd = head_stats(u, mask, size)
    xhat = cen * rstd
    dg = grad * gain
    mean = jnp.sum(dg, axis=-1, keepdims=True) * (1.0 / size)
    inner = jnp.sum(dg * xhat, axis=-1, keepdims=True) * (1.0 / size)
    back = rstd * ((dg - mean) * mask - xhat * inner)
    return back, jnp.sum(grad * xhat, axis=0, keepdims=True), jnp.sum(grad, axis=0, keepdims=True)


def head_at(h):
    return pl.ds(h * LANES, LANES)


def attend(q_ref, k_ref, v_ref, out_ref, lse_ref, heads, scale, block, real_keys):
    queries, keys = q_ref.shape[0], k_ref.shape[0]

    def step(i, _):
        here = pl.ds(pl.multiple_of(i * block, block), block)
        for h in range(heads):
            hs = head_at(h)
            scores = dot_nt(k_ref[:, hs], q_ref[here, hs]) * scale
            if real_keys < keys:
                place = lax.broadcasted_iota(jnp.int32, scores.shape, 0)
                scores = jnp.where(place < real_keys, scores, NEGATIVE)
            highest = jnp.max(scores, axis=0, keepdims=True)
            exponent = jnp.exp(scores - highest)
            denominator = jnp.sum(exponent, axis=0, keepdims=True)
            probs = (exponent * (1.0 / denominator)).astype(BF16)
            mixed = dot_tn(v_ref[:, hs], probs)
            out_ref[here, hs] = mixed.T.astype(BF16)
            lse_ref[i, pl.ds(h, 1), :] = highest + jnp.log(denominator)
        return 0

    lax.fori_loop(0, queries // block, step, 0)


def attend_back(q_ref, k_ref, v_ref, do_ref, lse_ref, dq_ref, dk_ref, dv_ref, heads, scale, block, real_keys):
    queries, keys = q_ref.shape[0], k_ref.shape[0]
    dk_ref[...] = jnp.zeros(dk_ref.shape, F32)
    dv_ref[...] = jnp.zeros(dv_ref.shape, F32)

    def step(i, _):
        here = pl.ds(pl.multiple_of(i * block, block), block)
        for h in range(heads):
            hs = head_at(h)
            q, k, v, do = q_ref[here, hs], k_ref[:, hs], v_ref[:, hs], do_ref[here, hs]
            scores = dot_nt(k, q) * scale
            if real_keys < keys:
                place = lax.broadcasted_iota(jnp.int32, scores.shape, 0)
                scores = jnp.where(place < real_keys, scores, NEGATIVE)
            probs = jnp.exp(scores - lse_ref[i, pl.ds(h, 1), :])
            grad_probs = dot_nt(v, do)
            inner = jnp.sum(probs * grad_probs, axis=0, keepdims=True)
            grad_scores = (probs * (grad_probs - inner)).astype(BF16)
            dv_ref[:, hs] += dot_nn(probs.astype(BF16), do)
            dk_ref[:, hs] += dot_nn(grad_scores, q) * scale
            dq_ref[here, hs] = dot_tn(k, grad_scores).T * scale
        return 0

    lax.fori_loop(0, queries // block, step, 0)


def first_body(dp, own, size, scale, heads, block, n):
    _, t, _, _, _, _ = tensor_place()
    d = lax.axis_index("dp")
    rows, width = n.residual.shape
    cols = n.bias_skip.shape[1]
    span = heads * LANES
    place = DpPlace(dp) if own else None
    peers = [(d, (t + o) % 4) for o in range(1, 4)] + (place.others() if own else [])
    bar = greet(peers)
    mine = block_rows(t, rows)
    kept = [
        pltpu.make_async_copy(n.latent, n.joined0.at[mine], n.own_sem.at[0]),
        pltpu.make_async_copy(n.skip_states, n.joined1.at[mine], n.own_sem.at[1]),
    ]
    if own:
        shards = [(n.skip_in, n.skip_full), (n.project_in, n.p_land), (n.out_in, n.out_land), (n.query_in, n.query_g),
                  (n.key_in, n.key_g), (n.value_in, n.value_g), (n.down_in, n.down_g)]
        kept += [pltpu.make_async_copy(a, b.at[d], n.own_sem.at[2 + i]) for i, (a, b) in enumerate(shards)]
    for cp in kept:
        cp.start()
    pl.semaphore_wait(bar, len(peers))
    spreads = [RowSpread(n.joined0, rows, *n.spread0), RowSpread(n.joined1, rows, *n.spread1)]
    for cp, spread in zip(kept, spreads):
        cp.wait()
        spread.send(0, rows)
    if own:
        n.small_land[d] = n.small[d]
        smalls = ToAll(place, lambda q: n.small.at[q], n.small_land, n.a_s, n.a_r)
        gathers = Gathers(place, *n.gather_sems)
        gathers.add(n.skip_in, n.skip_full, 2)
        smalls.arrived()
        given = jnp.concatenate([n.small_land[i] for i in range(dp)], axis=0)
        n.silu[...] = jax.nn.silu(given[:, : n.shift_in.shape[0]]).astype(BF16)
        n.counted[...] = jnp.sum(given[:, given.shape[1] - LANES :], axis=0, keepdims=True)
        part = dot_nn(n.silu[...], n.shift_in[...])
        for i in range(dp):
            n.shift_part[i] = part[i : i + 1, :]
        n.shift_land[d] = n.shift_part[d]
        shifts = ToAll(place, lambda q: n.shift_part.at[q], n.shift_land, n.b_s, n.b_r)
        for i in range(3):
            gathers.add(n.project_in.at[i], n.p_land.at[:, i])
        gathers.forward()
    spreads[0].forward()
    if own:
        gathers.add(n.out_in, n.out_land)
        gathers.add(n.query_in, n.query_g)
        gathers.add(n.key_in, n.key_g)
        gathers.add(n.value_in, n.value_g)
        gathers.forward()
    spreads[0].finish()
    if own:
        gathers.add(n.down_in, n.down_g, 4)
        gathers.arrived(0, 2)
        kept[2].wait()
        half = dp // 2
        skip_half = lambda i: n.skip_full[pl.ds(i * half, half)].reshape(width, cols)
    else:
        skip_half = lambda i: n.skip_in[pl.ds(i * width, width), :]
    for b in range(4):
        here = pl.ds(b * rows, rows)
        n.pre[here, pl.ds(0, cols)] = dot_nn(n.joined0[here, :], skip_half(0))
    spreads[1].forward()
    if own:
        gathers.forward()
    spreads[1].finish()
    copies = []
    for o in (2, 3, 1, 0):
        b = (t + o) % 4
        here = block_rows(b, rows)
        value = (n.pre[here, pl.ds(0, cols)] + dot_nn(n.joined1[here, :], skip_half(1)) + n.bias_skip[...]).astype(BF16)
        if o:
            n.skip_send[o] = value
            cp = remote(n.skip_send.at[o], n.skip_recv.at[t], n.p_s.at[o], n.p_r.at[o], (d, b))
            cp.start()
            copies.append(cp)
        else:
            n.skip_recv[t] = value
    if own:
        shifts.arrived()
        shift = n.row_bias[pl.ds(3, 1), :] + sum(n.shift_land[i] for i in range(dp))
    else:
        shift = n.shift_in[...]
    for cp in copies:
        cp.wait_recv()
    for s in range(4):
        n.skipped[:, s * cols : (s + 1) * cols] = n.skip_recv[s]
    spread = RowSpread(n.first_all, rows, *n.spread2)
    ch = rows // CHUNKS
    for k in range(CHUNKS):
        sl = pl.ds(k * ch, ch)
        cen, rstd = centre(n.skipped[sl, :].astype(F32))
        resid = cen * rstd * n.norm_gain[pl.ds(0, 1), :] + n.norm_bias[pl.ds(0, 1), :]
        n.residual[sl, :] = resid
        cen, rstd = centre(resid)
        first = cen * rstd * n.norm_gain[pl.ds(1, 1), :] + n.norm_bias[pl.ds(1, 1), :] + shift
        n.first_all[pl.ds(pl.multiple_of(t * rows + k * ch, ch), ch), :] = first.astype(BF16)
        spread.send(k * ch, ch)
    if own:
        gathers.forward()
    spread.forward()
    if own:
        gathers.forward()
    spread.finish()
    for cp in copies:
        cp.wait_send()
    for part in range(3):
        if own:
            gathers.arrived(2 + part, 3 + part)
            if part == 0:
                kept[3].wait()
            narrow = n.p_land[:, part].reshape(width, cols)
        else:
            narrow = n.project_in[part]
        n.project_wide[part] = dot_nn(narrow, n.fold[...]).astype(BF16)
    if own:
        gathers.forward()

    def project(i, _):
        here = pl.ds(pl.multiple_of(i * block, block), block)
        for part in range(3):
            out = dot_nn(n.first_all[here, :], n.project_wide[part]) + n.self_bias[part]
            if part < 2:
                n.pre[here, pl.ds(part * span, span)] = out
                for h in range(heads):
                    u = out[:, h * LANES : (h + 1) * LANES]
                    val = head_norm(u, n.mask[...], n.head_gain[pl.ds(part, 1), :], n.head_bias[pl.ds(part, 1), :], size)
                    val = turn(val, n.cosine[here, :], n.sine[here, :])
                    n.low[here, pl.ds(part * span + h * LANES, LANES)] = val.astype(BF16)
            else:
                n.low[here, pl.ds(part * span, span)] = out.astype(BF16)
        return 0

    lax.fori_loop(0, n.low.shape[0] // block, project, 0)
    if own:
        gathers.forward()
    attend(
        n.low.at[:, pl.ds(0, span)], n.low.at[:, pl.ds(span, span)], n.low.at[:, pl.ds(2 * span, span)],
        n.padded, n.lse, heads, scale, block, n.low.shape[0],
    )
    n.mixed[...] = dot_nt(n.padded[...], n.fold[...]).astype(BF16)
    if own:
        gathers.forward()
        gathers.arrived(5, 6)
        kept[4].wait()
        out_t = lambda: n.out_land[...].reshape(width, cols)
    else:
        out_t = lambda: n.out_in[...]
    reduce = TensorSum(*n.sum)
    reduce.start(lambda b: dot_nt(n.mixed[block_rows(b, rows), :], out_t()))
    if own:
        gathers.forward()
    spread = RowSpread(n.third_all, rows, *n.spread3)
    forward_rows(
        reduce, spread, n.third_all, n.residual, n.row_bias.at[pl.ds(0, 1)], n.norm_gain.at[pl.ds(2, 1)],
        n.norm_bias.at[pl.ds(2, 1)], n.second, rows,
    )
    if own:
        gathers.forward(2)
    spread.forward()
    if own:
        gathers.forward()
    spread.finish()
    reduce.sent()
    if own:
        gathers.forward()
        gathers.arrived(6, len(gathers.all))
        for cp in kept[5:]:
            cp.wait()
        for g in (gathers, smalls, shifts):
            g.sent()


def cross_body(dp, own, size, scale, heads, block, real, n):
    rows, width = n.second.shape
    span = heads * LANES
    d, _, _, _, sib, yp = tensor_place()
    place = DpPlace(dp) if own else None
    peers = [sib, yp] + (place.near() if own else [])
    bar = greet(peers)
    pl.semaphore_wait(bar, len(peers))
    if own:
        gathers = Gathers(place, *n.gather_sems)
        gathers.add(n.cross_out, n.cross_out_land)
        gathers.add(n.up_in, n.up_g, 4)
        kept = [pltpu.make_async_copy(a, b.at[d], n.own_sem.at[i])
                for i, (a, b) in enumerate(((n.cross_out, n.cross_out_land), (n.up_in, n.up_g)))]
        for cp in kept:
            cp.start()
    n.query_wide[...] = dot_nn(n.query[...], n.fold[...]).astype(BF16)
    for part, w in enumerate((n.key, n.value)):
        n.keyval_wide[part] = dot_nn(w[...], n.fold[...]).astype(BF16)
        out = dot_nn(n.text[...], n.keyval_wide[part]) + n.text_bias[part]
        if part == 0:
            n.text_pre[...] = out
            for h in range(heads):
                val = head_norm(out[:, h * LANES : (h + 1) * LANES], n.mask[...], n.head_gain[pl.ds(3, 1), :], n.head_bias[pl.ds(3, 1), :], size)
                n.text_low[:, head_at(h)] = val.astype(BF16)
        else:
            n.text_low[:, pl.ds(span, span)] = out.astype(BF16)
    if own:
        gathers.forward()

    def project(i, _):
        here = pl.ds(pl.multiple_of(i * block, block), block)
        out = dot_nn(n.third_all[here, :], n.query_wide[...]) + n.query_bias[...]
        n.pre[here, :] = out
        for h in range(heads):
            val = head_norm(out[:, h * LANES : (h + 1) * LANES], n.mask[...], n.head_gain[pl.ds(2, 1), :], n.head_bias[pl.ds(2, 1), :], size)
            n.low[here, head_at(h)] = turn(val, n.cosine[here, :], n.sine[here, :]).astype(BF16)
        return 0

    lax.fori_loop(0, n.low.shape[0] // block, project, 0)
    attend(n.low, n.text_low.at[:, pl.ds(0, span)], n.text_low.at[:, pl.ds(span, span)], n.padded, n.lse, heads, scale, block, real)
    n.mixed[...] = dot_nt(n.padded[...], n.fold[...]).astype(BF16)
    if own:
        gathers.forward()
        gathers.arrived(0, 1)
        kept[0].wait()
        out_t = lambda: n.cross_out_land[...].reshape(width, n.mixed.shape[1])
    else:
        out_t = lambda: n.cross_out[...]
    reduce = TensorSum(*n.sum)
    reduce.start(lambda b: dot_nt(n.mixed[block_rows(b, rows), :], out_t()))
    if own:
        gathers.forward()
    spread = RowSpread(n.fourth_all, rows, *n.spread)
    forward_rows(
        reduce, spread, n.fourth_all, n.second, n.row_bias.at[pl.ds(1, 1)], n.norm_gain.at[pl.ds(3, 1)],
        n.norm_bias.at[pl.ds(3, 1)], n.third_sum, rows,
    )
    if own:
        gathers.forward()
    spread.forward()
    if own:
        gathers.forward()
    spread.finish()
    reduce.sent()
    if own:
        gathers.arrived(1, len(gathers.all))
        kept[1].wait()
        gathers.sent()


def feed_body(n):
    rows = n.third_sum.shape[0]
    _, t, _, _, sib, yp = tensor_place()
    bar = greet((sib, yp))
    root, cube = float(np.sqrt(2.0 / np.pi)), 0.044715

    def product(b):
        here = block_rows(b, rows)
        x = dot_nn(n.fourth_all[here, :], n.up[...]) + n.hidden_bias[...]
        square = x * x
        th = jnp.tanh(root * (x + cube * (square * x)))
        cdf = 0.5 * (1.0 + th)
        active = (x * cdf).astype(BF16)
        n.active[here, :] = active
        slope = cdf + (0.5 * root) * x * (1.0 - th * th) * (1.0 + (3.0 * cube) * square)
        n.slope[here, :] = slope.astype(BF16)
        return dot_nt(active, n.down_t[...])

    reduce = TensorSum(*n.sum)
    reduce.start(product, lambda: pl.semaphore_wait(bar, 2))
    spread = RowSpread(n.grad_all, rows, *n.spread)
    ch = rows // CHUNKS
    sums = None
    for k in range(CHUNKS):
        sl, total = reduce.chunk(k)
        final = n.third_sum[sl, :] + (total + n.row_bias[pl.ds(2, 1), :])
        n.block_out[sl, :] = final.astype(BF16)
        grad = n.weight[sl, :] * (final - n.teacher[sl, :].astype(F32))
        n.grad_final[sl, :] = grad
        low = grad.astype(BF16)
        n.grad_all[pl.ds(pl.multiple_of(t * rows + k * ch, ch), ch), :] = low
        spread.send(k * ch, ch)
        sums = add_sums(sums, [low.astype(F32)])
    n.bias_mlp[...] = sums[0]
    spread.forward()
    spread.finish()
    reduce.sent()


def feed_back_body(dp, own, n):
    rows = n.third_sum.shape[0]
    _, _, _, _, sib, yp = tensor_place()
    place = DpPlace(dp) if own else None
    peers = [sib, yp] + (place.near() if own else [])
    bar = greet(peers)
    n.grad_down[...] = dot_tn(n.grad_all[...], n.active[...]).astype(BF16).reshape(n.grad_down.shape)
    pl.semaphore_wait(bar, len(peers))
    if own:
        down = GradScatter(place, n.grad_down, *n.down_bufs, *n.down_sems)

    def product(b):
        here = block_rows(b, rows)
        upper = (dot_nn(n.grad_all[here, :], n.down_t[...]) * n.slope[here, :].astype(F32)).astype(BF16)
        n.upper[here, :] = upper
        return dot_nt(upper, n.up[...])

    reduce = TensorSum(*n.sum)
    reduce.start(product)
    n.bias_hidden[...] = sum(
        jnp.sum(n.upper[pl.ds(b * rows, rows), :].astype(F32), axis=0, keepdims=True) for b in range(4)
    )
    n.grad_up[...] = dot_tn(n.fourth_all[...], n.upper[...]).astype(BF16).reshape(n.grad_up.shape)
    spread = RowSpread(n.c_all, rows, *n.spread)
    if own:
        down.steps(1)
    backward_rows(reduce, spread, n.c_all, n.third_sum, n.gain, n.grad_final, n.grad_third, (n.sum0, n.sum1, n.sum2), rows)
    if own:
        down.steps(2)
    spread.forward()
    if own:
        down.steps()
    spread.finish()
    reduce.sent()
    if own:
        n.down_mine[...] = down.result()
        down.sent()


def spread_heads(n, rows_in, w, do, block):
    def spread(i, _):
        here = pl.ds(pl.multiple_of(i * block, block), block)
        narrow = dot_nn(rows_in[here, :], w[...]).astype(BF16)
        do[here, :] = dot_nn(narrow, n.fold[...]).astype(BF16)
        return 0

    lax.fori_loop(0, do.shape[0] // block, spread, 0)


def cross_back_body(dp, own, size, scale, heads, block, real, n):
    rows = n.second.shape[0]
    span = heads * LANES
    d, t, _, _, sib, yp = tensor_place()
    place = DpPlace(dp) if own else None
    peers = [sib, yp] + (place.near() if own else [])
    bar = greet(peers)
    pl.semaphore_wait(bar, len(peers))
    if own:
        up = GradScatter(place, n.grad_up, *n.up_bufs, *n.up_sems)
    spread_heads(n, n.c_all, n.cross_out, n.do, block)
    attend_back(
        n.low, n.text_low.at[:, pl.ds(0, span)], n.text_low.at[:, pl.ds(span, span)],
        n.do, n.lse, n.dq, n.dk, n.dv, heads, scale, block, real,
    )
    n.gains[...] = jnp.zeros(n.gains.shape, F32)
    n.offsets[...] = jnp.zeros(n.offsets.shape, F32)
    n.sums[...] = jnp.zeros(n.sums.shape, F32)

    def finish(i, _):
        here = pl.ds(pl.multiple_of(i * block, block), block)
        for h in range(heads):
            hs = head_at(h)
            grad = turn_back(n.dq[here, hs], n.cosine[here, :], n.sine[here, :])
            grad, g, o = head_back(grad, n.pre[here, hs], n.mask[...], n.head_gain[pl.ds(2, 1), :], size)
            n.gains[pl.ds(0, 1), :] += g
            n.offsets[pl.ds(0, 1), :] += o
            grad_low = grad.astype(BF16)
            n.p[here, hs] = grad_low
            n.sums[:, hs] += jnp.sum(grad_low.astype(F32), axis=0, keepdims=True)
        return 0

    if own:
        up.steps(1)
    lax.fori_loop(0, n.p.shape[0] // block, finish, 0)
    reduce = TensorSum(*n.sum)
    reduce.start(lambda b: dot_nt(n.p[block_rows(b, rows), :], n.query_wide[...]))
    if own:
        up.steps(2)
    for h in range(heads):
        hs = head_at(h)
        grad, g, o = head_back(n.dk[:, hs], n.text_pre[:, hs], n.mask[...], n.head_gain[pl.ds(3, 1), :], size)
        n.gains[pl.ds(1, 1), :] += g
        n.offsets[pl.ds(1, 1), :] += o
        n.text_p[:, hs] = grad.astype(BF16)
        low_v = n.dv[:, hs].astype(BF16)
        n.text_p[:, pl.ds(span + h * LANES, LANES)] = low_v
        n.text_sums[:, hs] = jnp.sum(low_v.astype(F32), axis=0, keepdims=True)
    parts = n.grads.shape[0]

    def put(start, value):
        count = value.shape[0] // parts
        n.grads[:, pl.ds(start, count)] = value.astype(BF16).reshape(parts, count, value.shape[1])
        return start + count

    at = put(0, dot_tn(n.c_all[...], n.mixed[...]))
    at = put(at, dot_tn(n.third_all[...], dot_nt(n.p[...], n.fold[...]).astype(BF16)))
    for part in range(2):
        narrow = dot_nt(n.text_p[:, pl.ds(part * span, span)], n.fold[...]).astype(BF16)
        at = put(at, dot_tn(n.text[...], narrow))
    n.grad_text[...] = (
        dot_nt(n.text_p[:, pl.ds(0, span)], n.keyval_wide[0]) + dot_nt(n.text_p[:, pl.ds(span, span)], n.keyval_wide[1])
    ).astype(BF16)
    if own:
        up.steps()
    spread = RowSpread(n.s_all, rows, *n.spread)
    backward_rows(reduce, spread, n.s_all, n.second, n.gain, n.grad_third, n.grad_second, (n.sum0, n.sum1, n.sum2), rows)
    spread.forward()
    spread.finish()
    reduce.sent()
    if own:
        n.up_mine[...] = up.result()
        up.sent()


class TextSum:
    def __init__(self, part, total, land, yland, back, sems):
        _, _, _, self.c, self.sib, self.yp = tensor_place()
        self.part, self.total, self.land, self.yland, self.last, self.sems = part, total, land, yland, back, sems
        self.half = piece_rows(part.shape[0], 2, 1)
        self.copies = [remote(part, land, sems.at[0], sems.at[1], self.sib)]
        self.copies[0].start()

    def here(self, c):
        return pl.ds(pl.multiple_of(c * (self.part.shape[0] - self.half), 16), self.half)

    def along(self):
        self.copies[0].wait_recv()
        self.total[...] = (self.part[...].astype(F32) + self.land[...].astype(F32)).astype(BF16)
        cp = remote(self.total.at[self.here(self.c)], self.yland, self.sems.at[2], self.sems.at[3], self.yp)
        cp.start()
        self.copies.append(cp)

    def back(self):
        self.copies[1].wait_recv()
        self.copies[1].wait_send()
        mine = self.here(self.c)
        self.yland[...] = (self.total[mine, :].astype(F32) + self.yland[...].astype(F32)).astype(BF16)
        self.copies[0].wait_send()
        cp = remote(self.yland, self.last, self.sems.at[4], self.sems.at[5], self.sib)
        cp.start()
        self.copies.append(cp)

    def result(self, out):
        self.copies[2].wait_recv()
        out[self.here(self.c), :] = self.yland[...].astype(F32)
        out[self.here(1 - self.c), :] = self.last[...].astype(F32)
        self.copies[2].wait_send()


def self_back_body(dp, own, size, scale, heads, block, n):
    span = heads * LANES
    _, _, _, _, sib, yp = tensor_place()
    place = DpPlace(dp) if own else None
    peers = [sib, yp] + (place.near() if own else [])
    bar = greet(peers)
    pl.semaphore_wait(bar, len(peers))
    text = TextSum(n.text_part, n.text_total, n.text_land, n.text_yland, n.text_back, n.text_sems)
    if own:
        few = GradScatter(place, n.few_grads, *n.few_bufs, *n.few_sems)
    spread_heads(n, n.s_all, n.out_t, n.do, block)
    text.along()
    attend_back(
        n.low.at[:, pl.ds(0, span)], n.low.at[:, pl.ds(span, span)], n.low.at[:, pl.ds(2 * span, span)],
        n.do, n.lse, n.dq, n.dk, n.dv, heads, scale, block, n.low.shape[0],
    )
    text.back()
    if own:
        few.step()
    n.gains[...] = jnp.zeros(n.gains.shape, F32)
    n.offsets[...] = jnp.zeros(n.offsets.shape, F32)
    n.sums[...] = jnp.zeros(n.sums.shape, F32)

    def finish(i, _):
        here = pl.ds(pl.multiple_of(i * block, block), block)
        for part, grad_ref in enumerate((n.dq, n.dk, n.dv)):
            for h in range(heads):
                hs = head_at(h)
                wide = pl.ds(part * span + h * LANES, LANES)
                grad = grad_ref[here, hs]
                if part < 2:
                    grad = turn_back(grad, n.cosine[here, :], n.sine[here, :])
                    grad, g, o = head_back(grad, n.pre[here, wide], n.mask[...], n.head_gain[pl.ds(part, 1), :], size)
                    n.gains[pl.ds(part, 1), :] += g
                    n.offsets[pl.ds(part, 1), :] += o
                grad_low = grad.astype(BF16)
                n.p[here, wide] = grad_low
                if part != 1:
                    n.sums[:, wide] += jnp.sum(grad_low.astype(F32), axis=0, keepdims=True)
            n.p_low[part, here, :] = dot_nt(n.p[here, pl.ds(part * span, span)], n.fold[...]).astype(BF16)
        return 0

    lax.fori_loop(0, n.p.shape[0] // block, finish, 0)
    by_place = lambda v: v.astype(BF16).reshape(n.grad_out.shape)
    if own:
        few.steps()
    n.grad_out[...] = by_place(dot_tn(n.s_all[...], n.mixed[...]))
    for part in range(3):
        n.grad_project[:, part] = by_place(dot_tn(n.first_all[...], n.p_low[part]))
    text.result(n.grad_text)
    if own:
        n.few_mine[...] = few.result()
        few.sent()


PACK_ROWS, PACK_SUMS = 8, 16


def last_body(dp, own, n):
    _, t, _, _, _, _ = tensor_place()
    d = lax.axis_index("dp")
    rows, width = n.residual.shape
    cols = n.krecv.shape[2]
    place = DpPlace(dp) if own else None
    peers = [(d, (t + o) % 4) for o in range(1, 4)] + (place.others() if own else [])
    bar = greet(peers)
    reduce = TensorSum(*n.sum)
    scatters = []

    def scatter(source, buffers):
        i = len(scatters)
        scatters.append(GradScatter(place, source, *buffers, *n.scatter_sems[5 * i : 5 * i + 5]))

    def ready():
        pl.semaphore_wait(bar, len(peers))
        if own:
            scatter(n.grad_out, n.out_bufs)
            for i in range(3):
                scatter(n.grad_project.at[:, i], n.project_bufs[3 * i : 3 * i + 3])

    def product(b):
        here = block_rows(b, rows)
        span = n.project_wide.shape[2]
        total = dot_nt(n.p[here, pl.ds(0, span)], n.project_wide[0])
        for part in range(1, 3):
            total = total + dot_nt(n.p[here, pl.ds(part * span, span)], n.project_wide[part])
        return total

    reduce.start(product, ready)
    if own:
        scatters[0].steps()
    sums = None
    for k in range(CHUNKS):
        sl, total = reduce.chunk(k)
        back, xhat = norm_back(total, n.residual[sl, :], n.norm_gain[pl.ds(1, 1), :])
        grad = n.grad_second[sl, :] + back
        back0, xhat0 = norm_back(grad, n.skipped[sl, :].astype(F32), n.norm_gain[pl.ds(0, 1), :])
        low = back0.astype(BF16)
        for s in range(4):
            n.ksend[s, sl, :] = low[:, s * cols : (s + 1) * cols]
        sums = add_sums(sums, [low.astype(F32), total * xhat, total, grad * xhat0, grad])
    copies = []
    for o in (2, 3, 1):
        b = (t + o) % 4
        cp = remote(n.ksend.at[b], n.krecv.at[t], n.k_s.at[o], n.k_r.at[o], (d, b))
        cp.start()
        copies.append(cp)
    n.krecv[t] = n.ksend[t]
    bias_skip, gain_first, offset_first, gain_skip, offset_skip = sums
    n.tile[...] = offset_first
    n.tile_land[t] = n.tile[...]
    tiles = []
    for o in (1, 2, 3):
        cp = remote(n.tile, n.tile_land.at[t], n.t_s.at[o], n.t_r.at[o], (d, (t + o) % 4))
        cp.start()
        tiles.append(cp)
    n.pack[...] = n.pack_in[...]
    for i, v in enumerate((gain_skip, gain_first, offset_skip, offset_first, bias_skip)):
        n.pack[0, pl.ds(i, 1), :] = v
    shares = []
    for o in (1, 2, 3):
        b = (t + o) % 4
        cp = remote(n.pack.at[b], n.pack_in_land.at[t], n.ps_s.at[o], n.ps_r.at[o], (d, b))
        cp.start()
        shares.append(cp)
    n.pack_in_land[t] = n.pack[t]
    if own:
        scatters[1].steps()
    for cp in copies:
        cp.wait_recv()
    reduce.sent()
    halves = [TensorSum(*n.sum), TensorSum(*n.sum1)]
    for h, half in enumerate(halves):
        half.start(lambda b, h=h: dot_nt(n.krecv[b], n.skip_w[pl.ds(h * width, width), :]))
    k_all = n.krecv[...].reshape(4 * rows, cols)
    count = n.grad_skip_w.shape[0] // 2
    for h, joined in enumerate((n.joined0, n.joined1)):
        n.grad_skip_w[pl.ds(h * count, count)] = (
            dot_tn(joined[...], k_all).astype(BF16).reshape((count,) + n.grad_skip_w.shape[1:])
        )
    if own:
        scatter(n.grad_skip_w, n.skip_bufs)
    for cp in tiles:
        cp.wait_recv()
    shift_low = n.tile_land[0] + n.tile_land[1] + n.tile_land[2] + n.tile_land[3]
    n.low_out[...] = shift_low.astype(BF16).astype(F32)
    if own:
        n.low_land[d] = n.low_out[...]
        lows = ToAll(place, lambda q: n.low_out, n.low_land, n.l_s, n.l_r)
    for cp in shares:
        cp.wait_recv()
    n.pack_mine[...] = n.pack_in_land[0] + n.pack_in_land[1] + n.pack_in_land[2] + n.pack_in_land[3]
    if own:
        pack_cp = remote(n.pack_mine, n.pack_x, n.px_s.at[0], n.px_r.at[0], place.pair)
        pack_cp.start()
        scatters[2].steps()
        pack_cp.wait_recv()
        pack_cp.wait_send()
        n.pack_mine[...] = n.pack_mine[...] + n.pack_x[...]
        n.pack_z[place.zi] = n.pack_mine[...]
        packs = []
        for j in range(1, place.line):
            cp = remote(n.pack_mine, n.pack_z.at[place.zi], n.pz_s.at[j], n.pz_r.at[j], (place.ahead(j), place.t))
            cp.start()
            packs.append(cp)
    for half, out in zip(halves, (n.grad_latent, n.grad_skip)):
        for k in range(CHUNKS):
            sl, total = half.chunk(k)
            out[sl, :] = total
        half.sent()
        if own and out is n.grad_latent:
            scatters[3].steps()
            lows.arrived()
            low_all = jnp.concatenate([n.low_land[i] for i in range(dp)], axis=0)
            n.shift_grad[...] = dot_tn(n.silu[...], low_all.astype(BF16))
            n.shift_bias[...] = jnp.sum(low_all, axis=0, keepdims=True)
            for cp in packs:
                cp.wait_recv()
                cp.wait_send()
            total = n.pack_z[0]
            for i in range(1, place.line):
                total = total + n.pack_z[i]
            n.pack_mine[...] = total
    if not own:
        n.shift_grad[...] = n.low_out[...]
        n.shift_bias[...] = n.low_out[...]
    n.pack_t[t] = n.pack_mine[...]
    ends = []
    for o in (1, 2, 3):
        cp = remote(n.pack_mine, n.pack_t.at[t], n.pt_s.at[o], n.pt_r.at[o], (d, (t + o) % 4))
        cp.start()
        ends.append(cp)
    if own:
        scatters[4].steps()
    for cp in ends:
        cp.wait_recv()
        cp.wait_send()
    n.pack_out[...] = n.pack_t[...]
    if own:
        n.out_mine[...] = scatters[0].result()
        for i in range(3):
            n.project_mine[i] = scatters[1 + i].result()
        n.skip_mine[...] = scatters[4].result()
        for s in scatters:
            s.sent()
        lows.sent()
    for cp in copies + tiles + shares:
        cp.wait_send()


def fold_matrix(heads, size):
    out = np.zeros((heads * size, heads * LANES), np.float32)
    for h in range(heads):
        for e in range(size):
            out[h * size + e, h * LANES + (e % 2) * (LANES // 2) + e // 2] = 1.0
    return out


def body(
    latent, skip_states, text_states, condition, teacher, loss_mask, true_counts, positions,
    skip_proj, shift_proj, self_project, self_output, cross_query, cross_keyval, cross_output, hidden_up, hidden_down,
    norm_gain, norm_bias, head_gain, head_bias, column_bias, hidden_bias, row_bias,
):
    d, t = lax.axis_index("dp"), lax.axis_index("tensor")
    dp, tensor = lax.axis_size("dp"), lax.axis_size("tensor")
    rows, width = latent.shape
    group = rows * tensor
    size = head_gain.shape[1]
    cols = self_project.shape[2]
    heads = cols // size
    span = heads * LANES
    hidden = hidden_up.shape[1]
    text_len, text_width = text_states.shape[1:]
    text_pad = -(-text_len // 16) * 16
    scale = size ** (-0.5)
    block = min(256, group)
    r, text_share = shift_proj.shape[0], cross_keyval.shape[0]
    own = r % 16 == 0 and text_share % 16 == 0 and skip_proj.shape[0] % 32 == 0 and dp == 8
    parts = dp if own else 1
    line = max(dp // 2, 1) if own else 1
    dma, vm = pltpu.SemaphoreType.DMA, pltpu.VMEM
    few = lambda *shape: shape if own else (16, LANES)

    fold_np = fold_matrix(heads, size)
    fold = jnp.asarray(fold_np, BF16)
    one_np = fold_np[:size, :LANES]
    mask = jnp.asarray(one_np.sum(0, keepdims=True), F32)
    exact = functools.partial(jnp.dot, precision=lax.Precision.HIGHEST)
    gain_wide, offset_wide = exact(head_gain, jnp.asarray(one_np)), exact(head_bias, jnp.asarray(one_np))
    bias_cols = lax.dynamic_slice_in_dim(column_bias, t * cols, cols, 1)
    bias_wide = exact(bias_cols, jnp.asarray(fold_np))
    zero_wide = jnp.zeros((1, span), F32)
    self_bias = jnp.stack([bias_wide[0:1], zero_wide, bias_wide[1:2]])
    text_bias = jnp.stack([zero_wide, bias_wide[3:4]])
    hidden_cols_bias = lax.dynamic_slice_in_dim(hidden_bias, t * hidden, hidden, 0)[None]

    quarter = size // 4
    lane_np = np.zeros((2, LANES), np.float32)
    sign_np = np.zeros((1, LANES), np.float32)
    for i in range(size // 2):
        f = np.float32(10000.0 ** (-(i % quarter) / quarter))
        for half in range(2):
            lane_np[i // quarter, half * (LANES // 2) + i] = f
            sign_np[0, half * (LANES // 2) + i] = 2 * half - 1
    place = positions.astype(F32)
    angles = place[0][:, None] * lane_np[0] + place[1][:, None] * lane_np[1]
    cosine = jnp.cos(angles) * mask
    sine = jnp.sin(angles) * sign_np

    project_in = jnp.transpose(self_project, (1, 0, 2))
    shards = [self_output.T, cross_query, cross_output.T, cross_keyval[:, 0], cross_keyval[:, 1], hidden_up, hidden_down.T]
    if own:
        lanes = -(-r // LANES) * LANES
        slices = jnp.pad(condition.astype(F32).reshape(dp, r), ((0, 0), (0, lanes - r)))
        slices = jnp.concatenate([slices, jnp.broadcast_to(true_counts.astype(F32)[:, None], (dp, LANES))], axis=1)
        small = slices[:, None, :]
        skip_in, shift_in = skip_proj, shift_proj
    else:
        small_all = lax.all_gather(
            jnp.concatenate([condition.astype(F32), true_counts.astype(F32)[:, None]], axis=1), "dp", axis=0, tiled=True
        )
        silu_all = jax.nn.silu(small_all[:, :width]).astype(BF16)
        silu = lax.dynamic_slice_in_dim(silu_all, d * r, r, 1)
        shift_in = lax.psum_scatter(dot_nn(silu, shift_proj), "dp", scatter_dimension=0, tiled=True) + row_bias[3:4]
        small = jnp.zeros((1, 8, LANES), F32)
        skip_in = lax.all_gather(skip_proj, "dp", axis=0, tiled=True)
        project_in = lax.all_gather(project_in, "dp", axis=1, tiled=True)
        shards = [lax.all_gather(v, "dp", axis=0, tiled=True) for v in shards]
    full = shaped((group, width), BF16)
    mine = shaped((rows, width), F32)
    mine_low = shaped((rows, width), BF16)
    line_sum = shaped((1, width), F32)
    lse_shape = shaped((group // block, heads, block), F32)
    sum_scratch = TensorSum.scratch(rows, width)
    first = named_kernel(
        "first", 0, functools.partial(first_body, dp, own, size, scale, heads, block),
        dict(
            latent=latent, skip_states=skip_states, skip_in=skip_in, project_in=project_in, out_in=shards[0],
            query_in=shards[1], key_in=shards[3], value_in=shards[4], down_in=shards[6],
            small=small, shift_in=shift_in, bias_skip=bias_cols[4:5], self_bias=self_bias, cosine=cosine, sine=sine,
            norm_gain=norm_gain, norm_bias=norm_bias, row_bias=row_bias, head_gain=gain_wide, head_bias=offset_wide,
            mask=mask, fold=fold,
        ),
        dict(
            joined0=full, joined1=full, skip_full=shaped(few(dp, skip_proj.shape[0], cols), BF16), skipped=mine_low,
            residual=mine, first_all=full, silu=shaped(few(dp, r), BF16), counted=shaped((1, LANES), F32),
            project_wide=shaped((3, width, span), BF16), pre=shaped((group, 2 * span), F32),
            low=shaped((group, 3 * span), BF16), mixed=shaped((group, cols), BF16), lse=lse_shape,
            out_land=shaped(few(dp, r, cols), BF16), query_g=shaped(few(dp, r, cols), BF16),
            key_g=shaped(few(dp, text_share, cols), BF16), value_g=shaped(few(dp, text_share, cols), BF16),
            down_g=shaped(few(dp, r, hidden), BF16), third_all=full, second=mine,
        ),
        dict(
            p_land=vm(few(dp, 3, r, cols), BF16), padded=vm((group, span), BF16), skip_send=vm((4, rows, cols), BF16),
            skip_recv=vm((4, rows, cols), BF16), small_land=vm(small.shape, F32), shift_part=vm((dp, 1, width), F32),
            shift_land=vm((dp, 1, width), F32), sum=sum_scratch, own_sem=dma((9,)), a_s=dma((dp,)),
            a_r=dma((dp,)), b_s=dma((dp,)), b_r=dma((dp,)), p_s=dma((4,)), p_r=dma((4,)), gather_sems=Gathers.scratch(13, line),
            spread0=RowSpread.scratch(1),
            spread1=RowSpread.scratch(1), spread2=RowSpread.scratch(), spread3=RowSpread.scratch(),
        ),
        hbm=("latent", "skip_states", "query_in", "key_in", "value_in", "down_in", "query_g", "key_g", "value_g", "down_g")
        + (("skip_in", "project_in", "out_in") if own else ()),
    )
    if own:
        silu, counted = first.silu, first.counted[0, 0]
        skip_full = first.skip_full.reshape(2 * width, cols)
        out_t, query = [v.reshape(width, cols) for v in (first.out_land, first.query_g)]
        key, value = [v.reshape(text_width, cols) for v in (first.key_g, first.value_g)]
        down_t = first.down_g.reshape(width, hidden)
    else:
        counted, skip_full = jnp.sum(small_all[:, width]), skip_in
        out_t, query, cross_out_t, key, value, up_full, down_t = shards

    text = jnp.pad(text_states[0], ((0, text_pad - text_len), (0, 0)))
    cross = named_kernel(
        "cross", 1, functools.partial(cross_body, dp, own, size, scale, heads, block, text_len),
        dict(
            third_all=first.third_all, query=query, key=key, value=value, cross_out=shards[2], up_in=shards[5], text=text,
            text_bias=text_bias, query_bias=bias_wide[2:3], cosine=cosine, sine=sine, norm_gain=norm_gain,
            norm_bias=norm_bias, row_bias=row_bias, head_gain=gain_wide, head_bias=offset_wide, mask=mask, fold=fold,
            second=first.second,
        ),
        dict(
            query_wide=shaped((width, span), BF16), keyval_wide=shaped((2, text_width, span), BF16),
            text_pre=shaped((text_pad, span), F32), text_low=shaped((text_pad, 2 * span), BF16),
            pre=shaped((group, span), F32), low=shaped((group, span), BF16), mixed=shaped((group, cols), BF16),
            lse=lse_shape, fourth_all=full, third_sum=mine,
            cross_out_land=shaped(few(dp, r, cols), BF16), up_g=shaped(few(dp, r, hidden), BF16),
        ),
        dict(
            padded=vm((group, span), BF16), sum=sum_scratch, spread=RowSpread.scratch(),
            gather_sems=Gathers.scratch(5, line), own_sem=dma((2,)),
        ),
        hbm=("up_in", "up_g") + (("cross_out",) if own else ()),
    )
    if own:
        cross_out_t, up_full = cross.cross_out_land.reshape(width, cols), cross.up_g.reshape(width, hidden)

    row_ids = t * rows + jnp.arange(rows)
    weight = loss_mask.astype(F32) * (row_ids < true_counts[0]).astype(F32)
    loss_scale = dp * group / counted
    feed = named_kernel(
        "feed", 2, feed_body,
        dict(
            fourth_all=cross.fourth_all, up=up_full, hidden_bias=hidden_cols_bias, down_t=down_t, third_sum=cross.third_sum,
            row_bias=row_bias, teacher=teacher, weight=(loss_scale * weight)[:, None],
        ),
        dict(
            active=shaped((group, hidden), BF16), slope=shaped((group, hidden), BF16), grad_all=full, block_out=mine_low,
            grad_final=mine, bias_mlp=line_sum,
        ),
        dict(sum=sum_scratch, spread=RowSpread.scratch()),
    )

    back = named_kernel(
        "feed_back", 3, functools.partial(feed_back_body, dp, own),
        dict(
            grad_all=feed.grad_all, slope=feed.slope, active=feed.active, down_t=down_t, up=up_full,
            fourth_all=cross.fourth_all, third_sum=cross.third_sum, gain=norm_gain[3:4], grad_final=feed.grad_final,
        ),
        dict(
            c_all=full, grad_third=mine, sum0=line_sum, sum1=line_sum, sum2=line_sum, bias_hidden=shaped((1, hidden), F32),
            grad_up=shaped((parts, width // parts, hidden), BF16),
            **(dict(down_mine=shaped((r, hidden), F32)) if own else dict(grad_down=shaped((1, width, hidden), BF16))),
        ),
        dict(
            upper=vm((group, hidden), BF16), sum=sum_scratch, spread=RowSpread.scratch(),
            **(dict(grad_down=vm((dp, r, hidden), BF16), down_bufs=GradScatter.buffers((r, hidden)), down_sems=GradScatter.scratch()) if own else {}),
        ),
    )
    bias_cross_out, gain_fourth, offset_fourth = back.sum0, back.sum1, back.sum2

    few_rows = 2 * r + 2 * text_share if own else 2 * width + 2 * text_width
    cback = named_kernel(
        "cross_back", 4, functools.partial(cross_back_body, dp, own, size, scale, heads, block, text_len),
        dict(
            c_all=back.c_all, cross_out=cross_out_t, pre=cross.pre, low=cross.low, text_pre=cross.text_pre,
            text_low=cross.text_low, lse=cross.lse, cosine=cosine, sine=sine, head_gain=gain_wide, mask=mask, fold=fold,
            mixed=cross.mixed, third_all=first.third_all, text=text, keyval_wide=cross.keyval_wide,
            query_wide=cross.query_wide, second=first.second, gain=norm_gain[2:3], grad_third=back.grad_third,
            **(dict(grad_up=back.grad_up) if own else {}),
        ),
        dict(
            grads=shaped((parts, few_rows, cols), BF16), grad_text=shaped((text_pad, text_width), BF16),
            gains=shaped((2, LANES), F32), offsets=shaped((2, LANES), F32), sums=shaped((1, span), F32),
            text_sums=shaped((1, span), F32), s_all=full, grad_second=mine, sum0=line_sum, sum1=line_sum, sum2=line_sum,
            **(dict(up_mine=shaped((r, hidden), F32)) if own else {}),
        ),
        dict(
            p=vm((group, span), BF16), do=vm((group, span), BF16), dq=vm((group, span), F32), dk=vm((text_pad, span), F32),
            dv=vm((text_pad, span), F32), text_p=vm((text_pad, 2 * span), BF16), sum=sum_scratch, spread=RowSpread.scratch(),
            **(dict(up_bufs=GradScatter.buffers((r, hidden)), up_sems=GradScatter.scratch()) if own else {}),
        ),
        hbm=("grad_up",),
    )
    few_grads = cback.grads
    if not own:
        cuts = np.cumsum([0, width, width, text_width, text_width])
        few_grads = jnp.concatenate(
            [few_grads[0, a:b].reshape(dp, -1, cols) for a, b in zip(cuts[:-1], cuts[1:])], axis=1
        )
        few_mine = lax.psum_scatter(few_grads.reshape(-1, cols), "dp", scatter_dimension=0, tiled=True).astype(F32)
        down_mine = lax.psum_scatter(back.grad_down[0], "dp", scatter_dimension=0, tiled=True).astype(F32)
        up_mine = lax.psum_scatter(back.grad_up[0], "dp", scatter_dimension=0, tiled=True).astype(F32)
    else:
        down_mine, up_mine = back.down_mine, cback.up_mine

    sback = named_kernel(
        "self_back", 6, functools.partial(self_back_body, dp, own, size, scale, heads, block),
        dict(
            text_part=cback.grad_text, **(dict(few_grads=few_grads) if own else {}),
            s_all=cback.s_all, out_t=out_t, pre=first.pre, low=first.low, lse=first.lse, cosine=cosine, sine=sine,
            head_gain=gain_wide, mask=mask, fold=fold, mixed=first.mixed, first_all=first.first_all,
        ),
        dict(
            p=shaped((group, 3 * span), BF16), grad_out=shaped((parts, width // parts, cols), BF16),
            grad_project=shaped((parts, 3, width // parts, cols), BF16), gains=shaped((2, LANES), F32),
            offsets=shaped((2, LANES), F32), sums=shaped((1, 3 * span), F32), grad_text=shaped((text_pad, text_width), F32),
            **(dict(few_mine=shaped((few_rows, cols), F32)) if own else {}),
        ),
        dict(
            do=vm((group, span), BF16), dq=vm((group, span), F32), dk=vm((group, span), F32), dv=vm((group, span), F32),
            p_low=vm((3, group, cols), BF16), text_total=vm((text_pad, text_width), BF16),
            text_land=vm((text_pad, text_width), BF16), text_yland=vm((piece_rows(text_pad, 2, 1), text_width), BF16),
            text_back=vm((piece_rows(text_pad, 2, 1), text_width), BF16),
            text_sems=dma((6,)),
            **(dict(few_bufs=GradScatter.buffers((few_rows, cols)), few_sems=GradScatter.scratch()) if own else {}),
        ),
        hbm=("few_grads",),
    )
    grad_text = sback.grad_text[:text_len][None]
    if own:
        few_mine = sback.few_mine

    head_part = jnp.concatenate([sback.gains, cback.gains, sback.offsets, cback.offsets], axis=0).reshape(1, -1)
    column_rows = exact(
        jnp.concatenate([sback.sums[:, :span], sback.sums[:, 2 * span :], cback.sums, cback.text_sums], axis=0),
        jnp.asarray(fold_np.T),
    )
    own_cols = jnp.concatenate([column_rows.reshape(-1), back.bias_hidden[0]])
    col_rows = (4 * PACK_ROWS - PACK_SUMS) // 4
    own_cols = jnp.pad(own_cols, (0, col_rows * width - own_cols.shape[0])).reshape(1, col_rows, width)
    placed = jnp.where(jnp.arange(tensor)[:, None, None] == t, own_cols, 0.0).reshape(tensor * col_rows, width)
    pack_in = jnp.concatenate(
        [jnp.zeros((5, width), F32), cback.sum1, gain_fourth, cback.sum2, offset_fourth, cback.sum0, bias_cross_out,
         feed.bias_mlp, jnp.pad(head_part, ((0, 0), (0, width - head_part.shape[1]))),
         jnp.zeros((PACK_SUMS - 13, width), F32), placed], axis=0
    ).reshape(4, PACK_ROWS, width)
    skip_rows = 2 * width // dp if own else width
    pack_land = vm((4, PACK_ROWS, width), F32)
    last = named_kernel(
        "last", 5, functools.partial(last_body, dp, own),
        dict(
            p=sback.p, project_wide=first.project_wide, residual=first.residual, grad_second=cback.grad_second,
            skipped=first.skipped, norm_gain=norm_gain, skip_w=skip_full, joined0=first.joined0, joined1=first.joined1,
            silu=silu, pack_in=pack_in, grad_out=sback.grad_out, grad_project=sback.grad_project,
        ),
        dict(
            grad_latent=mine, grad_skip=mine, shift_grad=shaped((r if own else 1, width), F32), shift_bias=line_sum,
            pack_out=shaped((4, PACK_ROWS, width), F32),
            **(dict(out_mine=shaped((r, cols), F32), project_mine=shaped((3, r, cols), F32), skip_mine=shaped((skip_rows, cols), F32))
               if own else dict(grad_skip_w=shaped((2, width, cols), BF16))),
        ),
        dict(
            ksend=vm((4, rows, cols), BF16), krecv=vm((4, rows, cols), BF16), tile=vm((1, width), F32),
            tile_land=vm((4, 1, width), F32), low_out=vm((1, width), F32),
            low_land=vm((dp if own else 1, 1, width), F32), pack=vm((4, PACK_ROWS, width), F32), pack_in_land=pack_land,
            pack_mine=vm((PACK_ROWS, width), F32), pack_x=vm((PACK_ROWS, width), F32), pack_z=pack_land, pack_t=pack_land, sum=sum_scratch, sum1=sum_scratch,
            k_s=dma((4,)), k_r=dma((4,)), t_s=dma((4,)), t_r=dma((4,)), l_s=dma((dp,)), l_r=dma((dp,)), px_s=dma((1,)),
            px_r=dma((1,)), ps_s=dma((4,)), ps_r=dma((4,)), pz_s=dma((line,)), pz_r=dma((line,)), pt_s=dma((4,)), pt_r=dma((4,)),
            **(dict(
                grad_skip_w=vm((dp, skip_rows, cols), BF16), out_bufs=GradScatter.buffers((r, cols)),
                project_bufs=GradScatter.buffers((r, cols)) * 3, skip_bufs=GradScatter.buffers((skip_rows, cols)),
                scatter_sems=GradScatter.scratch() * 5,
            ) if own else {}),
        ),
        hbm=("grad_out", "grad_project"),
    )
    if own:
        out_mine, project_mine, skip_mine = last.out_mine, last.project_mine, last.skip_mine
        shift_grad, shift_bias, pack_sum = last.shift_grad, last.shift_bias, last.pack_out
    else:
        shift_all = lax.all_gather(last.shift_grad[:1], "dp", axis=0, tiled=True)
        shift_bias = jnp.sum(shift_all, axis=0, keepdims=True)
        shift_grad = dot_tn(silu, shift_all.astype(BF16))
        pack_sum = lax.psum(last.pack_out, "dp")
        out_mine = lax.psum_scatter(sback.grad_out[0], "dp", scatter_dimension=0, tiled=True).astype(F32)
        project_mine = lax.psum_scatter(sback.grad_project[0], "dp", scatter_dimension=1, tiled=True).astype(F32)
        skip_mine = lax.psum_scatter(last.grad_skip_w.reshape(-1, cols), "dp", scatter_dimension=0, tiled=True).astype(F32)
    pack_sum = pack_sum.reshape(4 * PACK_ROWS, width)
    cols_all = pack_sum[PACK_SUMS:].reshape(tensor, -1)
    column_sums = jnp.transpose(cols_all[:, : 4 * cols].reshape(tensor, 4, cols), (1, 0, 2)).reshape(4, width)
    hidden_sums = cols_all[:, 4 * cols : 4 * cols + hidden].reshape(-1)
    head_sums = exact(pack_sum[12, : 8 * LANES].reshape(8, LANES), jnp.asarray(one_np.T))
    return (
        feed.block_out,
        last.grad_latent,
        last.grad_skip,
        grad_text,
        skip_mine,
        shift_grad,
        jnp.transpose(project_mine, (1, 0, 2)),
        out_mine.T,
        few_mine[r : 2 * r],
        jnp.transpose(few_mine[2 * r :].reshape(2, text_share, cols), (1, 0, 2)),
        few_mine[:r].T,
        up_mine,
        down_mine.T,
        jnp.concatenate([pack_sum[0:2], pack_sum[5:7]]),
        jnp.concatenate([pack_sum[2:4], pack_sum[7:9]]),
        head_sums[:4],
        head_sums[4:],
        jnp.concatenate([column_sums, pack_sum[4:5]]),
        hidden_sums,
        jnp.concatenate([pack_sum[9:12], shift_bias]),
    )


def solution(mesh):
    both = ("dp", "tensor")
    rows2, split2, cross2 = P(both, None), P("dp", "tensor"), P("tensor", "dp")
    middle = P("dp", None, "tensor")
    return jax.shard_map(
        body,
        mesh=mesh,
        in_specs=(
            rows2, rows2, P("dp", None, None), P("dp", None), rows2, P(both), P("dp"), P(None, "dp"),
            split2, P("dp", None), middle, cross2, split2, middle, cross2, split2, cross2,
            P(), P(), P(), P(), P(), P(), P(),
        ),
        out_specs=(
            rows2, rows2, rows2, P("dp", None, None),
            split2, P("dp", None), middle, cross2, split2, middle, cross2, split2, cross2,
            P(), P(), P(), P(), P(), P(), P(),
        ),
        check_vma=False,
    )
```

```python
import functools
from types import SimpleNamespace

import jax
import jax.numpy as jnp
import numpy as np
from jax import lax
from jax.experimental import pallas as pl
from jax.experimental.pallas import tpu as pltpu
from jax.sharding import PartitionSpec as P

EPSILON = 1e-06
MESH = pl.DeviceIdType.MESH
BF16, F32 = jnp.bfloat16, jnp.float32
LANES = 128
CHUNKS = 2
VMEM_BYTES = 60 * 2**20
NEGATIVE = -1e30


def dot_nn(left, right):
    return jnp.dot(left, right, preferred_element_type=F32)


def dot_nt(left, right):
    return lax.dot_general(left, right, (((1,), (1,)), ((), ())), preferred_element_type=F32)


def dot_tn(left, right):
    return lax.dot_general(left, right, (((0,), (0,)), ((), ())), preferred_element_type=F32)


def centre(x):
    cen = x - jnp.mean(x, axis=-1, keepdims=True)
    spread = jnp.mean(cen * cen, axis=-1, keepdims=True)
    return cen, lax.rsqrt(spread + EPSILON)


def norm_back(total, x, gain):
    cen, rstd = centre(x)
    xhat = cen * rstd
    dg = total * gain
    back = rstd * (
        dg - jnp.mean(dg, axis=-1, keepdims=True) - xhat * jnp.mean(dg * xhat, axis=-1, keepdims=True)
    )
    return back, xhat


def remote(src, dst, send_sem, recv_sem, device):
    return pltpu.make_async_remote_copy(
        src_ref=src, dst_ref=dst, send_sem=send_sem, recv_sem=recv_sem, device_id=device, device_id_type=MESH
    )


def tensor_place():
    d, t = lax.axis_index("dp"), lax.axis_index("tensor")
    y, c = t // 2, t % 2
    return d, t, y, c, (d, 2 * y + 1 - c), (d, 2 * (1 - y) + c)


def greet(peers):
    bar = pltpu.get_barrier_semaphore()
    for peer in peers:
        pl.semaphore_signal(bar, inc=1, device_id=peer, device_id_type=MESH)
    return bar


class DpPlace:
    def __init__(self, dp):
        self.d, self.t = lax.axis_index("dp"), lax.axis_index("tensor")
        self.dp, self.line = dp, dp // 2
        self.zi, self.par = self.d // 2, self.d % 2
        self.pair = (2 * self.zi + 1 - self.par, self.t)
        self.e0, self.e3 = (3 - self.zi) // 3, self.zi // 3
        self.end = self.e0 + self.e3

    def at(self, zi):
        return 2 * zi + self.par

    def ahead(self, j):
        return 2 * ((self.zi + j) % self.line) + self.par

    def behind(self, j):
        return 2 * ((self.zi + self.line - j) % self.line) + self.par

    def near(self):
        return [self.pair] + [(self.ahead(j), self.t) for j in range(1, self.line)]

    def others(self):
        return [((self.d + j) % self.dp, self.t) for j in range(1, self.dp)]


class ToAll:
    def __init__(self, place, source, land, send_sem, recv_sem):
        self.copies = []
        for j in range(1, place.dp):
            q = (place.d + j) % place.dp
            cp = remote(source(q), land.at[place.d], send_sem.at[j], recv_sem.at[j], (q, place.t))
            cp.start()
            self.copies.append(cp)

    def arrived(self):
        for cp in self.copies:
            cp.wait_recv()

    def sent(self):
        for cp in self.copies:
            cp.wait_send()


class Gathers:
    def __init__(self, place, ahead, z_s, z_r, x_s, x_r):
        self.place, self.ahead, self.sems = place, ahead, (z_s, z_r, x_s, x_r)
        self.pieces, self.z, self.x, self.passed = [], [], [], 0

    def add(self, shard, land, pieces=1):
        start = 0
        for i in range(pieces):
            if pieces == 1:
                self.pieces.append((shard, land))
            else:
                count = piece_rows(shard.shape[0], pieces, i)
                self.pieces.append((shard.at[pl.ds(start, count)], land.at[:, pl.ds(start, count)]))
                start += count
        self.fill()

    def fill(self):
        place = self.place
        while len(self.z) < min(len(self.pieces), self.passed + self.ahead):
            k = len(self.z)
            shard, land = self.pieces[k]
            z_s, z_r, x_s, x_r = [v.at[k] for v in self.sems]
            self.z.append([
                remote(shard, land.at[place.d], z_s.at[j], z_r.at[j], (place.ahead(j), place.t)) for j in range(1, place.line)
            ])
            self.x.append([remote(shard, land.at[place.d], x_s.at[0], x_r.at[0], place.pair)])
            for cp in self.z[k] + self.x[k]:
                cp.start()

    def forward(self, count=1):
        for _ in range(count):
            k = self.passed
            _, land = self.pieces[k]
            _, _, x_s, x_r = [v.at[k] for v in self.sems]
            for j in range(1, self.place.line):
                self.z[k][j - 1].wait_recv()
                here = land.at[self.place.behind(j)]
                cp = remote(here, here, x_s.at[j], x_r.at[j], self.place.pair)
                cp.start()
                self.x[k].append(cp)
            self.passed += 1
            self.fill()

    def arrived(self, first, last):
        for cps in self.x[first:last]:
            for cp in cps:
                cp.wait_recv()

    def sent(self):
        for cps in self.z + self.x:
            for cp in cps:
                cp.wait_send()

    @staticmethod
    def scratch(count, line):
        return [pltpu.SemaphoreType.DMA((count, line))] * 4


def piece_rows(rows, pieces, i):
    tiles = rows // 16
    return 16 * (tiles * (i + 1) // pieces - tiles * i // pieces)


class GradScatter:
    def __init__(self, place, source, own, xland, zland, own_sem, x_s, x_r, z_s, z_r):
        self.place, self.own, self.xland, self.zland, self.z_s, self.z_r = place, own, xland, zland, z_s, z_r
        self.at, self.x, self.local, self.z = 0, [], [], []
        zi, e0, e3, end = place.zi, place.e0, place.e3, place.end
        self.order = [1 + 2 * e0, 3 - end, 2 - e0 + e3, 0]
        self.owners = [(zi + i) % 4 for i in self.order]
        self.routes = [
            (zi + 1 - 2 * e3, 3 * end, 1 - end),
            (self.owners[1], self.order[1] - 1, self.order[1]),
            (self.owners[2], self.order[2] - 1, self.order[2]),
        ]
        for k, j in enumerate(self.owners):
            cp = remote(source.at[2 * j + 1 - place.par], xland.at[j], x_s.at[k], x_r.at[k], place.pair)
            cp.start()
            self.x.append(cp)
            cp = pltpu.make_async_copy(source.at[2 * j + place.par], own.at[j], own_sem.at[k])
            cp.start()
            self.local.append(cp)

    def arrival(self, slot, sem):
        return remote(self.own.at[0], self.zland.at[slot], self.z_s.at[0], self.z_r.at[sem], self.place.pair)

    def step(self):
        k = self.at
        self.at += 1
        j = self.owners[k]
        self.local[k].wait()
        self.x[k].wait_recv()
        self.own[j] = (self.own[j].astype(F32) + self.xland[j].astype(F32)).astype(BF16)
        if k == 2:

            @pl.when(self.place.end == 0)
            def _():
                self.arrival(3, 0).wait_recv()
                self.own[j] = (self.own[j].astype(F32) + self.zland[3].astype(F32)).astype(BF16)

        to, slot, sem = self.routes[k]
        cp = remote(self.own.at[j], self.zland.at[slot], self.z_s.at[k], self.z_r.at[sem], (self.place.at(to), self.place.t))
        cp.start()
        self.z.append(cp)

    def steps(self, count=3):
        while self.at < min(3, count):
            self.step()

    def result(self):
        zi = self.place.zi
        self.local[3].wait()
        self.x[3].wait_recv()
        for slot in range(3):
            if slot == 1:
                self.arrival(1, 2).wait_recv()
            else:
                absent = 0 if slot == 0 else 3

                @pl.when(zi == absent)
                def _(slot=slot):
                    self.zland[slot] = jnp.zeros(self.zland.shape[1:], BF16)

                pl.when(zi != absent)(self.arrival(slot, slot + 1).wait_recv)
        total = self.own[zi].astype(F32) + self.xland[zi].astype(F32)
        for slot in range(3):
            total = total + self.zland[slot].astype(F32)
        return total

    def sent(self):
        for cp in self.x + self.z:
            cp.wait_send()

    @staticmethod
    def buffers(shape):
        return [pltpu.VMEM((4,) + shape, BF16)] * 3

    @staticmethod
    def scratch():
        return [pltpu.SemaphoreType.DMA((4,))] * 5


class TensorSum:
    def __init__(self, near, far, csend, crecv, ysend, yrecv, cs, cr, ys, yr):
        self.near, self.far, self.csend, self.crecv, self.ysend, self.yrecv = near, far, csend, crecv, ysend, yrecv
        self.cs, self.cr, self.ys, self.yr = cs, cr, ys, yr
        _, self.t, self.y, self.c, self.sib, self.yp = tensor_place()

    def core(self, i, value):
        self.csend[i] = value.astype(BF16)
        cp = remote(self.csend.at[i], self.crecv.at[i], self.cs.at[i], self.cr.at[i], self.sib)
        cp.start()
        return cp

    def start(self, product, ready=None, long=False):
        there, here = 2 * (1 - self.y), 2 * self.y
        first = product(there + 1 - self.c)
        if ready is not None:
            ready()
        self.c0 = self.core(0, first)
        self.far[...] = product(there + self.c)
        if not long:
            self.c1 = self.core(1, product(here + 1 - self.c))
        self.c0.wait_recv()
        self.ycs = []
        ch = self.far.shape[0] // CHUNKS
        for k in range(CHUNKS):
            sl = pl.ds(k * ch, ch)
            self.ysend[sl, :] = (self.far[sl, :] + self.crecv[0, sl, :].astype(F32)).astype(BF16)
            cp = remote(self.ysend.at[sl], self.yrecv.at[sl], self.ys.at[k], self.yr.at[k], self.yp)
            cp.start()
            self.ycs.append(cp)
        if long:
            self.c1 = self.core(1, product(here + 1 - self.c))
        self.near[...] = product(here + self.c)
        self.c1.wait_recv()

    def chunk(self, k):
        ch = self.far.shape[0] // CHUNKS
        sl = pl.ds(k * ch, ch)
        self.ycs[k].wait_recv()
        return sl, self.near[sl, :] + self.crecv[1, sl, :].astype(F32) + self.yrecv[sl, :].astype(F32)

    def sent(self):
        for cp in [self.c0, self.c1] + self.ycs:
            cp.wait_send()

    @staticmethod
    def scratch(rows, width):
        dma = pltpu.SemaphoreType.DMA
        vm = pltpu.VMEM
        return [
            vm((rows, width), F32), vm((rows, width), F32), vm((2, rows, width), BF16), vm((2, rows, width), BF16),
            vm((rows, width), BF16), vm((rows, width), BF16), dma((2,)), dma((2,)), dma((CHUNKS,)), dma((CHUNKS,)),
        ]


class RowSpread:
    def __init__(self, spread, rows, ys, yr, cs, cr, fs, fr):
        self.spread, self.rows = spread, rows
        self.sems = (ys, yr, cs, cr, fs, fr)
        _, self.t, self.y, self.c, self.sib, self.yp = tensor_place()
        self.parts, self.passed = [], []

    def at(self, owner, start, count):
        return self.spread.at[pl.ds(pl.multiple_of(owner * self.rows + start, 16), count)]

    def send(self, start, count):
        ys, yr, cs, cr, _, _ = self.sems
        k = len(self.parts)
        here = self.at(self.t, start, count)
        a = remote(here, here, ys.at[k], yr.at[k], self.yp)
        b = remote(here, here, cs.at[k], cr.at[k], self.sib)
        a.start()
        b.start()
        self.parts.append((a, b, start, count))

    def forward(self):
        fs, fr = self.sems[4:]
        for k, (a, _, start, count) in enumerate(self.parts):
            a.wait_recv()
            there = self.at(2 * (1 - self.y) + self.c, start, count)
            cp = remote(there, there, fs.at[k], fr.at[k], self.sib)
            cp.start()
            self.passed.append(cp)

    def finish(self):
        for (a, b, _, _), cp in zip(self.parts, self.passed):
            b.wait_recv()
            cp.wait_recv()
            a.wait_send()
            b.wait_send()
            cp.wait_send()

    @staticmethod
    def scratch(parts=CHUNKS):
        return [pltpu.SemaphoreType.DMA((parts,))] * 6


def shaped(shape, dtype):
    return jax.ShapeDtypeStruct(shape, dtype)


def named_kernel(name, collective_id, body, ins, outs, scratch, hbm=(), late=(), early=()):
    vm, anywhere = pl.BlockSpec(memory_space=pltpu.VMEM), pl.BlockSpec(memory_space=pl.ANY)
    flat = []
    for v in scratch.values():
        flat.extend(v if isinstance(v, list) else [v])
    buffers = [pltpu.VMEM(ins[k].shape, ins[k].dtype) for k in late] + [pltpu.VMEM(outs[k].shape, outs[k].dtype) for k in early]
    moved = len(buffers)
    if moved:
        buffers.append(pltpu.SemaphoreType.DMA((moved,)))

    def kernel(*refs):
        left = list(refs)
        n = SimpleNamespace()
        for k in [*ins, *outs]:
            setattr(n, k, left.pop(0))
        for k, v in scratch.items():
            if isinstance(v, list):
                setattr(n, k, [left.pop(0) for _ in v])
            else:
                setattr(n, k, left.pop(0))
        loads, stores, going = {}, {}, []
        for i, k in enumerate([*late, *early]):
            if k in ins:
                loads[k] = pltpu.make_async_copy(getattr(n, k), left[i], left[-1].at[i])
                loads[k].start()
            else:
                stores[k] = pltpu.make_async_copy(left[i], getattr(n, k), left[-1].at[i])
            setattr(n, k, left[i])

        def need(*names):
            for k in names:
                if k in loads:
                    loads.pop(k).wait()

        def done(*names):
            for k in names:
                if k in stores:
                    going.append(stores.pop(k))
                    going[-1].start()

        n.need, n.done = need, done
        body(n)
        need(*list(loads))
        done(*list(stores))
        for cp in going:
            cp.wait()

    talks = {} if collective_id is None else {"collective_id": collective_id, "has_side_effects": True}
    got = pl.pallas_call(
        kernel,
        out_shape=list(outs.values()),
        in_specs=[anywhere if k in hbm or k in late else vm for k in ins],
        out_specs=[anywhere if k in hbm or k in early else vm for k in outs],
        scratch_shapes=flat + buffers,
        compiler_params=pltpu.CompilerParams(vmem_limit_bytes=VMEM_BYTES, **talks),
        name=name,
    )(*ins.values())
    return SimpleNamespace(**dict(zip(outs, got)))


def block_rows(b, rows):
    return pl.ds(pl.multiple_of(b * rows, rows), rows)


def add_sums(sums, parts):
    parts = [jnp.sum(v, axis=0, keepdims=True) for v in parts]
    return parts if sums is None else [a + b for a, b in zip(sums, parts)]


def forward_rows(reduce, spread, spread_ref, resid, bias, gain, offset, out, rows):
    ch = rows // CHUNKS
    for k in range(CHUNKS):
        sl, total = reduce.chunk(k)
        value = resid[sl, :] + (total + bias[...])
        out[sl, :] = value
        cen, rstd = centre(value)
        low = (cen * rstd * gain[...] + offset[...]).astype(BF16)
        spread_ref[pl.ds(pl.multiple_of(reduce.t * rows + k * ch, ch), ch), :] = low
        spread.send(k * ch, ch)


def backward_rows(reduce, spread, spread_ref, x, gain, before, out, sum_refs, rows):
    ch = rows // CHUNKS
    sums = None
    for k in range(CHUNKS):
        sl, total = reduce.chunk(k)
        back, xhat = norm_back(total, x[sl, :], gain[...])
        grad = before[sl, :] + back
        out[sl, :] = grad
        low = grad.astype(BF16)
        spread_ref[pl.ds(pl.multiple_of(reduce.t * rows + k * ch, ch), ch), :] = low
        spread.send(k * ch, ch)
        sums = add_sums(sums, [low.astype(F32), total * xhat, total])
    for ref, v in zip(sum_refs, sums):
        ref[...] = v


def head_stats(u, mask, size):
    mean = jnp.sum(u, axis=-1, keepdims=True) * (1.0 / size)
    cen = (u - mean) * mask
    spread = jnp.sum(cen * cen, axis=-1, keepdims=True) * (1.0 / size)
    return cen, lax.rsqrt(spread + EPSILON)


def head_norm(u, mask, gain, offset, size):
    cen, rstd = head_stats(u, mask, size)
    return cen * rstd * gain + offset


def turn(u, cosine, sine):
    return u * cosine + pltpu.roll(u, LANES // 2, 1) * sine


def turn_back(u, cosine, sine):
    return u * cosine - pltpu.roll(u, LANES // 2, 1) * sine


def head_back(grad, u, mask, gain, size):
    cen, rstd = head_stats(u, mask, size)
    xhat = cen * rstd
    dg = grad * gain
    mean = jnp.sum(dg, axis=-1, keepdims=True) * (1.0 / size)
    inner = jnp.sum(dg * xhat, axis=-1, keepdims=True) * (1.0 / size)
    back = rstd * ((dg - mean) * mask - xhat * inner)
    return back, jnp.sum(grad * xhat, axis=0, keepdims=True), jnp.sum(grad, axis=0, keepdims=True)


def head_at(h):
    return pl.ds(h * LANES, LANES)


def in_halves(count, step, between):
    if between is None:
        lax.fori_loop(0, count, step, 0)
    else:
        for i in range(2):
            lax.fori_loop(i * count // 2, (i + 1) * count // 2, step, 0)
            between()


def attend(q_ref, k_ref, v_ref, out_ref, lse_ref, heads, scale, block, real_keys, between=None):
    queries, keys = q_ref.shape[0], k_ref.shape[0]

    def step(i, _):
        here = pl.ds(pl.multiple_of(i * block, block), block)
        for h in range(heads):
            hs = head_at(h)
            scores = dot_nt(k_ref[:, hs], q_ref[here, hs]) * scale
            if real_keys < keys:
                place = lax.broadcasted_iota(jnp.int32, scores.shape, 0)
                scores = jnp.where(place < real_keys, scores, NEGATIVE)
            highest = jnp.max(scores, axis=0, keepdims=True)
            exponent = jnp.exp(scores - highest)
            denominator = jnp.sum(exponent, axis=0, keepdims=True)
            probs = (exponent * (1.0 / denominator)).astype(BF16)
            mixed = dot_tn(v_ref[:, hs], probs)
            out_ref[here, hs] = mixed.T.astype(BF16)
            lse_ref[i, pl.ds(h, 1), :] = highest + jnp.log(denominator)
        return 0

    in_halves(queries // block, step, between)


def attend_back(q_ref, k_ref, v_ref, do_ref, lse_ref, dq_ref, dk_ref, dv_ref, heads, scale, block, real_keys, between=None):
    queries, keys = q_ref.shape[0], k_ref.shape[0]
    dk_ref[...] = jnp.zeros(dk_ref.shape, F32)
    dv_ref[...] = jnp.zeros(dv_ref.shape, F32)

    def step(i, _):
        here = pl.ds(pl.multiple_of(i * block, block), block)
        for h in range(heads):
            hs = head_at(h)
            q, k, v, do = q_ref[here, hs], k_ref[:, hs], v_ref[:, hs], do_ref[here, hs]
            scores = dot_nt(k, q) * scale
            if real_keys < keys:
                place = lax.broadcasted_iota(jnp.int32, scores.shape, 0)
                scores = jnp.where(place < real_keys, scores, NEGATIVE)
            probs = jnp.exp(scores - lse_ref[i, pl.ds(h, 1), :])
            grad_probs = dot_nt(v, do)
            inner = jnp.sum(probs * grad_probs, axis=0, keepdims=True)
            grad_scores = (probs * (grad_probs - inner)).astype(BF16)
            dv_ref[:, hs] += dot_nn(probs.astype(BF16), do)
            dk_ref[:, hs] += dot_nn(grad_scores, q) * scale
            dq_ref[here, hs] = dot_tn(k, grad_scores).T * scale
        return 0

    in_halves(queries // block, step, between)


def exact(left, right):
    return jnp.dot(left, right, precision=lax.Precision.HIGHEST, preferred_element_type=F32)


def my_cols(whole, t, cols):
    return sum(jnp.where(t == s, whole[:, s * cols : (s + 1) * cols], 0.0) for s in range(4))


def prepare(t, cols, n):
    n.gain_wide[...] = exact(n.head_gain[...], n.one[...])
    n.offset_wide[...] = exact(n.head_bias[...], n.one[...])
    mine = my_cols(n.column_bias[...], t, cols)
    n.bias_wide[...] = exact(mine, n.fold_f32[...])
    angles = n.positions[:, 0:1] * n.lanes[0:1, :] + n.positions[:, 1:2] * n.lanes[1:2, :]
    n.cosine[...] = jnp.cos(angles) * n.mask[...]
    n.sine[...] = jnp.sin(angles) * n.lanes[2:3, :]
    n.done("cosine", "sine")
    return mine[4:5, :]


def first_body(dp, own, size, scale, heads, block, n):
    _, t, _, _, _, _ = tensor_place()
    d = lax.axis_index("dp")
    rows, width = n.residual.shape
    cols = n.skip_send.shape[2]
    span = heads * LANES
    place = DpPlace(dp) if own else None
    peers = [(d, (t + o) % 4) for o in range(1, 4)] + (place.others() if own else [])
    bar = greet(peers)
    mine = block_rows(t, rows)
    kept = [
        pltpu.make_async_copy(n.latent, n.joined0.at[mine], n.own_sem.at[0]),
        pltpu.make_async_copy(n.skip_states, n.joined1.at[mine], n.own_sem.at[1]),
    ]
    if own:
        shards = [(n.skip_in, n.skip_full), (n.project_in, n.p_land), (n.out_in, n.out_land), (n.query_in, n.query_g),
                  (n.key_in, n.key_g), (n.value_in, n.value_g), (n.cross_out_in, n.cross_out_g), (n.down_in, n.down_g)]
        kept += [pltpu.make_async_copy(a, b.at[d], n.own_sem.at[2 + i]) for i, (a, b) in enumerate(shards)]
    for cp in kept:
        cp.start()
    pl.semaphore_wait(bar, len(peers))
    spreads = [RowSpread(n.joined0, rows, *n.spread0), RowSpread(n.joined1, rows, *n.spread1)]
    for cp, spread in zip(kept, spreads):
        cp.wait()
        spread.send(0, rows)
    if own:
        n.small_land[d] = n.small[d]
        smalls = ToAll(place, lambda q: n.small.at[q], n.small_land, n.a_s, n.a_r)
        gathers = Gathers(place, 2, *n.gather_sems)
        gathers.add(n.skip_in, n.skip_full, 2)
        smalls.arrived()
        given = jnp.concatenate([n.small_land[i] for i in range(dp)], axis=0)
        n.silu[...] = jax.nn.silu(given[:, : n.shift_in.shape[0]]).astype(BF16)
        n.counted[...] = jnp.sum(given[:, given.shape[1] - LANES :], axis=0, keepdims=True)
        part = dot_nn(n.silu[...], n.shift_in[...])
        for i in range(dp):
            n.shift_part[i] = part[i : i + 1, :]
        n.shift_land[d] = n.shift_part[d]
        shifts = ToAll(place, lambda q: n.shift_part.at[q], n.shift_land, n.b_s, n.b_r)
        for i in range(3):
            gathers.add(n.project_in.at[i], n.p_land.at[:, i])
    bias_skip = prepare(t, cols, n)
    if own:
        gathers.forward()
    spreads[0].forward()
    if own:
        gathers.add(n.out_in, n.out_land)
        gathers.add(n.query_in, n.query_g)
        gathers.add(n.key_in, n.key_g)
        gathers.add(n.value_in, n.value_g)
        gathers.add(n.cross_out_in, n.cross_out_g)
        gathers.forward()
    spreads[0].finish()
    if own:
        gathers.add(n.down_in, n.down_g, 3)
        gathers.arrived(0, 2)
        kept[2].wait()
        half = dp // 2
        skip_half = lambda i: n.skip_full[pl.ds(i * half, half)].reshape(width, cols)
    else:
        skip_half = lambda i: n.skip_in[pl.ds(i * width, width), :]
    for b in range(4):
        here = pl.ds(b * rows, rows)
        n.pre[here, pl.ds(0, cols)] = dot_nn(n.joined0[here, :], skip_half(0))
    spreads[1].forward()
    if own:
        gathers.forward()
    spreads[1].finish()
    copies = []
    for o in (2, 3, 1, 0):
        b = (t + o) % 4
        here = block_rows(b, rows)
        value = (n.pre[here, pl.ds(0, cols)] + dot_nn(n.joined1[here, :], skip_half(1)) + bias_skip).astype(BF16)
        if o:
            n.skip_send[o] = value
            cp = remote(n.skip_send.at[o], n.skip_recv.at[t], n.p_s.at[o], n.p_r.at[o], (d, b))
            cp.start()
            copies.append(cp)
        else:
            n.skip_recv[t] = value
    if own:
        shifts.arrived()
        shift = n.row_bias[pl.ds(3, 1), :] + sum(n.shift_land[i] for i in range(dp))
    else:
        shift = n.shift_in[...]
    for cp in copies:
        cp.wait_recv()
    for s in range(4):
        n.skipped[:, s * cols : (s + 1) * cols] = n.skip_recv[s]
    spread = RowSpread(n.first_all, rows, *n.spread2)
    ch = rows // CHUNKS
    for k in range(CHUNKS):
        sl = pl.ds(k * ch, ch)
        cen, rstd = centre(n.skipped[sl, :].astype(F32))
        resid = cen * rstd * n.norm_gain[pl.ds(0, 1), :] + n.norm_bias[pl.ds(0, 1), :]
        n.residual[sl, :] = resid
        cen, rstd = centre(resid)
        first = cen * rstd * n.norm_gain[pl.ds(1, 1), :] + n.norm_bias[pl.ds(1, 1), :] + shift
        n.first_all[pl.ds(pl.multiple_of(t * rows + k * ch, ch), ch), :] = first.astype(BF16)
        spread.send(k * ch, ch)
    if own:
        gathers.forward()
    spread.forward()
    if own:
        gathers.forward()
    spread.finish()
    for cp in copies:
        cp.wait_send()
    n.done("joined0", "joined1", "skip_full", "skipped", "residual", "first_all")
    for part in range(3):
        if own:
            gathers.arrived(2 + part, 3 + part)
            if part == 0:
                kept[3].wait()
            narrow = n.p_land[:, part].reshape(width, cols)
        else:
            narrow = n.project_in[part]
        n.project_wide[part] = dot_nn(narrow, n.fold[...]).astype(BF16)
    if own:
        gathers.forward()

    def project(i, _):
        here = pl.ds(pl.multiple_of(i * block, block), block)
        for part in range(3):
            out = dot_nn(n.first_all[here, :], n.project_wide[part])
            if part != 1:
                out = out + n.bias_wide[pl.ds(part // 2, 1), :]
            if part < 2:
                n.pre[here, pl.ds(part * span, span)] = out
                for h in range(heads):
                    u = out[:, h * LANES : (h + 1) * LANES]
                    val = head_norm(u, n.mask[...], n.gain_wide[pl.ds(part, 1), :], n.offset_wide[pl.ds(part, 1), :], size)
                    val = turn(val, n.cosine[here, :], n.sine[here, :])
                    n.low[here, pl.ds(part * span + h * LANES, LANES)] = val.astype(BF16)
            else:
                n.low[here, pl.ds(part * span, span)] = out.astype(BF16)
        return 0

    lax.fori_loop(0, n.low.shape[0] // block, project, 0)
    n.done("project_wide", "pre", "low")
    if own:
        gathers.forward()
    attend(
        n.low.at[:, pl.ds(0, span)], n.low.at[:, pl.ds(span, span)], n.low.at[:, pl.ds(2 * span, span)],
        n.padded, n.lse, heads, scale, block, n.low.shape[0], gathers.forward if own else None,
    )
    n.mixed[...] = dot_nt(n.padded[...], n.fold[...]).astype(BF16)
    n.done("mixed")
    if own:
        gathers.arrived(5, 6)
        kept[4].wait()
        out_t = lambda: n.out_land[...].reshape(width, cols)
    else:
        out_t = lambda: n.out_in[...]
    reduce = TensorSum(*n.sum)
    reduce.start(lambda b: dot_nt(n.mixed[block_rows(b, rows), :], out_t()))
    if own:
        gathers.forward()
    spread = RowSpread(n.third_all, rows, *n.spread3)
    forward_rows(
        reduce, spread, n.third_all, n.residual, n.row_bias.at[pl.ds(0, 1)], n.norm_gain.at[pl.ds(2, 1)],
        n.norm_bias.at[pl.ds(2, 1)], n.second, rows,
    )
    n.done("second")
    if own:
        gathers.forward()
    spread.forward()
    if own:
        gathers.forward()
    spread.finish()
    reduce.sent()
    if own:
        gathers.forward()
        gathers.arrived(6, len(gathers.pieces))
        for cp in kept[5:]:
            cp.wait()
        for g in (gathers, smalls, shifts):
            g.sent()


def cross_body(dp, own, size, scale, heads, block, real, n):
    rows, width = n.second.shape
    span = heads * LANES
    d, _, _, _, sib, yp = tensor_place()
    place = DpPlace(dp) if own else None
    peers = [sib, yp] + (place.near() if own else [])
    bar = greet(peers)
    pl.semaphore_wait(bar, len(peers))
    if own:
        gathers = Gathers(place, 2, *n.gather_sems)
        gathers.add(n.up_in, n.up_g, 4)
        gathers.add(n.down_in, n.down_g)
        kept = [pltpu.make_async_copy(a, b.at[d], n.own_sem.at[i])
                for i, (a, b) in enumerate(((n.up_in, n.up_g), (n.down_in, n.down_g)))]
        for cp in kept:
            cp.start()
    n.need("query", "key", "value", "text")
    n.query_wide[...] = dot_nn(n.query[...], n.fold[...]).astype(BF16)
    for part, w in enumerate((n.key, n.value)):
        n.keyval_wide[part] = dot_nn(w[...], n.fold[...]).astype(BF16)
        out = dot_nn(n.text[...], n.keyval_wide[part])
        if part == 0:
            n.text_pre[...] = out
            for h in range(heads):
                val = head_norm(out[:, h * LANES : (h + 1) * LANES], n.mask[...], n.head_gain[pl.ds(3, 1), :], n.head_bias[pl.ds(3, 1), :], size)
                n.text_low[:, head_at(h)] = val.astype(BF16)
        else:
            n.text_low[:, pl.ds(span, span)] = (out + n.bias_wide[pl.ds(3, 1), :]).astype(BF16)
    n.need("third_all", "cosine", "sine")

    def project(i, _):
        here = pl.ds(pl.multiple_of(i * block, block), block)
        out = dot_nn(n.third_all[here, :], n.query_wide[...]) + n.bias_wide[pl.ds(2, 1), :]
        n.pre[here, :] = out
        for h in range(heads):
            val = head_norm(out[:, h * LANES : (h + 1) * LANES], n.mask[...], n.head_gain[pl.ds(2, 1), :], n.head_bias[pl.ds(2, 1), :], size)
            n.low[here, head_at(h)] = turn(val, n.cosine[here, :], n.sine[here, :]).astype(BF16)
        return 0

    lax.fori_loop(0, n.low.shape[0] // block, project, 0)
    n.done("query_wide", "keyval_wide", "pre", "low")
    attend(n.low, n.text_low.at[:, pl.ds(0, span)], n.text_low.at[:, pl.ds(span, span)], n.padded, n.lse, heads, scale, block, real)
    n.mixed[...] = dot_nt(n.padded[...], n.fold[...]).astype(BF16)
    n.need("cross_out", "second")
    reduce = TensorSum(*n.sum)
    reduce.start(lambda b: dot_nt(n.mixed[block_rows(b, rows), :], n.cross_out[...]))
    n.done("mixed")
    if own:
        gathers.forward(2)
    spread = RowSpread(n.fourth_all, rows, *n.spread)
    forward_rows(
        reduce, spread, n.fourth_all, n.second, n.row_bias.at[pl.ds(1, 1)], n.norm_gain.at[pl.ds(3, 1)],
        n.norm_bias.at[pl.ds(3, 1)], n.third_sum, rows,
    )
    if own:
        gathers.forward()
    spread.forward()
    if own:
        gathers.forward()
    spread.finish()
    reduce.sent()
    if own:
        gathers.forward()
        gathers.arrived(0, len(gathers.pieces))
        for cp in kept:
            cp.wait()
        gathers.sent()


def load_down(own, n):
    if not own:
        return [], lambda: n.down_t[...]
    first = n.down_a.shape[1]
    copies = [
        pltpu.make_async_copy(n.down_a, n.down_t.at[:, pl.ds(0, first)], n.down_sem.at[0]),
        pltpu.make_async_copy(n.down_b, n.down_t.at[:, pl.ds(first, n.down_b.shape[1])], n.down_sem.at[1]),
    ]
    for cp in copies:
        cp.start()
    return copies, lambda: n.down_t[...].reshape(-1, n.down_t.shape[2])


def feed_body(own, n):
    rows = n.third_sum.shape[0]
    _, t, _, _, sib, yp = tensor_place()
    bar = greet((sib, yp))
    down_copies, down_t = load_down(own, n)
    hidden = n.up.shape[1]
    my_hidden = pl.ds(pl.multiple_of(t * hidden, LANES), hidden)
    seat = t * rows + lax.broadcasted_iota(jnp.int32, (rows, 1), 0)
    weight = n.loss_mask[...].astype(F32) * (seat < n.true_count[...]).astype(F32)
    weight = (n.total[...] / n.counted[:, 0:1]) * weight
    n.need("fourth_all", "up")
    root, cube = float(np.sqrt(2.0 / np.pi)), 0.044715

    def product(b):
        here = block_rows(b, rows)
        x = dot_nn(n.fourth_all[here, :], n.up[...]) + n.hidden_bias[:, my_hidden]
        square = x * x
        th = jnp.tanh(root * (x + cube * (square * x)))
        cdf = 0.5 * (1.0 + th)
        active = (x * cdf).astype(BF16)
        n.active[here, :] = active
        slope = cdf + (0.5 * root) * x * (1.0 - th * th) * (1.0 + (3.0 * cube) * square)
        n.slope[here, :] = slope.astype(BF16)
        while down_copies:
            down_copies.pop().wait()
        return dot_nt(active, down_t())

    reduce = TensorSum(*n.sum)
    reduce.start(product, lambda: pl.semaphore_wait(bar, 2), long=True)
    n.done("active", "slope")
    n.need("third_sum", "teacher")
    spread = RowSpread(n.grad_all, rows, *n.spread)
    ch = rows // CHUNKS
    sums = None
    for k in range(CHUNKS):
        sl, total = reduce.chunk(k)
        final = n.third_sum[sl, :] + (total + n.row_bias[pl.ds(2, 1), :])
        n.block_out[sl, :] = final.astype(BF16)
        grad = weight[k * ch : (k + 1) * ch, :] * (final - n.teacher[sl, :].astype(F32))
        n.grad_final[sl, :] = grad
        low = grad.astype(BF16)
        n.grad_all[pl.ds(pl.multiple_of(t * rows + k * ch, ch), ch), :] = low
        spread.send(k * ch, ch)
        sums = add_sums(sums, [low.astype(F32)])
    n.bias_mlp[...] = sums[0]
    n.done("block_out", "grad_final")
    spread.forward()
    spread.finish()
    reduce.sent()


def feed_back_body(dp, own, n):
    rows = n.third_sum.shape[0]
    _, _, _, _, sib, yp = tensor_place()
    place = DpPlace(dp) if own else None
    peers = [sib, yp] + (place.near() if own else [])
    bar = greet(peers)
    down_copies, down_t = load_down(own, n)
    n.need("grad_all", "active")
    n.grad_down[...] = dot_tn(n.grad_all[...], n.active[...]).astype(BF16).reshape(n.grad_down.shape)
    pl.semaphore_wait(bar, len(peers))
    if own:
        down = GradScatter(place, n.grad_down, *n.down_bufs, *n.down_sems)

    def product(b):
        here = block_rows(b, rows)
        upper = (dot_nn(n.grad_all[here, :], down_t()) * n.slope[here, :].astype(F32)).astype(BF16)
        n.upper[here, :] = upper
        return dot_nt(upper, n.up[...])

    for cp in down_copies:
        cp.wait()
    n.need("slope", "up")
    reduce = TensorSum(*n.sum)
    reduce.start(product, long=True)
    n.need("fourth_all", "third_sum", "grad_final")
    n.bias_hidden[...] = sum(
        jnp.sum(n.upper[pl.ds(b * rows, rows), :].astype(F32), axis=0, keepdims=True) for b in range(4)
    )
    n.grad_up[...] = dot_tn(n.fourth_all[...], n.upper[...]).astype(BF16).reshape(n.grad_up.shape)
    n.done("grad_up")
    spread = RowSpread(n.c_all, rows, *n.spread)
    if own:
        down.steps(1)
    backward_rows(reduce, spread, n.c_all, n.third_sum, n.gain, n.grad_final, n.grad_third, (n.sum0, n.sum1, n.sum2), rows)
    if own:
        down.steps(2)
    spread.forward()
    if own:
        down.steps()
    spread.finish()
    reduce.sent()
    if own:
        n.down_mine[...] = down.result()
        down.sent()


def spread_heads(n, rows_in, w, do, block):
    def spread(i, _):
        here = pl.ds(pl.multiple_of(i * block, block), block)
        narrow = dot_nn(rows_in[here, :], w[...]).astype(BF16)
        do[here, :] = dot_nn(narrow, n.fold[...]).astype(BF16)
        return 0

    lax.fori_loop(0, do.shape[0] // block, spread, 0)


def cross_back_body(dp, own, size, scale, heads, block, real, n):
    rows = n.second.shape[0]
    span = heads * LANES
    d, t, _, _, sib, yp = tensor_place()
    place = DpPlace(dp) if own else None
    peers = [sib, yp] + (place.near() if own else [])
    bar = greet(peers)
    pl.semaphore_wait(bar, len(peers))
    if own:
        up = GradScatter(place, n.grad_up, *n.up_bufs, *n.up_sems)
    n.need("c_all", "cross_out")
    spread_heads(n, n.c_all, n.cross_out, n.do, block)
    n.need("low", "text_low")
    attend_back(
        n.low, n.text_low.at[:, pl.ds(0, span)], n.text_low.at[:, pl.ds(span, span)],
        n.do, n.lse, n.dq, n.dk, n.dv, heads, scale, block, real,
    )
    n.gains[...] = jnp.zeros(n.gains.shape, F32)
    n.offsets[...] = jnp.zeros(n.offsets.shape, F32)
    n.sums[...] = jnp.zeros(n.sums.shape, F32)

    def finish(i, _):
        here = pl.ds(pl.multiple_of(i * block, block), block)
        for h in range(heads):
            hs = head_at(h)
            grad = turn_back(n.dq[here, hs], n.cosine[here, :], n.sine[here, :])
            grad, g, o = head_back(grad, n.pre[here, hs], n.mask[...], n.head_gain[pl.ds(2, 1), :], size)
            n.gains[pl.ds(0, 1), :] += g
            n.offsets[pl.ds(0, 1), :] += o
            grad_low = grad.astype(BF16)
            n.p[here, hs] = grad_low
            n.sums[:, hs] += jnp.sum(grad_low.astype(F32), axis=0, keepdims=True)
        return 0

    if own:
        up.steps(1)
    n.need("pre", "cosine", "sine")
    lax.fori_loop(0, n.p.shape[0] // block, finish, 0)
    n.need("query_wide")
    reduce = TensorSum(*n.sum)
    reduce.start(lambda b: dot_nt(n.p[block_rows(b, rows), :], n.query_wide[...]))
    if own:
        up.steps(2)
    n.need("text_pre", "mixed", "third_all", "text", "keyval_wide", "second", "grad_third")
    for h in range(heads):
        hs = head_at(h)
        grad, g, o = head_back(n.dk[:, hs], n.text_pre[:, hs], n.mask[...], n.head_gain[pl.ds(3, 1), :], size)
        n.gains[pl.ds(1, 1), :] += g
        n.offsets[pl.ds(1, 1), :] += o
        n.text_p[:, hs] = grad.astype(BF16)
        low_v = n.dv[:, hs].astype(BF16)
        n.text_p[:, pl.ds(span + h * LANES, LANES)] = low_v
        n.text_sums[:, hs] = jnp.sum(low_v.astype(F32), axis=0, keepdims=True)
    parts = n.grads.shape[0]

    def put(start, value):
        count = value.shape[0] // parts
        n.grads[:, pl.ds(start, count)] = value.astype(BF16).reshape(parts, count, value.shape[1])
        return start + count

    at = put(0, dot_tn(n.c_all[...], n.mixed[...]))
    at = put(at, dot_tn(n.third_all[...], dot_nt(n.p[...], n.fold[...]).astype(BF16)))
    for part in range(2):
        narrow = dot_nt(n.text_p[:, pl.ds(part * span, span)], n.fold[...]).astype(BF16)
        at = put(at, dot_tn(n.text[...], narrow))
    n.done("grads")
    n.grad_text[...] = (
        dot_nt(n.text_p[:, pl.ds(0, span)], n.keyval_wide[0]) + dot_nt(n.text_p[:, pl.ds(span, span)], n.keyval_wide[1])
    ).astype(BF16)
    if own:
        up.steps()
    spread = RowSpread(n.s_all, rows, *n.spread)
    backward_rows(reduce, spread, n.s_all, n.second, n.gain, n.grad_third, n.grad_second, (n.sum0, n.sum1, n.sum2), rows)
    spread.forward()
    spread.finish()
    reduce.sent()
    if own:
        n.up_mine[...] = up.result()
        up.sent()


class TextSum:
    def __init__(self, part, total, land, yland, back, sems):
        _, _, _, self.c, self.sib, self.yp = tensor_place()
        self.part, self.total, self.land, self.yland, self.last, self.sems = part, total, land, yland, back, sems
        self.half = piece_rows(part.shape[0], 2, 1)
        self.copies = [remote(part, land, sems.at[0], sems.at[1], self.sib)]
        self.copies[0].start()

    def here(self, c):
        return pl.ds(pl.multiple_of(c * (self.part.shape[0] - self.half), 16), self.half)

    def along(self):
        self.copies[0].wait_recv()
        self.total[...] = (self.part[...].astype(F32) + self.land[...].astype(F32)).astype(BF16)
        cp = remote(self.total.at[self.here(self.c)], self.yland, self.sems.at[2], self.sems.at[3], self.yp)
        cp.start()
        self.copies.append(cp)

    def back(self):
        self.copies[1].wait_recv()
        self.copies[1].wait_send()
        mine = self.here(self.c)
        self.yland[...] = (self.total[mine, :].astype(F32) + self.yland[...].astype(F32)).astype(BF16)
        self.copies[0].wait_send()
        cp = remote(self.yland, self.last, self.sems.at[4], self.sems.at[5], self.sib)
        cp.start()
        self.copies.append(cp)

    def result(self, out):
        self.copies[2].wait_recv()
        out[self.here(self.c), :] = self.yland[...].astype(F32)
        out[self.here(1 - self.c), :] = self.last[...].astype(F32)
        self.copies[2].wait_send()


def self_back_body(dp, own, size, scale, heads, block, n):
    span = heads * LANES
    _, _, _, _, sib, yp = tensor_place()
    place = DpPlace(dp) if own else None
    peers = [sib, yp] + (place.near() if own else [])
    bar = greet(peers)
    pl.semaphore_wait(bar, len(peers))
    text = TextSum(n.text_part, n.text_total, n.text_land, n.text_yland, n.text_back, n.text_sems)
    if own:
        few = GradScatter(place, n.few_grads, *n.few_bufs, *n.few_sems)
    n.need("s_all", "out_t")
    spread_heads(n, n.s_all, n.out_t, n.do, block)
    text.along()
    n.need("low")
    attend_back(
        n.low.at[:, pl.ds(0, span)], n.low.at[:, pl.ds(span, span)], n.low.at[:, pl.ds(2 * span, span)],
        n.do, n.lse, n.dq, n.dk, n.dv, heads, scale, block, n.low.shape[0], few.step if own else None,
    )
    text.back()
    n.need("pre", "cosine", "sine")
    n.gains[...] = jnp.zeros(n.gains.shape, F32)
    n.offsets[...] = jnp.zeros(n.offsets.shape, F32)
    n.sums[...] = jnp.zeros(n.sums.shape, F32)

    def finish(i, _):
        here = pl.ds(pl.multiple_of(i * block, block), block)
        for part, grad_ref in enumerate((n.dq, n.dk, n.dv)):
            for h in range(heads):
                hs = head_at(h)
                wide = pl.ds(part * span + h * LANES, LANES)
                grad = grad_ref[here, hs]
                if part < 2:
                    grad = turn_back(grad, n.cosine[here, :], n.sine[here, :])
                    grad, g, o = head_back(grad, n.pre[here, wide], n.mask[...], n.head_gain[pl.ds(part, 1), :], size)
                    n.gains[pl.ds(part, 1), :] += g
                    n.offsets[pl.ds(part, 1), :] += o
                grad_low = grad.astype(BF16)
                n.p[here, wide] = grad_low
                if part != 1:
                    n.sums[:, wide] += jnp.sum(grad_low.astype(F32), axis=0, keepdims=True)
            n.p_low[part, here, :] = dot_nt(n.p[here, pl.ds(part * span, span)], n.fold[...]).astype(BF16)
        return 0

    lax.fori_loop(0, n.p.shape[0] // block, finish, 0)
    by_place = lambda v: v.astype(BF16).reshape(n.grad_out.shape)
    if own:
        few.steps()
    n.done("p")
    n.need("mixed", "first_all")
    n.grad_out[...] = by_place(dot_tn(n.s_all[...], n.mixed[...]))
    for part in range(3):
        n.grad_project[:, part] = by_place(dot_tn(n.first_all[...], n.p_low[part]))
    n.done("grad_out", "grad_project")
    text.result(n.grad_text)
    if own:
        n.few_mine[...] = few.result()
        few.sent()


PACK_ROWS, PACK_SUMS = 8, 16


def last_body(dp, own, n):
    _, t, _, _, _, _ = tensor_place()
    d = lax.axis_index("dp")
    rows, width = n.residual.shape
    cols = n.krecv.shape[2]
    place = DpPlace(dp) if own else None
    peers = [(d, (t + o) % 4) for o in range(1, 4)] + (place.others() if own else [])
    bar = greet(peers)
    reduce = TensorSum(*n.sum)
    scatters = []

    def scatter(source, buffers):
        i = len(scatters)
        scatters.append(GradScatter(place, source, *buffers, *n.scatter_sems[5 * i : 5 * i + 5]))

    def ready():
        pl.semaphore_wait(bar, len(peers))
        if own:
            scatter(n.grad_out, n.out_bufs)
            for i in range(3):
                scatter(n.grad_project.at[:, i], n.project_bufs[3 * i : 3 * i + 3])

    def product(b):
        here = block_rows(b, rows)
        span = n.project_wide.shape[2]
        total = dot_nt(n.p[here, pl.ds(0, span)], n.project_wide[0])
        for part in range(1, 3):
            total = total + dot_nt(n.p[here, pl.ds(part * span, span)], n.project_wide[part])
        return total

    n.need("p", "project_wide")
    reduce.start(product, ready)
    n.need("residual", "grad_second", "skipped")
    if own:
        scatters[0].steps()
    sums = None
    for k in range(CHUNKS):
        sl, total = reduce.chunk(k)
        back, xhat = norm_back(total, n.residual[sl, :], n.norm_gain[pl.ds(1, 1), :])
        grad = n.grad_second[sl, :] + back
        back0, xhat0 = norm_back(grad, n.skipped[sl, :].astype(F32), n.norm_gain[pl.ds(0, 1), :])
        low = back0.astype(BF16)
        for s in range(4):
            n.ksend[s, sl, :] = low[:, s * cols : (s + 1) * cols]
        sums = add_sums(sums, [low.astype(F32), total * xhat, total, grad * xhat0, grad])
    copies = []
    for o in (2, 3, 1):
        b = (t + o) % 4
        cp = remote(n.ksend.at[b], n.krecv.at[t], n.k_s.at[o], n.k_r.at[o], (d, b))
        cp.start()
        copies.append(cp)
    n.krecv[t] = n.ksend[t]
    bias_skip, gain_first, offset_first, gain_skip, offset_skip = sums
    n.tile[...] = offset_first
    n.tile_land[t] = n.tile[...]
    tiles = []
    for o in (1, 2, 3):
        cp = remote(n.tile, n.tile_land.at[t], n.t_s.at[o], n.t_r.at[o], (d, (t + o) % 4))
        cp.start()
        tiles.append(cp)
    n.pack[...] = jnp.zeros(n.pack.shape, F32)
    lines = [gain_skip, gain_first, offset_skip, offset_first, bias_skip, n.gain_third[...], n.gain_fourth[...],
             n.offset_third[...], n.offset_fourth[...], n.bias_attn[...], n.bias_cross_out[...], n.bias_mlp[...]]
    for i, v in enumerate(lines):
        n.pack[i // PACK_ROWS, pl.ds(i % PACK_ROWS, 1), :] = v
    heads_at = len(lines)
    for i, v in enumerate((n.self_gains, n.cross_gains, n.self_offsets, n.cross_offsets)):
        for r in range(2):
            n.pack[heads_at // PACK_ROWS, pl.ds(heads_at % PACK_ROWS, 1), pl.ds((2 * i + r) * LANES, LANES)] = v[pl.ds(r, 1), :]
    span = n.project_wide.shape[2]
    wide = [n.self_sums[:, pl.ds(0, span)], n.self_sums[:, pl.ds(2 * span, span)], n.cross_sums[...], n.text_sums[...]]
    hidden = n.bias_hidden.shape[1]
    for s in range(4):
        seat = (t == s).astype(F32)
        block, row = divmod(PACK_SUMS + 4 * s, PACK_ROWS)
        for i, v in enumerate(wide):
            n.pack[block, pl.ds(row, 1), pl.ds(i * cols, cols)] = seat * exact(v, n.unfold[...])
        for i, start in enumerate(range(0, hidden, width)):
            count = min(width, hidden - start)
            n.pack[block, pl.ds(row + 1 + i, 1), pl.ds(0, count)] = seat * n.bias_hidden[:, pl.ds(start, count)]
    shares = []
    for o in (1, 2, 3):
        b = (t + o) % 4
        cp = remote(n.pack.at[b], n.pack_in_land.at[t], n.ps_s.at[o], n.ps_r.at[o], (d, b))
        cp.start()
        shares.append(cp)
    n.pack_in_land[t] = n.pack[t]
    if own:
        scatters[1].steps()
    for cp in copies:
        cp.wait_recv()
    reduce.sent()
    for cp in tiles:
        cp.wait_recv()
    n.low_out[...] = (n.tile_land[0] + n.tile_land[1] + n.tile_land[2] + n.tile_land[3]).astype(BF16).astype(F32)
    for cp in shares:
        cp.wait_recv()
    n.pack_mine[...] = n.pack_in_land[0] + n.pack_in_land[1] + n.pack_in_land[2] + n.pack_in_land[3]
    if own:
        n.low_land[d] = n.low_out[...]
        lows = ToAll(place, lambda q: n.low_out, n.low_land, n.l_s, n.l_r)
        pack_cp = remote(n.pack_mine, n.pack_x, n.px_s.at[0], n.px_r.at[0], place.pair)
        pack_cp.start()
    n.need("skip_w")
    halves = [TensorSum(*n.sum), TensorSum(*n.sum1)]
    for h, half in enumerate(halves):
        half.start(lambda b, h=h: dot_nt(n.krecv[b], n.skip_w[pl.ds(h * width, width), :]))
    if own:
        pack_cp.wait_recv()
        pack_cp.wait_send()
        n.pack_mine[...] = n.pack_mine[...] + n.pack_x[...]
        n.pack_z[place.zi] = n.pack_mine[...]
        packs = []
        for j in range(1, place.line):
            cp = remote(n.pack_mine, n.pack_z.at[place.zi], n.pz_s.at[j], n.pz_r.at[j], (place.ahead(j), place.t))
            cp.start()
            packs.append(cp)
        scatters[2].steps()
    n.need("joined0", "joined1")
    k_all = n.krecv[...].reshape(4 * rows, cols)
    count = n.grad_skip_w.shape[0] // 2
    for h, joined in enumerate((n.joined0, n.joined1)):
        n.grad_skip_w[pl.ds(h * count, count)] = (
            dot_tn(joined[...], k_all).astype(BF16).reshape((count,) + n.grad_skip_w.shape[1:])
        )
    if own:
        scatters[3].steps()
        scatter(n.grad_skip_w, n.skip_bufs)
        for cp in packs:
            cp.wait_recv()
            cp.wait_send()
        n.pack_mine[...] = sum(n.pack_z[i] for i in range(place.line))
    n.pack_t[t] = n.pack_mine[...]
    ends = []
    for o in (1, 2, 3):
        cp = remote(n.pack_mine, n.pack_t.at[t], n.pt_s.at[o], n.pt_r.at[o], (d, (t + o) % 4))
        cp.start()
        ends.append(cp)
    if own:
        scatters[4].steps()
        lows.arrived()
        low_all = jnp.concatenate([n.low_land[i] for i in range(dp)], axis=0)
        n.shift_grad[...] = dot_tn(n.silu[...], low_all.astype(BF16))
        n.shift_bias[...] = jnp.sum(low_all, axis=0, keepdims=True)
        n.out_mine[...] = scatters[0].result()
        for i in range(3):
            n.project_mine[i] = scatters[1 + i].result()
    else:
        n.shift_grad[...] = n.low_out[...]
        n.shift_bias[...] = n.low_out[...]
    for half, out in zip(halves, (n.grad_latent, n.grad_skip)):
        for k in range(CHUNKS):
            sl, total = half.chunk(k)
            out[sl, :] = total
        half.sent()
        n.done("grad_latent" if out is n.grad_latent else "grad_skip")
    for cp in ends:
        cp.wait_recv()
        cp.wait_send()
    n.pack_out[...] = n.pack_t[...]
    if own:
        n.skip_mine[...] = scatters[4].result()
        for s in scatters:
            s.sent()
        lows.sent()
    for cp in copies + tiles + shares:
        cp.wait_send()


def finish_body(cols, hidden, n):
    pairs = [(n.block_out, n.o_block), (n.grad_latent, n.o_latent), (n.grad_skip, n.o_skip), (n.skip_mine, n.o_skip_mine),
             (n.shift_grad, n.o_shift), (n.up_mine, n.o_up)]
    r = n.o_query.shape[0]
    for source, out in pairs:
        out[...] = source[...]
    n.o_query[...] = n.query_mine[pl.ds(n.query_mine.shape[0] - r if n.query_mine.shape[0] == r else r, r), :]
    n.o_text[...] = n.text_part[pl.ds(0, n.o_text.shape[0]), :]
    row = lambda i: n.pack[i // PACK_ROWS, pl.ds(i % PACK_ROWS, 1), :]
    for out, places in ((n.norm_gain, (0, 1, 5, 6)), (n.norm_bias, (2, 3, 7, 8)), (n.row_bias, (9, 10, 11))):
        for i, at in enumerate(places):
            out[pl.ds(i, 1), :] = row(at)
    n.row_bias[pl.ds(3, 1), :] = n.shift_bias[...]
    packed = row(12)
    for k, out in enumerate((n.head_gain, n.head_bias)):
        for i in range(4):
            at = (4 * k + i) * LANES
            out[pl.ds(i, 1), :] = exact(packed[:, at : at + LANES], n.unfold[...])
    width = packed.shape[1]
    for s in range(4):
        at = PACK_SUMS + 4 * s
        columns = row(at)
        for i in range(4):
            n.column_bias[pl.ds(i, 1), pl.ds(s * cols, cols)] = columns[:, i * cols : (i + 1) * cols]
        for i, start in enumerate(range(0, hidden, width)):
            count = min(width, hidden - start)
            n.hidden_bias[:, pl.ds(s * hidden + start, count)] = row(at + 1 + i)[:, :count]
    n.column_bias[pl.ds(4, 1), :] = row(4)


def fold_matrix(heads, size):
    out = np.zeros((heads * size, heads * LANES), np.float32)
    for h in range(heads):
        for e in range(size):
            out[h * size + e, h * LANES + (e % 2) * (LANES // 2) + e // 2] = 1.0
    return out


def body(
    latent, skip_states, text_states, condition, teacher, loss_mask, true_counts, positions,
    skip_proj, shift_proj, self_project, self_output, cross_query, cross_keyval, cross_output, hidden_up, hidden_down,
    norm_gain, norm_bias, head_gain, head_bias, column_bias, hidden_bias, row_bias,
):
    d, t = lax.axis_index("dp"), lax.axis_index("tensor")
    dp, tensor = lax.axis_size("dp"), lax.axis_size("tensor")
    rows, width = latent.shape
    group = rows * tensor
    size = head_gain.shape[1]
    cols = self_project.shape[2]
    heads = cols // size
    span = heads * LANES
    hidden = hidden_up.shape[1]
    text_len, text_width = text_states.shape[1:]
    text_pad = -(-text_len // 16) * 16
    scale = size ** (-0.5)
    block = min(256, group)
    r, text_share = shift_proj.shape[0], cross_keyval.shape[0]
    own = r % 16 == 0 and text_share % 16 == 0 and skip_proj.shape[0] % 32 == 0 and dp == 8
    parts = dp if own else 1
    line = max(dp // 2, 1) if own else 1
    dma, vm = pltpu.SemaphoreType.DMA, pltpu.VMEM
    few = lambda *shape: shape if own else (16, LANES)

    fold_np = fold_matrix(heads, size)
    fold = jnp.asarray(fold_np, BF16)
    one_np = fold_np[:size, :LANES]
    mask = jnp.asarray(one_np.sum(0, keepdims=True), F32)
    quarter = size // 4
    lane_np = np.zeros((2, LANES), np.float32)
    sign_np = np.zeros((1, LANES), np.float32)
    for i in range(size // 2):
        f = np.float32(10000.0 ** (-(i % quarter) / quarter))
        for half in range(2):
            lane_np[i // quarter, half * (LANES // 2) + i] = f
            sign_np[0, half * (LANES // 2) + i] = 2 * half - 1
    lanes_in = jnp.asarray(np.concatenate([lane_np, sign_np]))
    one = jnp.asarray(one_np)

    project_in = jnp.transpose(self_project, (1, 0, 2))
    shards = [self_output.T, cross_query, cross_output.T, cross_keyval[:, 0], cross_keyval[:, 1], hidden_up, hidden_down.T]
    if own:
        lanes = -(-r // LANES) * LANES
        slices = jnp.pad(condition.astype(F32).reshape(dp, r), ((0, 0), (0, lanes - r)))
        slices = jnp.concatenate([slices, jnp.broadcast_to(true_counts.astype(F32)[:, None], (dp, LANES))], axis=1)
        small = slices[:, None, :]
        skip_in, shift_in = skip_proj, shift_proj
    else:
        small_all = lax.all_gather(
            jnp.concatenate([condition.astype(F32), true_counts.astype(F32)[:, None]], axis=1), "dp", axis=0, tiled=True
        )
        silu_all = jax.nn.silu(small_all[:, :width]).astype(BF16)
        silu = lax.dynamic_slice_in_dim(silu_all, d * r, r, 1)
        shift_in = lax.psum_scatter(dot_nn(silu, shift_proj), "dp", scatter_dimension=0, tiled=True) + row_bias[3:4]
        small = jnp.zeros((1, 8, LANES), F32)
        skip_in = lax.all_gather(skip_proj, "dp", axis=0, tiled=True)
        project_in = lax.all_gather(project_in, "dp", axis=1, tiled=True)
        shards = [lax.all_gather(v, "dp", axis=0, tiled=True) for v in shards]
    early_rows = 128 if own else r
    down_parts = [shards[6][:early_rows], shards[6][early_rows:]] if own else [shards[6], shards[6]]
    full = shaped((group, width), BF16)
    mine = shaped((rows, width), F32)
    mine_low = shaped((rows, width), BF16)
    line_sum = shaped((1, width), F32)
    lse_shape = shaped((group // block, heads, block), F32)
    sum_scratch = TensorSum.scratch(rows, width)
    first = named_kernel(
        "first", 0, functools.partial(first_body, dp, own, size, scale, heads, block),
        dict(
            latent=latent, skip_states=skip_states, skip_in=skip_in, project_in=project_in, out_in=shards[0],
            query_in=shards[1], cross_out_in=shards[2], key_in=shards[3], value_in=shards[4], down_in=down_parts[0],
            small=small, shift_in=shift_in, column_bias=column_bias, positions=positions.T.astype(F32), lanes=lanes_in,
            norm_gain=norm_gain, norm_bias=norm_bias, row_bias=row_bias, head_gain=head_gain, head_bias=head_bias,
            one=one, fold_f32=jnp.asarray(fold_np), mask=mask, fold=fold,
        ),
        dict(
            joined0=full, joined1=full, skip_full=shaped(few(dp, skip_proj.shape[0], cols), BF16), skipped=mine_low,
            residual=mine, first_all=full, silu=shaped(few(dp, r), BF16), counted=shaped((1, LANES), F32),
            project_wide=shaped((3, width, span), BF16), pre=shaped((group, 2 * span), F32),
            low=shaped((group, 3 * span), BF16), mixed=shaped((group, cols), BF16), lse=lse_shape,
            out_land=shaped(few(dp, r, cols), BF16), query_g=shaped(few(dp, r, cols), BF16),
            key_g=shaped(few(dp, text_share, cols), BF16), value_g=shaped(few(dp, text_share, cols), BF16),
            cross_out_g=shaped(few(dp, r, cols), BF16), down_g=shaped(few(dp, early_rows, hidden), BF16), third_all=full, second=mine,
            gain_wide=shaped((4, LANES), F32), offset_wide=shaped((4, LANES), F32), bias_wide=shaped((column_bias.shape[0], span), F32),
            cosine=shaped((group, LANES), F32), sine=shaped((group, LANES), F32),
        ),
        dict(
            p_land=vm(few(dp, 3, r, cols), BF16), padded=vm((group, span), BF16), skip_send=vm((4, rows, cols), BF16),
            skip_recv=vm((4, rows, cols), BF16), small_land=vm(small.shape, F32), shift_part=vm((dp, 1, width), F32),
            shift_land=vm((dp, 1, width), F32), sum=sum_scratch, own_sem=dma((10,)), a_s=dma((dp,)),
            a_r=dma((dp,)), b_s=dma((dp,)), b_r=dma((dp,)), p_s=dma((4,)), p_r=dma((4,)), gather_sems=Gathers.scratch(13, line),
            spread0=RowSpread.scratch(1),
            spread1=RowSpread.scratch(1), spread2=RowSpread.scratch(), spread3=RowSpread.scratch(),
        ),
        hbm=("latent", "skip_states", "query_in", "cross_out_in", "key_in", "value_in", "down_in",
             "query_g", "cross_out_g", "key_g", "value_g", "down_g") + (("skip_in", "project_in", "out_in") if own else ()),
        early=("cosine", "sine", "joined0", "joined1", "skip_full", "skipped", "residual", "first_all", "project_wide", "pre", "low", "mixed", "second"),
    )
    if own:
        silu, counted = first.silu, first.counted
        skip_full = first.skip_full.reshape(2 * width, cols)
        out_t, query, cross_out_t = [v.reshape(width, cols) for v in (first.out_land, first.query_g, first.cross_out_g)]
        key, value = [v.reshape(text_width, cols) for v in (first.key_g, first.value_g)]
    else:
        counted, skip_full = jnp.full((1, LANES), jnp.sum(small_all[:, width])), skip_in
        out_t, query, cross_out_t, key, value, up_full, down_t = shards

    text = jnp.pad(text_states[0], ((0, text_pad - text_len), (0, 0)))
    cross = named_kernel(
        "cross", 1, functools.partial(cross_body, dp, own, size, scale, heads, block, text_len),
        dict(
            third_all=first.third_all, query=query, key=key, value=value, cross_out=cross_out_t, up_in=shards[5], down_in=down_parts[1], text=text,
            bias_wide=first.bias_wide, cosine=first.cosine, sine=first.sine, norm_gain=norm_gain,
            norm_bias=norm_bias, row_bias=row_bias, head_gain=first.gain_wide, head_bias=first.offset_wide, mask=mask, fold=fold,
            second=first.second,
        ),
        dict(
            query_wide=shaped((width, span), BF16), keyval_wide=shaped((2, text_width, span), BF16),
            text_pre=shaped((text_pad, span), F32), text_low=shaped((text_pad, 2 * span), BF16),
            pre=shaped((group, span), F32), low=shaped((group, span), BF16), mixed=shaped((group, cols), BF16),
            lse=lse_shape, fourth_all=full, third_sum=mine,
            up_g=shaped(few(dp, r, hidden), BF16), down_g=shaped(few(dp, r - early_rows, hidden), BF16),
        ),
        dict(
            padded=vm((group, span), BF16), sum=sum_scratch, spread=RowSpread.scratch(),
            gather_sems=Gathers.scratch(5, line), own_sem=dma((2,)),
        ),
        hbm=("up_in", "up_g", "down_in", "down_g"),
        late=("query", "key", "value", "text", "third_all", "cosine", "sine", "cross_out", "second"),
        early=("query_wide", "keyval_wide", "pre", "low", "mixed"),
    )
    if own:
        up_full = cross.up_g.reshape(width, hidden)
        down_ins = dict(down_a=first.down_g, down_b=cross.down_g)
        down_scratch = dict(down_t=vm((dp, r, hidden), BF16), down_sem=dma((2,)))
    else:
        down_ins, down_scratch = dict(down_t=down_t), {}

    feed = named_kernel(
        "feed", 2, functools.partial(feed_body, own),
        dict(
            fourth_all=cross.fourth_all, up=up_full, hidden_bias=hidden_bias[None], **down_ins, third_sum=cross.third_sum,
            row_bias=row_bias, teacher=teacher, loss_mask=loss_mask[:, None], true_count=true_counts[:, None],
            counted=counted, total=jnp.full((1, 1), dp * group, F32),
        ),
        dict(
            active=shaped((group, hidden), BF16), slope=shaped((group, hidden), BF16), grad_all=full, block_out=mine_low,
            grad_final=mine, bias_mlp=line_sum,
        ),
        dict(sum=sum_scratch, spread=RowSpread.scratch(), **down_scratch),
        hbm=("down_a", "down_b"),
        late=("fourth_all", "up", "third_sum", "teacher"),
        early=("active", "slope", "block_out", "grad_final"),
    )

    back = named_kernel(
        "feed_back", 3, functools.partial(feed_back_body, dp, own),
        dict(
            grad_all=feed.grad_all, slope=feed.slope, active=feed.active, **down_ins, up=up_full,
            fourth_all=cross.fourth_all, third_sum=cross.third_sum, gain=norm_gain[3:4], grad_final=feed.grad_final,
        ),
        dict(
            c_all=full, grad_third=mine, sum0=line_sum, sum1=line_sum, sum2=line_sum, bias_hidden=shaped((1, hidden), F32),
            grad_up=shaped((parts, width // parts, hidden), BF16),
            **(dict(down_mine=shaped((r, hidden), F32)) if own else dict(grad_down=shaped((1, width, hidden), BF16))),
        ),
        dict(
            upper=vm((group, hidden), BF16), sum=sum_scratch, spread=RowSpread.scratch(), **down_scratch,
            **(dict(grad_down=vm((dp, r, hidden), BF16), down_bufs=GradScatter.buffers((r, hidden)), down_sems=GradScatter.scratch()) if own else {}),
        ),
        hbm=("down_a", "down_b"),
        late=("grad_all", "active", "slope", "up", "fourth_all", "third_sum", "grad_final"),
        early=("grad_up",),
    )
    bias_cross_out, gain_fourth, offset_fourth = back.sum0, back.sum1, back.sum2

    few_rows = 2 * r + 2 * text_share if own else 2 * width + 2 * text_width
    cback = named_kernel(
        "cross_back", 4, functools.partial(cross_back_body, dp, own, size, scale, heads, block, text_len),
        dict(
            c_all=back.c_all, cross_out=cross_out_t, pre=cross.pre, low=cross.low, text_pre=cross.text_pre,
            text_low=cross.text_low, lse=cross.lse, cosine=first.cosine, sine=first.sine, head_gain=first.gain_wide, mask=mask, fold=fold,
            mixed=cross.mixed, third_all=first.third_all, text=text, keyval_wide=cross.keyval_wide,
            query_wide=cross.query_wide, second=first.second, gain=norm_gain[2:3], grad_third=back.grad_third,
            **(dict(grad_up=back.grad_up) if own else {}),
        ),
        dict(
            grads=shaped((parts, few_rows, cols), BF16), grad_text=shaped((text_pad, text_width), BF16),
            gains=shaped((2, LANES), F32), offsets=shaped((2, LANES), F32), sums=shaped((1, span), F32),
            text_sums=shaped((1, span), F32), s_all=full, grad_second=mine, sum0=line_sum, sum1=line_sum, sum2=line_sum,
            **(dict(up_mine=shaped((r, hidden), F32)) if own else {}),
        ),
        dict(
            p=vm((group, span), BF16), do=vm((group, span), BF16), dq=vm((group, span), F32), dk=vm((text_pad, span), F32),
            dv=vm((text_pad, span), F32), text_p=vm((text_pad, 2 * span), BF16), sum=sum_scratch, spread=RowSpread.scratch(),
            **(dict(up_bufs=GradScatter.buffers((r, hidden)), up_sems=GradScatter.scratch()) if own else {}),
        ),
        hbm=("grad_up",),
        late=("c_all", "cross_out", "low", "text_low", "pre", "cosine", "sine", "query_wide", "text_pre", "mixed", "third_all",
              "text", "keyval_wide", "second", "grad_third"),
        early=("grads",),
    )
    few_grads = cback.grads
    if not own:
        cuts = np.cumsum([0, width, width, text_width, text_width])
        few_grads = jnp.concatenate(
            [few_grads[0, a:b].reshape(dp, -1, cols) for a, b in zip(cuts[:-1], cuts[1:])], axis=1
        )
        few_mine = lax.psum_scatter(few_grads.reshape(-1, cols), "dp", scatter_dimension=0, tiled=True).astype(F32)
        down_mine = lax.psum_scatter(back.grad_down[0], "dp", scatter_dimension=0, tiled=True).astype(F32)
        up_mine = lax.psum_scatter(back.grad_up[0], "dp", scatter_dimension=0, tiled=True).astype(F32)
    else:
        down_mine, up_mine = back.down_mine, cback.up_mine

    sback = named_kernel(
        "self_back", 6, functools.partial(self_back_body, dp, own, size, scale, heads, block),
        dict(
            text_part=cback.grad_text, **(dict(few_grads=few_grads) if own else {}),
            s_all=cback.s_all, out_t=out_t, pre=first.pre, low=first.low, lse=first.lse, cosine=first.cosine, sine=first.sine,
            head_gain=first.gain_wide, mask=mask, fold=fold, mixed=first.mixed, first_all=first.first_all,
        ),
        dict(
            p=shaped((group, 3 * span), BF16), grad_out=shaped((parts, width // parts, cols), BF16),
            grad_project=shaped((parts, 3, width // parts, cols), BF16), gains=shaped((2, LANES), F32),
            offsets=shaped((2, LANES), F32), sums=shaped((1, 3 * span), F32), grad_text=shaped((text_pad, text_width), F32),
            **(dict(few_mine=shaped((few_rows, cols), F32)) if own else {}),
        ),
        dict(
            do=vm((group, span), BF16), dq=vm((group, span), F32), dk=vm((group, span), F32), dv=vm((group, span), F32),
            p_low=vm((3, group, cols), BF16), text_total=vm((text_pad, text_width), BF16),
            text_land=vm((text_pad, text_width), BF16), text_yland=vm((piece_rows(text_pad, 2, 1), text_width), BF16),
            text_back=vm((piece_rows(text_pad, 2, 1), text_width), BF16),
            text_sems=dma((6,)),
            **(dict(few_bufs=GradScatter.buffers((few_rows, cols)), few_sems=GradScatter.scratch()) if own else {}),
        ),
        hbm=("few_grads",),
        late=("s_all", "out_t", "low", "pre", "cosine", "sine", "mixed", "first_all"),
        early=("p", "grad_out", "grad_project"),
    )
    if own:
        few_mine = sback.few_mine

    skip_rows = 2 * width // dp if own else width
    pack_land = vm((4, PACK_ROWS, width), F32)
    last = named_kernel(
        "last", 5, functools.partial(last_body, dp, own),
        dict(
            p=sback.p, project_wide=first.project_wide, residual=first.residual, grad_second=cback.grad_second,
            skipped=first.skipped, norm_gain=norm_gain, skip_w=skip_full, joined0=first.joined0, joined1=first.joined1,
            silu=silu, gain_third=cback.sum1, gain_fourth=gain_fourth, offset_third=cback.sum2, offset_fourth=offset_fourth,
            bias_attn=cback.sum0, bias_cross_out=bias_cross_out, bias_mlp=feed.bias_mlp, self_gains=sback.gains,
            cross_gains=cback.gains, self_offsets=sback.offsets, cross_offsets=cback.offsets, self_sums=sback.sums,
            cross_sums=cback.sums, text_sums=cback.text_sums, bias_hidden=back.bias_hidden, unfold=jnp.asarray(fold_np.T),
            grad_out=sback.grad_out, grad_project=sback.grad_project,
        ),
        dict(
            grad_latent=mine, grad_skip=mine, shift_grad=shaped((r if own else 1, width), F32), shift_bias=line_sum,
            pack_out=shaped((4, PACK_ROWS, width), F32),
            **(dict(out_mine=shaped((r, cols), F32), project_mine=shaped((3, r, cols), F32), skip_mine=shaped((skip_rows, cols), F32))
               if own else dict(grad_skip_w=shaped((2, width, cols), BF16))),
        ),
        dict(
            ksend=vm((4, rows, cols), BF16), krecv=vm((4, rows, cols), BF16), tile=vm((1, width), F32),
            tile_land=vm((4, 1, width), F32), low_out=vm((1, width), F32),
            low_land=vm((dp if own else 1, 1, width), F32), pack=vm((4, PACK_ROWS, width), F32), pack_in_land=pack_land,
            pack_mine=vm((PACK_ROWS, width), F32), pack_x=vm((PACK_ROWS, width), F32), pack_z=pack_land, pack_t=pack_land, sum=sum_scratch, sum1=sum_scratch,
            k_s=dma((4,)), k_r=dma((4,)), t_s=dma((4,)), t_r=dma((4,)), l_s=dma((dp,)), l_r=dma((dp,)), px_s=dma((1,)),
            px_r=dma((1,)), ps_s=dma((4,)), ps_r=dma((4,)), pz_s=dma((line,)), pz_r=dma((line,)), pt_s=dma((4,)), pt_r=dma((4,)),
            **(dict(
                grad_skip_w=vm((dp, skip_rows, cols), BF16), out_bufs=GradScatter.buffers((r, cols)),
                project_bufs=GradScatter.buffers((r, cols)) * 3, skip_bufs=GradScatter.buffers((skip_rows, cols)),
                scatter_sems=GradScatter.scratch() * 5,
            ) if own else {}),
        ),
        hbm=("grad_out", "grad_project"),
        late=("p", "project_wide", "residual", "grad_second", "skipped", "skip_w", "joined0", "joined1"),
        early=("grad_latent", "grad_skip"),
    )
    if own:
        out_mine, project_mine, skip_mine = last.out_mine, last.project_mine, last.skip_mine
        shift_grad, shift_bias, pack_sum = last.shift_grad, last.shift_bias, last.pack_out
    else:
        shift_all = lax.all_gather(last.shift_grad[:1], "dp", axis=0, tiled=True)
        shift_bias = jnp.sum(shift_all, axis=0, keepdims=True)
        shift_grad = dot_tn(silu, shift_all.astype(BF16))
        pack_sum = lax.psum(last.pack_out, "dp")
        out_mine = lax.psum_scatter(sback.grad_out[0], "dp", scatter_dimension=0, tiled=True).astype(F32)
        project_mine = lax.psum_scatter(sback.grad_project[0], "dp", scatter_dimension=1, tiled=True).astype(F32)
        skip_mine = lax.psum_scatter(last.grad_skip_w.reshape(-1, cols), "dp", scatter_dimension=0, tiled=True).astype(F32)
    end = named_kernel(
        "finish", None, functools.partial(finish_body, cols, hidden),
        dict(
            pack=pack_sum, shift_bias=shift_bias, unfold=jnp.asarray(one_np.T), block_out=feed.block_out,
            grad_latent=last.grad_latent, grad_skip=last.grad_skip, skip_mine=skip_mine, shift_grad=shift_grad,
            up_mine=up_mine, query_mine=few_mine[r : 2 * r] if not own else few_mine, text_part=sback.grad_text,
        ),
        dict(
            norm_gain=shaped(norm_gain.shape, F32), norm_bias=shaped(norm_bias.shape, F32), head_gain=shaped(head_gain.shape, F32),
            head_bias=shaped(head_bias.shape, F32), column_bias=shaped(column_bias.shape, F32), hidden_bias=shaped((1, 4 * hidden), F32),
            row_bias=shaped(row_bias.shape, F32), o_block=mine_low, o_latent=mine, o_skip=mine, o_skip_mine=shaped(skip_mine.shape, F32),
            o_shift=shaped(shift_grad.shape, F32), o_up=shaped(up_mine.shape, F32), o_query=shaped((r, cols), F32),
            o_text=shaped((text_len, text_width), F32),
        ),
        {},
    )
    return (
        end.o_block,
        end.o_latent,
        end.o_skip,
        end.o_text[None],
        end.o_skip_mine,
        end.o_shift,
        jnp.transpose(project_mine, (1, 0, 2)),
        out_mine.T,
        end.o_query,
        jnp.transpose(few_mine[2 * r :].reshape(2, text_share, cols), (1, 0, 2)),
        few_mine[:r].T,
        end.o_up,
        down_mine.T,
        end.norm_gain,
        end.norm_bias,
        end.head_gain,
        end.head_bias,
        end.column_bias,
        end.hidden_bias[0],
        end.row_bias,
    )


def solution(mesh):
    both = ("dp", "tensor")
    rows2, split2, cross2 = P(both, None), P("dp", "tensor"), P("tensor", "dp")
    middle = P("dp", None, "tensor")
    return jax.shard_map(
        body,
        mesh=mesh,
        in_specs=(
            rows2, rows2, P("dp", None, None), P("dp", None), rows2, P(both), P("dp"), P(None, "dp"),
            split2, P("dp", None), middle, cross2, split2, middle, cross2, split2, cross2,
            P(), P(), P(), P(), P(), P(), P(),
        ),
        out_specs=(
            rows2, rows2, rows2, P("dp", None, None),
            split2, P("dp", None), middle, cross2, split2, middle, cross2, split2, cross2,
            P(), P(), P(), P(), P(), P(), P(),
        ),
        check_vma=False,
    )
```

```python
import functools
from types import SimpleNamespace

import jax
import jax.numpy as jnp
import numpy as np
from jax import lax
from jax.experimental import pallas as pl
from jax.experimental.pallas import tpu as pltpu
from jax.sharding import PartitionSpec as P

EPSILON = 1e-06
MESH = pl.DeviceIdType.MESH
BF16, F32 = jnp.bfloat16, jnp.float32
LANES = 128
CHUNKS = 2
VMEM_BYTES = 60 * 2**20
NEGATIVE = -1e30


def dot_nn(left, right):
    return jnp.dot(left, right, preferred_element_type=F32)


def dot_nt(left, right):
    return lax.dot_general(left, right, (((1,), (1,)), ((), ())), preferred_element_type=F32)


def dot_tn(left, right):
    return lax.dot_general(left, right, (((0,), (0,)), ((), ())), preferred_element_type=F32)


def centre(x):
    cen = x - jnp.mean(x, axis=-1, keepdims=True)
    spread = jnp.mean(cen * cen, axis=-1, keepdims=True)
    return cen, lax.rsqrt(spread + EPSILON)


def norm_back(total, x, gain):
    cen, rstd = centre(x)
    xhat = cen * rstd
    dg = total * gain
    back = rstd * (
        dg - jnp.mean(dg, axis=-1, keepdims=True) - xhat * jnp.mean(dg * xhat, axis=-1, keepdims=True)
    )
    return back, xhat


def remote(src, dst, send_sem, recv_sem, device):
    return pltpu.make_async_remote_copy(
        src_ref=src, dst_ref=dst, send_sem=send_sem, recv_sem=recv_sem, device_id=device, device_id_type=MESH
    )


def tensor_place():
    d, t = lax.axis_index("dp"), lax.axis_index("tensor")
    y, c = t // 2, t % 2
    return d, t, y, c, (d, 2 * y + 1 - c), (d, 2 * (1 - y) + c)


def greet(peers):
    bar = pltpu.get_barrier_semaphore()
    for peer in peers:
        pl.semaphore_signal(bar, inc=1, device_id=peer, device_id_type=MESH)
    return bar


class DpPlace:
    def __init__(self, dp):
        self.d, self.t = lax.axis_index("dp"), lax.axis_index("tensor")
        self.dp, self.line = dp, dp // 2
        self.zi, self.par = self.d // 2, self.d % 2
        self.pair = (2 * self.zi + 1 - self.par, self.t)
        self.e0, self.e3 = (3 - self.zi) // 3, self.zi // 3
        self.end = self.e0 + self.e3

    def at(self, zi):
        return 2 * zi + self.par

    def ahead(self, j):
        return 2 * ((self.zi + j) % self.line) + self.par

    def behind(self, j):
        return 2 * ((self.zi + self.line - j) % self.line) + self.par

    def near(self):
        return [self.pair] + [(self.ahead(j), self.t) for j in range(1, self.line)]

    def others(self):
        return [((self.d + j) % self.dp, self.t) for j in range(1, self.dp)]


class ToAll:
    def __init__(self, place, source, land, send_sem, recv_sem):
        self.copies = []
        for j in range(1, place.dp):
            q = (place.d + j) % place.dp
            cp = remote(source(q), land.at[place.d], send_sem.at[j], recv_sem.at[j], (q, place.t))
            cp.start()
            self.copies.append(cp)

    def arrived(self):
        for cp in self.copies:
            cp.wait_recv()

    def sent(self):
        for cp in self.copies:
            cp.wait_send()


class Gathers:
    def __init__(self, place, ahead, z_s, z_r, x_s, x_r):
        self.place, self.ahead, self.sems = place, ahead, (z_s, z_r, x_s, x_r)
        self.pieces, self.z, self.x, self.passed = [], [], [], 0

    def add(self, shard, land, pieces=1):
        start = 0
        for i in range(pieces):
            if pieces == 1:
                self.pieces.append((shard, land))
            else:
                count = piece_rows(shard.shape[0], pieces, i)
                self.pieces.append((shard.at[pl.ds(start, count)], land.at[:, pl.ds(start, count)]))
                start += count
        self.fill()

    def fill(self):
        place = self.place
        while len(self.z) < min(len(self.pieces), self.passed + self.ahead):
            k = len(self.z)
            shard, land = self.pieces[k]
            z_s, z_r, x_s, x_r = [v.at[k] for v in self.sems]
            self.z.append([
                remote(shard, land.at[place.d], z_s.at[j], z_r.at[j], (place.ahead(j), place.t)) for j in range(1, place.line)
            ])
            self.x.append([remote(shard, land.at[place.d], x_s.at[0], x_r.at[0], place.pair)])
            for cp in self.z[k] + self.x[k]:
                cp.start()

    def forward(self, count=1):
        for _ in range(count):
            k = self.passed
            _, land = self.pieces[k]
            _, _, x_s, x_r = [v.at[k] for v in self.sems]
            for j in range(1, self.place.line):
                self.z[k][j - 1].wait_recv()
                here = land.at[self.place.behind(j)]
                cp = remote(here, here, x_s.at[j], x_r.at[j], self.place.pair)
                cp.start()
                self.x[k].append(cp)
            self.passed += 1
            self.fill()

    def arrived(self, first, last):
        for cps in self.x[first:last]:
            for cp in cps:
                cp.wait_recv()

    def sent(self):
        for cps in self.z + self.x:
            for cp in cps:
                cp.wait_send()

    @staticmethod
    def scratch(count, line):
        return [pltpu.SemaphoreType.DMA((count, line))] * 4


def piece_rows(rows, pieces, i):
    tiles = rows // 16
    return 16 * (tiles * (i + 1) // pieces - tiles * i // pieces)


class GradScatter:
    def __init__(self, place, source, own, xland, zland, own_sem, x_s, x_r, z_s, z_r):
        self.place, self.own, self.xland, self.zland, self.z_s, self.z_r = place, own, xland, zland, z_s, z_r
        self.at, self.x, self.local, self.z = 0, [], [], []
        zi, e0, e3, end = place.zi, place.e0, place.e3, place.end
        self.order = [1 + 2 * e0, 3 - end, 2 - e0 + e3, 0]
        self.owners = [(zi + i) % 4 for i in self.order]
        self.routes = [
            (zi + 1 - 2 * e3, 3 * end, 1 - end),
            (self.owners[1], self.order[1] - 1, self.order[1]),
            (self.owners[2], self.order[2] - 1, self.order[2]),
        ]
        for k, j in enumerate(self.owners):
            cp = remote(source.at[2 * j + 1 - place.par], xland.at[j], x_s.at[k], x_r.at[k], place.pair)
            cp.start()
            self.x.append(cp)
            cp = pltpu.make_async_copy(source.at[2 * j + place.par], own.at[j], own_sem.at[k])
            cp.start()
            self.local.append(cp)

    def arrival(self, slot, sem):
        return remote(self.own.at[0], self.zland.at[slot], self.z_s.at[0], self.z_r.at[sem], self.place.pair)

    def step(self):
        k = self.at
        self.at += 1
        j = self.owners[k]
        self.local[k].wait()
        self.x[k].wait_recv()
        self.own[j] = (self.own[j].astype(F32) + self.xland[j].astype(F32)).astype(BF16)
        if k == 2:

            @pl.when(self.place.end == 0)
            def _():
                self.arrival(3, 0).wait_recv()
                self.own[j] = (self.own[j].astype(F32) + self.zland[3].astype(F32)).astype(BF16)

        to, slot, sem = self.routes[k]
        cp = remote(self.own.at[j], self.zland.at[slot], self.z_s.at[k], self.z_r.at[sem], (self.place.at(to), self.place.t))
        cp.start()
        self.z.append(cp)

    def steps(self, count=3):
        while self.at < min(3, count):
            self.step()

    def result(self):
        zi = self.place.zi
        self.local[3].wait()
        self.x[3].wait_recv()
        for slot in range(3):
            if slot == 1:
                self.arrival(1, 2).wait_recv()
            else:
                absent = 0 if slot == 0 else 3

                @pl.when(zi == absent)
                def _(slot=slot):
                    self.zland[slot] = jnp.zeros(self.zland.shape[1:], BF16)

                pl.when(zi != absent)(self.arrival(slot, slot + 1).wait_recv)
        total = self.own[zi].astype(F32) + self.xland[zi].astype(F32)
        for slot in range(3):
            total = total + self.zland[slot].astype(F32)
        return total

    def sent(self):
        for cp in self.x + self.z:
            cp.wait_send()

    @staticmethod
    def buffers(shape):
        return [pltpu.VMEM((4,) + shape, BF16)] * 3

    @staticmethod
    def scratch():
        return [pltpu.SemaphoreType.DMA((4,))] * 5


class TensorSum:
    def __init__(self, near, far, csend, crecv, ysend, yrecv, cs, cr, ys, yr):
        self.near, self.far, self.csend, self.crecv, self.ysend, self.yrecv = near, far, csend, crecv, ysend, yrecv
        self.cs, self.cr, self.ys, self.yr = cs, cr, ys, yr
        _, self.t, self.y, self.c, self.sib, self.yp = tensor_place()

    def core(self, i, value, k=0):
        sl = pl.ds(k * value.shape[0], value.shape[0])
        self.csend[i, sl, :] = value.astype(BF16)
        at = CHUNKS * i + k
        cp = remote(self.csend.at[i, sl], self.crecv.at[i, sl], self.cs.at[at], self.cr.at[at], self.sib)
        cp.start()
        return cp

    def start(self, product, ready=None, long=False):
        there, here = 2 * (1 - self.y), 2 * self.y
        rows = self.far.shape[0]
        ch = rows // CHUNKS
        part = lambda b, k: product(pl.ds(pl.multiple_of(b * rows + k * ch, ch), ch))
        self.ycs, self.c0 = [], []
        if long:
            for k in range(CHUNKS):
                sl = pl.ds(k * ch, ch)
                value = part(there + 1 - self.c, k)
                if ready is not None and k == 0:
                    ready()
                self.c0.append(self.core(0, value, k))
                self.far[sl, :] = part(there + self.c, k)
                self.along(k)
            self.c1 = self.core(1, product(block_rows(here + 1 - self.c, rows)))
        else:
            value = product(block_rows(there + 1 - self.c, rows))
            if ready is not None:
                ready()
            for k in range(CHUNKS):
                self.c0.append(self.core(0, value[k * ch : (k + 1) * ch, :], k))
            self.far[...] = product(block_rows(there + self.c, rows))
            self.c1 = self.core(1, product(block_rows(here + 1 - self.c, rows)))
            for k in range(CHUNKS):
                self.along(k)
        self.near[...] = product(block_rows(here + self.c, rows))
        self.c1.wait_recv()

    def along(self, k):
        ch = self.far.shape[0] // CHUNKS
        sl = pl.ds(k * ch, ch)
        self.c0[k].wait_recv()
        self.ysend[sl, :] = (self.far[sl, :] + self.crecv[0, sl, :].astype(F32)).astype(BF16)
        cp = remote(self.ysend.at[sl], self.yrecv.at[sl], self.ys.at[k], self.yr.at[k], self.yp)
        cp.start()
        self.ycs.append(cp)

    def chunk(self, k):
        ch = self.far.shape[0] // CHUNKS
        sl = pl.ds(k * ch, ch)
        self.ycs[k].wait_recv()
        return sl, self.near[sl, :] + self.crecv[1, sl, :].astype(F32) + self.yrecv[sl, :].astype(F32)

    def sent(self):
        for cp in self.c0 + [self.c1] + self.ycs:
            cp.wait_send()

    @staticmethod
    def scratch(rows, width):
        dma = pltpu.SemaphoreType.DMA
        vm = pltpu.VMEM
        return [
            vm((rows, width), F32), vm((rows, width), F32), vm((2, rows, width), BF16), vm((2, rows, width), BF16),
            vm((rows, width), BF16), vm((rows, width), BF16), dma((CHUNKS + 1,)), dma((CHUNKS + 1,)), dma((CHUNKS,)), dma((CHUNKS,)),
        ]


class RowSpread:
    def __init__(self, spread, rows, ys, yr, cs, cr, fs, fr):
        self.spread, self.rows = spread, rows
        self.sems = (ys, yr, cs, cr, fs, fr)
        _, self.t, self.y, self.c, self.sib, self.yp = tensor_place()
        self.parts, self.passed = [], []

    def at(self, owner, start, count):
        return self.spread.at[pl.ds(pl.multiple_of(owner * self.rows + start, 16), count)]

    def send(self, start, count):
        ys, yr, cs, cr, _, _ = self.sems
        k = len(self.parts)
        here = self.at(self.t, start, count)
        a = remote(here, here, ys.at[k], yr.at[k], self.yp)
        b = remote(here, here, cs.at[k], cr.at[k], self.sib)
        a.start()
        b.start()
        self.parts.append((a, b, start, count))

    def forward(self):
        fs, fr = self.sems[4:]
        for k, (a, _, start, count) in enumerate(self.parts):
            a.wait_recv()
            there = self.at(2 * (1 - self.y) + self.c, start, count)
            cp = remote(there, there, fs.at[k], fr.at[k], self.sib)
            cp.start()
            self.passed.append(cp)

    def finish(self):
        for (a, b, _, _), cp in zip(self.parts, self.passed):
            b.wait_recv()
            cp.wait_recv()
            a.wait_send()
            b.wait_send()
            cp.wait_send()

    @staticmethod
    def scratch(parts=CHUNKS):
        return [pltpu.SemaphoreType.DMA((parts,))] * 6


def shaped(shape, dtype):
    return jax.ShapeDtypeStruct(shape, dtype)


class Placed:
    def __init__(self, value, moves):
        self.value, self.moves = value, moves


def hbm(value):
    return Placed(value, False)


def late(value):
    return Placed(value, True)


def named_kernel(name, collective_id, body, ins, outs, scratch):
    vm, anywhere = pl.BlockSpec(memory_space=pltpu.VMEM), pl.BlockSpec(memory_space=pl.ANY)
    flat = []
    for v in scratch.values():
        flat.extend(v if isinstance(v, list) else [v])
    placed = {k: v for k, v in [*ins.items(), *outs.items()] if isinstance(v, Placed)}
    bare = lambda v: v.value if isinstance(v, Placed) else v
    specs = lambda group: [anywhere if k in placed else vm for k in group]
    moving = [k for k, v in placed.items() if v.moves]
    buffers = [pltpu.VMEM(placed[k].value.shape, placed[k].value.dtype) for k in moving]
    if moving:
        buffers.append(pltpu.SemaphoreType.DMA((len(moving),)))

    def kernel(*refs):
        left = list(refs)
        n = SimpleNamespace()
        for k in [*ins, *outs]:
            setattr(n, k, left.pop(0))
        for k, v in scratch.items():
            if isinstance(v, list):
                setattr(n, k, [left.pop(0) for _ in v])
            else:
                setattr(n, k, left.pop(0))
        loads, stores, going = {}, {}, []
        for i, k in enumerate(moving):
            outer, inner, sem = getattr(n, k), left[i], left[-1].at[i]
            if k in ins:
                loads[id(inner)] = pltpu.make_async_copy(outer, inner, sem)
                loads[id(inner)].start()
            else:
                stores[id(inner)] = pltpu.make_async_copy(inner, outer, sem)
            setattr(n, k, inner)

        def need(*wanted):
            for ref in wanted:
                if id(ref) in loads:
                    loads.pop(id(ref)).wait()

        def done(*ready):
            for ref in ready:
                if id(ref) in stores:
                    going.append(stores.pop(id(ref)))
                    going[-1].start()

        n.need, n.done = need, done
        body(n)
        for cp in loads.values():
            cp.wait()
        for cp in stores.values():
            cp.start()
        for cp in going + list(stores.values()):
            cp.wait()

    talks = {} if collective_id is None else dict(collective_id=collective_id, has_side_effects=True)
    got = pl.pallas_call(
        kernel,
        out_shape=[bare(v) for v in outs.values()],
        in_specs=specs(ins),
        out_specs=specs(outs),
        scratch_shapes=flat + buffers,
        compiler_params=pltpu.CompilerParams(vmem_limit_bytes=VMEM_BYTES, **talks),
        name=name,
    )(*[bare(v) for v in ins.values()])
    return SimpleNamespace(**dict(zip(outs, got)))


def block_rows(b, rows):
    return pl.ds(pl.multiple_of(b * rows, rows), rows)


def add_sums(sums, parts):
    parts = [jnp.sum(v, axis=0, keepdims=True) for v in parts]
    return parts if sums is None else [a + b for a, b in zip(sums, parts)]


def forward_rows(reduce, spread, spread_ref, resid, bias, gain, offset, out, rows):
    ch = rows // CHUNKS
    for k in range(CHUNKS):
        sl, total = reduce.chunk(k)
        value = resid[sl, :] + (total + bias[...])
        out[sl, :] = value
        cen, rstd = centre(value)
        low = (cen * rstd * gain[...] + offset[...]).astype(BF16)
        spread_ref[pl.ds(pl.multiple_of(reduce.t * rows + k * ch, ch), ch), :] = low
        spread.send(k * ch, ch)


def backward_rows(reduce, spread, spread_ref, x, gain, before, out, sum_refs, rows):
    ch = rows // CHUNKS
    sums = None
    for k in range(CHUNKS):
        sl, total = reduce.chunk(k)
        back, xhat = norm_back(total, x[sl, :], gain[...])
        grad = before[sl, :] + back
        out[sl, :] = grad
        low = grad.astype(BF16)
        spread_ref[pl.ds(pl.multiple_of(reduce.t * rows + k * ch, ch), ch), :] = low
        spread.send(k * ch, ch)
        sums = add_sums(sums, [low.astype(F32), total * xhat, total])
    for ref, v in zip(sum_refs, sums):
        ref[...] = v


def head_stats(u, mask, size):
    mean = jnp.sum(u, axis=-1, keepdims=True) * (1.0 / size)
    cen = (u - mean) * mask
    spread = jnp.sum(cen * cen, axis=-1, keepdims=True) * (1.0 / size)
    return cen, lax.rsqrt(spread + EPSILON)


def head_norm(u, mask, gain, offset, size):
    cen, rstd = head_stats(u, mask, size)
    return cen * rstd * gain + offset


def turn(u, cosine, sine):
    return u * cosine + pltpu.roll(u, LANES // 2, 1) * sine


def turn_back(u, cosine, sine):
    return u * cosine - pltpu.roll(u, LANES // 2, 1) * sine


def head_back(grad, u, mask, gain, size):
    cen, rstd = head_stats(u, mask, size)
    xhat = cen * rstd
    dg = grad * gain
    mean = jnp.sum(dg, axis=-1, keepdims=True) * (1.0 / size)
    inner = jnp.sum(dg * xhat, axis=-1, keepdims=True) * (1.0 / size)
    back = rstd * ((dg - mean) * mask - xhat * inner)
    return back, jnp.sum(grad * xhat, axis=0, keepdims=True), jnp.sum(grad, axis=0, keepdims=True)


def head_at(h):
    return pl.ds(h * LANES, LANES)


def in_halves(count, step, between):
    if between is None:
        lax.fori_loop(0, count, step, 0)
    else:
        for i in range(2):
            lax.fori_loop(i * count // 2, (i + 1) * count // 2, step, 0)
            between()


def attend(q_ref, k_ref, v_ref, out_ref, lse_ref, heads, scale, block, real_keys, between=None):
    queries, keys = q_ref.shape[0], k_ref.shape[0]

    def step(i, _):
        here = pl.ds(pl.multiple_of(i * block, block), block)
        for h in range(heads):
            hs = head_at(h)
            scores = dot_nt(k_ref[:, hs], q_ref[here, hs]) * scale
            if real_keys < keys:
                place = lax.broadcasted_iota(jnp.int32, scores.shape, 0)
                scores = jnp.where(place < real_keys, scores, NEGATIVE)
            highest = jnp.max(scores, axis=0, keepdims=True)
            exponent = jnp.exp(scores - highest)
            denominator = jnp.sum(exponent, axis=0, keepdims=True)
            probs = (exponent * (1.0 / denominator)).astype(BF16)
            mixed = dot_tn(v_ref[:, hs], probs)
            out_ref[here, hs] = mixed.T.astype(BF16)
            lse_ref[i, pl.ds(h, 1), :] = highest + jnp.log(denominator)
        return 0

    in_halves(queries // block, step, between)


def attend_back(q_ref, k_ref, v_ref, do_ref, lse_ref, dq_ref, dk_ref, dv_ref, heads, scale, block, real_keys, between=None):
    queries, keys = q_ref.shape[0], k_ref.shape[0]
    dk_ref[...] = jnp.zeros(dk_ref.shape, F32)
    dv_ref[...] = jnp.zeros(dv_ref.shape, F32)

    def step(i, _):
        here = pl.ds(pl.multiple_of(i * block, block), block)
        for h in range(heads):
            hs = head_at(h)
            q, k, v, do = q_ref[here, hs], k_ref[:, hs], v_ref[:, hs], do_ref[here, hs]
            scores = dot_nt(k, q) * scale
            if real_keys < keys:
                place = lax.broadcasted_iota(jnp.int32, scores.shape, 0)
                scores = jnp.where(place < real_keys, scores, NEGATIVE)
            probs = jnp.exp(scores - lse_ref[i, pl.ds(h, 1), :])
            grad_probs = dot_nt(v, do)
            inner = jnp.sum(probs * grad_probs, axis=0, keepdims=True)
            grad_scores = (probs * (grad_probs - inner)).astype(BF16)
            dv_ref[:, hs] += dot_nn(probs.astype(BF16), do)
            dk_ref[:, hs] += dot_nn(grad_scores, q) * scale
            dq_ref[here, hs] = dot_tn(k, grad_scores).T * scale
        return 0

    in_halves(queries // block, step, between)


def exact(left, right):
    return jnp.dot(left, right, precision=lax.Precision.HIGHEST, preferred_element_type=F32)


def my_cols(whole, t, cols):
    return sum(jnp.where(t == s, whole[:, s * cols : (s + 1) * cols], 0.0) for s in range(4))


def prepare(t, cols, n):
    n.gain_wide[...] = exact(n.head_gain[...], n.one[...])
    n.offset_wide[...] = exact(n.head_bias[...], n.one[...])
    mine = my_cols(n.column_bias[...], t, cols)
    n.bias_wide[...] = exact(mine, n.fold_f32[...])
    angles = lax.dot_general(
        n.positions[...].astype(F32), n.lanes[0:2, :], (((0,), (0,)), ((), ())), precision=lax.Precision.HIGHEST,
        preferred_element_type=F32,
    )
    n.cosine[...] = jnp.cos(angles) * n.mask[...]
    n.sine[...] = jnp.sin(angles) * n.lanes[2:3, :]
    n.done(n.cosine, n.sine)
    return mine[4:5, :]


def first_body(dp, own, size, scale, heads, block, n):
    _, t, _, _, _, _ = tensor_place()
    d = lax.axis_index("dp")
    rows, width = n.residual.shape
    cols = n.skip_send.shape[2]
    span = heads * LANES
    place = DpPlace(dp) if own else None
    peers = [(d, (t + o) % 4) for o in range(1, 4)] + (place.others() if own else [])
    bar = greet(peers)
    mine = block_rows(t, rows)
    kept = [
        pltpu.make_async_copy(n.latent, n.joined0.at[mine], n.own_sem.at[0]),
        pltpu.make_async_copy(n.skip_states, n.joined1.at[mine], n.own_sem.at[1]),
    ]
    if own:
        shards = [(n.skip_in, n.skip_full), (n.project_in, n.p_land), (n.out_in, n.out_land), (n.query_in, n.query_g),
                  (n.keyval_in.at[0], n.key_g), (n.keyval_in.at[1], n.value_g), (n.cross_out_in, n.cross_out_g),
                  (n.down_in.at[pl.ds(0, n.down_g.shape[1])], n.down_g)]
        kept += [pltpu.make_async_copy(a, b.at[d], n.own_sem.at[2 + i]) for i, (a, b) in enumerate(shards)]
    for cp in kept:
        cp.start()
    pl.semaphore_wait(bar, len(peers))
    spreads = [RowSpread(n.joined0, rows, *n.spread0), RowSpread(n.joined1, rows, *n.spread1)]
    for cp, spread in zip(kept, spreads):
        cp.wait()
        spread.send(0, rows)
    if own:
        count = jnp.broadcast_to(n.true_count[...].astype(F32), (1, LANES))
        share = n.shift_in.shape[0]
        for q in range(dp):
            n.small[q, :, pl.ds(0, share)] = n.condition[:, pl.ds(q * share, share)].astype(F32)
            n.small[q, :, pl.ds(n.small.shape[2] - LANES, LANES)] = count
        n.small_land[d] = n.small[d]
        smalls = ToAll(place, lambda q: n.small.at[q], n.small_land, n.a_s, n.a_r)
        gathers = Gathers(place, 2, *n.gather_sems)
        gathers.add(n.skip_in, n.skip_full, 2)
        smalls.arrived()
        given = jnp.concatenate([n.small_land[i] for i in range(dp)], axis=0)
        n.silu[...] = jax.nn.silu(given[:, : n.shift_in.shape[0]]).astype(BF16)
        n.counted[...] = jnp.sum(given[:, given.shape[1] - LANES :], axis=0, keepdims=True)
        part = dot_nn(n.silu[...], n.shift_in[...])
        for i in range(dp):
            n.shift_part[i] = part[i : i + 1, :]
        n.shift_land[d] = n.shift_part[d]
        shifts = ToAll(place, lambda q: n.shift_part.at[q], n.shift_land, n.b_s, n.b_r)
        for i in range(3):
            gathers.add(n.project_in.at[i], n.p_land.at[:, i])
    bias_skip = prepare(t, cols, n)
    if own:
        gathers.forward()
    spreads[0].forward()
    if own:
        gathers.add(n.out_in, n.out_land)
        gathers.add(n.query_in, n.query_g)
        gathers.add(n.keyval_in.at[0], n.key_g)
        gathers.add(n.keyval_in.at[1], n.value_g)
        gathers.add(n.cross_out_in, n.cross_out_g)
        gathers.forward()
    spreads[0].finish()
    if own:
        gathers.add(n.down_in.at[pl.ds(0, n.down_g.shape[1])], n.down_g, 3)
        gathers.arrived(0, 2)
        kept[2].wait()
        half = dp // 2
        skip_half = lambda i: n.skip_full[pl.ds(i * half, half)].reshape(width, cols)
    else:
        skip_half = lambda i: n.skip_in[pl.ds(i * width, width), :]
    for b in range(4):
        here = pl.ds(b * rows, rows)
        n.pre[here, pl.ds(0, cols)] = dot_nn(n.joined0[here, :], skip_half(0))
    spreads[1].forward()
    if own:
        gathers.forward()
    spreads[1].finish()
    copies = []
    for o in (2, 3, 1, 0):
        b = (t + o) % 4
        here = block_rows(b, rows)
        value = (n.pre[here, pl.ds(0, cols)] + dot_nn(n.joined1[here, :], skip_half(1)) + bias_skip).astype(BF16)
        if o:
            n.skip_send[o] = value
            cp = remote(n.skip_send.at[o], n.skip_recv.at[t], n.p_s.at[o], n.p_r.at[o], (d, b))
            cp.start()
            copies.append(cp)
        else:
            n.skip_recv[t] = value
    if own:
        shifts.arrived()
        shift = n.row_bias[pl.ds(3, 1), :] + sum(n.shift_land[i] for i in range(dp))
    else:
        shift = n.shift_in[...]
    for cp in copies:
        cp.wait_recv()
    for s in range(4):
        n.skipped[:, s * cols : (s + 1) * cols] = n.skip_recv[s]
    spread = RowSpread(n.first_all, rows, *n.spread2)
    ch = rows // CHUNKS
    for k in range(CHUNKS):
        sl = pl.ds(k * ch, ch)
        cen, rstd = centre(n.skipped[sl, :].astype(F32))
        resid = cen * rstd * n.norm_gain[pl.ds(0, 1), :] + n.norm_bias[pl.ds(0, 1), :]
        n.residual[sl, :] = resid
        cen, rstd = centre(resid)
        first = cen * rstd * n.norm_gain[pl.ds(1, 1), :] + n.norm_bias[pl.ds(1, 1), :] + shift
        n.first_all[pl.ds(pl.multiple_of(t * rows + k * ch, ch), ch), :] = first.astype(BF16)
        spread.send(k * ch, ch)
    if own:
        gathers.forward()
    spread.forward()
    if own:
        gathers.forward()
    spread.finish()
    for cp in copies:
        cp.wait_send()
    n.done(n.joined0, n.joined1, n.skip_full, n.skipped, n.residual, n.first_all)
    for part in range(3):
        if own:
            gathers.arrived(2 + part, 3 + part)
            if part == 0:
                kept[3].wait()
            narrow = n.p_land[:, part].reshape(width, cols)
        else:
            narrow = n.project_in[part]
        n.project_wide[part] = dot_nn(narrow, n.fold[...]).astype(BF16)
    if own:
        gathers.forward()

    def project(i, _):
        here = pl.ds(pl.multiple_of(i * block, block), block)
        for part in range(3):
            out = dot_nn(n.first_all[here, :], n.project_wide[part])
            if part != 1:
                out = out + n.bias_wide[pl.ds(part // 2, 1), :]
            if part < 2:
                n.pre[here, pl.ds(part * span, span)] = out
                for h in range(heads):
                    u = out[:, h * LANES : (h + 1) * LANES]
                    val = head_norm(u, n.mask[...], n.gain_wide[pl.ds(part, 1), :], n.offset_wide[pl.ds(part, 1), :], size)
                    val = turn(val, n.cosine[here, :], n.sine[here, :])
                    n.low[here, pl.ds(part * span + h * LANES, LANES)] = val.astype(BF16)
            else:
                n.low[here, pl.ds(part * span, span)] = out.astype(BF16)
        return 0

    lax.fori_loop(0, n.low.shape[0] // block, project, 0)
    n.done(n.project_wide, n.pre, n.low)
    if own:
        gathers.forward()
    attend(
        n.low.at[:, pl.ds(0, span)], n.low.at[:, pl.ds(span, span)], n.low.at[:, pl.ds(2 * span, span)],
        n.padded, n.lse, heads, scale, block, n.low.shape[0], gathers.forward if own else None,
    )
    n.mixed[...] = dot_nt(n.padded[...], n.fold[...]).astype(BF16)
    n.done(n.mixed)
    if own:
        gathers.arrived(5, 6)
        kept[4].wait()
        out_t = lambda: n.out_land[...].reshape(width, cols)
    else:
        out_t = lambda: n.out_in[...]
    reduce = TensorSum(*n.sum)
    reduce.start(lambda here: dot_nt(n.mixed[here, :], out_t()))
    if own:
        gathers.forward()
    spread = RowSpread(n.third_all, rows, *n.spread3)
    forward_rows(
        reduce, spread, n.third_all, n.residual, n.row_bias.at[pl.ds(0, 1)], n.norm_gain.at[pl.ds(2, 1)],
        n.norm_bias.at[pl.ds(2, 1)], n.second, rows,
    )
    n.done(n.second)
    if own:
        gathers.forward()
    spread.forward()
    if own:
        gathers.forward()
    spread.finish()
    reduce.sent()
    if own:
        gathers.forward()
        gathers.arrived(6, len(gathers.pieces))
        for cp in kept[5:]:
            cp.wait()
        for g in (gathers, smalls, shifts):
            g.sent()


def cross_body(dp, own, size, scale, heads, block, real, n):
    rows, width = n.second.shape
    span = heads * LANES
    d, _, _, _, sib, yp = tensor_place()
    place = DpPlace(dp) if own else None
    peers = [sib, yp] + (place.near() if own else [])
    bar = greet(peers)
    pl.semaphore_wait(bar, len(peers))
    if own:
        gathers = Gathers(place, 2, *n.gather_sems)
        gathers.add(n.up_in, n.up_g, 4)
        down_in = n.down_in.at[pl.ds(n.down_in.shape[0] - n.down_g.shape[1], n.down_g.shape[1])]
        gathers.add(down_in, n.down_g)
        kept = [pltpu.make_async_copy(a, b.at[d], n.own_sem.at[i])
                for i, (a, b) in enumerate(((n.up_in, n.up_g), (down_in, n.down_g)))]
        for cp in kept:
            cp.start()
    n.need(n.query, n.key, n.value, n.text)
    n.query_wide[...] = dot_nn(n.query[...], n.fold[...]).astype(BF16)
    for part, w in enumerate((n.key, n.value)):
        n.keyval_wide[part] = dot_nn(w[...], n.fold[...]).astype(BF16)
        out = dot_nn(n.text[...], n.keyval_wide[part])
        if part == 0:
            n.text_pre[...] = out
            for h in range(heads):
                val = head_norm(out[:, h * LANES : (h + 1) * LANES], n.mask[...], n.head_gain[pl.ds(3, 1), :], n.head_bias[pl.ds(3, 1), :], size)
                n.text_low[:, head_at(h)] = val.astype(BF16)
        else:
            n.text_low[:, pl.ds(span, span)] = (out + n.bias_wide[pl.ds(3, 1), :]).astype(BF16)
    n.need(n.third_all, n.cosine, n.sine)

    def project(i, _):
        here = pl.ds(pl.multiple_of(i * block, block), block)
        out = dot_nn(n.third_all[here, :], n.query_wide[...]) + n.bias_wide[pl.ds(2, 1), :]
        n.pre[here, :] = out
        for h in range(heads):
            val = head_norm(out[:, h * LANES : (h + 1) * LANES], n.mask[...], n.head_gain[pl.ds(2, 1), :], n.head_bias[pl.ds(2, 1), :], size)
            n.low[here, head_at(h)] = turn(val, n.cosine[here, :], n.sine[here, :]).astype(BF16)
        return 0

    lax.fori_loop(0, n.low.shape[0] // block, project, 0)
    n.done(n.query_wide, n.keyval_wide, n.pre, n.low)
    attend(n.low, n.text_low.at[:, pl.ds(0, span)], n.text_low.at[:, pl.ds(span, span)], n.padded, n.lse, heads, scale, block, real)
    n.mixed[...] = dot_nt(n.padded[...], n.fold[...]).astype(BF16)
    n.need(n.cross_out, n.second)
    reduce = TensorSum(*n.sum)
    reduce.start(lambda here: dot_nt(n.mixed[here, :], n.cross_out[...]))
    n.done(n.mixed)
    if own:
        gathers.forward(2)
    spread = RowSpread(n.fourth_all, rows, *n.spread)
    forward_rows(
        reduce, spread, n.fourth_all, n.second, n.row_bias.at[pl.ds(1, 1)], n.norm_gain.at[pl.ds(3, 1)],
        n.norm_bias.at[pl.ds(3, 1)], n.third_sum, rows,
    )
    if own:
        gathers.forward()
    spread.forward()
    if own:
        gathers.forward()
    spread.finish()
    reduce.sent()
    if own:
        gathers.forward()
        gathers.arrived(0, len(gathers.pieces))
        for cp in kept:
            cp.wait()
        gathers.sent()


def load_down(own, n):
    if not own:
        return [], lambda: n.down_t[...]
    first = n.down_a.shape[1]
    copies = [
        pltpu.make_async_copy(n.down_a, n.down_t.at[:, pl.ds(0, first)], n.down_sem.at[0]),
        pltpu.make_async_copy(n.down_b, n.down_t.at[:, pl.ds(first, n.down_b.shape[1])], n.down_sem.at[1]),
    ]
    for cp in copies:
        cp.start()
    return copies, lambda: n.down_t[...].reshape(-1, n.down_t.shape[2])


def feed_body(own, n):
    rows = n.third_sum.shape[0]
    _, t, _, _, sib, yp = tensor_place()
    bar = greet((sib, yp))
    down_copies, down_t = load_down(own, n)
    hidden = n.up.shape[1]
    tiles = hidden // LANES
    mine = sum(jnp.where(t == s, n.hidden_bias[pl.ds(s * tiles, tiles), :], 0.0) for s in range(4))
    hidden_bias = jnp.concatenate([mine[i : i + 1, :] for i in range(tiles)], axis=1)
    seat = t * rows + lax.broadcasted_iota(jnp.int32, (rows, 1), 0)
    mask = lax.dot_general(
        n.loss_mask[...].astype(F32), jnp.ones((1, LANES), F32), (((0,), (0,)), ((), ())), preferred_element_type=F32
    )[:, 0:1]
    weight = mask * (seat < n.true_count[...]).astype(F32)
    weight = (n.total[...] / n.counted[:, 0:1]) * weight
    n.need(n.fourth_all, n.up)
    root, cube = float(np.sqrt(2.0 / np.pi)), 0.044715

    def product(here):
        x = dot_nn(n.fourth_all[here, :], n.up[...]) + hidden_bias
        square = x * x
        th = jnp.tanh(root * (x + cube * (square * x)))
        cdf = 0.5 * (1.0 + th)
        active = (x * cdf).astype(BF16)
        n.active[here, :] = active
        slope = cdf + (0.5 * root) * x * (1.0 - th * th) * (1.0 + (3.0 * cube) * square)
        n.slope[here, :] = slope.astype(BF16)
        while down_copies:
            down_copies.pop().wait()
        return dot_nt(active, down_t())

    reduce = TensorSum(*n.sum)
    reduce.start(product, lambda: pl.semaphore_wait(bar, 2), long=True)
    n.done(n.active, n.slope)
    n.need(n.third_sum, n.teacher)
    spread = RowSpread(n.grad_all, rows, *n.spread)
    ch = rows // CHUNKS
    sums = None
    for k in range(CHUNKS):
        sl, total = reduce.chunk(k)
        final = n.third_sum[sl, :] + (total + n.row_bias[pl.ds(2, 1), :])
        n.block_out[sl, :] = final.astype(BF16)
        grad = weight[k * ch : (k + 1) * ch, :] * (final - n.teacher[sl, :].astype(F32))
        n.grad_final[sl, :] = grad
        low = grad.astype(BF16)
        n.grad_all[pl.ds(pl.multiple_of(t * rows + k * ch, ch), ch), :] = low
        spread.send(k * ch, ch)
        sums = add_sums(sums, [low.astype(F32)])
    n.bias_mlp[...] = sums[0]
    n.done(n.block_out, n.grad_final)
    spread.forward()
    spread.finish()
    reduce.sent()


def feed_back_body(dp, own, n):
    rows = n.third_sum.shape[0]
    _, _, _, _, sib, yp = tensor_place()
    place = DpPlace(dp) if own else None
    peers = [sib, yp] + (place.near() if own else [])
    bar = greet(peers)
    down_copies, down_t = load_down(own, n)
    n.need(n.grad_all, n.active)
    n.grad_down[...] = dot_tn(n.grad_all[...], n.active[...]).astype(BF16).reshape(n.grad_down.shape)
    pl.semaphore_wait(bar, len(peers))
    if own:
        down = GradScatter(place, n.grad_down, *n.down_bufs, *n.down_sems)

    def product(here):
        upper = (dot_nn(n.grad_all[here, :], down_t()) * n.slope[here, :].astype(F32)).astype(BF16)
        n.upper[here, :] = upper
        return dot_nt(upper, n.up[...])

    for cp in down_copies:
        cp.wait()
    n.need(n.slope, n.up)
    reduce = TensorSum(*n.sum)
    reduce.start(product, long=True)
    n.need(n.fourth_all, n.third_sum, n.grad_final)
    n.bias_hidden[...] = sum(
        jnp.sum(n.upper[pl.ds(b * rows, rows), :].astype(F32), axis=0, keepdims=True) for b in range(4)
    )
    n.grad_up[...] = dot_tn(n.fourth_all[...], n.upper[...]).astype(BF16).reshape(n.grad_up.shape)
    n.done(n.grad_up)
    spread = RowSpread(n.c_all, rows, *n.spread)
    if own:
        down.steps(1)
    backward_rows(reduce, spread, n.c_all, n.third_sum, n.norm_gain.at[pl.ds(3, 1)], n.grad_final, n.grad_third, (n.sum0, n.sum1, n.sum2), rows)
    if own:
        down.steps(2)
    spread.forward()
    if own:
        down.steps()
    spread.finish()
    reduce.sent()
    if own:
        n.down_mine[...] = down.result()
        down.sent()


def spread_heads(n, rows_in, w, do, block):
    def spread(i, _):
        here = pl.ds(pl.multiple_of(i * block, block), block)
        narrow = dot_nn(rows_in[here, :], w[...]).astype(BF16)
        do[here, :] = dot_nn(narrow, n.fold[...]).astype(BF16)
        return 0

    lax.fori_loop(0, do.shape[0] // block, spread, 0)


def cross_back_body(dp, own, size, scale, heads, block, real, n):
    rows = n.second.shape[0]
    span = heads * LANES
    d, t, _, _, sib, yp = tensor_place()
    place = DpPlace(dp) if own else None
    peers = [sib, yp] + (place.near() if own else [])
    bar = greet(peers)
    pl.semaphore_wait(bar, len(peers))
    if own:
        up = GradScatter(place, n.grad_up, *n.up_bufs, *n.up_sems)
    n.need(n.c_all, n.cross_out)
    spread_heads(n, n.c_all, n.cross_out, n.do, block)
    n.need(n.low, n.text_low)
    attend_back(
        n.low, n.text_low.at[:, pl.ds(0, span)], n.text_low.at[:, pl.ds(span, span)],
        n.do, n.lse, n.dq, n.dk, n.dv, heads, scale, block, real,
    )
    n.gains[...] = jnp.zeros(n.gains.shape, F32)
    n.offsets[...] = jnp.zeros(n.offsets.shape, F32)
    n.sums[...] = jnp.zeros(n.sums.shape, F32)

    def finish(i, _):
        here = pl.ds(pl.multiple_of(i * block, block), block)
        for h in range(heads):
            hs = head_at(h)
            grad = turn_back(n.dq[here, hs], n.cosine[here, :], n.sine[here, :])
            grad, g, o = head_back(grad, n.pre[here, hs], n.mask[...], n.head_gain[pl.ds(2, 1), :], size)
            n.gains[pl.ds(0, 1), :] += g
            n.offsets[pl.ds(0, 1), :] += o
            grad_low = grad.astype(BF16)
            n.p[here, hs] = grad_low
            n.sums[:, hs] += jnp.sum(grad_low.astype(F32), axis=0, keepdims=True)
        return 0

    if own:
        up.steps(1)
    n.need(n.pre, n.cosine, n.sine)
    lax.fori_loop(0, n.p.shape[0] // block, finish, 0)
    n.need(n.query_wide)
    reduce = TensorSum(*n.sum)
    reduce.start(lambda here: dot_nt(n.p[here, :], n.query_wide[...]))
    if own:
        up.steps(2)
    n.need(n.text_pre, n.mixed, n.third_all, n.text, n.keyval_wide, n.second, n.grad_third)
    for h in range(heads):
        hs = head_at(h)
        grad, g, o = head_back(n.dk[:, hs], n.text_pre[:, hs], n.mask[...], n.head_gain[pl.ds(3, 1), :], size)
        n.gains[pl.ds(1, 1), :] += g
        n.offsets[pl.ds(1, 1), :] += o
        n.text_p[:, hs] = grad.astype(BF16)
        low_v = n.dv[:, hs].astype(BF16)
        n.text_p[:, pl.ds(span + h * LANES, LANES)] = low_v
        n.text_sums[:, hs] = jnp.sum(low_v.astype(F32), axis=0, keepdims=True)
    parts = n.grads.shape[0]

    def put(start, value):
        count = value.shape[0] // parts
        n.grads[:, pl.ds(start, count)] = value.astype(BF16).reshape(parts, count, value.shape[1])
        return start + count

    at = put(0, dot_tn(n.c_all[...], n.mixed[...]))
    at = put(at, dot_tn(n.third_all[...], dot_nt(n.p[...], n.fold[...]).astype(BF16)))
    for part in range(2):
        narrow = dot_nt(n.text_p[:, pl.ds(part * span, span)], n.fold[...]).astype(BF16)
        at = put(at, dot_tn(n.text[...], narrow))
    n.done(n.grads)
    n.grad_text[...] = (
        dot_nt(n.text_p[:, pl.ds(0, span)], n.keyval_wide[0]) + dot_nt(n.text_p[:, pl.ds(span, span)], n.keyval_wide[1])
    ).astype(BF16)
    if own:
        up.steps()
    spread = RowSpread(n.s_all, rows, *n.spread)
    backward_rows(reduce, spread, n.s_all, n.second, n.norm_gain.at[pl.ds(2, 1)], n.grad_third, n.grad_second, (n.sum0, n.sum1, n.sum2), rows)
    spread.forward()
    spread.finish()
    reduce.sent()
    if own:
        n.up_mine[...] = up.result()
        up.sent()


class TextSum:
    def __init__(self, part, total, land, yland, back, sems):
        _, _, _, self.c, self.sib, self.yp = tensor_place()
        self.part, self.total, self.land, self.yland, self.last, self.sems = part, total, land, yland, back, sems
        self.half = piece_rows(part.shape[0], 2, 1)
        self.copies = [remote(part, land, sems.at[0], sems.at[1], self.sib)]
        self.copies[0].start()

    def here(self, c):
        return pl.ds(pl.multiple_of(c * (self.part.shape[0] - self.half), 16), self.half)

    def along(self):
        self.copies[0].wait_recv()
        self.total[...] = (self.part[...].astype(F32) + self.land[...].astype(F32)).astype(BF16)
        cp = remote(self.total.at[self.here(self.c)], self.yland, self.sems.at[2], self.sems.at[3], self.yp)
        cp.start()
        self.copies.append(cp)

    def back(self):
        self.copies[1].wait_recv()
        self.copies[1].wait_send()
        mine = self.here(self.c)
        self.yland[...] = (self.total[mine, :].astype(F32) + self.yland[...].astype(F32)).astype(BF16)
        self.copies[0].wait_send()
        cp = remote(self.yland, self.last, self.sems.at[4], self.sems.at[5], self.sib)
        cp.start()
        self.copies.append(cp)

    def result(self, out):
        self.copies[2].wait_recv()
        out[self.here(self.c), :] = self.yland[...].astype(F32)
        out[self.here(1 - self.c), :] = self.last[...].astype(F32)
        self.copies[2].wait_send()


def self_back_body(dp, own, size, scale, heads, block, n):
    span = heads * LANES
    _, _, _, _, sib, yp = tensor_place()
    place = DpPlace(dp) if own else None
    peers = [sib, yp] + (place.near() if own else [])
    bar = greet(peers)
    pl.semaphore_wait(bar, len(peers))
    text = TextSum(n.text_part, n.text_total, n.text_land, n.text_yland, n.text_back, n.text_sems)
    if own:
        few = GradScatter(place, n.few_grads, *n.few_bufs, *n.few_sems)
    n.need(n.s_all, n.out_t)
    spread_heads(n, n.s_all, n.out_t, n.do, block)
    text.along()
    n.need(n.low)
    attend_back(
        n.low.at[:, pl.ds(0, span)], n.low.at[:, pl.ds(span, span)], n.low.at[:, pl.ds(2 * span, span)],
        n.do, n.lse, n.dq, n.dk, n.dv, heads, scale, block, n.low.shape[0], few.step if own else None,
    )
    text.back()
    n.need(n.pre, n.cosine, n.sine)
    n.gains[...] = jnp.zeros(n.gains.shape, F32)
    n.offsets[...] = jnp.zeros(n.offsets.shape, F32)
    n.sums[...] = jnp.zeros(n.sums.shape, F32)

    def finish(i, _):
        here = pl.ds(pl.multiple_of(i * block, block), block)
        for part, grad_ref in enumerate((n.dq, n.dk, n.dv)):
            for h in range(heads):
                hs = head_at(h)
                wide = pl.ds(part * span + h * LANES, LANES)
                grad = grad_ref[here, hs]
                if part < 2:
                    grad = turn_back(grad, n.cosine[here, :], n.sine[here, :])
                    grad, g, o = head_back(grad, n.pre[here, wide], n.mask[...], n.head_gain[pl.ds(part, 1), :], size)
                    n.gains[pl.ds(part, 1), :] += g
                    n.offsets[pl.ds(part, 1), :] += o
                grad_low = grad.astype(BF16)
                n.p[here, wide] = grad_low
                if part != 1:
                    n.sums[:, wide] += jnp.sum(grad_low.astype(F32), axis=0, keepdims=True)
            n.p_low[part, here, :] = dot_nt(n.p[here, pl.ds(part * span, span)], n.fold[...]).astype(BF16)
        return 0

    lax.fori_loop(0, n.p.shape[0] // block, finish, 0)
    by_place = lambda v: v.astype(BF16).reshape(n.grad_out.shape)
    if own:
        few.steps()
    n.done(n.p)
    n.need(n.mixed, n.first_all)
    n.grad_out[...] = by_place(dot_tn(n.s_all[...], n.mixed[...]))
    for part in range(3):
        n.grad_project[:, part] = by_place(dot_tn(n.first_all[...], n.p_low[part]))
    n.done(n.grad_out, n.grad_project)
    text.result(n.grad_text)
    if own:
        n.few_mine[...] = few.result()
        few.sent()


PACK_ROWS, PACK_SUMS = 8, 16


def last_body(dp, own, n):
    _, t, _, _, _, _ = tensor_place()
    d = lax.axis_index("dp")
    rows, width = n.residual.shape
    cols = n.krecv.shape[1]
    place = DpPlace(dp) if own else None
    peers = [(d, (t + o) % 4) for o in range(1, 4)] + (place.others() if own else [])
    bar = greet(peers)
    reduce = TensorSum(*n.sum)
    scatters = []

    def scatter(source, buffers):
        i = len(scatters)
        scatters.append(GradScatter(place, source, *buffers, *n.scatter_sems[5 * i : 5 * i + 5]))

    def ready():
        pl.semaphore_wait(bar, len(peers))
        if own:
            scatter(n.grad_out, n.out_bufs)
            for i in range(3):
                scatter(n.grad_project.at[:, i], n.project_bufs[3 * i : 3 * i + 3])

    def product(here):
        span = n.project_wide.shape[2]
        total = dot_nt(n.p[here, pl.ds(0, span)], n.project_wide[0])
        for part in range(1, 3):
            total = total + dot_nt(n.p[here, pl.ds(part * span, span)], n.project_wide[part])
        return total

    n.need(n.p, n.project_wide)
    reduce.start(product, ready)
    n.need(n.residual, n.grad_second, n.skipped)
    if own:
        scatters[0].steps()
    sums = None
    for k in range(CHUNKS):
        sl, total = reduce.chunk(k)
        back, xhat = norm_back(total, n.residual[sl, :], n.norm_gain[pl.ds(1, 1), :])
        grad = n.grad_second[sl, :] + back
        back0, xhat0 = norm_back(grad, n.skipped[sl, :].astype(F32), n.norm_gain[pl.ds(0, 1), :])
        low = back0.astype(BF16)
        for s in range(4):
            n.ksend[s, sl, :] = low[:, s * cols : (s + 1) * cols]
        sums = add_sums(sums, [low.astype(F32), total * xhat, total, grad * xhat0, grad])
    copies = []
    for o in (2, 3, 1):
        b = (t + o) % 4
        cp = remote(n.ksend.at[b], n.krecv.at[block_rows(t, rows)], n.k_s.at[o], n.k_r.at[o], (d, b))
        cp.start()
        copies.append(cp)
    n.krecv[block_rows(t, rows), :] = n.ksend[t]
    bias_skip, gain_first, offset_first, gain_skip, offset_skip = sums
    n.tile[...] = offset_first
    n.tile_land[t] = n.tile[...]
    tiles = []
    for o in (1, 2, 3):
        cp = remote(n.tile, n.tile_land.at[t], n.t_s.at[o], n.t_r.at[o], (d, (t + o) % 4))
        cp.start()
        tiles.append(cp)
    n.pack[...] = jnp.zeros(n.pack.shape, F32)
    lines = [gain_skip, gain_first, offset_skip, offset_first, bias_skip, n.gain_third[...], n.gain_fourth[...],
             n.offset_third[...], n.offset_fourth[...], n.bias_attn[...], n.bias_cross_out[...], n.bias_mlp[...]]
    for i, v in enumerate(lines):
        n.pack[i // PACK_ROWS, pl.ds(i % PACK_ROWS, 1), :] = v
    heads_at = len(lines)
    for i, v in enumerate((n.self_gains, n.cross_gains, n.self_offsets, n.cross_offsets)):
        for r in range(2):
            n.pack[heads_at // PACK_ROWS, pl.ds(heads_at % PACK_ROWS, 1), pl.ds((2 * i + r) * LANES, LANES)] = v[pl.ds(r, 1), :]
    span = n.project_wide.shape[2]
    wide = [n.self_sums[:, pl.ds(0, span)], n.self_sums[:, pl.ds(2 * span, span)], n.cross_sums[...], n.text_sums[...]]
    hidden = n.bias_hidden.shape[1]
    for s in range(4):
        seat = (t == s).astype(F32)
        block, row = divmod(PACK_SUMS + 4 * s, PACK_ROWS)
        for i, v in enumerate(wide):
            n.pack[block, pl.ds(row, 1), pl.ds(i * cols, cols)] = seat * exact(v, n.unfold[...])
        for i, start in enumerate(range(0, hidden, width)):
            count = min(width, hidden - start)
            n.pack[block, pl.ds(row + 1 + i, 1), pl.ds(0, count)] = seat * n.bias_hidden[:, pl.ds(start, count)]
    shares = []
    for o in (1, 2, 3):
        b = (t + o) % 4
        cp = remote(n.pack.at[b], n.pack_in_land.at[t], n.ps_s.at[o], n.ps_r.at[o], (d, b))
        cp.start()
        shares.append(cp)
    n.pack_in_land[t] = n.pack[t]
    if own:
        scatters[1].steps()
    for cp in copies:
        cp.wait_recv()
    reduce.sent()
    for cp in tiles:
        cp.wait_recv()
    n.low_out[...] = (n.tile_land[0] + n.tile_land[1] + n.tile_land[2] + n.tile_land[3]).astype(BF16).astype(F32)
    for cp in shares:
        cp.wait_recv()
    n.pack_mine[...] = n.pack_in_land[0] + n.pack_in_land[1] + n.pack_in_land[2] + n.pack_in_land[3]
    if own:
        n.low_land[d] = n.low_out[...]
        lows = ToAll(place, lambda q: n.low_out, n.low_land, n.l_s, n.l_r)
        pack_cp = remote(n.pack_mine, n.pack_x, n.px_s.at[0], n.px_r.at[0], place.pair)
        pack_cp.start()
    n.need(n.skip_w)
    halves = [TensorSum(*n.sum), TensorSum(*n.sum1)]
    for h, half in enumerate(halves):
        half.start(lambda here, h=h: dot_nt(n.krecv[here, :], n.skip_w[pl.ds(h * width, width), :]))
    if own:
        pack_cp.wait_recv()
        pack_cp.wait_send()
        n.pack_mine[...] = n.pack_mine[...] + n.pack_x[...]
        n.pack_z[place.zi] = n.pack_mine[...]
        packs = []
        for j in range(1, place.line):
            cp = remote(n.pack_mine, n.pack_z.at[place.zi], n.pz_s.at[j], n.pz_r.at[j], (place.ahead(j), place.t))
            cp.start()
            packs.append(cp)
        scatters[2].steps()
    n.need(n.joined0, n.joined1)
    k_all = n.krecv[...]
    count = n.grad_skip_w.shape[0] // 2
    for h, joined in enumerate((n.joined0, n.joined1)):
        n.grad_skip_w[pl.ds(h * count, count)] = (
            dot_tn(joined[...], k_all).astype(BF16).reshape((count,) + n.grad_skip_w.shape[1:])
        )
    if own:
        scatters[3].steps()
        scatter(n.grad_skip_w, n.skip_bufs)
        scatters[4].steps()
        for cp in packs:
            cp.wait_recv()
            cp.wait_send()
        n.pack_mine[...] = sum(n.pack_z[i] for i in range(place.line))
    n.pack_t[t] = n.pack_mine[...]
    ends = []
    for o in (1, 2, 3):
        cp = remote(n.pack_mine, n.pack_t.at[t], n.pt_s.at[o], n.pt_r.at[o], (d, (t + o) % 4))
        cp.start()
        ends.append(cp)
    if own:
        lows.arrived()
        low_all = jnp.concatenate([n.low_land[i] for i in range(dp)], axis=0)
        n.shift_grad[...] = dot_tn(n.silu[...], low_all.astype(BF16))
        n.shift_bias[...] = jnp.sum(low_all, axis=0, keepdims=True)
        n.out_mine[...] = scatters[0].result()
        for i in range(3):
            n.project_mine[i] = scatters[1 + i].result()
    else:
        n.shift_grad[...] = n.low_out[...]
        n.shift_bias[...] = n.low_out[...]
    for half, out in zip(halves, (n.grad_latent, n.grad_skip)):
        for k in range(CHUNKS):
            sl, total = half.chunk(k)
            out[sl, :] = total
        half.sent()
        n.done(out)
    for cp in ends:
        cp.wait_recv()
        cp.wait_send()
    n.pack_out[...] = n.pack_t[...]
    if own:
        n.skip_mine[...] = scatters[4].result()
        for s in scatters:
            s.sent()
        lows.sent()
    for cp in copies + tiles + shares:
        cp.wait_send()


def finish_body(hidden, n):
    r, cols = n.o_query.shape
    pairs = [(n.out_mine, n.o_out), (n.down_mine, n.o_down), (n.project_mine, n.o_project), (n.block_out, n.o_block), (n.grad_latent, n.o_latent), (n.grad_skip, n.o_skip), (n.skip_mine, n.o_skip_mine),
             (n.shift_grad, n.o_shift), (n.up_mine, n.o_up)]
    for source, out in pairs:
        out[...] = source[...]
    n.o_query[...] = n.few_mine[pl.ds(r, r), :]
    n.o_cross_out[...] = n.few_mine[pl.ds(0, r), :]
    for i in range(2):
        count = n.o_keyval.shape[2]
        n.o_keyval[i] = n.few_mine[pl.ds(2 * r + i * count, count), :].T
    n.o_text[...] = n.text_part[pl.ds(0, n.o_text.shape[0]), :]
    row = lambda i: n.pack[i // PACK_ROWS, pl.ds(i % PACK_ROWS, 1), :]
    for out, places in ((n.norm_gain, (0, 1, 5, 6)), (n.norm_bias, (2, 3, 7, 8)), (n.row_bias, (9, 10, 11))):
        for i, at in enumerate(places):
            out[pl.ds(i, 1), :] = row(at)
    n.row_bias[pl.ds(3, 1), :] = n.shift_bias[...]
    packed = row(12)
    for k, out in enumerate((n.head_gain, n.head_bias)):
        for i in range(4):
            at = (4 * k + i) * LANES
            out[pl.ds(i, 1), :] = exact(packed[:, at : at + LANES], n.unfold[...])
    width = packed.shape[1]
    for s in range(4):
        at = PACK_SUMS + 4 * s
        columns = row(at)
        for i in range(4):
            n.column_bias[pl.ds(i, 1), pl.ds(s * cols, cols)] = columns[:, i * cols : (i + 1) * cols]
        for i, start in enumerate(range(0, hidden, width)):
            count = min(width, hidden - start)
            n.hidden_bias[:, pl.ds(s * hidden + start, count)] = row(at + 1 + i)[:, :count]
    n.column_bias[pl.ds(4, 1), :] = row(4)


def fold_matrix(heads, size):
    out = np.zeros((heads * size, heads * LANES), np.float32)
    for h in range(heads):
        for e in range(size):
            out[h * size + e, h * LANES + (e % 2) * (LANES // 2) + e // 2] = 1.0
    return out


def body(
    latent, skip_states, text_states, condition, teacher, loss_mask, true_counts, positions,
    skip_proj, shift_proj, self_project, self_output, cross_query, cross_keyval, cross_output, hidden_up, hidden_down,
    norm_gain, norm_bias, head_gain, head_bias, column_bias, hidden_bias, row_bias,
):
    d, t = lax.axis_index("dp"), lax.axis_index("tensor")
    dp, tensor = lax.axis_size("dp"), lax.axis_size("tensor")
    rows, width = latent.shape
    group = rows * tensor
    size = head_gain.shape[1]
    cols = self_project.shape[2]
    heads = cols // size
    span = heads * LANES
    hidden = hidden_up.shape[1]
    text_len, text_width = text_states.shape[1:]
    text_pad = -(-text_len // 16) * 16
    scale = size ** (-0.5)
    block = min(256, group)
    r, text_share = shift_proj.shape[0], cross_keyval.shape[0]
    own = r % 16 == 0 and text_share % 16 == 0 and skip_proj.shape[0] % 32 == 0 and dp == 8
    parts = dp if own else 1
    line = max(dp // 2, 1) if own else 1
    dma, vm = pltpu.SemaphoreType.DMA, pltpu.VMEM
    few = lambda *shape: shape if own else (16, LANES)

    fold_np = fold_matrix(heads, size)
    fold = jnp.asarray(fold_np, BF16)
    one_np = fold_np[:size, :LANES]
    mask = jnp.asarray(one_np.sum(0, keepdims=True), F32)
    quarter = size // 4
    lane_np = np.zeros((2, LANES), np.float32)
    sign_np = np.zeros((1, LANES), np.float32)
    for i in range(size // 2):
        f = np.float32(10000.0 ** (-(i % quarter) / quarter))
        for half in range(2):
            lane_np[i // quarter, half * (LANES // 2) + i] = f
            sign_np[0, half * (LANES // 2) + i] = 2 * half - 1
    lanes_in = jnp.asarray(np.concatenate([lane_np, sign_np]))
    one = jnp.asarray(one_np)

    project_in = jnp.transpose(self_project, (1, 0, 2))
    shards = [self_output.T, cross_query, cross_output.T, jnp.transpose(cross_keyval, (1, 0, 2)), hidden_up, hidden_down.T]
    if own:
        small_shape = (dp, 1, -(-r // LANES) * LANES + LANES)
        skip_in, shift_in = skip_proj, shift_proj
    else:
        small_all = lax.all_gather(
            jnp.concatenate([condition.astype(F32), true_counts.astype(F32)[:, None]], axis=1), "dp", axis=0, tiled=True
        )
        silu_all = jax.nn.silu(small_all[:, :width]).astype(BF16)
        silu = lax.dynamic_slice_in_dim(silu_all, d * r, r, 1)
        shift_in = lax.psum_scatter(dot_nn(silu, shift_proj), "dp", scatter_dimension=0, tiled=True) + row_bias[3:4]
        small_shape = (1, 8, LANES)
        skip_in = lax.all_gather(skip_proj, "dp", axis=0, tiled=True)
        project_in = lax.all_gather(project_in, "dp", axis=1, tiled=True)
        shards = [lax.all_gather(v, "dp", axis=v.ndim - 2, tiled=True) for v in shards]
    early_rows = 128 if own else r
    full = shaped((group, width), BF16)
    mine = shaped((rows, width), F32)
    mine_low = shaped((rows, width), BF16)
    line_sum = shaped((1, width), F32)
    lse_shape = shaped((group // block, heads, block), F32)
    sum_scratch = TensorSum.scratch(rows, width)
    first = named_kernel(
        "first", 0, functools.partial(first_body, dp, own, size, scale, heads, block),
        dict(
            latent=hbm(latent), skip_states=hbm(skip_states), skip_in=hbm(skip_in) if own else skip_in, project_in=hbm(project_in) if own else project_in, out_in=hbm(shards[0]) if own else shards[0],
            query_in=hbm(shards[1]), cross_out_in=hbm(shards[2]), keyval_in=hbm(shards[3]), down_in=hbm(shards[5]),
            condition=condition, true_count=true_counts[:, None], shift_in=shift_in, column_bias=column_bias, positions=positions, lanes=lanes_in,
            norm_gain=norm_gain, norm_bias=norm_bias, row_bias=row_bias, head_gain=head_gain, head_bias=head_bias,
            one=one, fold_f32=jnp.asarray(fold_np), mask=mask, fold=fold,
        ),
        dict(
            joined0=late(full), joined1=late(full), skip_full=late(shaped(few(dp, skip_proj.shape[0], cols), BF16)), skipped=late(mine_low),
            residual=late(mine), first_all=late(full), silu=shaped(few(dp, r), BF16), counted=shaped((1, LANES), F32),
            project_wide=late(shaped((3, width, span), BF16)), pre=late(shaped((group, 2 * span), F32)),
            low=late(shaped((group, 3 * span), BF16)), mixed=late(shaped((group, cols), BF16)), lse=lse_shape,
            out_land=shaped(few(dp, r, cols), BF16), query_g=hbm(shaped(few(dp, r, cols), BF16)),
            key_g=hbm(shaped(few(dp, text_share, cols), BF16)), value_g=hbm(shaped(few(dp, text_share, cols), BF16)),
            cross_out_g=hbm(shaped(few(dp, r, cols), BF16)), down_g=hbm(shaped(few(dp, early_rows, hidden), BF16)), third_all=full, second=late(mine),
            gain_wide=shaped((4, LANES), F32), offset_wide=shaped((4, LANES), F32), bias_wide=shaped((column_bias.shape[0], span), F32),
            cosine=late(shaped((group, LANES), F32)), sine=late(shaped((group, LANES), F32)),
        ),
        dict(
            p_land=vm(few(dp, 3, r, cols), BF16), padded=vm((group, span), BF16), skip_send=vm((4, rows, cols), BF16),
            skip_recv=vm((4, rows, cols), BF16), small=vm(small_shape, F32), small_land=vm(small_shape, F32), shift_part=vm((dp, 1, width), F32),
            shift_land=vm((dp, 1, width), F32), sum=sum_scratch, own_sem=dma((10,)), a_s=dma((dp,)),
            a_r=dma((dp,)), b_s=dma((dp,)), b_r=dma((dp,)), p_s=dma((4,)), p_r=dma((4,)), gather_sems=Gathers.scratch(13, line),
            spread0=RowSpread.scratch(1),
            spread1=RowSpread.scratch(1), spread2=RowSpread.scratch(), spread3=RowSpread.scratch(),
        ),
    )
    if own:
        silu, counted = first.silu, first.counted
        skip_full = first.skip_full.reshape(2 * width, cols)
        out_t, query, cross_out_t = [v.reshape(width, cols) for v in (first.out_land, first.query_g, first.cross_out_g)]
        key, value = [v.reshape(text_width, cols) for v in (first.key_g, first.value_g)]
    else:
        counted, skip_full = jnp.full((1, LANES), jnp.sum(small_all[:, width])), skip_in
        out_t, query, cross_out_t, (key, value), up_full, down_t = shards

    text = jnp.pad(text_states[0], ((0, text_pad - text_len), (0, 0)))
    cross = named_kernel(
        "cross", 1, functools.partial(cross_body, dp, own, size, scale, heads, block, text_len),
        dict(
            query=late(query), key=late(key), value=late(value), cross_out=late(cross_out_t), up_in=hbm(shards[4]), down_in=hbm(shards[5]), text=late(text), third_all=late(first.third_all),
            bias_wide=first.bias_wide, cosine=late(first.cosine), sine=late(first.sine), norm_gain=norm_gain,
            norm_bias=norm_bias, row_bias=row_bias, head_gain=first.gain_wide, head_bias=first.offset_wide, mask=mask, fold=fold,
            second=late(first.second),
        ),
        dict(
            query_wide=late(shaped((width, span), BF16)), keyval_wide=late(shaped((2, text_width, span), BF16)),
            text_pre=shaped((text_pad, span), F32), text_low=shaped((text_pad, 2 * span), BF16),
            pre=late(shaped((group, span), F32)), low=late(shaped((group, span), BF16)), mixed=late(shaped((group, cols), BF16)),
            lse=lse_shape, fourth_all=full, third_sum=mine,
            up_g=hbm(shaped(few(dp, r, hidden), BF16)), down_g=hbm(shaped(few(dp, r - early_rows, hidden), BF16)),
        ),
        dict(
            padded=vm((group, span), BF16), sum=sum_scratch, spread=RowSpread.scratch(),
            gather_sems=Gathers.scratch(5, line), own_sem=dma((2,)),
        ),
    )
    if own:
        up_full = cross.up_g.reshape(width, hidden)
        down_ins = dict(down_a=hbm(first.down_g), down_b=hbm(cross.down_g))
        down_scratch = dict(down_t=vm((dp, r, hidden), BF16), down_sem=dma((2,)))
    else:
        down_ins, down_scratch = dict(down_t=down_t), {}

    feed = named_kernel(
        "feed", 2, functools.partial(feed_body, own),
        dict(
            fourth_all=late(cross.fourth_all), up=late(up_full), hidden_bias=hidden_bias.reshape(-1, LANES), **down_ins, third_sum=late(cross.third_sum),
            row_bias=row_bias, teacher=late(teacher), loss_mask=loss_mask[None], true_count=true_counts[:, None],
            counted=counted, total=jnp.full((1, 1), dp * group, F32),
        ),
        dict(
            active=late(shaped((group, hidden), BF16)), slope=late(shaped((group, hidden), BF16)), grad_all=full, block_out=late(mine_low),
            grad_final=late(mine), bias_mlp=line_sum,
        ),
        dict(sum=sum_scratch, spread=RowSpread.scratch(), **down_scratch),
    )

    back = named_kernel(
        "feed_back", 3, functools.partial(feed_back_body, dp, own),
        dict(
            grad_all=late(feed.grad_all), active=late(feed.active), **down_ins, slope=late(feed.slope), up=late(up_full),
            fourth_all=late(cross.fourth_all), third_sum=late(cross.third_sum), norm_gain=norm_gain, grad_final=late(feed.grad_final),
        ),
        dict(
            c_all=full, grad_third=mine, sum0=line_sum, sum1=line_sum, sum2=line_sum, bias_hidden=shaped((1, hidden), F32),
            grad_up=late(shaped((parts, width // parts, hidden), BF16)),
            **(dict(down_mine=shaped((r, hidden), F32)) if own else dict(grad_down=shaped((1, width, hidden), BF16))),
        ),
        dict(
            upper=vm((group, hidden), BF16), sum=sum_scratch, spread=RowSpread.scratch(), **down_scratch,
            **(dict(grad_down=vm((dp, r, hidden), BF16), down_bufs=GradScatter.buffers((r, hidden)), down_sems=GradScatter.scratch()) if own else {}),
        ),
    )
    bias_cross_out, gain_fourth, offset_fourth = back.sum0, back.sum1, back.sum2

    few_rows = 2 * r + 2 * text_share if own else 2 * width + 2 * text_width
    cback = named_kernel(
        "cross_back", 4, functools.partial(cross_back_body, dp, own, size, scale, heads, block, text_len),
        dict(
            c_all=late(back.c_all), cross_out=late(cross_out_t), low=late(cross.low), text_low=late(cross.text_low), pre=late(cross.pre),
            text_pre=late(cross.text_pre), lse=cross.lse, cosine=late(first.cosine), sine=late(first.sine), head_gain=first.gain_wide, mask=mask, fold=fold,
            mixed=late(cross.mixed), third_all=late(first.third_all), text=late(text), keyval_wide=late(cross.keyval_wide),
            query_wide=late(cross.query_wide), second=late(first.second), norm_gain=norm_gain, grad_third=late(back.grad_third),
            **(dict(grad_up=hbm(back.grad_up)) if own else {}),
        ),
        dict(
            grads=late(shaped((parts, few_rows, cols), BF16)), grad_text=shaped((text_pad, text_width), BF16),
            gains=shaped((2, LANES), F32), offsets=shaped((2, LANES), F32), sums=shaped((1, span), F32),
            text_sums=shaped((1, span), F32), s_all=full, grad_second=mine, sum0=line_sum, sum1=line_sum, sum2=line_sum,
            **(dict(up_mine=shaped((r, hidden), F32)) if own else {}),
        ),
        dict(
            p=vm((group, span), BF16), do=vm((group, span), BF16), dq=vm((group, span), F32), dk=vm((text_pad, span), F32),
            dv=vm((text_pad, span), F32), text_p=vm((text_pad, 2 * span), BF16), sum=sum_scratch, spread=RowSpread.scratch(),
            **(dict(up_bufs=GradScatter.buffers((r, hidden)), up_sems=GradScatter.scratch()) if own else {}),
        ),
    )
    few_grads = cback.grads
    if not own:
        cuts = np.cumsum([0, width, width, text_width, text_width])
        few_grads = jnp.concatenate(
            [few_grads[0, a:b].reshape(dp, -1, cols) for a, b in zip(cuts[:-1], cuts[1:])], axis=1
        )
        few_mine = lax.psum_scatter(few_grads.reshape(-1, cols), "dp", scatter_dimension=0, tiled=True).astype(F32)
        down_mine = lax.psum_scatter(back.grad_down[0], "dp", scatter_dimension=0, tiled=True).astype(F32)
        up_mine = lax.psum_scatter(back.grad_up[0], "dp", scatter_dimension=0, tiled=True).astype(F32)
    else:
        down_mine, up_mine = back.down_mine, cback.up_mine

    sback = named_kernel(
        "self_back", 6, functools.partial(self_back_body, dp, own, size, scale, heads, block),
        dict(
            text_part=cback.grad_text, **(dict(few_grads=hbm(few_grads)) if own else {}),
            s_all=late(cback.s_all), out_t=late(out_t), low=late(first.low), pre=late(first.pre), lse=first.lse, cosine=late(first.cosine), sine=late(first.sine),
            head_gain=first.gain_wide, mask=mask, fold=fold, mixed=late(first.mixed), first_all=late(first.first_all),
        ),
        dict(
            p=late(shaped((group, 3 * span), BF16)), grad_out=late(shaped((parts, width // parts, cols), BF16)),
            grad_project=late(shaped((parts, 3, width // parts, cols), BF16)), gains=shaped((2, LANES), F32),
            offsets=shaped((2, LANES), F32), sums=shaped((1, 3 * span), F32), grad_text=shaped((text_pad, text_width), F32),
            **(dict(few_mine=shaped((few_rows, cols), F32)) if own else {}),
        ),
        dict(
            do=vm((group, span), BF16), dq=vm((group, span), F32), dk=vm((group, span), F32), dv=vm((group, span), F32),
            p_low=vm((3, group, cols), BF16), text_total=vm((text_pad, text_width), BF16),
            text_land=vm((text_pad, text_width), BF16), text_yland=vm((piece_rows(text_pad, 2, 1), text_width), BF16),
            text_back=vm((piece_rows(text_pad, 2, 1), text_width), BF16),
            text_sems=dma((6,)),
            **(dict(few_bufs=GradScatter.buffers((few_rows, cols)), few_sems=GradScatter.scratch()) if own else {}),
        ),
    )
    if own:
        few_mine = sback.few_mine

    skip_rows = 2 * width // dp if own else width
    pack_land = vm((4, PACK_ROWS, width), F32)
    last = named_kernel(
        "last", 5, functools.partial(last_body, dp, own),
        dict(
            p=late(sback.p), project_wide=late(first.project_wide), residual=late(first.residual), grad_second=late(cback.grad_second),
            skipped=late(first.skipped), norm_gain=norm_gain, skip_w=late(skip_full), joined0=late(first.joined0), joined1=late(first.joined1),
            silu=silu, gain_third=cback.sum1, gain_fourth=gain_fourth, offset_third=cback.sum2, offset_fourth=offset_fourth,
            bias_attn=cback.sum0, bias_cross_out=bias_cross_out, bias_mlp=feed.bias_mlp, self_gains=sback.gains,
            cross_gains=cback.gains, self_offsets=sback.offsets, cross_offsets=cback.offsets, self_sums=sback.sums,
            cross_sums=cback.sums, text_sums=cback.text_sums, bias_hidden=back.bias_hidden, unfold=jnp.asarray(fold_np.T),
            grad_out=hbm(sback.grad_out), grad_project=hbm(sback.grad_project),
        ),
        dict(
            grad_latent=late(mine), grad_skip=late(mine), shift_grad=shaped((r if own else 1, width), F32), shift_bias=line_sum,
            pack_out=shaped((4, PACK_ROWS, width), F32),
            **(dict(out_mine=shaped((r, cols), F32), project_mine=shaped((3, r, cols), F32), skip_mine=shaped((skip_rows, cols), F32))
               if own else dict(grad_skip_w=shaped((2, width, cols), BF16))),
        ),
        dict(
            ksend=vm((4, rows, cols), BF16), krecv=vm((group, cols), BF16), tile=vm((1, width), F32),
            tile_land=vm((4, 1, width), F32), low_out=vm((1, width), F32),
            low_land=vm((dp if own else 1, 1, width), F32), pack=vm((4, PACK_ROWS, width), F32), pack_in_land=pack_land,
            pack_mine=vm((PACK_ROWS, width), F32), pack_x=vm((PACK_ROWS, width), F32), pack_z=pack_land, pack_t=pack_land, sum=sum_scratch, sum1=sum_scratch,
            k_s=dma((4,)), k_r=dma((4,)), t_s=dma((4,)), t_r=dma((4,)), l_s=dma((dp,)), l_r=dma((dp,)), px_s=dma((1,)),
            px_r=dma((1,)), ps_s=dma((4,)), ps_r=dma((4,)), pz_s=dma((line,)), pz_r=dma((line,)), pt_s=dma((4,)), pt_r=dma((4,)),
            **(dict(
                grad_skip_w=vm((dp, skip_rows, cols), BF16), out_bufs=GradScatter.buffers((r, cols)),
                project_bufs=GradScatter.buffers((r, cols)) * 3, skip_bufs=GradScatter.buffers((skip_rows, cols)),
                scatter_sems=GradScatter.scratch() * 5,
            ) if own else {}),
        ),
    )
    if own:
        out_mine, project_mine, skip_mine = last.out_mine, last.project_mine, last.skip_mine
        shift_grad, shift_bias, pack_sum = last.shift_grad, last.shift_bias, last.pack_out
    else:
        shift_all = lax.all_gather(last.shift_grad[:1], "dp", axis=0, tiled=True)
        shift_bias = jnp.sum(shift_all, axis=0, keepdims=True)
        shift_grad = dot_tn(silu, shift_all.astype(BF16))
        pack_sum = lax.psum(last.pack_out, "dp")
        out_mine = lax.psum_scatter(sback.grad_out[0], "dp", scatter_dimension=0, tiled=True).astype(F32)
        project_mine = lax.psum_scatter(sback.grad_project[0], "dp", scatter_dimension=1, tiled=True).astype(F32)
        skip_mine = lax.psum_scatter(last.grad_skip_w.reshape(-1, cols), "dp", scatter_dimension=0, tiled=True).astype(F32)
    end = named_kernel(
        "finish", None, functools.partial(finish_body, hidden),
        dict(
            pack=pack_sum, shift_bias=shift_bias, unfold=jnp.asarray(one_np.T), block_out=feed.block_out,
            grad_latent=last.grad_latent, grad_skip=last.grad_skip, skip_mine=skip_mine, shift_grad=shift_grad,
            up_mine=up_mine, few_mine=few_mine, text_part=sback.grad_text,
            out_mine=out_mine, down_mine=down_mine, project_mine=project_mine,
        ),
        dict(
            norm_gain=shaped(norm_gain.shape, F32), norm_bias=shaped(norm_bias.shape, F32), head_gain=shaped(head_gain.shape, F32),
            head_bias=shaped(head_bias.shape, F32), column_bias=shaped(column_bias.shape, F32), hidden_bias=shaped((1, 4 * hidden), F32),
            row_bias=shaped(row_bias.shape, F32), o_block=mine_low, o_latent=mine, o_skip=mine, o_skip_mine=shaped(skip_mine.shape, F32),
            o_shift=shaped(shift_grad.shape, F32), o_up=shaped(up_mine.shape, F32), o_query=shaped((r, cols), F32),
            o_text=shaped((text_len, text_width), F32), o_out=shaped((r, cols), F32), o_cross_out=shaped((r, cols), F32),
            o_down=shaped((r, hidden), F32), o_project=shaped((3, r, cols), F32), o_keyval=shaped((2, cols, text_share), F32),
        ),
        {},
    )
    return (
        end.o_block,
        end.o_latent,
        end.o_skip,
        end.o_text[None],
        end.o_skip_mine,
        end.o_shift,
        jnp.transpose(end.o_project, (1, 0, 2)),
        end.o_out.T,
        end.o_query,
        jnp.transpose(end.o_keyval, (2, 0, 1)),
        end.o_cross_out.T,
        end.o_up,
        end.o_down.T,
        end.norm_gain,
        end.norm_bias,
        end.head_gain,
        end.head_bias,
        end.column_bias,
        end.hidden_bias[0],
        end.row_bias,
    )


def solution(mesh):
    both = ("dp", "tensor")
    rows2, split2, cross2 = P(both, None), P("dp", "tensor"), P("tensor", "dp")
    middle = P("dp", None, "tensor")
    return jax.shard_map(
        body,
        mesh=mesh,
        in_specs=(
            rows2, rows2, P("dp", None, None), P("dp", None), rows2, P(both), P("dp"), P(None, "dp"),
            split2, P("dp", None), middle, cross2, split2, middle, cross2, split2, cross2,
            P(), P(), P(), P(), P(), P(), P(),
        ),
        out_specs=(
            rows2, rows2, rows2, P("dp", None, None),
            split2, P("dp", None), middle, cross2, split2, middle, cross2, split2, cross2,
            P(), P(), P(), P(), P(), P(), P(),
        ),
        check_vma=False,
    )
```

```python
import functools
from types import SimpleNamespace

import jax
import jax.numpy as jnp
import numpy as np
from jax import lax
from jax.experimental import pallas as pl
from jax.experimental.pallas import tpu as pltpu
from jax.sharding import PartitionSpec as P

EPSILON = 1e-06
MESH = pl.DeviceIdType.MESH
BF16, F32 = jnp.bfloat16, jnp.float32
LANES = 128
CHUNKS = 2
VMEM_BYTES = 60 * 2**20
NEGATIVE = -1e30


def dot_nn(left, right):
    return jnp.dot(left, right, preferred_element_type=F32)


def dot_nt(left, right):
    return lax.dot_general(left, right, (((1,), (1,)), ((), ())), preferred_element_type=F32)


def dot_tn(left, right):
    return lax.dot_general(left, right, (((0,), (0,)), ((), ())), preferred_element_type=F32)


def centre(x):
    cen = x - jnp.mean(x, axis=-1, keepdims=True)
    spread = jnp.mean(cen * cen, axis=-1, keepdims=True)
    return cen, lax.rsqrt(spread + EPSILON)


def norm_back(total, x, gain):
    cen, rstd = centre(x)
    xhat = cen * rstd
    dg = total * gain
    back = rstd * (
        dg - jnp.mean(dg, axis=-1, keepdims=True) - xhat * jnp.mean(dg * xhat, axis=-1, keepdims=True)
    )
    return back, xhat


def remote(src, dst, send_sem, recv_sem, device):
    return pltpu.make_async_remote_copy(
        src_ref=src, dst_ref=dst, send_sem=send_sem, recv_sem=recv_sem, device_id=device, device_id_type=MESH
    )


def tensor_place():
    d, t = lax.axis_index("dp"), lax.axis_index("tensor")
    y, c = t // 2, t % 2
    return d, t, y, c, (d, 2 * y + 1 - c), (d, 2 * (1 - y) + c)


def greet(peers):
    bar = pltpu.get_barrier_semaphore()
    for peer in peers:
        pl.semaphore_signal(bar, inc=1, device_id=peer, device_id_type=MESH)
    return bar


class DpPlace:
    def __init__(self, dp):
        self.d, self.t = lax.axis_index("dp"), lax.axis_index("tensor")
        self.dp, self.line = dp, dp // 2
        self.zi, self.par = self.d // 2, self.d % 2
        self.pair = (2 * self.zi + 1 - self.par, self.t)
        self.e0, self.e3 = (3 - self.zi) // 3, self.zi // 3
        self.end = self.e0 + self.e3

    def at(self, zi):
        return 2 * zi + self.par

    def ahead(self, j):
        return 2 * ((self.zi + j) % self.line) + self.par

    def behind(self, j):
        return 2 * ((self.zi + self.line - j) % self.line) + self.par

    def near(self):
        return [self.pair] + [(self.ahead(j), self.t) for j in range(1, self.line)]

    def others(self):
        return [((self.d + j) % self.dp, self.t) for j in range(1, self.dp)]


class ToAll:
    def __init__(self, place, source, land, send_sem, recv_sem):
        self.copies = []
        for j in range(1, place.dp):
            q = (place.d + j) % place.dp
            cp = remote(source(q), land.at[place.d], send_sem.at[j], recv_sem.at[j], (q, place.t))
            cp.start()
            self.copies.append(cp)

    def arrived(self):
        for cp in self.copies:
            cp.wait_recv()

    def sent(self):
        for cp in self.copies:
            cp.wait_send()


class LineSpread:
    def __init__(self, place, shard, land, owner_par, z_s, z_r):
        self.place, self.land, self.z_s, self.z_r, self.par = place, land, z_s, z_r, owner_par
        here = land.at[2 * place.zi + owner_par]
        self.direct = {j: remote(shard, here, z_s.at[j], z_r.at[j], (place.ahead(j), place.t)) for j in (2, 1, 3)}
        for j, cp in self.direct.items():
            self.when(j, cp.start)
        self.order = (2, 1 + 2 * place.e0, 3 - 2 * place.e0)
        source = land.at[self.owner(2)]
        end = 3 * (place.zi // 2)
        self.inner = remote(source, source, z_s.at[0], z_r.at[1 + 2 * (place.zi // 2)], (place.at(end), place.t))

    def owner(self, j):
        return 2 * ((self.place.zi + 4 - j) % 4) + self.par

    def when(self, j, act):
        if j == 2:
            act()
        else:
            pl.when(self.place.zi != (0 if j == 3 else 3))(act)

    def arrival(self, i):
        j = self.order[i]
        here = self.land.at[self.owner(j)]
        remote(here, here, self.z_s.at[j], self.z_r.at[j], self.place.pair).wait_recv()
        if i == 0:
            pl.when(self.place.end == 0)(self.inner.start)
        return self.owner(j), j

    def sent(self):
        for j, cp in self.direct.items():
            self.when(j, cp.wait_send)
        pl.when(self.place.end == 0)(self.inner.wait_send)


class LineFirst:
    def __init__(self, place, shard, land, z_s, z_r, x_s, x_r):
        self.place, self.land, self.x_s, self.x_r = place, land, x_s, x_r
        self.line = LineSpread(place, shard, land, place.par, z_s.at[0], z_r.at[0])
        self.x = []
        self.cross(shard, place.d, 0)

    def cross(self, source, owner, j):
        cp = remote(source, self.land.at[owner], self.x_s.at[j], self.x_r.at[j], self.place.pair)
        cp.start()
        self.x.append(cp)

    def pass_on(self, arrivals):
        for i in arrivals:
            owner, j = self.line.arrival(i)
            self.cross(self.land.at[owner], owner, j)

    def early(self):
        self.pass_on((0, 1))

    def later(self):
        self.pass_on((2,))

    def arrived(self):
        for cp in self.x:
            cp.wait_recv()

    def sent(self):
        self.line.sent()
        for cp in self.x:
            cp.wait_send()


class PairFirst:
    def __init__(self, place, shard, land, z_s, z_r, x_s, x_r):
        self.place, self.land, self.sems = place, land, (z_s, z_r)
        self.lines = [LineSpread(place, shard, land, place.par, z_s.at[0], z_r.at[0])]
        self.x = remote(shard, land.at[place.d], x_s.at[0], x_r.at[0], place.pair)
        self.x.start()

    def early(self):
        self.x.wait_recv()
        z_s, z_r = self.sems
        par = 1 - self.place.par
        other = self.land.at[2 * self.place.zi + par]
        self.lines.append(LineSpread(self.place, other, self.land, par, z_s.at[1], z_r.at[1]))

    def later(self):
        for line in self.lines:
            line.arrival(0)

    def arrived(self):
        for line in self.lines:
            line.arrival(1)
            line.arrival(2)

    def sent(self):
        self.x.wait_send()
        for line in self.lines:
            line.sent()


class Gathers:
    def __init__(self, place, ahead, z_s, z_r, x_s, x_r):
        self.place, self.ahead, self.sems = place, ahead, (z_s, z_r, x_s, x_r)
        self.pieces, self.going, self.passed, self.ended = [], [], 0, 0

    def add(self, shard, land, pieces=1, kind=LineFirst):
        start = 0
        for i in range(pieces):
            if pieces == 1:
                self.pieces.append((kind, shard, land))
            else:
                count = piece_rows(shard.shape[0], pieces, i)
                self.pieces.append((kind, shard.at[pl.ds(start, count)], land.at[:, pl.ds(start, count)]))
                start += count
        self.fill()

    def fill(self):
        while len(self.going) < min(len(self.pieces), self.passed + self.ahead):
            k = len(self.going)
            kind, shard, land = self.pieces[k]
            self.going.append(kind(self.place, shard, land, *[v.at[k] for v in self.sems]))

    def forward(self, count=1):
        for _ in range(count):
            self.end(self.passed)
            self.going[self.passed].early()
            self.passed += 1
            self.fill()

    def end(self, last):
        while self.ended < last:
            self.going[self.ended].later()
            self.ended += 1

    def arrived(self, first, last):
        self.end(last)
        for g in self.going[first:last]:
            g.arrived()

    def sent(self):
        for g in self.going:
            g.sent()

    @staticmethod
    def scratch(count):
        dma = pltpu.SemaphoreType.DMA
        return [dma((count, 2, 4)), dma((count, 2, 4)), dma((count, 4)), dma((count, 4))]


def piece_rows(rows, pieces, i):
    tiles = rows // 16
    return 16 * (tiles * (i + 1) // pieces - tiles * i // pieces)


class GradScatter:
    def __init__(self, place, source, own, xland, zland, own_sem, x_s, x_r, z_s, z_r):
        self.place, self.own, self.xland, self.zland, self.z_s, self.z_r = place, own, xland, zland, z_s, z_r
        self.at, self.x, self.local, self.z = 0, [], [], []
        zi, e0, e3, end = place.zi, place.e0, place.e3, place.end
        self.order = [1 + 2 * e0, 3 - end, 2 - e0 + e3, 0]
        self.owners = [(zi + i) % 4 for i in self.order]
        self.routes = [
            (zi + 1 - 2 * e3, 3 * end, 1 - end),
            (self.owners[1], self.order[1] - 1, self.order[1]),
            (self.owners[2], self.order[2] - 1, self.order[2]),
        ]
        for k, j in enumerate(self.owners):
            cp = remote(source.at[2 * j + 1 - place.par], xland.at[j], x_s.at[k], x_r.at[k], place.pair)
            cp.start()
            self.x.append(cp)
            cp = pltpu.make_async_copy(source.at[2 * j + place.par], own.at[j], own_sem.at[k])
            cp.start()
            self.local.append(cp)

    def arrival(self, slot, sem):
        return remote(self.own.at[0], self.zland.at[slot], self.z_s.at[0], self.z_r.at[sem], self.place.pair)

    def step(self):
        k = self.at
        self.at += 1
        j = self.owners[k]
        self.local[k].wait()
        self.x[k].wait_recv()
        self.own[j] = (self.own[j].astype(F32) + self.xland[j].astype(F32)).astype(BF16)
        if k == 2:

            @pl.when(self.place.end == 0)
            def _():
                self.arrival(3, 0).wait_recv()
                self.own[j] = (self.own[j].astype(F32) + self.zland[3].astype(F32)).astype(BF16)

        to, slot, sem = self.routes[k]
        cp = remote(self.own.at[j], self.zland.at[slot], self.z_s.at[k], self.z_r.at[sem], (self.place.at(to), self.place.t))
        cp.start()
        self.z.append(cp)

    def steps(self, count=3):
        while self.at < min(3, count):
            self.step()

    def result(self):
        zi = self.place.zi
        self.local[3].wait()
        self.x[3].wait_recv()
        for slot in range(3):
            if slot == 1:
                self.arrival(1, 2).wait_recv()
            else:
                absent = 0 if slot == 0 else 3

                @pl.when(zi == absent)
                def _(slot=slot):
                    self.zland[slot] = jnp.zeros(self.zland.shape[1:], BF16)

                pl.when(zi != absent)(self.arrival(slot, slot + 1).wait_recv)
        total = self.own[zi].astype(F32) + self.xland[zi].astype(F32)
        for slot in range(3):
            total = total + self.zland[slot].astype(F32)
        return total

    def sent(self):
        for cp in self.x + self.z:
            cp.wait_send()

    @staticmethod
    def buffers(shape):
        return [pltpu.VMEM((4,) + shape, BF16)] * 3

    @staticmethod
    def scratch():
        return [pltpu.SemaphoreType.DMA((4,))] * 5


class TensorSum:
    def __init__(self, near, far, csend, crecv, ysend, yrecv, cs, cr, ys, yr):
        self.near, self.far, self.csend, self.crecv, self.ysend, self.yrecv = near, far, csend, crecv, ysend, yrecv
        self.cs, self.cr, self.ys, self.yr = cs, cr, ys, yr
        _, self.t, self.y, self.c, self.sib, self.yp = tensor_place()

    def core(self, i, value, k=0):
        sl = pl.ds(k * value.shape[0], value.shape[0])
        self.csend[i, sl, :] = value.astype(BF16)
        at = CHUNKS * i + k
        cp = remote(self.csend.at[i, sl], self.crecv.at[i, sl], self.cs.at[at], self.cr.at[at], self.sib)
        cp.start()
        return cp

    def start(self, product, ready=None, long=False):
        there, here = 2 * (1 - self.y), 2 * self.y
        rows = self.far.shape[0]
        ch = rows // CHUNKS
        part = lambda b, k: product(pl.ds(pl.multiple_of(b * rows + k * ch, ch), ch))
        self.ycs, self.c0 = [], []
        if long:
            for k in range(CHUNKS):
                sl = pl.ds(k * ch, ch)
                value = part(there + 1 - self.c, k)
                if ready is not None and k == 0:
                    ready()
                self.c0.append(self.core(0, value, k))
                self.far[sl, :] = part(there + self.c, k)
                self.along(k)
            self.c1 = self.core(1, product(block_rows(here + 1 - self.c, rows)))
        else:
            value = product(block_rows(there + 1 - self.c, rows))
            if ready is not None:
                ready()
            for k in range(CHUNKS):
                self.c0.append(self.core(0, value[k * ch : (k + 1) * ch, :], k))
            self.far[...] = product(block_rows(there + self.c, rows))
            self.c1 = self.core(1, product(block_rows(here + 1 - self.c, rows)))
            for k in range(CHUNKS):
                self.along(k)
        self.near[...] = product(block_rows(here + self.c, rows))
        self.c1.wait_recv()

    def along(self, k):
        ch = self.far.shape[0] // CHUNKS
        sl = pl.ds(k * ch, ch)
        self.c0[k].wait_recv()
        self.ysend[sl, :] = (self.far[sl, :] + self.crecv[0, sl, :].astype(F32)).astype(BF16)
        cp = remote(self.ysend.at[sl], self.yrecv.at[sl], self.ys.at[k], self.yr.at[k], self.yp)
        cp.start()
        self.ycs.append(cp)

    def chunk(self, k):
        ch = self.far.shape[0] // CHUNKS
        sl = pl.ds(k * ch, ch)
        self.ycs[k].wait_recv()
        return sl, self.near[sl, :] + self.crecv[1, sl, :].astype(F32) + self.yrecv[sl, :].astype(F32)

    def sent(self):
        for cp in self.c0 + [self.c1] + self.ycs:
            cp.wait_send()

    @staticmethod
    def scratch(rows, width):
        dma = pltpu.SemaphoreType.DMA
        vm = pltpu.VMEM
        return [
            vm((rows, width), F32), vm((rows, width), F32), vm((2, rows, width), BF16), vm((2, rows, width), BF16),
            vm((rows, width), BF16), vm((rows, width), BF16), dma((CHUNKS + 1,)), dma((CHUNKS + 1,)), dma((CHUNKS,)), dma((CHUNKS,)),
        ]


class RowSpread:
    def __init__(self, spread, rows, ys, yr, cs, cr, fs, fr):
        self.spread, self.rows = spread, rows
        self.sems = (ys, yr, cs, cr, fs, fr)
        _, self.t, self.y, self.c, self.sib, self.yp = tensor_place()
        self.parts, self.passed = [], []

    def at(self, owner, start, count):
        return self.spread.at[pl.ds(pl.multiple_of(owner * self.rows + start, 16), count)]

    def send(self, start, count):
        ys, yr, cs, cr, _, _ = self.sems
        k = len(self.parts)
        here = self.at(self.t, start, count)
        a = remote(here, here, ys.at[k], yr.at[k], self.yp)
        b = remote(here, here, cs.at[k], cr.at[k], self.sib)
        a.start()
        b.start()
        self.parts.append((a, b, start, count))

    def forward(self):
        fs, fr = self.sems[4:]
        for k, (a, _, start, count) in enumerate(self.parts):
            a.wait_recv()
            there = self.at(2 * (1 - self.y) + self.c, start, count)
            cp = remote(there, there, fs.at[k], fr.at[k], self.sib)
            cp.start()
            self.passed.append(cp)

    def finish(self):
        for (a, b, _, _), cp in zip(self.parts, self.passed):
            b.wait_recv()
            cp.wait_recv()
            a.wait_send()
            b.wait_send()
            cp.wait_send()

    @staticmethod
    def scratch(parts=CHUNKS):
        return [pltpu.SemaphoreType.DMA((parts,))] * 6


def shaped(shape, dtype):
    return jax.ShapeDtypeStruct(shape, dtype)


class Placed:
    def __init__(self, value, moves):
        self.value, self.moves = value, moves


def hbm(value):
    return Placed(value, False)


def late(value):
    return Placed(value, True)


def named_kernel(name, collective_id, body, ins, outs, scratch):
    vm, anywhere = pl.BlockSpec(memory_space=pltpu.VMEM), pl.BlockSpec(memory_space=pl.ANY)
    flat = []
    for v in scratch.values():
        flat.extend(v if isinstance(v, list) else [v])
    placed = {k: v for k, v in [*ins.items(), *outs.items()] if isinstance(v, Placed)}
    bare = lambda v: v.value if isinstance(v, Placed) else v
    specs = lambda group: [anywhere if k in placed else vm for k in group]
    moving = [k for k, v in placed.items() if v.moves]
    buffers = [pltpu.VMEM(placed[k].value.shape, placed[k].value.dtype) for k in moving]
    if moving:
        buffers.append(pltpu.SemaphoreType.DMA((len(moving),)))

    def kernel(*refs):
        left = list(refs)
        n = SimpleNamespace()
        for k in [*ins, *outs]:
            setattr(n, k, left.pop(0))
        for k, v in scratch.items():
            if isinstance(v, list):
                setattr(n, k, [left.pop(0) for _ in v])
            else:
                setattr(n, k, left.pop(0))
        loads, stores, going = {}, {}, []
        for i, k in enumerate(moving):
            outer, inner, sem = getattr(n, k), left[i], left[-1].at[i]
            if k in ins:
                loads[id(inner)] = pltpu.make_async_copy(outer, inner, sem)
                loads[id(inner)].start()
            else:
                stores[id(inner)] = pltpu.make_async_copy(inner, outer, sem)
            setattr(n, k, inner)

        def need(*wanted):
            for ref in wanted:
                if id(ref) in loads:
                    loads.pop(id(ref)).wait()

        def done(*ready):
            for ref in ready:
                if id(ref) in stores:
                    going.append(stores.pop(id(ref)))
                    going[-1].start()

        n.need, n.done = need, done
        body(n)
        for cp in loads.values():
            cp.wait()
        for cp in stores.values():
            cp.start()
        for cp in going + list(stores.values()):
            cp.wait()

    talks = {} if collective_id is None else dict(collective_id=collective_id, has_side_effects=True)
    got = pl.pallas_call(
        kernel,
        out_shape=[bare(v) for v in outs.values()],
        in_specs=specs(ins),
        out_specs=specs(outs),
        scratch_shapes=flat + buffers,
        compiler_params=pltpu.CompilerParams(vmem_limit_bytes=VMEM_BYTES, **talks),
        name=name,
    )(*[bare(v) for v in ins.values()])
    return SimpleNamespace(**dict(zip(outs, got)))


def block_rows(b, rows):
    return pl.ds(pl.multiple_of(b * rows, rows), rows)


def add_sums(sums, parts):
    parts = [jnp.sum(v, axis=0, keepdims=True) for v in parts]
    return parts if sums is None else [a + b for a, b in zip(sums, parts)]


def forward_rows(reduce, spread, spread_ref, resid, bias, gain, offset, out, rows):
    ch = rows // CHUNKS
    for k in range(CHUNKS):
        sl, total = reduce.chunk(k)
        value = resid[sl, :] + (total + bias[...])
        out[sl, :] = value
        cen, rstd = centre(value)
        low = (cen * rstd * gain[...] + offset[...]).astype(BF16)
        spread_ref[pl.ds(pl.multiple_of(reduce.t * rows + k * ch, ch), ch), :] = low
        spread.send(k * ch, ch)


def backward_rows(reduce, spread, spread_ref, x, gain, before, out, sum_refs, rows):
    ch = rows // CHUNKS
    sums = None
    for k in range(CHUNKS):
        sl, total = reduce.chunk(k)
        back, xhat = norm_back(total, x[sl, :], gain[...])
        grad = before[sl, :] + back
        out[sl, :] = grad
        low = grad.astype(BF16)
        spread_ref[pl.ds(pl.multiple_of(reduce.t * rows + k * ch, ch), ch), :] = low
        spread.send(k * ch, ch)
        sums = add_sums(sums, [low.astype(F32), total * xhat, total])
    for ref, v in zip(sum_refs, sums):
        ref[...] = v


def head_stats(u, mask, size):
    mean = jnp.sum(u, axis=-1, keepdims=True) * (1.0 / size)
    cen = (u - mean) * mask
    spread = jnp.sum(cen * cen, axis=-1, keepdims=True) * (1.0 / size)
    return cen, lax.rsqrt(spread + EPSILON)


def head_norm(u, mask, gain, offset, size):
    cen, rstd = head_stats(u, mask, size)
    return cen * rstd * gain + offset


def turn(u, cosine, sine):
    return u * cosine + pltpu.roll(u, LANES // 2, 1) * sine


def turn_back(u, cosine, sine):
    return u * cosine - pltpu.roll(u, LANES // 2, 1) * sine


def head_back(grad, u, mask, gain, size):
    cen, rstd = head_stats(u, mask, size)
    xhat = cen * rstd
    dg = grad * gain
    mean = jnp.sum(dg, axis=-1, keepdims=True) * (1.0 / size)
    inner = jnp.sum(dg * xhat, axis=-1, keepdims=True) * (1.0 / size)
    back = rstd * ((dg - mean) * mask - xhat * inner)
    return back, jnp.sum(grad * xhat, axis=0, keepdims=True), jnp.sum(grad, axis=0, keepdims=True)


def head_at(h):
    return pl.ds(h * LANES, LANES)


def in_halves(count, step, between):
    if between is None:
        lax.fori_loop(0, count, step, 0)
    else:
        for i in range(2):
            lax.fori_loop(i * count // 2, (i + 1) * count // 2, step, 0)
            between()


def attend(q_ref, k_ref, v_ref, out_ref, lse_ref, heads, scale, block, real_keys, between=None):
    queries, keys = q_ref.shape[0], k_ref.shape[0]

    def step(i, _):
        here = pl.ds(pl.multiple_of(i * block, block), block)
        for h in range(heads):
            hs = head_at(h)
            scores = dot_nt(k_ref[:, hs], q_ref[here, hs]) * scale
            if real_keys < keys:
                place = lax.broadcasted_iota(jnp.int32, scores.shape, 0)
                scores = jnp.where(place < real_keys, scores, NEGATIVE)
            highest = jnp.max(scores, axis=0, keepdims=True)
            exponent = jnp.exp(scores - highest)
            denominator = jnp.sum(exponent, axis=0, keepdims=True)
            probs = (exponent * (1.0 / denominator)).astype(BF16)
            mixed = dot_tn(v_ref[:, hs], probs)
            out_ref[here, hs] = mixed.T.astype(BF16)
            lse_ref[i, pl.ds(h, 1), :] = highest + jnp.log(denominator)
        return 0

    in_halves(queries // block, step, between)


def attend_back(q_ref, k_ref, v_ref, do_ref, lse_ref, dq_ref, dk_ref, dv_ref, heads, scale, block, real_keys, between=None):
    queries, keys = q_ref.shape[0], k_ref.shape[0]
    dk_ref[...] = jnp.zeros(dk_ref.shape, F32)
    dv_ref[...] = jnp.zeros(dv_ref.shape, F32)

    def step(i, _):
        here = pl.ds(pl.multiple_of(i * block, block), block)
        for h in range(heads):
            hs = head_at(h)
            q, k, v, do = q_ref[here, hs], k_ref[:, hs], v_ref[:, hs], do_ref[here, hs]
            scores = dot_nt(k, q) * scale
            if real_keys < keys:
                place = lax.broadcasted_iota(jnp.int32, scores.shape, 0)
                scores = jnp.where(place < real_keys, scores, NEGATIVE)
            probs = jnp.exp(scores - lse_ref[i, pl.ds(h, 1), :])
            grad_probs = dot_nt(v, do)
            inner = jnp.sum(probs * grad_probs, axis=0, keepdims=True)
            grad_scores = (probs * (grad_probs - inner)).astype(BF16)
            dv_ref[:, hs] += dot_nn(probs.astype(BF16), do)
            dk_ref[:, hs] += dot_nn(grad_scores, q) * scale
            dq_ref[here, hs] = dot_tn(k, grad_scores).T * scale
        return 0

    in_halves(queries // block, step, between)


def exact(left, right):
    return jnp.dot(left, right, precision=lax.Precision.HIGHEST, preferred_element_type=F32)


def my_cols(whole, t, cols):
    return sum(jnp.where(t == s, whole[:, s * cols : (s + 1) * cols], 0.0) for s in range(4))


def prepare(t, cols, n):
    n.gain_wide[...] = exact(n.head_gain[...], n.one[...])
    n.offset_wide[...] = exact(n.head_bias[...], n.one[...])
    mine = my_cols(n.column_bias[...], t, cols)
    n.bias_wide[...] = exact(mine, n.fold_f32[...])
    angles = lax.dot_general(
        n.positions[...].astype(F32), n.lanes[0:2, :], (((0,), (0,)), ((), ())), precision=lax.Precision.HIGHEST,
        preferred_element_type=F32,
    )
    n.cosine[...] = jnp.cos(angles) * n.mask[...]
    n.sine[...] = jnp.sin(angles) * n.lanes[2:3, :]
    n.done(n.cosine, n.sine)
    return mine[4:5, :]


def first_body(dp, own, size, scale, heads, block, n):
    _, t, _, _, _, _ = tensor_place()
    d = lax.axis_index("dp")
    rows, width = n.residual.shape
    cols = n.skip_send.shape[2]
    span = heads * LANES
    place = DpPlace(dp) if own else None
    peers = [(d, (t + o) % 4) for o in range(1, 4)] + (place.others() if own else [])
    bar = greet(peers)
    mine = block_rows(t, rows)
    kept = [
        pltpu.make_async_copy(n.latent, n.joined0.at[mine], n.own_sem.at[0]),
        pltpu.make_async_copy(n.skip_states, n.joined1.at[mine], n.own_sem.at[1]),
    ]
    if own:
        shards = [(n.skip_in, n.skip_full), (n.project_in, n.p_land), (n.out_in, n.out_land), (n.query_in, n.query_g),
                  (n.keyval_in.at[0], n.key_g), (n.keyval_in.at[1], n.value_g), (n.cross_out_in, n.cross_out_g),
                  (n.down_in.at[pl.ds(0, n.down_g.shape[1])], n.down_g)]
        kept += [pltpu.make_async_copy(a, b.at[d], n.own_sem.at[2 + i]) for i, (a, b) in enumerate(shards)]
    for cp in kept:
        cp.start()
    pl.semaphore_wait(bar, len(peers))
    spreads = [RowSpread(n.joined0, rows, *n.spread0), RowSpread(n.joined1, rows, *n.spread1)]
    for cp, spread in zip(kept, spreads):
        cp.wait()
        spread.send(0, rows)
    if own:
        count = jnp.broadcast_to(n.true_count[...].astype(F32), (1, LANES))
        share = n.shift_in.shape[0]
        for q in range(dp):
            n.small[q, :, pl.ds(0, share)] = n.condition[:, pl.ds(q * share, share)].astype(F32)
            n.small[q, :, pl.ds(n.small.shape[2] - LANES, LANES)] = count
        n.small_land[d] = n.small[d]
        smalls = ToAll(place, lambda q: n.small.at[q], n.small_land, n.a_s, n.a_r)
        gathers = Gathers(place, 3, *n.gather_sems)
        gathers.add(n.skip_in, n.skip_full, 2)
        smalls.arrived()
        given = jnp.concatenate([n.small_land[i] for i in range(dp)], axis=0)
        n.silu[...] = jax.nn.silu(given[:, : n.shift_in.shape[0]]).astype(BF16)
        n.counted[...] = jnp.sum(given[:, given.shape[1] - LANES :], axis=0, keepdims=True)
        part = dot_nn(n.silu[...], n.shift_in[...])
        for i in range(dp):
            n.shift_part[i] = part[i : i + 1, :]
        n.shift_land[d] = n.shift_part[d]
        shifts = ToAll(place, lambda q: n.shift_part.at[q], n.shift_land, n.b_s, n.b_r)
        for i in range(3):
            gathers.add(n.project_in.at[i], n.p_land.at[:, i])
    bias_skip = prepare(t, cols, n)
    if own:
        gathers.forward()
    spreads[0].forward()
    if own:
        gathers.add(n.out_in, n.out_land)
        gathers.add(n.query_in, n.query_g)
        gathers.add(n.keyval_in.at[0], n.key_g)
        gathers.add(n.keyval_in.at[1], n.value_g)
        gathers.add(n.cross_out_in, n.cross_out_g)
        gathers.forward()
    spreads[0].finish()
    if own:
        gathers.add(n.down_in.at[pl.ds(0, n.down_g.shape[1])], n.down_g, 3, PairFirst)
        gathers.arrived(0, 2)
        kept[2].wait()
        half = dp // 2
        skip_half = lambda i: n.skip_full[pl.ds(i * half, half)].reshape(width, cols)
    else:
        skip_half = lambda i: n.skip_in[pl.ds(i * width, width), :]
    for b in range(4):
        here = pl.ds(b * rows, rows)
        n.pre[here, pl.ds(0, cols)] = dot_nn(n.joined0[here, :], skip_half(0))
    spreads[1].forward()
    if own:
        gathers.forward()
    spreads[1].finish()
    copies = []
    for o in (2, 3, 1, 0):
        b = (t + o) % 4
        here = block_rows(b, rows)
        value = (n.pre[here, pl.ds(0, cols)] + dot_nn(n.joined1[here, :], skip_half(1)) + bias_skip).astype(BF16)
        if o:
            n.skip_send[o] = value
            cp = remote(n.skip_send.at[o], n.skip_recv.at[t], n.p_s.at[o], n.p_r.at[o], (d, b))
            cp.start()
            copies.append(cp)
        else:
            n.skip_recv[t] = value
    if own:
        shifts.arrived()
        shift = n.row_bias[pl.ds(3, 1), :] + sum(n.shift_land[i] for i in range(dp))
    else:
        shift = n.shift_in[...]
    for cp in copies:
        cp.wait_recv()
    for s in range(4):
        n.skipped[:, s * cols : (s + 1) * cols] = n.skip_recv[s]
    spread = RowSpread(n.first_all, rows, *n.spread2)
    ch = rows // CHUNKS
    for k in range(CHUNKS):
        sl = pl.ds(k * ch, ch)
        cen, rstd = centre(n.skipped[sl, :].astype(F32))
        resid = cen * rstd * n.norm_gain[pl.ds(0, 1), :] + n.norm_bias[pl.ds(0, 1), :]
        n.residual[sl, :] = resid
        cen, rstd = centre(resid)
        first = cen * rstd * n.norm_gain[pl.ds(1, 1), :] + n.norm_bias[pl.ds(1, 1), :] + shift
        n.first_all[pl.ds(pl.multiple_of(t * rows + k * ch, ch), ch), :] = first.astype(BF16)
        spread.send(k * ch, ch)
    if own:
        gathers.forward()
    spread.forward()
    if own:
        gathers.forward()
    spread.finish()
    for cp in copies:
        cp.wait_send()
    n.done(n.joined0, n.joined1, n.skip_full, n.skipped, n.residual, n.first_all)
    for part in range(3):
        if own:
            gathers.arrived(2 + part, 3 + part)
            if part == 0:
                kept[3].wait()
            narrow = n.p_land[:, part].reshape(width, cols)
        else:
            narrow = n.project_in[part]
        n.project_wide[part] = dot_nn(narrow, n.fold[...]).astype(BF16)
    if own:
        gathers.forward(2)

    def project(i, _):
        here = pl.ds(pl.multiple_of(i * block, block), block)
        for part in range(3):
            out = dot_nn(n.first_all[here, :], n.project_wide[part])
            if part != 1:
                out = out + n.bias_wide[pl.ds(part // 2, 1), :]
            if part < 2:
                n.pre[here, pl.ds(part * span, span)] = out
                for h in range(heads):
                    u = out[:, h * LANES : (h + 1) * LANES]
                    val = head_norm(u, n.mask[...], n.gain_wide[pl.ds(part, 1), :], n.offset_wide[pl.ds(part, 1), :], size)
                    val = turn(val, n.cosine[here, :], n.sine[here, :])
                    n.low[here, pl.ds(part * span + h * LANES, LANES)] = val.astype(BF16)
            else:
                n.low[here, pl.ds(part * span, span)] = out.astype(BF16)
        return 0

    lax.fori_loop(0, n.low.shape[0] // block, project, 0)
    n.done(n.project_wide, n.pre, n.low)
    if own:
        gathers.forward(2)
    attend(
        n.low.at[:, pl.ds(0, span)], n.low.at[:, pl.ds(span, span)], n.low.at[:, pl.ds(2 * span, span)],
        n.padded, n.lse, heads, scale, block, n.low.shape[0], gathers.forward if own else None,
    )
    n.mixed[...] = dot_nt(n.padded[...], n.fold[...]).astype(BF16)
    n.done(n.mixed)
    if own:
        gathers.arrived(5, 6)
        kept[4].wait()
        out_t = lambda: n.out_land[...].reshape(width, cols)
    else:
        out_t = lambda: n.out_in[...]
    reduce = TensorSum(*n.sum)
    reduce.start(lambda here: dot_nt(n.mixed[here, :], out_t()))
    if own:
        gathers.forward()
    spread = RowSpread(n.third_all, rows, *n.spread3)
    forward_rows(
        reduce, spread, n.third_all, n.residual, n.row_bias.at[pl.ds(0, 1)], n.norm_gain.at[pl.ds(2, 1)],
        n.norm_bias.at[pl.ds(2, 1)], n.second, rows,
    )
    n.done(n.second)
    if own:
        gathers.forward()
    spread.forward()
    if own:
        gathers.end(len(gathers.pieces))
    spread.finish()
    reduce.sent()
    if own:
        gathers.arrived(6, len(gathers.pieces))
        for cp in kept[5:]:
            cp.wait()
        for g in (gathers, smalls, shifts):
            g.sent()


def cross_body(dp, own, size, scale, heads, block, real, n):
    rows, width = n.second.shape
    span = heads * LANES
    d, _, _, _, sib, yp = tensor_place()
    place = DpPlace(dp) if own else None
    peers = [sib, yp] + (place.near() if own else [])
    bar = greet(peers)
    pl.semaphore_wait(bar, len(peers))
    if own:
        gathers = Gathers(place, 3, *n.gather_sems)
        gathers.add(n.up_in, n.up_g, 4)
        down_in = n.down_in.at[pl.ds(n.down_in.shape[0] - n.down_g.shape[1], n.down_g.shape[1])]
        gathers.add(down_in, n.down_g, 1, PairFirst)
        kept = [pltpu.make_async_copy(a, b.at[d], n.own_sem.at[i])
                for i, (a, b) in enumerate(((n.up_in, n.up_g), (down_in, n.down_g)))]
        for cp in kept:
            cp.start()
    n.need(n.query, n.key, n.value, n.text)
    n.query_wide[...] = dot_nn(n.query[...], n.fold[...]).astype(BF16)
    for part, w in enumerate((n.key, n.value)):
        n.keyval_wide[part] = dot_nn(w[...], n.fold[...]).astype(BF16)
        out = dot_nn(n.text[...], n.keyval_wide[part])
        if part == 0:
            n.text_pre[...] = out
            for h in range(heads):
                val = head_norm(out[:, h * LANES : (h + 1) * LANES], n.mask[...], n.head_gain[pl.ds(3, 1), :], n.head_bias[pl.ds(3, 1), :], size)
                n.text_low[:, head_at(h)] = val.astype(BF16)
        else:
            n.text_low[:, pl.ds(span, span)] = (out + n.bias_wide[pl.ds(3, 1), :]).astype(BF16)
    n.need(n.third_all, n.cosine, n.sine)

    def project(i, _):
        here = pl.ds(pl.multiple_of(i * block, block), block)
        out = dot_nn(n.third_all[here, :], n.query_wide[...]) + n.bias_wide[pl.ds(2, 1), :]
        n.pre[here, :] = out
        for h in range(heads):
            val = head_norm(out[:, h * LANES : (h + 1) * LANES], n.mask[...], n.head_gain[pl.ds(2, 1), :], n.head_bias[pl.ds(2, 1), :], size)
            n.low[here, head_at(h)] = turn(val, n.cosine[here, :], n.sine[here, :]).astype(BF16)
        return 0

    lax.fori_loop(0, n.low.shape[0] // block, project, 0)
    n.done(n.query_wide, n.keyval_wide, n.pre, n.low)
    attend(n.low, n.text_low.at[:, pl.ds(0, span)], n.text_low.at[:, pl.ds(span, span)], n.padded, n.lse, heads, scale, block, real)
    n.mixed[...] = dot_nt(n.padded[...], n.fold[...]).astype(BF16)
    n.need(n.cross_out, n.second)
    reduce = TensorSum(*n.sum)
    reduce.start(lambda here: dot_nt(n.mixed[here, :], n.cross_out[...]))
    n.done(n.mixed)
    if own:
        gathers.forward(2)
    spread = RowSpread(n.fourth_all, rows, *n.spread)
    forward_rows(
        reduce, spread, n.fourth_all, n.second, n.row_bias.at[pl.ds(1, 1)], n.norm_gain.at[pl.ds(3, 1)],
        n.norm_bias.at[pl.ds(3, 1)], n.third_sum, rows,
    )
    if own:
        gathers.forward()
    spread.forward()
    if own:
        gathers.forward()
    spread.finish()
    reduce.sent()
    if own:
        gathers.forward()
        gathers.arrived(0, len(gathers.pieces))
        for cp in kept:
            cp.wait()
        gathers.sent()


def load_down(own, n):
    if not own:
        return [], lambda: n.down_t[...]
    first = n.down_a.shape[1]
    copies = [
        pltpu.make_async_copy(n.down_a, n.down_t.at[:, pl.ds(0, first)], n.down_sem.at[0]),
        pltpu.make_async_copy(n.down_b, n.down_t.at[:, pl.ds(first, n.down_b.shape[1])], n.down_sem.at[1]),
    ]
    for cp in copies:
        cp.start()
    return copies, lambda: n.down_t[...].reshape(-1, n.down_t.shape[2])


def feed_body(own, n):
    rows = n.third_sum.shape[0]
    _, t, _, _, sib, yp = tensor_place()
    bar = greet((sib, yp))
    down_copies, down_t = load_down(own, n)
    hidden = n.up.shape[1]
    tiles = hidden // LANES
    mine = sum(jnp.where(t == s, n.hidden_bias[pl.ds(s * tiles, tiles), :], 0.0) for s in range(4))
    hidden_bias = jnp.concatenate([mine[i : i + 1, :] for i in range(tiles)], axis=1)
    seat = t * rows + lax.broadcasted_iota(jnp.int32, (rows, 1), 0)
    mask = lax.dot_general(
        n.loss_mask[...].astype(F32), jnp.ones((1, LANES), F32), (((0,), (0,)), ((), ())), preferred_element_type=F32
    )[:, 0:1]
    weight = mask * (seat < n.true_count[...]).astype(F32)
    weight = (n.total[...] / n.counted[:, 0:1]) * weight
    n.need(n.fourth_all, n.up)
    root, cube = float(np.sqrt(2.0 / np.pi)), 0.044715

    def product(here):
        x = dot_nn(n.fourth_all[here, :], n.up[...]) + hidden_bias
        square = x * x
        th = jnp.tanh(root * (x + cube * (square * x)))
        cdf = 0.5 * (1.0 + th)
        active = (x * cdf).astype(BF16)
        n.active[here, :] = active
        slope = cdf + (0.5 * root) * x * (1.0 - th * th) * (1.0 + (3.0 * cube) * square)
        n.slope[here, :] = slope.astype(BF16)
        while down_copies:
            down_copies.pop().wait()
        return dot_nt(active, down_t())

    reduce = TensorSum(*n.sum)
    reduce.start(product, lambda: pl.semaphore_wait(bar, 2), long=True)
    n.done(n.active, n.slope)
    n.need(n.third_sum, n.teacher)
    spread = RowSpread(n.grad_all, rows, *n.spread)
    ch = rows // CHUNKS
    sums = None
    for k in range(CHUNKS):
        sl, total = reduce.chunk(k)
        final = n.third_sum[sl, :] + (total + n.row_bias[pl.ds(2, 1), :])
        n.block_out[sl, :] = final.astype(BF16)
        grad = weight[k * ch : (k + 1) * ch, :] * (final - n.teacher[sl, :].astype(F32))
        n.grad_final[sl, :] = grad
        low = grad.astype(BF16)
        n.grad_all[pl.ds(pl.multiple_of(t * rows + k * ch, ch), ch), :] = low
        spread.send(k * ch, ch)
        sums = add_sums(sums, [low.astype(F32)])
    n.bias_mlp[...] = sums[0]
    n.done(n.block_out, n.grad_final)
    spread.forward()
    spread.finish()
    reduce.sent()


def feed_back_body(dp, own, n):
    rows = n.third_sum.shape[0]
    _, _, _, _, sib, yp = tensor_place()
    place = DpPlace(dp) if own else None
    peers = [sib, yp] + (place.near() if own else [])
    bar = greet(peers)
    down_copies, down_t = load_down(own, n)
    n.need(n.grad_all, n.active)
    n.grad_down[...] = dot_tn(n.grad_all[...], n.active[...]).astype(BF16).reshape(n.grad_down.shape)
    pl.semaphore_wait(bar, len(peers))
    if own:
        down = GradScatter(place, n.grad_down, *n.down_bufs, *n.down_sems)

    def product(here):
        upper = (dot_nn(n.grad_all[here, :], down_t()) * n.slope[here, :].astype(F32)).astype(BF16)
        n.upper[here, :] = upper
        return dot_nt(upper, n.up[...])

    for cp in down_copies:
        cp.wait()
    n.need(n.slope, n.up)
    reduce = TensorSum(*n.sum)
    reduce.start(product, long=True)
    n.need(n.fourth_all, n.third_sum, n.grad_final)
    n.bias_hidden[...] = sum(
        jnp.sum(n.upper[pl.ds(b * rows, rows), :].astype(F32), axis=0, keepdims=True) for b in range(4)
    )
    n.grad_up[...] = dot_tn(n.fourth_all[...], n.upper[...]).astype(BF16).reshape(n.grad_up.shape)
    n.done(n.grad_up)
    spread = RowSpread(n.c_all, rows, *n.spread)
    if own:
        down.steps(1)
    backward_rows(reduce, spread, n.c_all, n.third_sum, n.norm_gain.at[pl.ds(3, 1)], n.grad_final, n.grad_third, (n.sum0, n.sum1, n.sum2), rows)
    if own:
        down.steps(2)
    spread.forward()
    if own:
        down.steps()
    spread.finish()
    reduce.sent()
    if own:
        n.down_mine[...] = down.result()
        down.sent()


def spread_heads(n, rows_in, w, do, block):
    def spread(i, _):
        here = pl.ds(pl.multiple_of(i * block, block), block)
        narrow = dot_nn(rows_in[here, :], w[...]).astype(BF16)
        do[here, :] = dot_nn(narrow, n.fold[...]).astype(BF16)
        return 0

    lax.fori_loop(0, do.shape[0] // block, spread, 0)


def cross_back_body(dp, own, size, scale, heads, block, real, n):
    rows = n.second.shape[0]
    span = heads * LANES
    d, t, _, _, sib, yp = tensor_place()
    place = DpPlace(dp) if own else None
    peers = [sib, yp] + (place.near() if own else [])
    bar = greet(peers)
    pl.semaphore_wait(bar, len(peers))
    if own:
        up = GradScatter(place, n.grad_up, *n.up_bufs, *n.up_sems)
    n.need(n.c_all, n.cross_out)
    spread_heads(n, n.c_all, n.cross_out, n.do, block)
    n.need(n.low, n.text_low)
    attend_back(
        n.low, n.text_low.at[:, pl.ds(0, span)], n.text_low.at[:, pl.ds(span, span)],
        n.do, n.lse, n.dq, n.dk, n.dv, heads, scale, block, real,
    )
    n.gains[...] = jnp.zeros(n.gains.shape, F32)
    n.offsets[...] = jnp.zeros(n.offsets.shape, F32)
    n.sums[...] = jnp.zeros(n.sums.shape, F32)

    def finish(i, _):
        here = pl.ds(pl.multiple_of(i * block, block), block)
        for h in range(heads):
            hs = head_at(h)
            grad = turn_back(n.dq[here, hs], n.cosine[here, :], n.sine[here, :])
            grad, g, o = head_back(grad, n.pre[here, hs], n.mask[...], n.head_gain[pl.ds(2, 1), :], size)
            n.gains[pl.ds(0, 1), :] += g
            n.offsets[pl.ds(0, 1), :] += o
            grad_low = grad.astype(BF16)
            n.p[here, hs] = grad_low
            n.sums[:, hs] += jnp.sum(grad_low.astype(F32), axis=0, keepdims=True)
        return 0

    if own:
        up.steps(1)
    n.need(n.pre, n.cosine, n.sine)
    lax.fori_loop(0, n.p.shape[0] // block, finish, 0)
    n.need(n.query_wide)
    reduce = TensorSum(*n.sum)
    reduce.start(lambda here: dot_nt(n.p[here, :], n.query_wide[...]))
    if own:
        up.steps(2)
    n.need(n.text_pre, n.mixed, n.third_all, n.text, n.keyval_wide, n.second, n.grad_third)
    for h in range(heads):
        hs = head_at(h)
        grad, g, o = head_back(n.dk[:, hs], n.text_pre[:, hs], n.mask[...], n.head_gain[pl.ds(3, 1), :], size)
        n.gains[pl.ds(1, 1), :] += g
        n.offsets[pl.ds(1, 1), :] += o
        n.text_p[:, hs] = grad.astype(BF16)
        low_v = n.dv[:, hs].astype(BF16)
        n.text_p[:, pl.ds(span + h * LANES, LANES)] = low_v
        n.text_sums[:, hs] = jnp.sum(low_v.astype(F32), axis=0, keepdims=True)
    parts = n.grads.shape[0]

    def put(start, value):
        count = value.shape[0] // parts
        n.grads[:, pl.ds(start, count)] = value.astype(BF16).reshape(parts, count, value.shape[1])
        return start + count

    at = put(0, dot_tn(n.c_all[...], n.mixed[...]))
    at = put(at, dot_tn(n.third_all[...], dot_nt(n.p[...], n.fold[...]).astype(BF16)))
    for part in range(2):
        narrow = dot_nt(n.text_p[:, pl.ds(part * span, span)], n.fold[...]).astype(BF16)
        at = put(at, dot_tn(n.text[...], narrow))
    n.done(n.grads)
    n.grad_text[...] = (
        dot_nt(n.text_p[:, pl.ds(0, span)], n.keyval_wide[0]) + dot_nt(n.text_p[:, pl.ds(span, span)], n.keyval_wide[1])
    ).astype(BF16)
    if own:
        up.steps()
    spread = RowSpread(n.s_all, rows, *n.spread)
    backward_rows(reduce, spread, n.s_all, n.second, n.norm_gain.at[pl.ds(2, 1)], n.grad_third, n.grad_second, (n.sum0, n.sum1, n.sum2), rows)
    spread.forward()
    spread.finish()
    reduce.sent()
    if own:
        n.up_mine[...] = up.result()
        up.sent()


class TextSum:
    def __init__(self, part, total, land, yland, back, sems):
        _, _, _, self.c, self.sib, self.yp = tensor_place()
        self.part, self.total, self.land, self.yland, self.last, self.sems = part, total, land, yland, back, sems
        self.half = piece_rows(part.shape[0], 2, 1)
        self.copies = [remote(part, land, sems.at[0], sems.at[1], self.sib)]
        self.copies[0].start()

    def here(self, c):
        return pl.ds(pl.multiple_of(c * (self.part.shape[0] - self.half), 16), self.half)

    def along(self):
        self.copies[0].wait_recv()
        self.total[...] = (self.part[...].astype(F32) + self.land[...].astype(F32)).astype(BF16)
        cp = remote(self.total.at[self.here(self.c)], self.yland, self.sems.at[2], self.sems.at[3], self.yp)
        cp.start()
        self.copies.append(cp)

    def back(self):
        self.copies[1].wait_recv()
        self.copies[1].wait_send()
        mine = self.here(self.c)
        self.yland[...] = (self.total[mine, :].astype(F32) + self.yland[...].astype(F32)).astype(BF16)
        self.copies[0].wait_send()
        cp = remote(self.yland, self.last, self.sems.at[4], self.sems.at[5], self.sib)
        cp.start()
        self.copies.append(cp)

    def result(self, out):
        self.copies[2].wait_recv()
        out[self.here(self.c), :] = self.yland[...].astype(F32)
        out[self.here(1 - self.c), :] = self.last[...].astype(F32)
        self.copies[2].wait_send()


def self_back_body(dp, own, size, scale, heads, block, n):
    span = heads * LANES
    _, _, _, _, sib, yp = tensor_place()
    place = DpPlace(dp) if own else None
    peers = [sib, yp] + (place.near() if own else [])
    bar = greet(peers)
    pl.semaphore_wait(bar, len(peers))
    text = TextSum(n.text_part, n.text_total, n.text_land, n.text_yland, n.text_back, n.text_sems)
    if own:
        few = GradScatter(place, n.few_grads, *n.few_bufs, *n.few_sems)
    n.need(n.s_all, n.out_t)
    spread_heads(n, n.s_all, n.out_t, n.do, block)
    text.along()
    n.need(n.low)
    attend_back(
        n.low.at[:, pl.ds(0, span)], n.low.at[:, pl.ds(span, span)], n.low.at[:, pl.ds(2 * span, span)],
        n.do, n.lse, n.dq, n.dk, n.dv, heads, scale, block, n.low.shape[0], few.step if own else None,
    )
    text.back()
    n.need(n.pre, n.cosine, n.sine)
    n.gains[...] = jnp.zeros(n.gains.shape, F32)
    n.offsets[...] = jnp.zeros(n.offsets.shape, F32)
    n.sums[...] = jnp.zeros(n.sums.shape, F32)

    def finish(i, _):
        here = pl.ds(pl.multiple_of(i * block, block), block)
        for part, grad_ref in enumerate((n.dq, n.dk, n.dv)):
            for h in range(heads):
                hs = head_at(h)
                wide = pl.ds(part * span + h * LANES, LANES)
                grad = grad_ref[here, hs]
                if part < 2:
                    grad = turn_back(grad, n.cosine[here, :], n.sine[here, :])
                    grad, g, o = head_back(grad, n.pre[here, wide], n.mask[...], n.head_gain[pl.ds(part, 1), :], size)
                    n.gains[pl.ds(part, 1), :] += g
                    n.offsets[pl.ds(part, 1), :] += o
                grad_low = grad.astype(BF16)
                n.p[here, wide] = grad_low
                if part != 1:
                    n.sums[:, wide] += jnp.sum(grad_low.astype(F32), axis=0, keepdims=True)
            n.p_low[part, here, :] = dot_nt(n.p[here, pl.ds(part * span, span)], n.fold[...]).astype(BF16)
        return 0

    lax.fori_loop(0, n.p.shape[0] // block, finish, 0)
    by_place = lambda v: v.astype(BF16).reshape(n.grad_out.shape)
    if own:
        few.steps()
    n.done(n.p)
    n.need(n.mixed, n.first_all)
    n.grad_out[...] = by_place(dot_tn(n.s_all[...], n.mixed[...]))
    for part in range(3):
        n.grad_project[:, part] = by_place(dot_tn(n.first_all[...], n.p_low[part]))
    n.done(n.grad_out, n.grad_project)
    text.result(n.grad_text)
    if own:
        n.few_mine[...] = few.result()
        few.sent()


PACK_ROWS, PACK_SUMS = 8, 16


def last_body(dp, own, n):
    _, t, _, _, _, _ = tensor_place()
    d = lax.axis_index("dp")
    rows, width = n.residual.shape
    cols = n.krecv.shape[1]
    place = DpPlace(dp) if own else None
    peers = [(d, (t + o) % 4) for o in range(1, 4)] + (place.others() if own else [])
    bar = greet(peers)
    reduce = TensorSum(*n.sum)
    scatters = []

    def scatter(source, buffers):
        i = len(scatters)
        scatters.append(GradScatter(place, source, *buffers, *n.scatter_sems[5 * i : 5 * i + 5]))

    def ready():
        pl.semaphore_wait(bar, len(peers))
        if own:
            scatter(n.grad_out, n.out_bufs)
            for i in range(3):
                scatter(n.grad_project.at[:, i], n.project_bufs[3 * i : 3 * i + 3])

    def product(here):
        span = n.project_wide.shape[2]
        total = dot_nt(n.p[here, pl.ds(0, span)], n.project_wide[0])
        for part in range(1, 3):
            total = total + dot_nt(n.p[here, pl.ds(part * span, span)], n.project_wide[part])
        return total

    n.need(n.p, n.project_wide)
    reduce.start(product, ready)
    n.need(n.residual, n.grad_second, n.skipped)
    if own:
        scatters[0].steps()
    sums = None
    for k in range(CHUNKS):
        sl, total = reduce.chunk(k)
        back, xhat = norm_back(total, n.residual[sl, :], n.norm_gain[pl.ds(1, 1), :])
        grad = n.grad_second[sl, :] + back
        back0, xhat0 = norm_back(grad, n.skipped[sl, :].astype(F32), n.norm_gain[pl.ds(0, 1), :])
        low = back0.astype(BF16)
        for s in range(4):
            n.ksend[s, sl, :] = low[:, s * cols : (s + 1) * cols]
        sums = add_sums(sums, [low.astype(F32), total * xhat, total, grad * xhat0, grad])
    copies = []
    for o in (2, 3, 1):
        b = (t + o) % 4
        cp = remote(n.ksend.at[b], n.krecv.at[block_rows(t, rows)], n.k_s.at[o], n.k_r.at[o], (d, b))
        cp.start()
        copies.append(cp)
    n.krecv[block_rows(t, rows), :] = n.ksend[t]
    bias_skip, gain_first, offset_first, gain_skip, offset_skip = sums
    n.tile[...] = offset_first
    n.tile_land[t] = n.tile[...]
    tiles = []
    for o in (1, 2, 3):
        cp = remote(n.tile, n.tile_land.at[t], n.t_s.at[o], n.t_r.at[o], (d, (t + o) % 4))
        cp.start()
        tiles.append(cp)
    n.pack[...] = jnp.zeros(n.pack.shape, F32)
    lines = [gain_skip, gain_first, offset_skip, offset_first, bias_skip, n.gain_third[...], n.gain_fourth[...],
             n.offset_third[...], n.offset_fourth[...], n.bias_attn[...], n.bias_cross_out[...], n.bias_mlp[...]]
    for i, v in enumerate(lines):
        n.pack[i // PACK_ROWS, pl.ds(i % PACK_ROWS, 1), :] = v
    heads_at = len(lines)
    for i, v in enumerate((n.self_gains, n.cross_gains, n.self_offsets, n.cross_offsets)):
        for r in range(2):
            n.pack[heads_at // PACK_ROWS, pl.ds(heads_at % PACK_ROWS, 1), pl.ds((2 * i + r) * LANES, LANES)] = v[pl.ds(r, 1), :]
    span = n.project_wide.shape[2]
    wide = [n.self_sums[:, pl.ds(0, span)], n.self_sums[:, pl.ds(2 * span, span)], n.cross_sums[...], n.text_sums[...]]
    hidden = n.bias_hidden.shape[1]
    for s in range(4):
        seat = (t == s).astype(F32)
        block, row = divmod(PACK_SUMS + 4 * s, PACK_ROWS)
        for i, v in enumerate(wide):
            n.pack[block, pl.ds(row, 1), pl.ds(i * cols, cols)] = seat * exact(v, n.unfold[...])
        for i, start in enumerate(range(0, hidden, width)):
            count = min(width, hidden - start)
            n.pack[block, pl.ds(row + 1 + i, 1), pl.ds(0, count)] = seat * n.bias_hidden[:, pl.ds(start, count)]
    shares = []
    for o in (1, 2, 3):
        b = (t + o) % 4
        cp = remote(n.pack.at[b], n.pack_in_land.at[t], n.ps_s.at[o], n.ps_r.at[o], (d, b))
        cp.start()
        shares.append(cp)
    n.pack_in_land[t] = n.pack[t]
    if own:
        scatters[1].steps()
    for cp in copies:
        cp.wait_recv()
    reduce.sent()
    for cp in tiles:
        cp.wait_recv()
    n.low_out[...] = (n.tile_land[0] + n.tile_land[1] + n.tile_land[2] + n.tile_land[3]).astype(BF16).astype(F32)
    for cp in shares:
        cp.wait_recv()
    n.pack_mine[...] = n.pack_in_land[0] + n.pack_in_land[1] + n.pack_in_land[2] + n.pack_in_land[3]
    if own:
        n.low_land[d] = n.low_out[...]
        lows = ToAll(place, lambda q: n.low_out, n.low_land, n.l_s, n.l_r)
        pack_cp = remote(n.pack_mine, n.pack_x, n.px_s.at[0], n.px_r.at[0], place.pair)
        pack_cp.start()
    n.need(n.joined0, n.joined1)
    k_all = n.krecv[...]
    count = n.grad_skip_w.shape[0] // 2
    for h, joined in enumerate((n.joined0, n.joined1)):
        n.grad_skip_w[pl.ds(h * count, count)] = (
            dot_tn(joined[...], k_all).astype(BF16).reshape((count,) + n.grad_skip_w.shape[1:])
        )
    if own:
        scatter(n.grad_skip_w, n.skip_bufs)
    n.need(n.skip_w)
    halves = [TensorSum(*n.sum), TensorSum(*n.sum1)]
    for h, half in enumerate(halves):
        half.start(lambda here, h=h: dot_nt(n.krecv[here, :], n.skip_w[pl.ds(h * width, width), :]))
    if own:
        pack_cp.wait_recv()
        pack_cp.wait_send()
        n.pack_mine[...] = n.pack_mine[...] + n.pack_x[...]
        n.pack_z[place.zi] = n.pack_mine[...]
        packs = []
        for j in range(1, place.line):
            cp = remote(n.pack_mine, n.pack_z.at[place.zi], n.pz_s.at[j], n.pz_r.at[j], (place.ahead(j), place.t))
            cp.start()
            packs.append(cp)
        scatters[2].steps()
        scatters[3].steps()
        scatters[4].steps()
        for cp in packs:
            cp.wait_recv()
            cp.wait_send()
        n.pack_mine[...] = sum(n.pack_z[i] for i in range(place.line))
    n.pack_t[t] = n.pack_mine[...]
    ends = []
    for o in (1, 2, 3):
        cp = remote(n.pack_mine, n.pack_t.at[t], n.pt_s.at[o], n.pt_r.at[o], (d, (t + o) % 4))
        cp.start()
        ends.append(cp)
    if own:
        lows.arrived()
        low_all = jnp.concatenate([n.low_land[i] for i in range(dp)], axis=0)
        n.shift_grad[...] = dot_tn(n.silu[...], low_all.astype(BF16))
        n.shift_bias[...] = jnp.sum(low_all, axis=0, keepdims=True)
        n.out_mine[...] = scatters[0].result()
        for i in range(3):
            n.project_mine[i] = scatters[1 + i].result()
    else:
        n.shift_grad[...] = n.low_out[...]
        n.shift_bias[...] = n.low_out[...]
    for half, out in zip(halves, (n.grad_latent, n.grad_skip)):
        for k in range(CHUNKS):
            sl, total = half.chunk(k)
            out[sl, :] = total
        half.sent()
        n.done(out)
    for cp in ends:
        cp.wait_recv()
        cp.wait_send()
    n.pack_out[...] = n.pack_t[...]
    if own:
        n.skip_mine[...] = scatters[4].result()
        for s in scatters:
            s.sent()
        lows.sent()
    for cp in copies + tiles + shares:
        cp.wait_send()


def finish_body(hidden, n):
    r, cols = n.o_query.shape
    pairs = [(n.out_mine, n.o_out), (n.down_mine, n.o_down), (n.project_mine, n.o_project), (n.block_out, n.o_block), (n.grad_latent, n.o_latent), (n.grad_skip, n.o_skip), (n.skip_mine, n.o_skip_mine),
             (n.shift_grad, n.o_shift), (n.up_mine, n.o_up)]
    for source, out in pairs:
        out[...] = source[...]
    n.o_query[...] = n.few_mine[pl.ds(r, r), :]
    n.o_cross_out[...] = n.few_mine[pl.ds(0, r), :]
    for i in range(2):
        count = n.o_keyval.shape[2]
        n.o_keyval[i] = n.few_mine[pl.ds(2 * r + i * count, count), :].T
    n.o_text[...] = n.text_part[pl.ds(0, n.o_text.shape[0]), :]
    row = lambda i: n.pack[i // PACK_ROWS, pl.ds(i % PACK_ROWS, 1), :]
    for out, places in ((n.norm_gain, (0, 1, 5, 6)), (n.norm_bias, (2, 3, 7, 8)), (n.row_bias, (9, 10, 11))):
        for i, at in enumerate(places):
            out[pl.ds(i, 1), :] = row(at)
    n.row_bias[pl.ds(3, 1), :] = n.shift_bias[...]
    packed = row(12)
    for k, out in enumerate((n.head_gain, n.head_bias)):
        for i in range(4):
            at = (4 * k + i) * LANES
            out[pl.ds(i, 1), :] = exact(packed[:, at : at + LANES], n.unfold[...])
    width = packed.shape[1]
    for s in range(4):
        at = PACK_SUMS + 4 * s
        columns = row(at)
        for i in range(4):
            n.column_bias[pl.ds(i, 1), pl.ds(s * cols, cols)] = columns[:, i * cols : (i + 1) * cols]
        for i, start in enumerate(range(0, hidden, width)):
            count = min(width, hidden - start)
            n.hidden_bias[:, pl.ds(s * hidden + start, count)] = row(at + 1 + i)[:, :count]
    n.column_bias[pl.ds(4, 1), :] = row(4)


def fold_matrix(heads, size):
    out = np.zeros((heads * size, heads * LANES), np.float32)
    for h in range(heads):
        for e in range(size):
            out[h * size + e, h * LANES + (e % 2) * (LANES // 2) + e // 2] = 1.0
    return out


def body(
    latent, skip_states, text_states, condition, teacher, loss_mask, true_counts, positions,
    skip_proj, shift_proj, self_project, self_output, cross_query, cross_keyval, cross_output, hidden_up, hidden_down,
    norm_gain, norm_bias, head_gain, head_bias, column_bias, hidden_bias, row_bias,
):
    d, t = lax.axis_index("dp"), lax.axis_index("tensor")
    dp, tensor = lax.axis_size("dp"), lax.axis_size("tensor")
    rows, width = latent.shape
    group = rows * tensor
    size = head_gain.shape[1]
    cols = self_project.shape[2]
    heads = cols // size
    span = heads * LANES
    hidden = hidden_up.shape[1]
    text_len, text_width = text_states.shape[1:]
    text_pad = -(-text_len // 16) * 16
    scale = size ** (-0.5)
    block = min(256, group)
    r, text_share = shift_proj.shape[0], cross_keyval.shape[0]
    own = r % 16 == 0 and text_share % 16 == 0 and skip_proj.shape[0] % 32 == 0 and dp == 8
    parts = dp if own else 1
    line = max(dp // 2, 1) if own else 1
    dma, vm = pltpu.SemaphoreType.DMA, pltpu.VMEM
    few = lambda *shape: shape if own else (16, LANES)

    fold_np = fold_matrix(heads, size)
    fold = jnp.asarray(fold_np, BF16)
    one_np = fold_np[:size, :LANES]
    mask = jnp.asarray(one_np.sum(0, keepdims=True), F32)
    quarter = size // 4
    lane_np = np.zeros((2, LANES), np.float32)
    sign_np = np.zeros((1, LANES), np.float32)
    for i in range(size // 2):
        f = np.float32(10000.0 ** (-(i % quarter) / quarter))
        for half in range(2):
            lane_np[i // quarter, half * (LANES // 2) + i] = f
            sign_np[0, half * (LANES // 2) + i] = 2 * half - 1
    lanes_in = jnp.asarray(np.concatenate([lane_np, sign_np]))
    one = jnp.asarray(one_np)

    project_in = jnp.transpose(self_project, (1, 0, 2))
    shards = [self_output.T, cross_query, cross_output.T, jnp.transpose(cross_keyval, (1, 0, 2)), hidden_up, hidden_down.T]
    if own:
        small_shape = (dp, 1, -(-r // LANES) * LANES + LANES)
        skip_in, shift_in = skip_proj, shift_proj
    else:
        small_all = lax.all_gather(
            jnp.concatenate([condition.astype(F32), true_counts.astype(F32)[:, None]], axis=1), "dp", axis=0, tiled=True
        )
        silu_all = jax.nn.silu(small_all[:, :width]).astype(BF16)
        silu = lax.dynamic_slice_in_dim(silu_all, d * r, r, 1)
        shift_in = lax.psum_scatter(dot_nn(silu, shift_proj), "dp", scatter_dimension=0, tiled=True) + row_bias[3:4]
        small_shape = (1, 8, LANES)
        skip_in = lax.all_gather(skip_proj, "dp", axis=0, tiled=True)
        project_in = lax.all_gather(project_in, "dp", axis=1, tiled=True)
        shards = [lax.all_gather(v, "dp", axis=v.ndim - 2, tiled=True) for v in shards]
    early_rows = 128 if own else r
    full = shaped((group, width), BF16)
    mine = shaped((rows, width), F32)
    mine_low = shaped((rows, width), BF16)
    line_sum = shaped((1, width), F32)
    lse_shape = shaped((group // block, heads, block), F32)
    sum_scratch = TensorSum.scratch(rows, width)
    first = named_kernel(
        "first", 0, functools.partial(first_body, dp, own, size, scale, heads, block),
        dict(
            latent=hbm(latent), skip_states=hbm(skip_states), skip_in=hbm(skip_in) if own else skip_in, project_in=hbm(project_in) if own else project_in, out_in=hbm(shards[0]) if own else shards[0],
            query_in=hbm(shards[1]), cross_out_in=hbm(shards[2]), keyval_in=hbm(shards[3]), down_in=hbm(shards[5]),
            condition=condition, true_count=true_counts[:, None], shift_in=shift_in, column_bias=column_bias, positions=positions, lanes=lanes_in,
            norm_gain=norm_gain, norm_bias=norm_bias, row_bias=row_bias, head_gain=head_gain, head_bias=head_bias,
            one=one, fold_f32=jnp.asarray(fold_np), mask=mask, fold=fold,
        ),
        dict(
            joined0=late(full), joined1=late(full), skip_full=late(shaped(few(dp, skip_proj.shape[0], cols), BF16)), skipped=late(mine_low),
            residual=late(mine), first_all=late(full), silu=shaped(few(dp, r), BF16), counted=shaped((1, LANES), F32),
            project_wide=late(shaped((3, width, span), BF16)), pre=late(shaped((group, 2 * span), F32)),
            low=late(shaped((group, 3 * span), BF16)), mixed=late(shaped((group, cols), BF16)), lse=lse_shape,
            out_land=shaped(few(dp, r, cols), BF16), query_g=hbm(shaped(few(dp, r, cols), BF16)),
            key_g=hbm(shaped(few(dp, text_share, cols), BF16)), value_g=hbm(shaped(few(dp, text_share, cols), BF16)),
            cross_out_g=hbm(shaped(few(dp, r, cols), BF16)), down_g=hbm(shaped(few(dp, early_rows, hidden), BF16)), third_all=full, second=late(mine),
            gain_wide=shaped((4, LANES), F32), offset_wide=shaped((4, LANES), F32), bias_wide=shaped((column_bias.shape[0], span), F32),
            cosine=late(shaped((group, LANES), F32)), sine=late(shaped((group, LANES), F32)),
        ),
        dict(
            p_land=vm(few(dp, 3, r, cols), BF16), padded=vm((group, span), BF16), skip_send=vm((4, rows, cols), BF16),
            skip_recv=vm((4, rows, cols), BF16), small=vm(small_shape, F32), small_land=vm(small_shape, F32), shift_part=vm((dp, 1, width), F32),
            shift_land=vm((dp, 1, width), F32), sum=sum_scratch, own_sem=dma((10,)), a_s=dma((dp,)),
            a_r=dma((dp,)), b_s=dma((dp,)), b_r=dma((dp,)), p_s=dma((4,)), p_r=dma((4,)), gather_sems=Gathers.scratch(13),
            spread0=RowSpread.scratch(1),
            spread1=RowSpread.scratch(1), spread2=RowSpread.scratch(), spread3=RowSpread.scratch(),
        ),
    )
    if own:
        silu, counted = first.silu, first.counted
        skip_full = first.skip_full.reshape(2 * width, cols)
        out_t, query, cross_out_t = [v.reshape(width, cols) for v in (first.out_land, first.query_g, first.cross_out_g)]
        key, value = [v.reshape(text_width, cols) for v in (first.key_g, first.value_g)]
    else:
        counted, skip_full = jnp.full((1, LANES), jnp.sum(small_all[:, width])), skip_in
        out_t, query, cross_out_t, (key, value), up_full, down_t = shards

    text = jnp.pad(text_states[0], ((0, text_pad - text_len), (0, 0)))
    cross = named_kernel(
        "cross", 1, functools.partial(cross_body, dp, own, size, scale, heads, block, text_len),
        dict(
            query=late(query), key=late(key), value=late(value), cross_out=late(cross_out_t), up_in=hbm(shards[4]), down_in=hbm(shards[5]), text=late(text), third_all=late(first.third_all),
            bias_wide=first.bias_wide, cosine=late(first.cosine), sine=late(first.sine), norm_gain=norm_gain,
            norm_bias=norm_bias, row_bias=row_bias, head_gain=first.gain_wide, head_bias=first.offset_wide, mask=mask, fold=fold,
            second=late(first.second),
        ),
        dict(
            query_wide=late(shaped((width, span), BF16)), keyval_wide=late(shaped((2, text_width, span), BF16)),
            text_pre=shaped((text_pad, span), F32), text_low=shaped((text_pad, 2 * span), BF16),
            pre=late(shaped((group, span), F32)), low=late(shaped((group, span), BF16)), mixed=late(shaped((group, cols), BF16)),
            lse=lse_shape, fourth_all=full, third_sum=mine,
            up_g=hbm(shaped(few(dp, r, hidden), BF16)), down_g=hbm(shaped(few(dp, r - early_rows, hidden), BF16)),
        ),
        dict(
            padded=vm((group, span), BF16), sum=sum_scratch, spread=RowSpread.scratch(),
            gather_sems=Gathers.scratch(5), own_sem=dma((2,)),
        ),
    )
    if own:
        up_full = cross.up_g.reshape(width, hidden)
        down_ins = dict(down_a=hbm(first.down_g), down_b=hbm(cross.down_g))
        down_scratch = dict(down_t=vm((dp, r, hidden), BF16), down_sem=dma((2,)))
    else:
        down_ins, down_scratch = dict(down_t=down_t), {}

    feed = named_kernel(
        "feed", 2, functools.partial(feed_body, own),
        dict(
            fourth_all=late(cross.fourth_all), up=late(up_full), hidden_bias=hidden_bias.reshape(-1, LANES), **down_ins, third_sum=late(cross.third_sum),
            row_bias=row_bias, teacher=late(teacher), loss_mask=loss_mask[None], true_count=true_counts[:, None],
            counted=counted, total=jnp.full((1, 1), dp * group, F32),
        ),
        dict(
            active=late(shaped((group, hidden), BF16)), slope=late(shaped((group, hidden), BF16)), grad_all=full, block_out=late(mine_low),
            grad_final=late(mine), bias_mlp=line_sum,
        ),
        dict(sum=sum_scratch, spread=RowSpread.scratch(), **down_scratch),
    )

    back = named_kernel(
        "feed_back", 3, functools.partial(feed_back_body, dp, own),
        dict(
            grad_all=late(feed.grad_all), active=late(feed.active), **down_ins, slope=late(feed.slope), up=late(up_full),
            fourth_all=late(cross.fourth_all), third_sum=late(cross.third_sum), norm_gain=norm_gain, grad_final=late(feed.grad_final),
        ),
        dict(
            c_all=full, grad_third=mine, sum0=line_sum, sum1=line_sum, sum2=line_sum, bias_hidden=shaped((1, hidden), F32),
            grad_up=late(shaped((parts, width // parts, hidden), BF16)),
            **(dict(down_mine=shaped((r, hidden), F32)) if own else dict(grad_down=shaped((1, width, hidden), BF16))),
        ),
        dict(
            upper=vm((group, hidden), BF16), sum=sum_scratch, spread=RowSpread.scratch(), **down_scratch,
            **(dict(grad_down=vm((dp, r, hidden), BF16), down_bufs=GradScatter.buffers((r, hidden)), down_sems=GradScatter.scratch()) if own else {}),
        ),
    )
    bias_cross_out, gain_fourth, offset_fourth = back.sum0, back.sum1, back.sum2

    few_rows = 2 * r + 2 * text_share if own else 2 * width + 2 * text_width
    cback = named_kernel(
        "cross_back", 4, functools.partial(cross_back_body, dp, own, size, scale, heads, block, text_len),
        dict(
            c_all=late(back.c_all), cross_out=late(cross_out_t), low=late(cross.low), text_low=late(cross.text_low), pre=late(cross.pre),
            text_pre=late(cross.text_pre), lse=cross.lse, cosine=late(first.cosine), sine=late(first.sine), head_gain=first.gain_wide, mask=mask, fold=fold,
            mixed=late(cross.mixed), third_all=late(first.third_all), text=late(text), keyval_wide=late(cross.keyval_wide),
            query_wide=late(cross.query_wide), second=late(first.second), norm_gain=norm_gain, grad_third=late(back.grad_third),
            **(dict(grad_up=hbm(back.grad_up)) if own else {}),
        ),
        dict(
            grads=late(shaped((parts, few_rows, cols), BF16)), grad_text=shaped((text_pad, text_width), BF16),
            gains=shaped((2, LANES), F32), offsets=shaped((2, LANES), F32), sums=shaped((1, span), F32),
            text_sums=shaped((1, span), F32), s_all=full, grad_second=mine, sum0=line_sum, sum1=line_sum, sum2=line_sum,
            **(dict(up_mine=shaped((r, hidden), F32)) if own else {}),
        ),
        dict(
            p=vm((group, span), BF16), do=vm((group, span), BF16), dq=vm((group, span), F32), dk=vm((text_pad, span), F32),
            dv=vm((text_pad, span), F32), text_p=vm((text_pad, 2 * span), BF16), sum=sum_scratch, spread=RowSpread.scratch(),
            **(dict(up_bufs=GradScatter.buffers((r, hidden)), up_sems=GradScatter.scratch()) if own else {}),
        ),
    )
    few_grads = cback.grads
    if not own:
        cuts = np.cumsum([0, width, width, text_width, text_width])
        few_grads = jnp.concatenate(
            [few_grads[0, a:b].reshape(dp, -1, cols) for a, b in zip(cuts[:-1], cuts[1:])], axis=1
        )
        few_mine = lax.psum_scatter(few_grads.reshape(-1, cols), "dp", scatter_dimension=0, tiled=True).astype(F32)
        down_mine = lax.psum_scatter(back.grad_down[0], "dp", scatter_dimension=0, tiled=True).astype(F32)
        up_mine = lax.psum_scatter(back.grad_up[0], "dp", scatter_dimension=0, tiled=True).astype(F32)
    else:
        down_mine, up_mine = back.down_mine, cback.up_mine

    sback = named_kernel(
        "self_back", 6, functools.partial(self_back_body, dp, own, size, scale, heads, block),
        dict(
            text_part=cback.grad_text, **(dict(few_grads=hbm(few_grads)) if own else {}),
            s_all=late(cback.s_all), out_t=late(out_t), low=late(first.low), pre=late(first.pre), lse=first.lse, cosine=late(first.cosine), sine=late(first.sine),
            head_gain=first.gain_wide, mask=mask, fold=fold, mixed=late(first.mixed), first_all=late(first.first_all),
        ),
        dict(
            p=late(shaped((group, 3 * span), BF16)), grad_out=late(shaped((parts, width // parts, cols), BF16)),
            grad_project=late(shaped((parts, 3, width // parts, cols), BF16)), gains=shaped((2, LANES), F32),
            offsets=shaped((2, LANES), F32), sums=shaped((1, 3 * span), F32), grad_text=shaped((text_pad, text_width), F32),
            **(dict(few_mine=shaped((few_rows, cols), F32)) if own else {}),
        ),
        dict(
            do=vm((group, span), BF16), dq=vm((group, span), F32), dk=vm((group, span), F32), dv=vm((group, span), F32),
            p_low=vm((3, group, cols), BF16), text_total=vm((text_pad, text_width), BF16),
            text_land=vm((text_pad, text_width), BF16), text_yland=vm((piece_rows(text_pad, 2, 1), text_width), BF16),
            text_back=vm((piece_rows(text_pad, 2, 1), text_width), BF16),
            text_sems=dma((6,)),
            **(dict(few_bufs=GradScatter.buffers((few_rows, cols)), few_sems=GradScatter.scratch()) if own else {}),
        ),
    )
    if own:
        few_mine = sback.few_mine

    skip_rows = 2 * width // dp if own else width
    pack_land = vm((4, PACK_ROWS, width), F32)
    last = named_kernel(
        "last", 5, functools.partial(last_body, dp, own),
        dict(
            p=late(sback.p), project_wide=late(first.project_wide), residual=late(first.residual), grad_second=late(cback.grad_second),
            skipped=late(first.skipped), norm_gain=norm_gain, skip_w=late(skip_full), joined0=late(first.joined0), joined1=late(first.joined1),
            silu=silu, gain_third=cback.sum1, gain_fourth=gain_fourth, offset_third=cback.sum2, offset_fourth=offset_fourth,
            bias_attn=cback.sum0, bias_cross_out=bias_cross_out, bias_mlp=feed.bias_mlp, self_gains=sback.gains,
            cross_gains=cback.gains, self_offsets=sback.offsets, cross_offsets=cback.offsets, self_sums=sback.sums,
            cross_sums=cback.sums, text_sums=cback.text_sums, bias_hidden=back.bias_hidden, unfold=jnp.asarray(fold_np.T),
            grad_out=hbm(sback.grad_out), grad_project=hbm(sback.grad_project),
        ),
        dict(
            grad_latent=late(mine), grad_skip=late(mine), shift_grad=shaped((r if own else 1, width), F32), shift_bias=line_sum,
            pack_out=shaped((4, PACK_ROWS, width), F32),
            **(dict(out_mine=shaped((r, cols), F32), project_mine=shaped((3, r, cols), F32), skip_mine=shaped((skip_rows, cols), F32))
               if own else dict(grad_skip_w=shaped((2, width, cols), BF16))),
        ),
        dict(
            ksend=vm((4, rows, cols), BF16), krecv=vm((group, cols), BF16), tile=vm((1, width), F32),
            tile_land=vm((4, 1, width), F32), low_out=vm((1, width), F32),
            low_land=vm((dp if own else 1, 1, width), F32), pack=vm((4, PACK_ROWS, width), F32), pack_in_land=pack_land,
            pack_mine=vm((PACK_ROWS, width), F32), pack_x=vm((PACK_ROWS, width), F32), pack_z=pack_land, pack_t=pack_land, sum=sum_scratch, sum1=sum_scratch,
            k_s=dma((4,)), k_r=dma((4,)), t_s=dma((4,)), t_r=dma((4,)), l_s=dma((dp,)), l_r=dma((dp,)), px_s=dma((1,)),
            px_r=dma((1,)), ps_s=dma((4,)), ps_r=dma((4,)), pz_s=dma((line,)), pz_r=dma((line,)), pt_s=dma((4,)), pt_r=dma((4,)),
            **(dict(
                grad_skip_w=vm((dp, skip_rows, cols), BF16), out_bufs=GradScatter.buffers((r, cols)),
                project_bufs=GradScatter.buffers((r, cols)) * 3, skip_bufs=GradScatter.buffers((skip_rows, cols)),
                scatter_sems=GradScatter.scratch() * 5,
            ) if own else {}),
        ),
    )
    if own:
        out_mine, project_mine, skip_mine = last.out_mine, last.project_mine, last.skip_mine
        shift_grad, shift_bias, pack_sum = last.shift_grad, last.shift_bias, last.pack_out
    else:
        shift_all = lax.all_gather(last.shift_grad[:1], "dp", axis=0, tiled=True)
        shift_bias = jnp.sum(shift_all, axis=0, keepdims=True)
        shift_grad = dot_tn(silu, shift_all.astype(BF16))
        pack_sum = lax.psum(last.pack_out, "dp")
        out_mine = lax.psum_scatter(sback.grad_out[0], "dp", scatter_dimension=0, tiled=True).astype(F32)
        project_mine = lax.psum_scatter(sback.grad_project[0], "dp", scatter_dimension=1, tiled=True).astype(F32)
        skip_mine = lax.psum_scatter(last.grad_skip_w.reshape(-1, cols), "dp", scatter_dimension=0, tiled=True).astype(F32)
    end = named_kernel(
        "finish", None, functools.partial(finish_body, hidden),
        dict(
            pack=pack_sum, shift_bias=shift_bias, unfold=jnp.asarray(one_np.T), block_out=feed.block_out,
            grad_latent=last.grad_latent, grad_skip=last.grad_skip, skip_mine=skip_mine, shift_grad=shift_grad,
            up_mine=up_mine, few_mine=few_mine, text_part=sback.grad_text,
            out_mine=out_mine, down_mine=down_mine, project_mine=project_mine,
        ),
        dict(
            norm_gain=shaped(norm_gain.shape, F32), norm_bias=shaped(norm_bias.shape, F32), head_gain=shaped(head_gain.shape, F32),
            head_bias=shaped(head_bias.shape, F32), column_bias=shaped(column_bias.shape, F32), hidden_bias=shaped((1, 4 * hidden), F32),
            row_bias=shaped(row_bias.shape, F32), o_block=mine_low, o_latent=mine, o_skip=mine, o_skip_mine=shaped(skip_mine.shape, F32),
            o_shift=shaped(shift_grad.shape, F32), o_up=shaped(up_mine.shape, F32), o_query=shaped((r, cols), F32),
            o_text=shaped((text_len, text_width), F32), o_out=shaped((r, cols), F32), o_cross_out=shaped((r, cols), F32),
            o_down=shaped((r, hidden), F32), o_project=shaped((3, r, cols), F32), o_keyval=shaped((2, cols, text_share), F32),
        ),
        {},
    )
    return (
        end.o_block,
        end.o_latent,
        end.o_skip,
        end.o_text[None],
        end.o_skip_mine,
        end.o_shift,
        jnp.transpose(end.o_project, (1, 0, 2)),
        end.o_out.T,
        end.o_query,
        jnp.transpose(end.o_keyval, (2, 0, 1)),
        end.o_cross_out.T,
        end.o_up,
        end.o_down.T,
        end.norm_gain,
        end.norm_bias,
        end.head_gain,
        end.head_bias,
        end.column_bias,
        end.hidden_bias[0],
        end.row_bias,
    )


def solution(mesh):
    both = ("dp", "tensor")
    rows2, split2, cross2 = P(both, None), P("dp", "tensor"), P("tensor", "dp")
    middle = P("dp", None, "tensor")
    return jax.shard_map(
        body,
        mesh=mesh,
        in_specs=(
            rows2, rows2, P("dp", None, None), P("dp", None), rows2, P(both), P("dp"), P(None, "dp"),
            split2, P("dp", None), middle, cross2, split2, middle, cross2, split2, cross2,
            P(), P(), P(), P(), P(), P(), P(),
        ),
        out_specs=(
            rows2, rows2, rows2, P("dp", None, None),
            split2, P("dp", None), middle, cross2, split2, middle, cross2, split2, cross2,
            P(), P(), P(), P(), P(), P(), P(),
        ),
        check_vma=False,
    )
```
